32 devices in a mesh: dp: 8 (over z, y), fsdp: 4 (over x, core).
Axes of the slice: x: 2, y: 2, z: 4, core: 2. Of those that a mesh axis runs over, the one named last changes fastest.
Arguments:
- latents: bfloat16 [32, 864, 768], P(('dp', 'fsdp')), may hold values from -6 to 6
- text_rows: bfloat16 [32, 256, 768], P(('dp', 'fsdp')), may hold values from -6 to 6
- out_grad: bfloat16 [32, 864, 768], P(('dp', 'fsdp')), as said below
- frame_len: int32 [32], P(('dp', 'fsdp')), may hold values from 86 to 860, as said below
- text_len: int32 [32], P(('dp', 'fsdp')), may hold values from 77 to 256, as said below
- timestep: int32 [32], P(('dp', 'fsdp')), may hold values from 0 to 999
- w_ada: bfloat16 [768, 6912], P('dp', 'fsdp'), may hold values from -0.625 to 0.625
- w_qkv: bfloat16 [768, 2304], P('dp', 'fsdp'), may hold values from -0.21875 to 0.21875
- w_out: bfloat16 [768, 768], P('dp', 'fsdp'), may hold values from -0.625 to 0.625
- w_cq: bfloat16 [768, 768], P('dp', 'fsdp'), may hold values from -0.21875 to 0.21875
- w_ckv: bfloat16 [768, 1536], P('dp', 'fsdp'), may hold values from -0.21875 to 0.21875
- w_cout: bfloat16 [768, 768], P('dp', 'fsdp'), may hold values from -0.625 to 0.625
- w_fc1: bfloat16 [768, 3072], P('dp', 'fsdp'), may hold values from -0.21875 to 0.21875
- w_fc2: bfloat16 [3072, 768], P('dp', 'fsdp'), may hold values from -0.109375 to 0.109375
Outputs:
- layer_out: float32 [32, 864, 768], P(('dp', 'fsdp'))
- latent_grad: float32 [32, 864, 768], P(('dp', 'fsdp'))
- text_grad: float32 [32, 256, 768], P(('dp', 'fsdp'))
- grad_ada: float32 [768, 6912], P('dp', 'fsdp')
- grad_qkv: float32 [768, 2304], P('dp', 'fsdp')
- grad_out: float32 [768, 768], P('dp', 'fsdp')
- grad_cq: float32 [768, 768], P('dp', 'fsdp')
- grad_ckv: float32 [768, 1536], P('dp', 'fsdp')
- grad_cout: float32 [768, 768], P('dp', 'fsdp')
- grad_fc1: float32 [768, 3072], P('dp', 'fsdp')
- grad_fc2: float32 [3072, 768], P('dp', 'fsdp')
The draws below stay inside these ranges and needn't reach their ends.
Inputs may be any that keep to these rules, and one draw needn't show every extreme that they name: A clip's frames fill slots 0 to frame_len - 1; some clip has exactly 860 frames. A clip's text rows fill slots 0 to text_len - 1; some clip uses all 256 slots. out_grad is exactly zero at every slot >= frame_len of its clip.
All inputs are finite; a program needn't handle non-finite values.
Results may differ from the reference program's by a relative error of at most 0.034.
Values may be sent and summed in bfloat16 or wider, within the bound.
A program may use at most 192 MiB of HBM per device.

```python
import math
import jax
import jax.numpy as jnp
from jax import lax

D = 768
HEADS = 12
FF = 3072
E = 768
SLOTS = 864
TEXT = 256
CLIPS = 32


def frame_lengths(key):
    key = jax.random.fold_in(key, 17)
    key_lens, key_pick = jax.random.split(key)
    lengths = jax.random.randint(key_lens, (CLIPS,), SLOTS // 10, SLOTS - 3)
    chosen = jax.random.randint(key_pick, (), 0, CLIPS)
    return jnp.where(jnp.arange(CLIPS) == chosen, SLOTS - 4, lengths).astype(jnp.int32)


def draw_frame_len(key, part):
    return frame_lengths(key)


def draw_out_grad(key, part):
    lengths = frame_lengths(key)
    key = jax.random.fold_in(key, 41)
    values = jnp.clip(jax.random.normal(key, (CLIPS, SLOTS, D), jnp.float32), -6.0, 6.0)
    live = jnp.arange(SLOTS)[None, :] < lengths[:, None]
    return jnp.where(live[:, :, None], values, 0.0).astype(jnp.bfloat16)


def draw_text_len(key, part):
    key = jax.random.fold_in(key, 29)
    key_lens, key_pick = jax.random.split(key)
    lengths = jax.random.randint(key_lens, (CLIPS,), TEXT * 3 // 10 + 1, TEXT + 1)
    chosen = jax.random.randint(key_pick, (), 0, CLIPS)
    return jnp.where(jnp.arange(CLIPS) == chosen, TEXT, lengths).astype(jnp.int32)


def with_ends(drawn, key, low, high):
    longest = drawn.shape.index(max(drawn.shape))
    spots = []
    for shift in (0, 1):
        where = [jax.random.randint(jax.random.fold_in(key, axis), (), 0, length) for axis, length in enumerate(drawn.shape)]
        where[longest] = (where[longest] + shift) % drawn.shape[longest]
        spots.append(tuple(where))
    return drawn.at[spots[0]].set(low).at[spots[1]].set(high)


def levels(stream_key, shape, cuts, low, top_value):
    level = 1.0
    for position, parts in cuts:
        heights = jax.random.uniform(jax.random.fold_in(jax.random.fold_in(stream_key, 6), position), (parts,), jnp.float32, low / len(cuts), top_value / len(cuts))
        level = level * jnp.repeat(jnp.exp(heights), shape[position] // parts).reshape((-1,) + (1,) * (len(shape) - 1 - position))
    return level


def scatter_about(own_key, extent, deviation, limit, cuts=(), held_as=jnp.bfloat16):
    drawn = deviation * jax.random.normal(own_key, extent, jnp.float32)
    if cuts:
        drawn = drawn * levels(own_key, extent, cuts, -0.22, 0.18)
    return jnp.clip(drawn, -limit, limit).astype(held_as)


def setup_inputs(seed: int = 0) -> dict:
    key_list = jax.random.split(jax.random.key(seed), 15)
    return {
        "latents": scatter_about(key_list[0], (CLIPS, SLOTS, D), 1.0, 6.0, ((0, 32),)),
        "text_rows": scatter_about(key_list[1], (CLIPS, TEXT, E), 1.0, 6.0, ((0, 32),)),
        "out_grad": draw_out_grad(jax.random.fold_in(key_list[14], 71), 0),
        "frame_len": draw_frame_len(jax.random.fold_in(key_list[14], 71), 0),
        "text_len": draw_text_len(jax.random.fold_in(key_list[14], 71), 0),
        "timestep": with_ends(jax.random.randint(key_list[5], (CLIPS,), 0, 1000), jax.random.fold_in(key_list[5], 1), 0, 999).astype(jnp.int32),
        "w_ada": scatter_about(key_list[6], (D, 9 * D), (D // 8) ** -0.5, 0.625, ((0, 8), (1, 4))),
        "w_qkv": scatter_about(key_list[7], (D, 3 * D), D ** -0.5, 0.21875, ((0, 8), (1, 4))),
        "w_out": scatter_about(key_list[8], (D, D), (D // 8) ** -0.5, 0.625, ((0, 8), (1, 4))),
        "w_cq": scatter_about(key_list[9], (D, D), D ** -0.5, 0.21875, ((0, 8), (1, 4))),
        "w_ckv": scatter_about(key_list[10], (E, 2 * D), E ** -0.5, 0.21875, ((0, 8), (1, 4))),
        "w_cout": scatter_about(key_list[11], (D, D), (D // 8) ** -0.5, 0.625, ((0, 8), (1, 4))),
        "w_fc1": scatter_about(key_list[12], (D, FF), D ** -0.5, 0.21875, ((0, 8), (1, 4))),
        "w_fc2": scatter_about(key_list[13], (FF, D), FF ** -0.5, 0.109375, ((0, 8), (1, 4))),
    }


@jax.custom_vjp
def low(v):
    return lax.optimization_barrier(v.astype(jnp.bfloat16)).astype(jnp.float32)

@jax.custom_vjp
def low_back(v):
    return v

def low_keep(v):
    return (low(v), None)

def low_pass(kept, grad):
    return (grad,)

def back_keep(v):
    return (v, None)

def back_low(kept, grad):
    return (low(grad),)
low.defvjp(low_keep, low_pass)
low_back.defvjp(back_keep, back_low)
highest = lax.Precision.HIGHEST
norm_eps = 1e-06

def sinusoid(time_value, model_width):
    half_width = model_width // 2
    frequency = jnp.exp(-math.log(10000.0) * jnp.arange(half_width, dtype=jnp.float32) / half_width)
    angles = time_value.astype(jnp.float32) * frequency
    return jnp.concatenate([jnp.cos(angles), jnp.sin(angles)], axis=-1)

def normalize(values):
    center = values - lax.optimization_barrier(jnp.mean(values, -1, keepdims=True))
    spread = lax.optimization_barrier(jnp.mean(center * center, -1, keepdims=True))
    return center * lax.rsqrt(spread + norm_eps)

def attention(queries, key_rows, value_rows, key_valid):
    factor = queries.shape[-1] ** (-0.5)
    scores = jnp.einsum('shd,thd->hst', queries, key_rows, precision=highest) * factor
    scores = low_back(scores)
    scores = jnp.where(key_valid[None, None, :], scores, -1e+30)
    shares = low(jax.nn.softmax(scores, axis=-1))
    mixed_heads = jnp.einsum('hst,thd->shd', shares, value_rows, precision=highest)
    return mixed_heads.reshape(mixed_heads.shape[0], -1)

def clip_forward(params, latent, text_block, frame_count, text_count, time_value):
    w_ada, w_qkv, w_out, w_cq, w_ckv, w_cout, w_fc1, w_fc2 = params
    model_width = latent.shape[-1]
    slot_count = latent.shape[0]
    text_slots = text_block.shape[0]
    frame_valid = jnp.arange(slot_count) < frame_count
    text_valid = jnp.arange(text_slots) < text_count
    condition = low(jax.nn.silu(sinusoid(time_value, model_width)))
    modulation = low_back(jnp.dot(condition[None, :], w_ada, precision=highest)).reshape(9, model_width)
    hidden = low(normalize(latent) * (1.0 + modulation[1]) + modulation[0])
    packed = low(low_back(jnp.dot(hidden, w_qkv, precision=highest))).reshape(slot_count, 3, HEADS, -1)
    mixed_heads = low(low_back(attention(packed[:, 0], packed[:, 1], packed[:, 2], frame_valid)))
    branch = low_back(jnp.dot(mixed_heads, w_out, precision=highest))
    after_self = latent + modulation[2] * branch
    hidden = low(normalize(after_self) * (1.0 + modulation[4]) + modulation[3])
    queries = low(low_back(jnp.dot(hidden, w_cq, precision=highest))).reshape(slot_count, HEADS, -1)
    memory = low(low_back(jnp.dot(low(text_block), w_ckv, precision=highest))).reshape(text_slots, 2, HEADS, -1)
    mixed_heads = low(low_back(attention(queries, memory[:, 0], memory[:, 1], text_valid)))
    branch = low_back(jnp.dot(mixed_heads, w_cout, precision=highest))
    after_cross = after_self + modulation[5] * branch
    hidden = low(normalize(after_cross) * (1.0 + modulation[7]) + modulation[6])
    pre_gelu = low_back(jnp.dot(hidden, w_fc1, precision=highest))
    activated = low(jax.nn.gelu(pre_gelu, approximate=True))
    branch = low_back(jnp.dot(activated, w_fc2, precision=highest))
    return after_cross + modulation[8] * branch

def reference(latents, text_rows, out_grad, frame_len, text_len, timestep, w_ada, w_qkv, w_out, w_cq, w_ckv, w_cout, w_fc1, w_fc2):
    weights = tuple((matrix.astype(jnp.float32) for matrix in (w_ada, w_qkv, w_out, w_cq, w_ckv, w_cout, w_fc1, w_fc2)))

    def one_clip(params, packed):
        return clip_forward(params, *packed)
    checkpointed = jax.checkpoint(one_clip)

    def whole_batch(params, frames, text_batch):

        def mapped(packed):
            return checkpointed(params, packed)
        return lax.map(mapped, (frames, text_batch, frame_len, text_len, timestep))
    forward, pullback = jax.vjp(whole_batch, weights, latents.astype(jnp.float32), text_rows.astype(jnp.float32))
    weight_grads, latent_grad, text_grad = pullback(out_grad.astype(jnp.float32))
    return (forward, latent_grad, text_grad, weight_grads[0], weight_grads[1], weight_grads[2], weight_grads[3], weight_grads[4], weight_grads[5], weight_grads[6], weight_grads[7])
```

```python
import functools
import math

import jax
import jax.numpy as jnp
from jax import lax
from jax.experimental import pallas as pl
from jax.experimental.pallas import tpu as pltpu
from jax.sharding import PartitionSpec as P

HEADS = 12


norm_eps = 1e-06


def sinusoid(time_value, model_width):
    half_width = model_width // 2
    frequency = jnp.exp(-math.log(10000.0) * jnp.arange(half_width, dtype=jnp.float32) / half_width)
    angles = time_value.astype(jnp.float32) * frequency
    return jnp.concatenate([jnp.cos(angles), jnp.sin(angles)], axis=-1)


def normalize(values):
    center = values - jnp.mean(values, -1, keepdims=True)
    spread = jnp.mean(center * center, -1, keepdims=True)
    inverse = lax.rsqrt(spread + norm_eps)
    return (center * inverse, inverse)


def norm_back(upstream, normed, inverse, scale_row):
    dshift = jnp.sum(upstream, 0)
    dscale = jnp.sum(upstream * normed, 0)
    scaled = upstream * (1.0 + scale_row)
    centered = (
        scaled
        - jnp.mean(scaled, -1, keepdims=True)
        - normed * jnp.mean(scaled * normed, -1, keepdims=True)
    )
    return (inverse * centered, dshift, dscale)


def outer_sum(left, right):
    return lax.dot_general(
        left, right, (((0,), (0,)), ((), ())), preferred_element_type=jnp.float32
    )


def through(gradient, matrix):
    return lax.dot_general(
        gradient, matrix, (((1,), (1,)), ((), ())), preferred_element_type=jnp.float32
    )


def gelu_tanh(values):
    return jax.nn.gelu(values, approximate=True)


def group_count(head_count):
    return head_count // 4


def split_groups(array, groups):
    rows, head_count, head_size = array.shape
    return jnp.moveaxis(array.reshape(rows, groups, head_count // groups, head_size), 1, 0)


def join_groups(array):
    return jnp.moveaxis(array, 0, 1).reshape(array.shape[1], -1)


def attend_forward(query_rows, key_rows, value_rows, key_valid):
    factor = query_rows.shape[-1] ** (-0.5)
    groups = group_count(query_rows.shape[1])

    def one_group(packed):
        query_part, key_part, value_part = packed
        scores = (
            jnp.einsum("shd,thd->hst", query_part, key_part, preferred_element_type=jnp.float32)
            * factor
        )
        scores = jnp.where(key_valid[None, None, :], scores, -1e30)
        largest = jnp.max(scores, -1, keepdims=True)
        exponent = jnp.exp(scores - largest)
        summed = jnp.sum(exponent, -1, keepdims=True)
        shares = (exponent / summed).astype(jnp.bfloat16)
        mixed_part = jnp.einsum(
            "hst,thd->shd", shares, value_part, preferred_element_type=jnp.float32
        )
        return (mixed_part.astype(jnp.bfloat16), (largest + jnp.log(summed))[..., 0])

    mixed_heads, log_total = lax.map(
        one_group,
        (
            split_groups(query_rows, groups),
            split_groups(key_rows, groups),
            split_groups(value_rows, groups),
        ),
    )
    return (join_groups(mixed_heads), log_total)


def attend_back(query_rows, key_rows, value_rows, key_valid, log_total, upstream):
    factor = query_rows.shape[-1] ** (-0.5)
    groups = group_count(query_rows.shape[1])
    upstream_heads = upstream.reshape(query_rows.shape)

    def one_group(packed):
        query_part, key_part, value_part, log_part, upstream_part = packed
        scores = (
            jnp.einsum("shd,thd->hst", query_part, key_part, preferred_element_type=jnp.float32)
            * factor
        )
        scores = jnp.where(key_valid[None, None, :], scores, -1e30)
        shares = jnp.exp(scores - log_part[..., None])
        share_grad = jnp.einsum(
            "shd,thd->hst", upstream_part, value_part, preferred_element_type=jnp.float32
        )
        score_grad = (
            shares * (share_grad - jnp.sum(shares * share_grad, -1, keepdims=True))
        ).astype(jnp.bfloat16)
        query_grad = (
            jnp.einsum("hst,thd->shd", score_grad, key_part, preferred_element_type=jnp.float32)
            * factor
        )
        key_grad = (
            jnp.einsum("hst,shd->thd", score_grad, query_part, preferred_element_type=jnp.float32)
            * factor
        )
        value_grad = jnp.einsum(
            "hst,shd->thd",
            shares.astype(jnp.bfloat16),
            upstream_part,
            preferred_element_type=jnp.float32,
        )
        return (query_grad, key_grad, value_grad)

    query_grad, key_grad, value_grad = lax.map(
        one_group,
        (
            split_groups(query_rows, groups),
            split_groups(key_rows, groups),
            split_groups(value_rows, groups),
            log_total,
            split_groups(upstream_heads, groups),
        ),
    )
    return (join_groups(query_grad), join_groups(key_grad), join_groups(value_grad))


MESH = pl.DeviceIdType.MESH


class Grid:
    def __init__(self, dp_size, fsdp_size):
        self.dp = dp_size
        self.fsdp = fsdp_size
        self.ny = 2
        self.nz = dp_size // 2

    def fits(self, matrices):
        if self.fsdp != 4 or self.dp % 2:
            return False
        for matrix in matrices:
            rows, columns = matrix.shape
            if rows % 32 or (2 * columns) % 128:
                return False
        return True


def pair_halves(matrix, core):
    half = matrix.shape[0] // 2
    mine = lax.dynamic_slice_in_dim(matrix, core * half, half, 0)
    other = lax.dynamic_slice_in_dim(matrix, (1 - core) * half, half, 0)
    return mine, other


def core_swap(value, fsdp_size):
    pairs = [(i, i ^ 1) for i in range(fsdp_size)]
    return lax.ppermute(value, "fsdp", pairs)


def place(nz):
    dp_index = lax.axis_index("dp")
    fsdp_index = lax.axis_index("fsdp")
    return dp_index // 2, dp_index % 2, fsdp_index // 2, fsdp_index % 2


def device(z, y, x, core):
    return {"dp": z * 2 + y, "fsdp": x * 2 + core}


def greet(partners):
    barrier = pltpu.get_barrier_semaphore()
    for partner in partners:
        pl.semaphore_signal(barrier, inc=1, device_id=partner, device_id_type=MESH)
    pl.semaphore_wait(barrier, len(partners))


def gather_kernel(nz, count, *refs):
    blocks = refs[:count]
    wholes = refs[count : 2 * count]
    local_sem, send_sem, recv_sem = refs[2 * count :]
    z, y, x, core = place(nz)
    sibling = device(z, y, x, 1 - core)
    first = device(z, y * (1 - core) + (1 - y) * core, (1 - x) * (1 - core) + x * core, core)
    second = device(z, (1 - y) * (1 - core) + y * core, x * (1 - core) + (1 - x) * core, core)
    others = [device((z + step) % nz, y, x, core) for step in range(1, nz)]
    greet([sibling, first, second, *others])

    def columns(ref, which):
        half = ref.shape[-1] // 2
        return pl.ds(pl.multiple_of(which * half, 128), half)

    def remote(item, slot, src, dst, partner):
        return pltpu.make_async_remote_copy(
            src_ref=src,
            dst_ref=dst,
            send_sem=send_sem.at[item, slot],
            recv_sem=recv_sem.at[item, slot],
            device_id=partner,
            device_id_type=MESH,
        )

    def local(item):
        whole = wholes[item]
        return pltpu.make_async_copy(
            blocks[item], whole.at[z, y, core, :, columns(whole, x)], local_sem.at[item]
        )

    def along_z(item):
        whole = wholes[item]
        spot = whole.at[z, y, core, :, columns(whole, x)]
        return [
            remote(item, step, blocks[item], spot, partner) for step, partner in enumerate(others)
        ]

    def stage_first(item):
        whole = wholes[item]
        part = whole.at[:, y, core, :, columns(whole, x)]
        return [remote(item, nz - 1, part, part, first)]

    def stage_second(item):
        whole = wholes[item]
        copies = []
        for k in range(2):
            row = y * (1 - core) + k * core
            column = k * (1 - core) + x * core
            part = whole.at[:, row, core, :, columns(whole, column)]
            copies.append(remote(item, nz + k, part, part, second))
        return copies

    def stage_core(item):
        part = wholes[item].at[:, :, core]
        return [remote(item, nz + 2, part, part, sibling)]

    stages = [along_z, stage_first, stage_second, stage_core]
    for item in range(count):
        local(item).start()
        for copy in along_z(item):
            copy.start()
    for step in range(count + 3):
        for depth in range(1, 4):
            item = step - depth + 1
            if 0 <= item < count:
                if depth == 1:
                    local(item).wait()
                for copy in stages[depth - 1](item):
                    copy.wait_recv()
                for copy in stages[depth](item):
                    copy.start()
    for item in range(count):
        for copy in stage_core(item):
            copy.wait_recv()
    for item in range(count):
        for stage in stages:
            for copy in stage(item):
                copy.wait_send()


def gather_weights(grid, matrices):
    if not grid.fits(matrices):
        return tuple(
            lax.all_gather(lax.all_gather(m, "fsdp", axis=1, tiled=True), "dp", axis=0, tiled=True)
            for m in matrices
        )
    core = lax.axis_index("fsdp") % 2
    halves = [pair_halves(matrix, core) for matrix in matrices]
    swapped = [core_swap(other, grid.fsdp) for _, other in halves]
    blocks = []
    for (mine, _), theirs in zip(halves, swapped):
        both = jnp.where(
            core == 0,
            jnp.concatenate([mine, theirs], 1),
            jnp.concatenate([theirs, mine], 1),
        )
        blocks.append(both)
    count = len(blocks)
    nz = grid.nz
    shapes = [
        jax.ShapeDtypeStruct((nz, 2, 2, b.shape[0], b.shape[1] * 2), b.dtype) for b in blocks
    ]
    wholes = pl.pallas_call(
        functools.partial(gather_kernel, nz, count),
        out_shape=shapes,
        in_specs=[pl.BlockSpec(memory_space=pl.ANY)] * count,
        out_specs=[pl.BlockSpec(memory_space=pl.ANY)] * count,
        scratch_shapes=[
            pltpu.SemaphoreType.DMA((count,)),
            pltpu.SemaphoreType.DMA((count, nz + 3)),
            pltpu.SemaphoreType.DMA((count, nz + 3)),
        ],
        compiler_params=pltpu.CompilerParams(collective_id=0, has_side_effects=True),
        name="gather_weights",
    )(*blocks)
    return tuple(w.reshape(-1, w.shape[-1]) for w in wholes)


def reduce_kernel(nz, count, *refs):
    grads = refs[:count]
    sums = refs[count : 2 * count]
    rest = refs[2 * count :]
    kept, from_core, from_first, from_second, from_z = (
        rest[i * count : (i + 1) * count] for i in range(5)
    )
    local_sem, send_sem, recv_sem = rest[5 * count :]
    z, y, x, core = place(nz)
    sibling = device(z, y, x, 1 - core)
    first = device(z, (1 - y) * (1 - core) + y * core, x * (1 - core) + (1 - x) * core, core)
    second = device(z, y * (1 - core) + (1 - y) * core, (1 - x) * (1 - core) + x * core, core)
    others = [((z + step) % nz, step) for step in range(1, nz)]
    greet([sibling, first, second, *[device(other, y, x, core) for other, _ in others]])

    def columns(ref, which):
        half = ref.shape[-1] // 2
        return pl.ds(pl.multiple_of(which * half, 128), half)

    def remote(item, slot, src, dst, partner):
        return pltpu.make_async_remote_copy(
            src_ref=src,
            dst_ref=dst,
            send_sem=send_sem.at[item, slot],
            recv_sem=recv_sem.at[item, slot],
            device_id=partner,
            device_id_type=MESH,
        )

    def local(item):
        return pltpu.make_async_copy(grads[item].at[:, :, core], kept[item], local_sem.at[item])

    def stage_core(item):
        return [remote(item, nz + 2, grads[item].at[:, :, 1 - core], from_core[item], sibling)]

    def stage_first(item):
        copies = []
        for k in range(2):
            row = (1 - y) * (1 - core) + k * core
            column = k * (1 - core) + (1 - x) * core
            part = kept[item].at[:, row, :, columns(kept[item], column)]
            copies.append(remote(item, nz + k, part, from_first[item].at[:, k], first))
        return copies

    def stage_second(item):
        row = y * (1 - core) + (1 - y) * core
        column = (1 - x) * (1 - core) + x * core
        part = kept[item].at[:, row, :, columns(kept[item], column)]
        return [remote(item, nz - 1, part, from_second[item], second)]

    def along_z(item):
        copies = []
        for other, step in others:
            part = kept[item].at[other, y, :, columns(kept[item], x)]
            copies.append(
                remote(item, step - 1, part, from_z[item].at[step - 1], device(other, y, x, core))
            )
        return copies

    def add_core(item):
        def one(step, carry):
            a, b = step // 2, step % 2
            kept[item][a, b] = (
                kept[item][a, b].astype(jnp.float32) + from_core[item][a, b].astype(jnp.float32)
            ).astype(jnp.bfloat16)
            return carry

        lax.fori_loop(0, nz * 2, one, 0)

    def add_first(item):
        for k in range(2):
            row = y * (1 - core) + k * core
            column = columns(kept[item], k * (1 - core) + x * core)

            def one(a, carry):
                kept[item][a, row, :, column] = (
                    kept[item][a, row, :, column].astype(jnp.float32)
                    + from_first[item][a, k].astype(jnp.float32)
                ).astype(jnp.bfloat16)
                return carry

            lax.fori_loop(0, nz, one, 0)

    def add_second(item):
        column = columns(kept[item], x)

        def one(a, carry):
            kept[item][a, y, :, column] = (
                kept[item][a, y, :, column].astype(jnp.float32)
                + from_second[item][a].astype(jnp.float32)
            ).astype(jnp.bfloat16)
            return carry

        lax.fori_loop(0, nz, one, 0)

    def add_z(item):
        total = kept[item][z, y, :, columns(kept[item], x)].astype(jnp.float32)
        for step in range(nz - 1):
            total += from_z[item][step].astype(jnp.float32)
        sums[item][...] = total

    stages = [stage_core, stage_first, stage_second, along_z]
    adds = [add_core, add_first, add_second, add_z]
    for item in range(count):
        local(item).start()
        for copy in stage_core(item):
            copy.start()
    for step in range(count + 3):
        for depth in range(4):
            item = step - depth
            if 0 <= item < count:
                if depth == 0:
                    local(item).wait()
                for copy in stages[depth](item):
                    copy.wait_recv()
                adds[depth](item)
                if depth < 3:
                    for copy in stages[depth + 1](item):
                        copy.start()
    for item in range(count):
        for stage in stages:
            for copy in stage(item):
                copy.wait_send()


def reduce_gradients(grid, gradients):
    rounded = [g.astype(jnp.bfloat16) for g in gradients]
    blocks = [
        jax.ShapeDtypeStruct((g.shape[0] // grid.dp, g.shape[1] // grid.fsdp), jnp.bfloat16)
        for g in gradients
    ]
    if not grid.fits(blocks):
        out = []
        for g in rounded:
            part = lax.psum_scatter(g, "dp", scatter_dimension=0, tiled=True)
            part = lax.psum_scatter(part, "fsdp", scatter_dimension=1, tiled=True)
            out.append(part.astype(jnp.float32))
        return tuple(out)
    nz = grid.nz
    count = len(rounded)
    shaped = [g.reshape(nz, 2, 2, g.shape[0] // (nz * 4), g.shape[1]) for g in rounded]
    rows = [g.shape[3] for g in shaped]
    widths = [g.shape[4] for g in shaped]
    bf16 = jnp.bfloat16
    scratch = [pltpu.VMEM((nz, 2, r, w), bf16) for r, w in zip(rows, widths)]
    scratch += [pltpu.VMEM((nz, 2, r, w), bf16) for r, w in zip(rows, widths)]
    scratch += [pltpu.VMEM((nz, 2, r, w // 2), bf16) for r, w in zip(rows, widths)]
    scratch += [pltpu.VMEM((nz, r, w // 2), bf16) for r, w in zip(rows, widths)]
    scratch += [pltpu.VMEM((nz - 1, r, w // 2), bf16) for r, w in zip(rows, widths)]
    scratch += [
        pltpu.SemaphoreType.DMA((count,)),
        pltpu.SemaphoreType.DMA((count, nz + 3)),
        pltpu.SemaphoreType.DMA((count, nz + 3)),
    ]
    sums = pl.pallas_call(
        functools.partial(reduce_kernel, nz, count),
        out_shape=[
            jax.ShapeDtypeStruct((r, w // 2), jnp.float32) for r, w in zip(rows, widths)
        ],
        in_specs=[pl.BlockSpec(memory_space=pl.ANY)] * count,
        out_specs=[pl.BlockSpec(memory_space=pltpu.VMEM)] * count,
        scratch_shapes=scratch,
        compiler_params=pltpu.CompilerParams(
            collective_id=1, has_side_effects=True, vmem_limit_bytes=56 * 1024 * 1024
        ),
        name="reduce_gradients",
    )(*shaped)
    core = lax.axis_index("fsdp") % 2
    out = []
    for total in sums:
        half = total.shape[1] // 2
        mine = lax.dynamic_slice_in_dim(total, core * half, half, 1)
        other = lax.dynamic_slice_in_dim(total, (1 - core) * half, half, 1)
        theirs = core_swap(other, grid.fsdp)
        out.append(
            jnp.where(
                core == 0,
                jnp.concatenate([mine, theirs], 0),
                jnp.concatenate([theirs, mine], 0),
            )
        )
    return tuple(out)


def modulate(grid, timestep, w_ada):
    rows, columns = w_ada.shape
    model_width = rows * grid.dp
    times = lax.all_gather(timestep, ("dp", "fsdp"), axis=0, tiled=True)
    conditions = jax.nn.silu(
        jax.vmap(lambda value: sinusoid(value, model_width))(times)
    ).astype(jnp.bfloat16)
    mine = lax.dynamic_slice_in_dim(conditions, lax.axis_index("dp") * rows, rows, 1)
    partial = jnp.dot(mine, w_ada, preferred_element_type=jnp.float32)
    summed = lax.psum_scatter(partial, "dp", scatter_dimension=0, tiled=True)
    mixed = lax.all_to_all(summed, "fsdp", split_axis=0, concat_axis=0, tiled=True)
    return mine, mixed.reshape(9, model_width)


def ada_gradient(grid, conditions, dmodulation):
    spread = dmodulation.reshape(grid.fsdp, -1)
    swapped = lax.all_to_all(spread, "fsdp", split_axis=0, concat_axis=0, tiled=True)
    everyone = lax.all_gather(swapped, "dp", axis=0, tiled=True)
    return outer_sum(conditions, everyone)


def body(
    latents,
    text_rows,
    out_grad,
    frame_len,
    text_len,
    timestep,
    w_ada,
    w_qkv,
    w_out,
    w_cq,
    w_ckv,
    w_cout,
    w_fc1,
    w_fc2,
    *,
    dp_size,
    fsdp_size,
):
    grid = Grid(dp_size, fsdp_size)
    matrices = (w_qkv, w_out, w_cq, w_ckv, w_cout, w_fc1, w_fc2)
    full_qkv, full_out, full_cq, full_ckv, full_cout, full_fc1, full_fc2 = gather_weights(
        grid, matrices
    )
    conditions, modulation = modulate(grid, timestep, w_ada)
    latent = latents[0].astype(jnp.float32)
    text_block = text_rows[0]
    slot_count = latent.shape[0]
    model_width = latent.shape[1]
    text_slots = text_block.shape[0]
    head_size = model_width // HEADS
    frame_valid = jnp.arange(slot_count) < frame_len[0]
    text_valid = jnp.arange(text_slots) < text_len[0]
    normed_one, inverse_one = normalize(latent)
    hidden_one = (normed_one * (1.0 + modulation[1]) + modulation[0]).astype(jnp.bfloat16)
    packed = jnp.dot(hidden_one, full_qkv, preferred_element_type=jnp.float32).astype(jnp.bfloat16)
    packed = packed.reshape(slot_count, 3, HEADS, head_size)
    mixed_one, log_one = attend_forward(packed[:, 0], packed[:, 1], packed[:, 2], frame_valid)
    branch_one = jnp.dot(mixed_one, full_out, preferred_element_type=jnp.float32)
    after_self = latent + modulation[2] * branch_one
    normed_two, inverse_two = normalize(after_self)
    hidden_two = (normed_two * (1.0 + modulation[4]) + modulation[3]).astype(jnp.bfloat16)
    query_two = jnp.dot(hidden_two, full_cq, preferred_element_type=jnp.float32).astype(
        jnp.bfloat16
    )
    query_two = query_two.reshape(slot_count, HEADS, head_size)
    memory = jnp.dot(text_block, full_ckv, preferred_element_type=jnp.float32).astype(jnp.bfloat16)
    memory = memory.reshape(text_slots, 2, HEADS, head_size)
    mixed_two, log_two = attend_forward(query_two, memory[:, 0], memory[:, 1], text_valid)
    branch_two = jnp.dot(mixed_two, full_cout, preferred_element_type=jnp.float32)
    after_cross = after_self + modulation[5] * branch_two
    normed_three, inverse_three = normalize(after_cross)
    hidden_three = (normed_three * (1.0 + modulation[7]) + modulation[6]).astype(jnp.bfloat16)
    pre_gelu = jnp.dot(hidden_three, full_fc1, preferred_element_type=jnp.float32)
    activated = gelu_tanh(pre_gelu).astype(jnp.bfloat16)
    branch_three = jnp.dot(activated, full_fc2, preferred_element_type=jnp.float32)
    layer_out = after_cross + modulation[8] * branch_three
    upstream = out_grad[0].astype(jnp.float32)
    dbranch_three = (modulation[8] * upstream).astype(jnp.bfloat16)
    dgate_three = jnp.sum(upstream * branch_three, 0)
    grad_fc2 = outer_sum(activated, dbranch_three)
    dactivated = through(dbranch_three, full_fc2)
    gelu_value, gelu_pull = jax.vjp(gelu_tanh, pre_gelu)
    dinner = gelu_pull(dactivated)[0].astype(jnp.bfloat16)
    grad_fc1 = outer_sum(hidden_three, dinner)
    back_three, dshift_three, dscale_three = norm_back(
        through(dinner, full_fc1), normed_three, inverse_three, modulation[7]
    )
    dcross = upstream + back_three
    dbranch_two = (modulation[5] * dcross).astype(jnp.bfloat16)
    dgate_two = jnp.sum(dcross * branch_two, 0)
    grad_cout = outer_sum(mixed_two, dbranch_two)
    dmixed_two = through(dbranch_two, full_cout).astype(jnp.bfloat16)
    dquery_two, dkeys_two, dvalues_two = attend_back(
        query_two, memory[:, 0], memory[:, 1], text_valid, log_two, dmixed_two
    )
    dquery_flat = dquery_two.astype(jnp.bfloat16)
    dmemory = jnp.concatenate([dkeys_two, dvalues_two], -1).astype(jnp.bfloat16)
    grad_cq = outer_sum(hidden_two, dquery_flat)
    grad_ckv = outer_sum(text_block, dmemory)
    text_grad = through(dmemory, full_ckv)
    back_two, dshift_two, dscale_two = norm_back(
        through(dquery_flat, full_cq), normed_two, inverse_two, modulation[4]
    )
    grad_self = dcross + back_two
    dbranch_one = (modulation[2] * grad_self).astype(jnp.bfloat16)
    dgate_one = jnp.sum(grad_self * branch_one, 0)
    grad_out = outer_sum(mixed_one, dbranch_one)
    dmixed_one = through(dbranch_one, full_out).astype(jnp.bfloat16)
    dquery_one, dkeys_one, dvalues_one = attend_back(
        packed[:, 0], packed[:, 1], packed[:, 2], frame_valid, log_one, dmixed_one
    )
    dpacked = jnp.concatenate([dquery_one, dkeys_one, dvalues_one], -1).astype(jnp.bfloat16)
    grad_qkv = outer_sum(hidden_one, dpacked)
    back_one, dshift_one, dscale_one = norm_back(
        through(dpacked, full_qkv), normed_one, inverse_one, modulation[1]
    )
    latent_grad = grad_self + back_one
    dmodulation = (
        jnp.stack(
            [
                dshift_one,
                dscale_one,
                dgate_one,
                dshift_two,
                dscale_two,
                dgate_two,
                dshift_three,
                dscale_three,
                dgate_three,
            ]
        )
        .reshape(1, -1)
        .astype(jnp.bfloat16)
    )
    grad_ada = ada_gradient(grid, conditions, dmodulation)
    owned = reduce_gradients(
        grid, (grad_qkv, grad_out, grad_cq, grad_ckv, grad_cout, grad_fc1, grad_fc2)
    )
    owned_grads = (grad_ada, *owned)
    return (
        layer_out[None],
        latent_grad[None],
        text_grad[None],
        owned_grads[0],
        owned_grads[1],
        owned_grads[2],
        owned_grads[3],
        owned_grads[4],
        owned_grads[5],
        owned_grads[6],
        owned_grads[7],
    )


def solution(mesh):
    placed = (
        P(("dp", "fsdp"), None, None),
        P(("dp", "fsdp"), None, None),
        P(("dp", "fsdp"), None, None),
        P(("dp", "fsdp")),
        P(("dp", "fsdp")),
        P(("dp", "fsdp")),
        P("dp", "fsdp"),
        P("dp", "fsdp"),
        P("dp", "fsdp"),
        P("dp", "fsdp"),
        P("dp", "fsdp"),
        P("dp", "fsdp"),
        P("dp", "fsdp"),
        P("dp", "fsdp"),
    )
    return jax.shard_map(
        functools.partial(body, dp_size=mesh.shape["dp"], fsdp_size=mesh.shape["fsdp"]),
        mesh=mesh,
        in_specs=placed,
        out_specs=(
            P(("dp", "fsdp"), None, None),
            P(("dp", "fsdp"), None, None),
            P(("dp", "fsdp"), None, None),
            P("dp", "fsdp"),
            P("dp", "fsdp"),
            P("dp", "fsdp"),
            P("dp", "fsdp"),
            P("dp", "fsdp"),
            P("dp", "fsdp"),
            P("dp", "fsdp"),
            P("dp", "fsdp"),
        ),
        check_vma=False,
    )
```

```python
import functools
import math

import jax
import jax.numpy as jnp
from jax import lax
from jax.experimental import pallas as pl
from jax.experimental.pallas import tpu as pltpu
from jax.sharding import PartitionSpec as P

HEADS = 12


norm_eps = 1e-06


def sinusoid(time_value, model_width):
    half_width = model_width // 2
    frequency = jnp.exp(-math.log(10000.0) * jnp.arange(half_width, dtype=jnp.float32) / half_width)
    angles = time_value.astype(jnp.float32) * frequency
    return jnp.concatenate([jnp.cos(angles), jnp.sin(angles)], axis=-1)


def normalize(values):
    center = values - jnp.mean(values, -1, keepdims=True)
    spread = jnp.mean(center * center, -1, keepdims=True)
    inverse = lax.rsqrt(spread + norm_eps)
    return (center * inverse, inverse)


def norm_back(upstream, normed, inverse, scale_row):
    dshift = jnp.sum(upstream, 0)
    dscale = jnp.sum(upstream * normed, 0)
    scaled = upstream * (1.0 + scale_row)
    centered = (
        scaled
        - jnp.mean(scaled, -1, keepdims=True)
        - normed * jnp.mean(scaled * normed, -1, keepdims=True)
    )
    return (inverse * centered, dshift, dscale)


def outer_sum(left, right):
    return lax.dot_general(
        left, right, (((0,), (0,)), ((), ())), preferred_element_type=jnp.float32
    )


MESH = pl.DeviceIdType.MESH


class Grid:
    def __init__(self, dp_size, fsdp_size):
        self.dp = dp_size
        self.fsdp = fsdp_size
        self.ny = 2
        self.nz = dp_size // 2

    def fits(self, matrices):
        if self.fsdp != 4 or self.dp % 2:
            return False
        for matrix in matrices:
            rows, columns = matrix.shape
            if rows % 32 or (2 * columns) % 128:
                return False
        return True


def pair_halves(matrix, core):
    half = matrix.shape[0] // 2
    mine = lax.dynamic_slice_in_dim(matrix, core * half, half, 0)
    other = lax.dynamic_slice_in_dim(matrix, (1 - core) * half, half, 0)
    return mine, other


def core_swap(value, fsdp_size):
    pairs = [(i, i ^ 1) for i in range(fsdp_size)]
    return lax.ppermute(value, "fsdp", pairs)


def place(nz):
    dp_index = lax.axis_index("dp")
    fsdp_index = lax.axis_index("fsdp")
    return dp_index // 2, dp_index % 2, fsdp_index // 2, fsdp_index % 2


def device(z, y, x, core):
    return {"dp": z * 2 + y, "fsdp": x * 2 + core}


def greet(partners):
    barrier = pltpu.get_barrier_semaphore()
    for partner in partners:
        pl.semaphore_signal(barrier, inc=1, device_id=partner, device_id_type=MESH)
    pl.semaphore_wait(barrier, len(partners))


def gather_kernel(nz, count, *refs):
    blocks = refs[:count]
    wholes = refs[count : 2 * count]
    local_sem, send_sem, recv_sem = refs[2 * count :]
    z, y, x, core = place(nz)
    sibling = device(z, y, x, 1 - core)
    first = device(z, y * (1 - core) + (1 - y) * core, (1 - x) * (1 - core) + x * core, core)
    second = device(z, (1 - y) * (1 - core) + y * core, x * (1 - core) + (1 - x) * core, core)
    others = [device((z + step) % nz, y, x, core) for step in range(1, nz)]
    greet([sibling, first, second, *others])

    def columns(ref, which):
        half = ref.shape[-1] // 2
        return pl.ds(pl.multiple_of(which * half, 128), half)

    def remote(item, slot, src, dst, partner):
        return pltpu.make_async_remote_copy(
            src_ref=src,
            dst_ref=dst,
            send_sem=send_sem.at[item, slot],
            recv_sem=recv_sem.at[item, slot],
            device_id=partner,
            device_id_type=MESH,
        )

    def local(item):
        whole = wholes[item]
        return pltpu.make_async_copy(
            blocks[item], whole.at[z, y, core, :, columns(whole, x)], local_sem.at[item]
        )

    def along_z(item):
        whole = wholes[item]
        spot = whole.at[z, y, core, :, columns(whole, x)]
        return [
            remote(item, step, blocks[item], spot, partner) for step, partner in enumerate(others)
        ]

    def stage_first(item):
        whole = wholes[item]
        part = whole.at[:, y, core, :, columns(whole, x)]
        return [remote(item, nz - 1, part, part, first)]

    def stage_second(item):
        whole = wholes[item]
        copies = []
        for k in range(2):
            row = y * (1 - core) + k * core
            column = k * (1 - core) + x * core
            part = whole.at[:, row, core, :, columns(whole, column)]
            copies.append(remote(item, nz + k, part, part, second))
        return copies

    def stage_core(item):
        part = wholes[item].at[:, :, core]
        return [remote(item, nz + 2, part, part, sibling)]

    stages = [along_z, stage_first, stage_second, stage_core]
    for item in range(count):
        local(item).start()
        for copy in along_z(item):
            copy.start()
    for step in range(count + 3):
        for depth in range(1, 4):
            item = step - depth + 1
            if 0 <= item < count:
                if depth == 1:
                    local(item).wait()
                for copy in stages[depth - 1](item):
                    copy.wait_recv()
                for copy in stages[depth](item):
                    copy.start()
    for item in range(count):
        for copy in stage_core(item):
            copy.wait_recv()
    for item in range(count):
        for stage in stages:
            for copy in stage(item):
                copy.wait_send()


def gather_weights(grid, matrices):
    if not grid.fits(matrices):
        return tuple(
            lax.all_gather(
                lax.all_gather(m, "fsdp", axis=1, tiled=True), "dp", axis=0, tiled=True
            ).reshape(4, 2, 2, m.shape[0] * grid.dp // 16, m.shape[1] * grid.fsdp)
            for m in matrices
        )
    core = lax.axis_index("fsdp") % 2
    halves = [pair_halves(matrix, core) for matrix in matrices]
    swapped = [core_swap(other, grid.fsdp) for _, other in halves]
    blocks = []
    for (mine, _), theirs in zip(halves, swapped):
        both = jnp.where(
            core == 0,
            jnp.concatenate([mine, theirs], 1),
            jnp.concatenate([theirs, mine], 1),
        )
        blocks.append(both)
    count = len(blocks)
    nz = grid.nz
    shapes = [
        jax.ShapeDtypeStruct((nz, 2, 2, b.shape[0], b.shape[1] * 2), b.dtype) for b in blocks
    ]
    wholes = pl.pallas_call(
        functools.partial(gather_kernel, nz, count),
        out_shape=shapes,
        in_specs=[pl.BlockSpec(memory_space=pl.ANY)] * count,
        out_specs=[pl.BlockSpec(memory_space=pl.ANY)] * count,
        scratch_shapes=[
            pltpu.SemaphoreType.DMA((count,)),
            pltpu.SemaphoreType.DMA((count, nz + 3)),
            pltpu.SemaphoreType.DMA((count, nz + 3)),
        ],
        compiler_params=pltpu.CompilerParams(collective_id=0, has_side_effects=True),
        name="gather_weights",
    )(*blocks)
    return tuple(wholes)


def reduce_kernel(nz, count, *refs):
    grads = refs[:count]
    sums = refs[count : 2 * count]
    rest = refs[2 * count :]
    kept, from_core, from_first, from_second, from_z = (
        rest[i * count : (i + 1) * count] for i in range(5)
    )
    local_sem, send_sem, recv_sem = rest[5 * count :]
    z, y, x, core = place(nz)
    sibling = device(z, y, x, 1 - core)
    first = device(z, (1 - y) * (1 - core) + y * core, x * (1 - core) + (1 - x) * core, core)
    second = device(z, y * (1 - core) + (1 - y) * core, (1 - x) * (1 - core) + x * core, core)
    others = [((z + step) % nz, step) for step in range(1, nz)]
    greet([sibling, first, second, *[device(other, y, x, core) for other, _ in others]])

    def columns(ref, which):
        half = ref.shape[-1] // 2
        return pl.ds(pl.multiple_of(which * half, 128), half)

    def remote(item, slot, src, dst, partner):
        return pltpu.make_async_remote_copy(
            src_ref=src,
            dst_ref=dst,
            send_sem=send_sem.at[item, slot],
            recv_sem=recv_sem.at[item, slot],
            device_id=partner,
            device_id_type=MESH,
        )

    def local(item):
        return pltpu.make_async_copy(grads[item].at[:, :, core], kept[item], local_sem.at[item])

    def stage_core(item):
        return [remote(item, nz + 2, grads[item].at[:, :, 1 - core], from_core[item], sibling)]

    def stage_first(item):
        copies = []
        for k in range(2):
            row = (1 - y) * (1 - core) + k * core
            column = k * (1 - core) + (1 - x) * core
            part = kept[item].at[:, row, :, columns(kept[item], column)]
            copies.append(remote(item, nz + k, part, from_first[item].at[:, k], first))
        return copies

    def stage_second(item):
        row = y * (1 - core) + (1 - y) * core
        column = (1 - x) * (1 - core) + x * core
        part = kept[item].at[:, row, :, columns(kept[item], column)]
        return [remote(item, nz - 1, part, from_second[item], second)]

    def along_z(item):
        copies = []
        for other, step in others:
            part = kept[item].at[other, y, :, columns(kept[item], x)]
            copies.append(
                remote(item, step - 1, part, from_z[item].at[step - 1], device(other, y, x, core))
            )
        return copies

    def add_core(item):
        def one(step, carry):
            a, b = step // 2, step % 2
            kept[item][a, b] = (
                kept[item][a, b].astype(jnp.float32) + from_core[item][a, b].astype(jnp.float32)
            ).astype(jnp.bfloat16)
            return carry

        lax.fori_loop(0, nz * 2, one, 0)

    def add_first(item):
        for k in range(2):
            row = y * (1 - core) + k * core
            column = columns(kept[item], k * (1 - core) + x * core)

            def one(a, carry):
                kept[item][a, row, :, column] = (
                    kept[item][a, row, :, column].astype(jnp.float32)
                    + from_first[item][a, k].astype(jnp.float32)
                ).astype(jnp.bfloat16)
                return carry

            lax.fori_loop(0, nz, one, 0)

    def add_second(item):
        column = columns(kept[item], x)

        def one(a, carry):
            kept[item][a, y, :, column] = (
                kept[item][a, y, :, column].astype(jnp.float32)
                + from_second[item][a].astype(jnp.float32)
            ).astype(jnp.bfloat16)
            return carry

        lax.fori_loop(0, nz, one, 0)

    def add_z(item):
        total = kept[item][z, y, :, columns(kept[item], x)].astype(jnp.float32)
        for step in range(nz - 1):
            total += from_z[item][step].astype(jnp.float32)
        sums[item][...] = total

    stages = [stage_core, stage_first, stage_second, along_z]
    adds = [add_core, add_first, add_second, add_z]
    for item in range(count):
        local(item).start()
        for copy in stage_core(item):
            copy.start()
    for step in range(count + 3):
        for depth in range(4):
            item = step - depth
            if 0 <= item < count:
                if depth == 0:
                    local(item).wait()
                for copy in stages[depth](item):
                    copy.wait_recv()
                adds[depth](item)
                if depth < 3:
                    for copy in stages[depth + 1](item):
                        copy.start()
    for item in range(count):
        for stage in stages:
            for copy in stage(item):
                copy.wait_send()


def reduce_gradients(grid, gradients):
    rounded = [g.reshape(-1, g.shape[-1]) for g in gradients]
    blocks = [
        jax.ShapeDtypeStruct((g.shape[0] // grid.dp, g.shape[1] // grid.fsdp), jnp.bfloat16)
        for g in rounded
    ]
    if not grid.fits(blocks):
        out = []
        for g in rounded:
            part = lax.psum_scatter(g, "dp", scatter_dimension=0, tiled=True)
            part = lax.psum_scatter(part, "fsdp", scatter_dimension=1, tiled=True)
            out.append(part.astype(jnp.float32))
        return tuple(out)
    nz = grid.nz
    count = len(rounded)
    shaped = list(gradients)
    rows = [g.shape[3] for g in shaped]
    widths = [g.shape[4] for g in shaped]
    bf16 = jnp.bfloat16
    scratch = [pltpu.VMEM((nz, 2, r, w), bf16) for r, w in zip(rows, widths)]
    scratch += [pltpu.VMEM((nz, 2, r, w), bf16) for r, w in zip(rows, widths)]
    scratch += [pltpu.VMEM((nz, 2, r, w // 2), bf16) for r, w in zip(rows, widths)]
    scratch += [pltpu.VMEM((nz, r, w // 2), bf16) for r, w in zip(rows, widths)]
    scratch += [pltpu.VMEM((nz - 1, r, w // 2), bf16) for r, w in zip(rows, widths)]
    scratch += [
        pltpu.SemaphoreType.DMA((count,)),
        pltpu.SemaphoreType.DMA((count, nz + 3)),
        pltpu.SemaphoreType.DMA((count, nz + 3)),
    ]
    sums = pl.pallas_call(
        functools.partial(reduce_kernel, nz, count),
        out_shape=[
            jax.ShapeDtypeStruct((r, w // 2), jnp.float32) for r, w in zip(rows, widths)
        ],
        in_specs=[pl.BlockSpec(memory_space=pl.ANY)] * count,
        out_specs=[pl.BlockSpec(memory_space=pltpu.VMEM)] * count,
        scratch_shapes=scratch,
        compiler_params=pltpu.CompilerParams(
            collective_id=1, has_side_effects=True, vmem_limit_bytes=56 * 1024 * 1024
        ),
        name="reduce_gradients",
    )(*shaped)
    core = lax.axis_index("fsdp") % 2
    out = []
    for total in sums:
        half = total.shape[1] // 2
        mine = lax.dynamic_slice_in_dim(total, core * half, half, 1)
        other = lax.dynamic_slice_in_dim(total, (1 - core) * half, half, 1)
        theirs = core_swap(other, grid.fsdp)
        out.append(
            jnp.where(
                core == 0,
                jnp.concatenate([mine, theirs], 0),
                jnp.concatenate([theirs, mine], 0),
            )
        )
    return tuple(out)


def modulate(grid, timestep, w_ada):
    rows, columns = w_ada.shape
    model_width = rows * grid.dp
    times = lax.all_gather(timestep, ("dp", "fsdp"), axis=0, tiled=True)
    conditions = jax.nn.silu(
        jax.vmap(lambda value: sinusoid(value, model_width))(times)
    ).astype(jnp.bfloat16)
    mine = lax.dynamic_slice_in_dim(conditions, lax.axis_index("dp") * rows, rows, 1)
    partial = jnp.dot(mine, w_ada, preferred_element_type=jnp.float32)
    summed = lax.psum_scatter(partial, "dp", scatter_dimension=0, tiled=True)
    mixed = lax.all_to_all(summed, "fsdp", split_axis=0, concat_axis=0, tiled=True)
    return mine, mixed.reshape(9, model_width)


def ada_gradient(grid, conditions, dmodulation):
    spread = dmodulation.reshape(grid.fsdp, -1)
    swapped = lax.all_to_all(spread, "fsdp", split_axis=0, concat_axis=0, tiled=True)
    everyone = lax.all_gather(swapped, "dp", axis=0, tiled=True)
    return outer_sum(conditions, everyone)


F32 = jnp.float32
BF16 = jnp.bfloat16
NT = (((1,), (1,)), ((), ()))
TN = (((0,), (0,)), ((), ()))


def flat(value):
    return value.reshape(-1, value.shape[-1])


def dot(left, right):
    return jnp.dot(left, right, preferred_element_type=F32)


def dot_nt(left, right):
    return lax.dot_general(left, right, NT, preferred_element_type=F32)


def dot_tn(left, right):
    return lax.dot_general(left, right, TN, preferred_element_type=F32)


def tiles(total, size, body):
    def step(t, carry):
        body(pl.ds(pl.multiple_of(t * size, size), size))
        return carry

    lax.fori_loop(0, total // size, step, 0)


def row_tile(rows):
    for size in (432, 288, 256, 128):
        if rows % size == 0:
            return size
    return rows


def gelu_pair(inner):
    slope = math.sqrt(2.0 / math.pi)
    square = inner * inner
    turned = jnp.tanh(inner * (slope + (slope * 0.044715) * square))
    half = 0.5 + 0.5 * turned
    rise = inner * (slope + (3.0 * slope * 0.044715) * square)
    return inner * half, half + (0.5 - 0.5 * turned * turned) * rise


def half_lanes(shape):
    return lax.broadcasted_iota(jnp.int32, shape, 1) < shape[1] // 2


def attend(queries, keys, values, bias, mixed, heads_wide, size):
    query_ref, query_at = queries
    key_ref, key_at = keys
    value_ref, value_at = values
    mixed_ref, mixed_at = mixed
    rows = mixed_ref.shape[0]
    width = 2 * heads_wide

    def pair(p, carry):
        def at(start):
            return pl.ds(pl.multiple_of(start + p * width, width), width)

        key_pair = key_ref[:, at(key_at)]
        value_pair = value_ref[:, at(value_at)]
        low = half_lanes((size, width))
        for start in range(0, rows, size):
            scaled = query_ref[start : start + size, at(query_at)] * BF16(heads_wide**-0.5)
            outs = []
            for head in range(2):
                own = jnp.where(low if head == 0 else ~low, scaled, BF16(0))
                scores = dot_nt(own, key_pair) + bias[...]
                raised = jnp.exp(scores - jnp.max(scores, -1, keepdims=True))
                summed = jnp.sum(raised, -1, keepdims=True)
                outs.append(dot(raised.astype(BF16), value_pair) * (1.0 / summed))
            mixed_ref[start : start + size, at(mixed_at)] = jnp.where(
                low, outs[0], outs[1]
            ).astype(BF16)
        return carry

    return pair


def attend_back(queries, keys, values, bias, upstream, heads_wide, size):
    query_ref, query_at = queries
    key_ref, key_at = keys
    value_ref, value_at = values
    rows = upstream.shape[0]
    slots = bias.shape[1]
    width = 2 * heads_wide
    factor = BF16(heads_wide**-0.5)

    def pair(p, carry):
        def at(start):
            return pl.ds(pl.multiple_of(start + p * width, width), width)

        key_pair = key_ref[:, at(key_at)]
        value_pair = value_ref[:, at(value_at)]
        low = half_lanes((size, width))
        low_keys = half_lanes((slots, width))
        key_grad = jnp.zeros((slots, width), F32)
        value_grad = jnp.zeros((slots, width), F32)
        for start in range(0, rows, size):
            scaled = query_ref[start : start + size, at(query_at)] * factor
            above = upstream[start : start + size, at(0)]
            query_grad = jnp.zeros((size, width), F32)
            for head in range(2):
                mask = low if head == 0 else ~low
                own = jnp.where(mask, scaled, BF16(0))
                own_above = jnp.where(mask, above, BF16(0))
                own_keys = jnp.where(low_keys if head == 0 else ~low_keys, key_pair, BF16(0))
                scores = dot_nt(own, key_pair) + bias[...]
                raised = jnp.exp(scores - jnp.max(scores, -1, keepdims=True))
                shares = raised * (1.0 / jnp.sum(raised, -1, keepdims=True))
                share_grad = dot_nt(own_above, value_pair)
                total = jnp.sum(shares * share_grad, -1, keepdims=True)
                score_grad = (shares * (share_grad - total)).astype(BF16)
                value_grad += dot_tn(shares.astype(BF16), own_above)
                key_grad += dot_tn(score_grad, own)
                query_grad += dot(score_grad, own_keys)
            query_ref[start : start + size, at(query_at)] = (
                query_grad * heads_wide**-0.5
            ).astype(BF16)
        key_ref[:, at(key_at)] = key_grad.astype(BF16)
        value_ref[:, at(value_at)] = value_grad.astype(BF16)
        return carry

    return pair


class Loads:
    def __init__(self, sems):
        self.sems = sems
        self.copies = {}

    def start(self, name, src, dst):
        copy = pltpu.make_async_copy(src, dst, self.sems.at[len(self.copies)])
        copy.start()
        self.copies[name] = copy

    def wait(self, *names):
        for name in names:
            self.copies[name].wait()


WEIGHTS = ("qkv", "out", "cq", "ckv", "cout", "fc1", "fc2")


def forward_kernel(*refs):
    (lat, text, og, mod, frame_bias, text_bias), refs = refs[:6], refs[6:]
    given, refs = dict(zip(WEIGHTS, refs[:7])), refs[7:]
    (layer_out, dcross_out, qkv_out, h1_out, mixed1_out, h2_out, q2_out, mixed2_out), refs = (
        refs[:8],
        refs[8:],
    )
    (memory_out, after_out, branch_out, fc1_out, fc2_out, rows_out), refs = refs[:6], refs[6:]
    held, refs = dict(zip(WEIGHTS, refs[:7])), refs[7:]
    big, wide, h3, db3, memory, after_self, branch_1, branch_2, after_cross, result, sems = refs
    slots, model = lat.shape
    inner_width = held["fc1"].shape[-1]
    head = model // HEADS
    size = row_tile(slots)
    loads = Loads(sems)
    for name in WEIGHTS:
        loads.start(name, given[name], held[name])

    def need(name):
        loads.wait(name)

    def row(k):
        return mod[k : k + 1, :]

    big[slots:, :] = jnp.zeros((big.shape[0] - slots, inner_width), BF16)

    def norm_1(rows):
        normed, _ = normalize(lat[rows, :].astype(F32))
        wide[rows, 0:model] = (normed * (1.0 + row(1)) + row(0)).astype(BF16)

    tiles(slots, size, norm_1)
    need("qkv")
    for part in range(3):
        columns = slice(part * model, (part + 1) * model)

        def project(rows):
            big[rows, columns] = dot(
                wide[rows, 0:model], flat(held["qkv"][:, :, :, :, columns])
            ).astype(BF16)

        tiles(slots, size, project)
    loads.start("qkv_out", big.at[0:slots, 0 : 3 * model], qkv_out)
    loads.start("h1_out", wide.at[:, 0:model], h1_out)
    pair = attend(
        (big, 0), (big, model), (big, 2 * model), frame_bias, (wide, model), head, size
    )
    lax.fori_loop(0, HEADS // 2, pair, 0)
    loads.start("mixed1_out", wide.at[:, model : 2 * model], mixed1_out)
    need("out")
    need("cq")

    def join_1(rows):
        branch = dot(wide[rows, model : 2 * model], flat(held["out"][...]))
        branch_1[rows, :] = branch
        after = lat[rows, :].astype(F32) + row(2) * branch
        after_self[rows, :] = after
        normed, _ = normalize(after)
        hidden = (normed * (1.0 + row(4)) + row(3)).astype(BF16)
        wide[rows, 2 * model : 3 * model] = hidden
        wide[rows, 3 * model : 4 * model] = dot(hidden, flat(held["cq"][...])).astype(BF16)

    tiles(slots, size, join_1)
    loads.start("branch_out", branch_1, branch_out)
    loads.start("after_out", after_self, after_out)
    loads.start("h2_out", wide.at[:, 2 * model : 3 * model], h2_out)
    loads.start("q2_out", wide.at[:, 3 * model : 4 * model], q2_out)
    need("ckv")
    for part in range(2):
        columns = slice(part * model, (part + 1) * model)
        memory[:, columns] = dot(text[...], flat(held["ckv"][:, :, :, :, columns])).astype(BF16)
    loads.start("memory_out", memory, memory_out)
    mixed2 = big.at[0:slots, 3 * model : 4 * model]
    pair = attend(
        (wide, 3 * model), (memory, 0), (memory, model), text_bias, (mixed2, 0), head, size
    )
    lax.fori_loop(0, HEADS // 2, pair, 0)
    loads.start("mixed2_out", mixed2, mixed2_out)
    need("cout")

    def join_2(rows):
        branch = dot(mixed2[rows, :], flat(held["cout"][...]))
        branch_2[rows, :] = branch
        after = after_self[rows, :] + row(5) * branch
        after_cross[rows, :] = after
        normed, _ = normalize(after)
        h3[rows, :] = (normed * (1.0 + row(7)) + row(6)).astype(BF16)
        db3[rows, :] = (row(8) * og[rows, :].astype(F32)).astype(BF16)

    tiles(slots, size, join_2)
    need("fc1")
    need("fc2")
    loads.wait("qkv_out", "h1_out", "mixed1_out", "h2_out", "q2_out", "mixed2_out")
    rows_out[...] = jnp.zeros_like(rows_out)
    fc2_lead = held["fc2"].shape[0] * held["fc2"].shape[1]

    def feed(rows):
        hidden = h3[rows, :]
        above = db3[rows, :]
        for part in range(inner_width // model):
            columns = slice(part * model, (part + 1) * model)
            matrix_1 = flat(held["fc1"][:, :, :, :, columns])
            per = held["fc2"].shape[0] // (inner_width // model)
            matrix_2 = flat(held["fc2"][part * per : (part + 1) * per])
            activated, slope = gelu_pair(dot(hidden, matrix_1))
            activated = activated.astype(BF16)
            dinner = (dot_nt(above, matrix_2) * slope).astype(BF16)
            big[rows, columns] = activated
            wide[rows, columns] = dinner
            forward = dot(activated, matrix_2)
            backward = dot_nt(dinner, matrix_1)
            if part == 0:
                branch, upstream = forward, backward
            else:
                branch += forward
                upstream += backward
        entering = after_cross[rows, :]
        grad = og[rows, :].astype(F32)
        result[rows, :] = entering + row(8) * branch
        normed, inverse = normalize(entering)
        back, dshift, dscale = norm_back(upstream, normed, inverse, row(7))
        dcross = grad + back
        after_cross[rows, :] = dcross
        rows_out[0:1, :] += jnp.sum(grad * branch, 0, keepdims=True)
        rows_out[1:2, :] += dshift[None]
        rows_out[2:3, :] += dscale[None]
        rows_out[3:4, :] += jnp.sum(dcross * branch_2[rows, :], 0, keepdims=True)

    tiles(slots, size, feed)
    loads.start("layer_out", result, layer_out)
    loads.start("dcross_out", after_cross, dcross_out)
    second = held["fc2"]

    def grad_2(t, carry):
        a, b = t // second.shape[1], t % second.shape[1]
        count = inner_width // fc2_lead
        columns = pl.ds(pl.multiple_of(t * count, 128), count)
        product = dot_tn(big[0:slots, columns], db3[...]).astype(BF16)
        second[a, b] = product.reshape(second.shape[2:])
        return carry

    lax.fori_loop(0, fc2_lead, grad_2, 0)
    loads.start("fc2_out", second, fc2_out)

    def grad_1(columns):
        product = dot_tn(h3[...], wide[:, columns]).astype(BF16)
        held["fc1"][:, :, :, :, columns] = product.reshape(held["fc1"].shape[:4] + (-1,))

    tiles(inner_width, 512, grad_1)
    loads.start("fc1_out", held["fc1"], fc1_out)
    loads.wait("branch_out", "after_out", "memory_out", "layer_out", "dcross_out", "fc1_out")
    loads.wait("fc2_out")


def forward(latent, text_block, upstream, modulation, frame_bias, text_bias, matrices):
    slots, model = latent.shape
    text_slots = text_block.shape[0]
    padded = frame_bias.shape[1]
    inner_width = matrices[5].shape[-1]
    shaped = jax.ShapeDtypeStruct
    narrow = shaped((slots, model), BF16)
    full = shaped((slots, model), F32)
    outs = [
        full,
        full,
        shaped((slots, 3 * model), BF16),
        narrow,
        narrow,
        narrow,
        narrow,
        narrow,
        shaped((text_slots, 2 * model), BF16),
        full,
        full,
        shaped(matrices[5].shape, BF16),
        shaped(matrices[6].shape, BF16),
        shaped((8, model), F32),
    ]
    vmem = pl.BlockSpec(memory_space=pltpu.VMEM)
    anywhere = pl.BlockSpec(memory_space=pl.ANY)
    scratch = [pltpu.VMEM(m.shape, BF16) for m in matrices]
    scratch += [
        pltpu.VMEM((padded, inner_width), BF16),
        pltpu.VMEM((slots, inner_width), BF16),
        pltpu.VMEM((slots, model), BF16),
        pltpu.VMEM((slots, model), BF16),
        pltpu.VMEM((text_slots, 2 * model), BF16),
    ]
    scratch += [pltpu.VMEM((slots, model), F32)] * 5
    scratch += [pltpu.SemaphoreType.DMA((24,))]
    return pl.pallas_call(
        forward_kernel,
        out_shape=outs,
        in_specs=[vmem] * 6 + [anywhere] * 7,
        out_specs=[anywhere] * 13 + [vmem],
        scratch_shapes=scratch,
        compiler_params=pltpu.CompilerParams(vmem_limit_bytes=62 * 1024 * 1024),
        name="forward",
    )(latent, text_block, upstream, modulation, frame_bias, text_bias, *matrices)


BACK = ("qkv", "out", "cq", "ckv", "cout")


def backward_kernel(*refs):
    (lat, text, mod, frame_bias, text_bias), refs = refs[:5], refs[5:]
    names = ("dcross", "qkv_act", "h1", "mixed1", "h2", "q2", "mixed2", "memory", "after", "branch")
    given, refs = dict(zip(names, refs[:10])), refs[10:]
    matrices, refs = dict(zip(BACK, refs[:5])), refs[5:]
    (latent_out, text_out, rows_out), refs = refs[:3], refs[3:]
    grads_out, refs = dict(zip(BACK, refs[:5])), refs[5:]
    act, refs = dict(zip(names, refs[:10])), refs[10:]
    held, refs = dict(zip(BACK, refs[:5])), refs[5:]
    grad_qkv, above, sems = refs
    slots, model = lat.shape
    head = model // HEADS
    size = row_tile(slots)
    loads = Loads(sems)
    for name in ("dcross", "mixed2", "q2", "memory", "h2", "after", "branch", "mixed1", "h1"):
        loads.start(name, given[name], act[name])
    loads.start("qkv_act", given["qkv_act"], act["qkv_act"].at[0:slots, :])
    for name in ("cout", "cq", "ckv", "out", "qkv"):
        loads.start("w" + name, matrices[name], held[name])

    def row(k):
        return mod[k : k + 1, :]

    def place_grad(target, name, columns, left, right):
        product = dot_tn(left, right).astype(BF16)
        target[:, :, :, :, columns] = product.reshape(target.shape[:4] + (-1,))

    rows_out[...] = jnp.zeros_like(rows_out)
    dcross = act["dcross"]
    loads.wait("dcross", "wcout")

    def enter_2(rows):
        small = (row(5) * dcross[rows, :]).astype(BF16)
        above[0, rows, :] = small
        above[1, rows, :] = dot_nt(small, flat(held["cout"][...])).astype(BF16)

    tiles(slots, size, enter_2)
    loads.wait("mixed2")
    place_grad(held["cout"], "cout", slice(0, model), act["mixed2"][...], above[0])
    loads.start("gcout", held["cout"], grads_out["cout"])
    loads.wait("q2", "memory")
    pair = attend_back(
        (act["q2"], 0), (act["memory"], 0), (act["memory"], model), text_bias, above.at[1], head, size
    )
    lax.fori_loop(0, HEADS // 2, pair, 0)
    loads.wait("wcq", "wckv", "after", "branch", "h2")
    text_out[...] = dot_nt(act["memory"][...], flat(held["ckv"][...]))
    for part in range(2):
        columns = slice(part * model, (part + 1) * model)
        place_grad(held["ckv"], "ckv", columns, text[...], act["memory"][:, columns])
    loads.start("gckv", held["ckv"], grads_out["ckv"])
    loads.wait("wout")

    def leave_2(rows):
        upstream = dot_nt(act["q2"][rows, :], flat(held["cq"][...]))
        normed, inverse = normalize(act["after"][rows, :])
        back, dshift, dscale = norm_back(upstream, normed, inverse, row(4))
        dself = dcross[rows, :] + back
        dcross[rows, :] = dself
        rows_out[0:1, :] += dshift[None]
        rows_out[1:2, :] += dscale[None]
        rows_out[2:3, :] += jnp.sum(dself * act["branch"][rows, :], 0, keepdims=True)
        small = (row(2) * dself).astype(BF16)
        above[0, rows, :] = small
        above[1, rows, :] = dot_nt(small, flat(held["out"][...])).astype(BF16)

    tiles(slots, size, leave_2)
    place_grad(held["cq"], "cq", slice(0, model), act["h2"][...], act["q2"][...])
    loads.start("gcq", held["cq"], grads_out["cq"])
    loads.wait("mixed1")
    place_grad(held["out"], "out", slice(0, model), act["mixed1"][...], above[0])
    loads.start("gout", held["out"], grads_out["out"])
    loads.wait("qkv_act")
    packed = act["qkv_act"]
    packed[slots:, :] = jnp.zeros((packed.shape[0] - slots, 3 * model), BF16)
    pair = attend_back(
        (packed, 0), (packed, model), (packed, 2 * model), frame_bias, above.at[1], head, 288
    )
    lax.fori_loop(0, HEADS // 2, pair, 0)
    loads.wait("h1", "wqkv")
    for part in range(3):
        columns = slice(part * model, (part + 1) * model)
        place_grad(grad_qkv, "qkv", columns, act["h1"][...], packed[0:slots, columns])
    loads.start("gqkv", grad_qkv, grads_out["qkv"])

    def leave_1(rows):
        upstream = dot_nt(packed[rows, :], flat(held["qkv"][...]))
        normed, inverse = normalize(lat[rows, :].astype(F32))
        back, dshift, dscale = norm_back(upstream, normed, inverse, row(1))
        dcross[rows, :] = dcross[rows, :] + back
        rows_out[3:4, :] += dshift[None]
        rows_out[4:5, :] += dscale[None]

    tiles(slots, size, leave_1)
    loads.start("latent", dcross, latent_out)
    loads.wait("gcout", "gckv", "gcq", "gout", "gqkv", "latent")


def backward(latent, text_block, modulation, frame_bias, text_bias, kept, matrices):
    slots, model = latent.shape
    text_slots = text_block.shape[0]
    padded = frame_bias.shape[1]
    shaped = jax.ShapeDtypeStruct
    outs = [
        shaped((slots, model), F32),
        shaped((text_slots, model), F32),
        shaped((8, model), F32),
    ]
    outs += [shaped(m.shape, BF16) for m in matrices]
    vmem = pl.BlockSpec(memory_space=pltpu.VMEM)
    anywhere = pl.BlockSpec(memory_space=pl.ANY)
    scratch = [pltpu.VMEM(k.shape, k.dtype) for k in kept]
    scratch[1] = pltpu.VMEM((padded, 3 * model), BF16)
    scratch += [pltpu.VMEM(m.shape, BF16) for m in matrices]
    scratch += [
        pltpu.VMEM(matrices[0].shape, BF16),
        pltpu.VMEM((2, slots, model), BF16),
        pltpu.SemaphoreType.DMA((24,)),
    ]
    return pl.pallas_call(
        backward_kernel,
        out_shape=outs,
        in_specs=[vmem] * 5 + [anywhere] * 15,
        out_specs=[anywhere, vmem, vmem] + [anywhere] * 5,
        scratch_shapes=scratch,
        compiler_params=pltpu.CompilerParams(vmem_limit_bytes=62 * 1024 * 1024),
        name="backward",
    )(latent, text_block, modulation, frame_bias, text_bias, *kept, *matrices)


def body(
    latents,
    text_rows,
    out_grad,
    frame_len,
    text_len,
    timestep,
    w_ada,
    w_qkv,
    w_out,
    w_cq,
    w_ckv,
    w_cout,
    w_fc1,
    w_fc2,
    *,
    dp_size,
    fsdp_size,
):
    grid = Grid(dp_size, fsdp_size)
    matrices = gather_weights(grid, (w_qkv, w_out, w_cq, w_ckv, w_cout, w_fc1, w_fc2))
    conditions, modulation = modulate(grid, timestep, w_ada)
    slot_count, model_width = latents.shape[1:]
    text_slots = text_rows.shape[1]
    padded = -(-slot_count // 128) * 128
    frame_bias = jnp.where(jnp.arange(padded) < frame_len[0], 0.0, -1e30).astype(F32)[None]
    text_bias = jnp.where(jnp.arange(text_slots) < text_len[0], 0.0, -1e30).astype(F32)[None]
    modulation = jnp.pad(modulation, ((0, 7), (0, 0)))
    results = forward(
        latents[0], text_rows[0], out_grad[0], modulation, frame_bias, text_bias, matrices
    )
    layer_out = results[0]
    kept = results[1:11]
    grad_fc1, grad_fc2, rows_3 = results[11:]
    results = backward(
        latents[0], text_rows[0], modulation, frame_bias, text_bias, kept, matrices[:5]
    )
    latent_grad, text_grad, rows_1 = results[:3]
    order = (
        rows_1[3:4],
        rows_1[4:5],
        rows_1[2:3],
        rows_1[0:1],
        rows_1[1:2],
        rows_3[3:4],
        rows_3[1:2],
        rows_3[2:3],
        rows_3[0:1],
    )
    dmodulation = jnp.concatenate(order, 0).reshape(1, -1).astype(BF16)
    grad_ada = ada_gradient(grid, conditions, dmodulation)
    owned = reduce_gradients(grid, (*results[3:8], grad_fc1, grad_fc2))
    return (
        layer_out[None],
        latent_grad[None],
        text_grad[None],
        grad_ada,
        *owned,
    )


def solution(mesh):
    placed = (P(("dp", "fsdp"), None, None),) * 3 + (P(("dp", "fsdp")),) * 3 + (P("dp", "fsdp"),) * 8
    return jax.shard_map(
        functools.partial(body, dp_size=mesh.shape["dp"], fsdp_size=mesh.shape["fsdp"]),
        mesh=mesh,
        in_specs=placed,
        out_specs=(P(("dp", "fsdp"), None, None),) * 3 + (P("dp", "fsdp"),) * 8,
        check_vma=False,
    )
```

```python
import functools
import math

import jax
import jax.numpy as jnp
from jax import lax
from jax.experimental import pallas as pl
from jax.experimental.pallas import tpu as pltpu
from jax.sharding import PartitionSpec as P

HEADS = 12


norm_eps = 1e-06


def sinusoid(time_value, model_width):
    half_width = model_width // 2
    frequency = jnp.exp(-math.log(10000.0) * jnp.arange(half_width, dtype=jnp.float32) / half_width)
    angles = time_value.astype(jnp.float32) * frequency
    return jnp.concatenate([jnp.cos(angles), jnp.sin(angles)], axis=-1)


def normalize(values):
    center = values - jnp.mean(values, -1, keepdims=True)
    spread = jnp.mean(center * center, -1, keepdims=True)
    inverse = lax.rsqrt(spread + norm_eps)
    return (center * inverse, inverse)


def norm_back(upstream, normed, inverse, scale_row):
    dshift = jnp.sum(upstream, 0)
    dscale = jnp.sum(upstream * normed, 0)
    scaled = upstream * (1.0 + scale_row)
    centered = (
        scaled
        - jnp.mean(scaled, -1, keepdims=True)
        - normed * jnp.mean(scaled * normed, -1, keepdims=True)
    )
    return (inverse * centered, dshift, dscale)


def outer_sum(left, right):
    return lax.dot_general(
        left, right, (((0,), (0,)), ((), ())), preferred_element_type=jnp.float32
    )


MESH = pl.DeviceIdType.MESH


class Grid:
    def __init__(self, dp_size, fsdp_size):
        self.dp = dp_size
        self.fsdp = fsdp_size
        self.ny = 2
        self.nz = dp_size // 2

    def fits(self, matrices):
        if self.fsdp != 4 or self.dp != 8:
            return False
        for matrix in matrices:
            rows, columns = matrix.shape
            if rows % 32 or (2 * columns) % 128:
                return False
        return True


def pair_halves(matrix, core):
    half = matrix.shape[0] // 2
    mine = lax.dynamic_slice_in_dim(matrix, core * half, half, 0)
    other = lax.dynamic_slice_in_dim(matrix, (1 - core) * half, half, 0)
    return mine, other


def core_swap(value, fsdp_size):
    pairs = [(i, i ^ 1) for i in range(fsdp_size)]
    return lax.ppermute(value, "fsdp", pairs)


def place():
    dp_index = lax.axis_index("dp")
    fsdp_index = lax.axis_index("fsdp")
    return dp_index // 2, dp_index % 2, fsdp_index // 2, fsdp_index % 2


def device(z, y, x, core):
    return {"dp": z * 2 + y, "fsdp": x * 2 + core}


def greet(partners):
    barrier = pltpu.get_barrier_semaphore()
    for partner in partners:
        pl.semaphore_signal(barrier, inc=1, device_id=partner, device_id_type=MESH)
    pl.semaphore_wait(barrier, len(partners))


def gather_kernel(nz, count, *refs):
    blocks = refs[:count]
    wholes = refs[count : 2 * count]
    local_sem, send_sem, recv_sem = refs[2 * count :]
    z, y, x, core = place()
    sibling = device(z, y, x, 1 - core)
    first = device(z, y * (1 - core) + (1 - y) * core, (1 - x) * (1 - core) + x * core, core)
    second = device(z, (1 - y) * (1 - core) + y * core, x * (1 - core) + (1 - x) * core, core)
    others = [device((z + step) % nz, y, x, core) for step in range(1, nz)]
    greet([sibling, first, second, *others])

    def columns(ref, which):
        half = ref.shape[-1] // 2
        return pl.ds(pl.multiple_of(which * half, 128), half)

    def remote(item, slot, src, dst, partner):
        return pltpu.make_async_remote_copy(
            src_ref=src,
            dst_ref=dst,
            send_sem=send_sem.at[item, slot],
            recv_sem=recv_sem.at[item, slot],
            device_id=partner,
            device_id_type=MESH,
        )

    def local(item):
        whole = wholes[item]
        return pltpu.make_async_copy(
            blocks[item], whole.at[z, y, core, :, columns(whole, x)], local_sem.at[item]
        )

    def along_z(item):
        whole = wholes[item]
        spot = whole.at[z, y, core, :, columns(whole, x)]
        return [
            remote(item, step, blocks[item], spot, partner) for step, partner in enumerate(others)
        ]

    def stage_first(item):
        whole = wholes[item]
        part = whole.at[:, y, core, :, columns(whole, x)]
        return [remote(item, nz - 1, part, part, first)]

    def stage_second(item):
        whole = wholes[item]
        copies = []
        for k in range(2):
            row = y * (1 - core) + k * core
            column = k * (1 - core) + x * core
            part = whole.at[:, row, core, :, columns(whole, column)]
            copies.append(remote(item, nz + k, part, part, second))
        return copies

    def stage_core(item):
        part = wholes[item].at[:, :, core]
        return [remote(item, nz + 2, part, part, sibling)]

    stages = [along_z, stage_first, stage_second, stage_core]
    for item in range(count):
        local(item).start()
        for copy in along_z(item):
            copy.start()
    for step in range(count + 3):
        for depth in range(1, 4):
            item = step - depth + 1
            if 0 <= item < count:
                if depth == 1:
                    local(item).wait()
                for copy in stages[depth - 1](item):
                    copy.wait_recv()
                for copy in stages[depth](item):
                    copy.start()
    for item in range(count):
        for copy in stage_core(item):
            copy.wait_recv()
    for item in range(count):
        for stage in stages:
            for copy in stage(item):
                copy.wait_send()


def gather_weights(grid, matrices):
    if not grid.fits(matrices):
        return tuple(
            lax.all_gather(
                lax.all_gather(m, "fsdp", axis=1, tiled=True), "dp", axis=0, tiled=True
            ).reshape(4, 2, 2, m.shape[0] * grid.dp // 16, m.shape[1] * grid.fsdp)
            for m in matrices
        )
    core = lax.axis_index("fsdp") % 2
    halves = [pair_halves(matrix, core) for matrix in matrices]
    swapped = [core_swap(other, grid.fsdp) for _, other in halves]
    blocks = []
    for (mine, _), theirs in zip(halves, swapped):
        both = jnp.where(
            core == 0,
            jnp.concatenate([mine, theirs], 1),
            jnp.concatenate([theirs, mine], 1),
        )
        blocks.append(both)
    count = len(blocks)
    nz = grid.nz
    shapes = [
        jax.ShapeDtypeStruct((nz, 2, 2, b.shape[0], b.shape[1] * 2), b.dtype) for b in blocks
    ]
    wholes = pl.pallas_call(
        functools.partial(gather_kernel, nz, count),
        out_shape=shapes,
        in_specs=[pl.BlockSpec(memory_space=pl.ANY)] * count,
        out_specs=[pl.BlockSpec(memory_space=pl.ANY)] * count,
        scratch_shapes=[
            pltpu.SemaphoreType.DMA((count,)),
            pltpu.SemaphoreType.DMA((count, nz + 3)),
            pltpu.SemaphoreType.DMA((count, nz + 3)),
        ],
        compiler_params=pltpu.CompilerParams(collective_id=0, has_side_effects=True),
        name="gather_weights",
    )(*blocks)
    return tuple(wholes)


def reduce_kernel(nz, count, *refs):
    grads = refs[:count]
    sums = refs[count : 2 * count]
    rest = refs[2 * count :]
    kept, from_core, from_first, from_second, from_z = (
        rest[i * count : (i + 1) * count] for i in range(5)
    )
    local_sem, send_sem, recv_sem = rest[5 * count :]
    z, y, x, core = place()
    sibling = device(z, y, x, 1 - core)
    first = device(z, (1 - y) * (1 - core) + y * core, x * (1 - core) + (1 - x) * core, core)
    second = device(z, y * (1 - core) + (1 - y) * core, (1 - x) * (1 - core) + x * core, core)
    others = [((z + step) % nz, step) for step in range(1, nz)]
    greet([sibling, first, second, *[device(other, y, x, core) for other, _ in others]])

    def columns(ref, which):
        half = ref.shape[-1] // 2
        return pl.ds(pl.multiple_of(which * half, 128), half)

    def remote(item, slot, src, dst, partner):
        return pltpu.make_async_remote_copy(
            src_ref=src,
            dst_ref=dst,
            send_sem=send_sem.at[item, slot],
            recv_sem=recv_sem.at[item, slot],
            device_id=partner,
            device_id_type=MESH,
        )

    def local(item):
        return pltpu.make_async_copy(grads[item].at[:, :, core], kept[item], local_sem.at[item])

    def stage_core(item):
        return [remote(item, nz + 2, grads[item].at[:, :, 1 - core], from_core[item], sibling)]

    def stage_first(item):
        copies = []
        for k in range(2):
            row = (1 - y) * (1 - core) + k * core
            column = k * (1 - core) + (1 - x) * core
            part = kept[item].at[:, row, :, columns(kept[item], column)]
            copies.append(remote(item, nz + k, part, from_first[item].at[:, k], first))
        return copies

    def stage_second(item):
        row = y * (1 - core) + (1 - y) * core
        column = (1 - x) * (1 - core) + x * core
        part = kept[item].at[:, row, :, columns(kept[item], column)]
        return [remote(item, nz - 1, part, from_second[item], second)]

    def along_z(item):
        copies = []
        for other, step in others:
            part = kept[item].at[other, y, :, columns(kept[item], x)]
            copies.append(
                remote(item, step - 1, part, from_z[item].at[step - 1], device(other, y, x, core))
            )
        return copies

    def add_core(item):
        def one(step, carry):
            a, b = step // 2, step % 2
            kept[item][a, b] = (
                kept[item][a, b].astype(jnp.float32) + from_core[item][a, b].astype(jnp.float32)
            ).astype(jnp.bfloat16)
            return carry

        lax.fori_loop(0, nz * 2, one, 0)

    def add_first(item):
        for k in range(2):
            row = y * (1 - core) + k * core
            column = columns(kept[item], k * (1 - core) + x * core)

            def one(a, carry):
                kept[item][a, row, :, column] = (
                    kept[item][a, row, :, column].astype(jnp.float32)
                    + from_first[item][a, k].astype(jnp.float32)
                ).astype(jnp.bfloat16)
                return carry

            lax.fori_loop(0, nz, one, 0)

    def add_second(item):
        column = columns(kept[item], x)

        def one(a, carry):
            kept[item][a, y, :, column] = (
                kept[item][a, y, :, column].astype(jnp.float32)
                + from_second[item][a].astype(jnp.float32)
            ).astype(jnp.bfloat16)
            return carry

        lax.fori_loop(0, nz, one, 0)

    def add_z(item):
        total = kept[item][z, y, :, columns(kept[item], x)].astype(jnp.float32)
        for step in range(nz - 1):
            total += from_z[item][step].astype(jnp.float32)
        sums[item][...] = total

    stages = [stage_core, stage_first, stage_second, along_z]
    adds = [add_core, add_first, add_second, add_z]
    for item in range(count):
        local(item).start()
        for copy in stage_core(item):
            copy.start()
    for step in range(count + 3):
        for depth in range(4):
            item = step - depth
            if 0 <= item < count:
                if depth == 0:
                    local(item).wait()
                for copy in stages[depth](item):
                    copy.wait_recv()
                adds[depth](item)
                if depth < 3:
                    for copy in stages[depth + 1](item):
                        copy.start()
    for item in range(count):
        for stage in stages:
            for copy in stage(item):
                copy.wait_send()


def reduce_gradients(grid, gradients):
    rounded = [g.reshape(-1, g.shape[-1]) for g in gradients]
    blocks = [
        jax.ShapeDtypeStruct((g.shape[0] // grid.dp, g.shape[1] // grid.fsdp), jnp.bfloat16)
        for g in rounded
    ]
    if not grid.fits(blocks):
        out = []
        for g in rounded:
            part = lax.psum_scatter(g, "dp", scatter_dimension=0, tiled=True)
            part = lax.psum_scatter(part, "fsdp", scatter_dimension=1, tiled=True)
            out.append(part.astype(jnp.float32))
        return tuple(out)
    nz = grid.nz
    count = len(rounded)
    shaped = list(gradients)
    rows = [g.shape[3] for g in shaped]
    widths = [g.shape[4] for g in shaped]
    bf16 = jnp.bfloat16
    scratch = [pltpu.VMEM((nz, 2, r, w), bf16) for r, w in zip(rows, widths)]
    scratch += [pltpu.VMEM((nz, 2, r, w), bf16) for r, w in zip(rows, widths)]
    scratch += [pltpu.VMEM((nz, 2, r, w // 2), bf16) for r, w in zip(rows, widths)]
    scratch += [pltpu.VMEM((nz, r, w // 2), bf16) for r, w in zip(rows, widths)]
    scratch += [pltpu.VMEM((nz - 1, r, w // 2), bf16) for r, w in zip(rows, widths)]
    scratch += [
        pltpu.SemaphoreType.DMA((count,)),
        pltpu.SemaphoreType.DMA((count, nz + 3)),
        pltpu.SemaphoreType.DMA((count, nz + 3)),
    ]
    sums = pl.pallas_call(
        functools.partial(reduce_kernel, nz, count),
        out_shape=[
            jax.ShapeDtypeStruct((r, w // 2), jnp.float32) for r, w in zip(rows, widths)
        ],
        in_specs=[pl.BlockSpec(memory_space=pl.ANY)] * count,
        out_specs=[pl.BlockSpec(memory_space=pltpu.VMEM)] * count,
        scratch_shapes=scratch,
        compiler_params=pltpu.CompilerParams(
            collective_id=1, has_side_effects=True, vmem_limit_bytes=56 * 1024 * 1024
        ),
        name="reduce_gradients",
    )(*shaped)
    core = lax.axis_index("fsdp") % 2
    out = []
    for total in sums:
        half = total.shape[1] // 2
        mine = lax.dynamic_slice_in_dim(total, core * half, half, 1)
        other = lax.dynamic_slice_in_dim(total, (1 - core) * half, half, 1)
        theirs = core_swap(other, grid.fsdp)
        out.append(
            jnp.where(
                core == 0,
                jnp.concatenate([mine, theirs], 0),
                jnp.concatenate([theirs, mine], 0),
            )
        )
    return tuple(out)


def modulate(grid, timestep, w_ada):
    rows, columns = w_ada.shape
    model_width = rows * grid.dp
    times = lax.all_gather(timestep, ("dp", "fsdp"), axis=0, tiled=True)
    conditions = jax.nn.silu(
        jax.vmap(lambda value: sinusoid(value, model_width))(times)
    ).astype(jnp.bfloat16)
    mine = lax.dynamic_slice_in_dim(conditions, lax.axis_index("dp") * rows, rows, 1)
    partial = jnp.dot(mine, w_ada, preferred_element_type=jnp.float32)
    summed = lax.psum_scatter(partial, "dp", scatter_dimension=0, tiled=True)
    mixed = lax.all_to_all(summed, "fsdp", split_axis=0, concat_axis=0, tiled=True)
    return mine, mixed.reshape(9, model_width)


def ada_gradient(grid, conditions, dmodulation):
    spread = dmodulation.reshape(grid.fsdp, -1)
    swapped = lax.all_to_all(spread, "fsdp", split_axis=0, concat_axis=0, tiled=True)
    everyone = lax.all_gather(swapped, "dp", axis=0, tiled=True)
    return outer_sum(conditions, everyone)


def ada_inputs(grid, timestep, w_ada):
    rows, columns = w_ada.shape
    condition = jax.nn.silu(sinusoid(timestep[0], rows * grid.dp)).astype(jnp.bfloat16)
    mine = jnp.pad(
        condition.astype(jnp.float32).reshape(grid.dp, 1, rows), ((0, 0), (0, 0), (0, 128 - rows))
    )
    span = -(-columns // 128) * 128
    spare = span - columns
    block = jnp.where(
        lax.axis_index("fsdp") % 2 == 0,
        jnp.pad(w_ada, ((0, 128 - rows), (0, spare))),
        jnp.pad(w_ada, ((0, 128 - rows), (spare, 0))),
    )
    return mine, block


F32 = jnp.float32
BF16 = jnp.bfloat16
NT = (((1,), (1,)), ((), ()))
TN = (((0,), (0,)), ((), ()))


def flat(value):
    return value.reshape(-1, value.shape[-1])


def dot(left, right):
    return jnp.dot(left, right, preferred_element_type=F32)


def dot_nt(left, right):
    return lax.dot_general(left, right, NT, preferred_element_type=F32)


def dot_tn(left, right):
    return lax.dot_general(left, right, TN, preferred_element_type=F32)


def tiles(total, size, body):
    def step(t, carry):
        body(pl.ds(pl.multiple_of(t * size, size), size))
        return carry

    lax.fori_loop(0, total // size, step, 0)


def row_tile(rows):
    for size in (432, 288, 256, 128):
        if rows % size == 0:
            return size
    return rows


def gelu_pair(inner):
    slope = math.sqrt(2.0 / math.pi)
    square = inner * inner
    turned = jnp.tanh(inner * (slope + (slope * 0.044715) * square))
    half = 0.5 + 0.5 * turned
    rise = inner * (slope + (3.0 * slope * 0.044715) * square)
    return inner * half, half + (0.5 - 0.5 * turned * turned) * rise


def half_lanes(shape):
    return lax.broadcasted_iota(jnp.int32, shape, 1) < shape[1] // 2


def attend(queries, keys, values, bias, mixed, heads_wide, size):
    query_ref, query_at = queries
    key_ref, key_at = keys
    value_ref, value_at = values
    mixed_ref, mixed_at = mixed
    rows = mixed_ref.shape[0]
    width = 2 * heads_wide

    def pair(p, carry):
        def at(start):
            return pl.ds(pl.multiple_of(start + p * width, width), width)

        key_pair = key_ref[:, at(key_at)]
        value_pair = value_ref[:, at(value_at)]
        low = half_lanes((size, width))
        for start in range(0, rows, size):
            scaled = query_ref[start : start + size, at(query_at)] * BF16(heads_wide**-0.5)
            outs = []
            for head in range(2):
                own = jnp.where(low if head == 0 else ~low, scaled, BF16(0))
                scores = dot_nt(own, key_pair) + bias[...]
                raised = jnp.exp(scores - jnp.max(scores, -1, keepdims=True))
                summed = jnp.sum(raised, -1, keepdims=True)
                outs.append(dot(raised.astype(BF16), value_pair) * (1.0 / summed))
            mixed_ref[start : start + size, at(mixed_at)] = jnp.where(
                low, outs[0], outs[1]
            ).astype(BF16)
        return carry

    return pair


def attend_back(queries, keys, values, bias, upstream, heads_wide, size):
    query_ref, query_at = queries
    key_ref, key_at = keys
    value_ref, value_at = values
    rows = upstream.shape[0]
    slots = bias.shape[1]
    width = 2 * heads_wide
    factor = BF16(heads_wide**-0.5)

    def pair(p, carry):
        def at(start):
            return pl.ds(pl.multiple_of(start + p * width, width), width)

        key_pair = key_ref[:, at(key_at)]
        value_pair = value_ref[:, at(value_at)]
        low = half_lanes((size, width))
        low_keys = half_lanes((slots, width))
        key_grad = jnp.zeros((slots, width), F32)
        value_grad = jnp.zeros((slots, width), F32)
        for start in range(0, rows, size):
            scaled = query_ref[start : start + size, at(query_at)] * factor
            above = upstream[start : start + size, at(0)]
            query_grad = jnp.zeros((size, width), F32)
            for head in range(2):
                mask = low if head == 0 else ~low
                own = jnp.where(mask, scaled, BF16(0))
                own_above = jnp.where(mask, above, BF16(0))
                own_keys = jnp.where(low_keys if head == 0 else ~low_keys, key_pair, BF16(0))
                scores = dot_nt(own, key_pair) + bias[...]
                raised = jnp.exp(scores - jnp.max(scores, -1, keepdims=True))
                shares = raised * (1.0 / jnp.sum(raised, -1, keepdims=True))
                share_grad = dot_nt(own_above, value_pair)
                total = jnp.sum(shares * share_grad, -1, keepdims=True)
                score_grad = (shares * (share_grad - total)).astype(BF16)
                value_grad += dot_tn(shares.astype(BF16), own_above)
                key_grad += dot_tn(score_grad, own)
                query_grad += dot(score_grad, own_keys)
            query_ref[start : start + size, at(query_at)] = (
                query_grad * heads_wide**-0.5
            ).astype(BF16)
        key_ref[:, at(key_at)] = key_grad.astype(BF16)
        value_ref[:, at(value_at)] = value_grad.astype(BF16)
        return carry

    return pair


class Loads:
    def __init__(self, sems):
        self.sems = sems
        self.copies = {}

    def start(self, name, src, dst):
        copy = pltpu.make_async_copy(src, dst, self.sems.at[len(self.copies)])
        copy.start()
        self.copies[name] = copy

    def wait(self, *names):
        for name in names:
            self.copies[name].wait()


WEIGHTS = ("qkv", "out", "cq", "ckv", "cout", "fc1", "fc2")
PARTS = 4


def half_columns(ref, which, first=0, width=None):
    half = ref.shape[-1] // 2
    if width is None:
        width = half
    return pl.ds(pl.multiple_of(which * half + first, 128), width)


class Item:
    def __init__(self, name, rows=None, first=0, width=None):
        self.name = name
        self.rows = rows
        self.first = first
        self.width = width


def gather_items(held):
    items = []
    rows = held["qkv"].shape[3]
    items += [Item("qkv", (r, 16)) for r in range(0, rows, 16)]
    items += [Item("out"), Item("cq"), Item("ckv"), Item("cout")]
    rows = held["fc2"].shape[3]
    items += [Item("fc2", (r, rows // 4)) for r in range(0, rows, rows // 4)]
    width = held["fc1"].shape[-1] // 2 // PARTS
    items += [Item("fc1", None, part * width, width) for part in range(PARTS)]
    return items


class Gather:
    def __init__(self, where, given, held, own, swapped, items, sems):
        self.z, self.y, self.x, self.core = where
        self.given, self.held, self.own, self.swapped, self.items = given, held, own, swapped, items
        self.swap_sem, self.send_sem, self.recv_sem = sems
        self.nz = held["out"].shape[0]
        z, y, x, core = where
        self.sibling = device(z, y, x, 1 - core)
        self.first = device(
            z, y * (1 - core) + (1 - y) * core, (1 - x) * (1 - core) + x * core, core
        )
        self.second = device(
            z, (1 - y) * (1 - core) + y * core, x * (1 - core) + (1 - x) * core, core
        )
        self.others = [device((z + step) % self.nz, y, x, core) for step in range(1, self.nz)]
        self.done = 0

    def swap(self, number):
        name = WEIGHTS[number]
        rows = self.own[name].shape[0]
        start = pl.multiple_of((1 - self.core) * rows, 16)
        return pltpu.make_async_remote_copy(
            src_ref=self.given[name].at[pl.ds(start, rows), :],
            dst_ref=self.swapped[name],
            send_sem=self.swap_sem.at[0, number],
            recv_sem=self.swap_sem.at[1, number],
            device_id=self.sibling,
            device_id_type=MESH,
        )

    def keep(self, number):
        name = WEIGHTS[number]
        rows = self.own[name].shape[0]
        start = pl.multiple_of(self.core * rows, 16)
        return pltpu.make_async_copy(
            self.given[name].at[pl.ds(start, rows), :], self.own[name], self.swap_sem.at[2, number]
        )

    def assemble(self, number):
        name = WEIGHTS[number]
        self.keep(number).wait()
        self.swap(number).wait_recv()
        mine, theirs = self.own[name][...], self.swapped[name][...]
        whole = self.held[name]
        whole[self.z, self.y, self.core, :, half_columns(whole, self.x)] = jnp.where(
            self.core == 0,
            jnp.concatenate([mine, theirs], 1),
            jnp.concatenate([theirs, mine], 1),
        )

    def remote(self, number, slot, part, partner):
        return pltpu.make_async_remote_copy(
            src_ref=part,
            dst_ref=part,
            send_sem=self.send_sem.at[number, slot],
            recv_sem=self.recv_sem.at[number, slot],
            device_id=partner,
            device_id_type=MESH,
        )

    def view(self, number):
        item = self.items[number]
        whole = self.held[item.name]
        rows = slice(None) if item.rows is None else pl.ds(*item.rows)
        return whole, rows, lambda which: half_columns(whole, which, item.first, item.width)

    def along_z(self, number):
        whole, rows, columns = self.view(number)
        part = whole.at[self.z, self.y, self.core, rows, columns(self.x)]
        return [self.remote(number, s, part, partner) for s, partner in enumerate(self.others)]

    def to_first(self, number):
        whole, rows, columns = self.view(number)
        part = whole.at[:, self.y, self.core, rows, columns(self.x)]
        return [self.remote(number, self.nz - 1, part, self.first)]

    def to_second(self, number):
        whole, rows, columns = self.view(number)
        copies = []
        for k in range(2):
            row = self.y * (1 - self.core) + k * self.core
            column = k * (1 - self.core) + self.x * self.core
            part = whole.at[:, row, self.core, rows, columns(column)]
            copies.append(self.remote(number, self.nz + k, part, self.second))
        return copies

    def to_core(self, number):
        whole, rows, columns = self.view(number)
        if self.items[number].width is None:
            parts = [whole.at[:, :, self.core, rows, :]]
        else:
            parts = [whole.at[:, :, self.core, rows, columns(k)] for k in range(2)]
        return [
            self.remote(number, self.nz + 2 + k, part, self.sibling) for k, part in enumerate(parts)
        ]

    def advance(self, steps):
        stages = [self.along_z, self.to_first, self.to_second, self.to_core]
        while self.done < steps:
            for depth in range(1, 4):
                number = self.done - depth + 1
                if 0 <= number < len(self.items):
                    for copy in stages[depth - 1](number):
                        copy.wait_recv()
                    for copy in stages[depth](number):
                        copy.start()
            self.done += 1

    def numbers(self, name):
        return [i for i, item in enumerate(self.items) if item.name == name]

    def need(self, numbers):
        self.advance(max(numbers) + 3)
        for number in numbers:
            for copy in self.to_core(number):
                copy.wait_recv()

    def sent(self, numbers):
        for number in numbers:
            for stage in (self.along_z, self.to_first, self.to_second, self.to_core):
                for copy in stage(number):
                    copy.wait_send()


def everyone(dp_size, fsdp_size, body):
    count = dp_size * fsdp_size
    me = lax.axis_index("dp") * fsdp_size + lax.axis_index("fsdp")

    def one(step, carry):
        body(step, (me + step) % count, me)
        return carry

    lax.fori_loop(1, count, one, 0)


def modulate_start(dp_size, fsdp_size, mine, everything, sems):
    def copy(step, target, me, row):
        return pltpu.make_async_remote_copy(
            src_ref=mine.at[row],
            dst_ref=everything.at[me],
            send_sem=sems.at[0, step - 1],
            recv_sem=sems.at[1, step - 1],
            device_id={"dp": target // fsdp_size, "fsdp": target % fsdp_size},
            device_id_type=MESH,
        )

    return copy


def forward_kernel(comm, *refs):
    (lat, text, og, frame_bias, text_bias), refs = refs[:5], refs[5:]
    if comm:
        (mine, w_ada), refs = refs[:2], refs[2:]
    else:
        (mod_in,), refs = refs[:1], refs[1:]
    given, refs = dict(zip(WEIGHTS, refs[:7])), refs[7:]
    (layer_out, dcross_out, qkv_out, h1_out, mixed1_out, h2_out, q2_out, mixed2_out), refs = (
        refs[:8],
        refs[8:],
    )
    (memory_out, after_out, branch_out), refs = refs[:3], refs[3:]
    kept_out, refs = dict(zip(BACK, refs[:5])), refs[5:]
    (fc1_out, fc2_out, rows_out, mod, conditions), refs = refs[:5], refs[5:]
    held, refs = dict(zip(WEIGHTS, refs[:7])), refs[7:]
    big, wide, h3, db3, act, din, memory, after_self, branch_1, branch_2, after_cross, result = (
        refs[:12]
    )
    refs = refs[12:]
    slots, model = lat.shape
    inner_width = held["fc1"].shape[-1]
    head = model // HEADS
    size = row_tile(slots)
    if comm:
        dp_size, fsdp_size = comm
        (everybody, partial, modulations, ada_sems), refs = refs[:4], refs[4:]
        own, refs = dict(zip(WEIGHTS, refs[:7])), refs[7:]
        swapped, refs = dict(zip(WEIGHTS, refs[:7])), refs[7:]
        gather_sems, sems = refs[:3], refs[3]
        items = gather_items(held)
        gather = Gather(place(), given, held, own, swapped, items, gather_sems)
        order = [WEIGHTS.index(n) for n in dict.fromkeys(item.name for item in items)]
        for number in order:
            gather.keep(number).start()
        barrier = pltpu.get_barrier_semaphore()

        def greet_one(step, target, me):
            pl.semaphore_signal(
                barrier,
                inc=1,
                device_id={"dp": target // fsdp_size, "fsdp": target % fsdp_size},
                device_id_type=MESH,
            )

        everyone(dp_size, fsdp_size, greet_one)
        pl.semaphore_wait(barrier, dp_size * fsdp_size - 1)
        for number in order:
            gather.swap(number).start()
        dp_index = lax.axis_index("dp")
        me = dp_index * fsdp_size + lax.axis_index("fsdp")
        send_1 = modulate_start(dp_size, fsdp_size, mine, everybody, ada_sems.at[0])
        send_2 = modulate_start(dp_size, fsdp_size, partial, modulations, ada_sems.at[1])
        everyone(dp_size, fsdp_size, lambda s, t, m: send_1(s, t, m, t // fsdp_size).start())
        everybody[me] = mine[dp_index]

        def launch(name):
            gather.assemble(WEIGHTS.index(name))
            for number in gather.numbers(name):
                for copy in gather.along_z(number):
                    copy.start()

        launch("qkv")
        everyone(dp_size, fsdp_size, lambda s, t, m: send_1(s, t, m, t // fsdp_size).wait_recv())
        for k in range(dp_size * fsdp_size):
            conditions[k : k + 1, :] = everybody[k]
        product = dot(conditions[...].astype(BF16), w_ada[...])
        for k in range(dp_size * fsdp_size):
            partial[k] = product[k : k + 1, :]
        everyone(dp_size, fsdp_size, lambda s, t, m: send_2(s, t, m, t).start())
        modulations[me] = partial[me]
        for number in order[1:]:
            launch(WEIGHTS[number])
        gather.advance(2)
        everyone(dp_size, fsdp_size, lambda s, t, m: send_2(s, t, m, t).wait_recv())
        mod[...] = jnp.zeros_like(mod)
        span = partial.shape[-1]
        for j in range(fsdp_size):
            total = modulations[j]
            for i in range(1, dp_size):
                total += modulations[i * fsdp_size + j]
            start = j * mod.shape[1] // fsdp_size // 128 * 128
            mod[:, start : start + span] += total
    else:
        sems = refs[0]
        mod[...] = mod_in[...]
        conditions[...] = jnp.zeros_like(conditions)
    loads = Loads(sems)
    if not comm:
        for name in WEIGHTS:
            loads.start(name, given[name], held[name])

    def need(name, part=None):
        if not comm:
            if not part:
                loads.wait(name)
            return
        numbers = gather.numbers(name)
        gather.need(numbers if part is None else [numbers[part]])

    def hook(p, plan):
        if comm:
            for at, steps in plan:

                @pl.when(p == at)
                def _():
                    gather.advance(steps)

    def row(k):
        return mod[:, k * model : (k + 1) * model]

    big[slots:, :] = jnp.zeros((big.shape[0] - slots, big.shape[1]), BF16)

    def norm_1(rows):
        normed, _ = normalize(lat[rows, :].astype(F32))
        wide[rows, 0:model] = (normed * (1.0 + row(1)) + row(0)).astype(BF16)

    tiles(slots, size, norm_1)
    need("qkv")
    for part in range(3):
        columns = slice(part * model, (part + 1) * model)

        def project(rows):
            big[rows, columns] = dot(
                wide[rows, 0:model], flat(held["qkv"][:, :, :, :, columns])
            ).astype(BF16)

        tiles(slots, size, project)
    loads.start("qkv_out", big.at[0:slots, 0 : 3 * model], qkv_out)
    loads.start("h1_out", wide.at[:, 0:model], h1_out)
    if comm:
        loads.start("kept_qkv", held["qkv"], kept_out["qkv"])
    pair = attend(
        (big, 0), (big, model), (big, 2 * model), frame_bias, (wide, model), head, size
    )

    def pair_1(p, carry):
        hook(p, ((1, 6), (2, 7), (4, 8), (5, 9)))
        return pair(p, carry)

    lax.fori_loop(0, HEADS // 2, pair_1, 0)
    loads.start("mixed1_out", wide.at[:, model : 2 * model], mixed1_out)
    need("out")
    need("cq")

    def join_1(rows):
        branch = dot(wide[rows, model : 2 * model], flat(held["out"][...]))
        branch_1[rows, :] = branch
        after = lat[rows, :].astype(F32) + row(2) * branch
        after_self[rows, :] = after
        normed, _ = normalize(after)
        hidden = (normed * (1.0 + row(4)) + row(3)).astype(BF16)
        wide[rows, 2 * model : 3 * model] = hidden
        wide[rows, 3 * model : 4 * model] = dot(hidden, flat(held["cq"][...])).astype(BF16)

    tiles(slots, size, join_1)
    loads.start("branch_out", branch_1, branch_out)
    loads.start("after_out", after_self, after_out)
    loads.start("h2_out", wide.at[:, 2 * model : 3 * model], h2_out)
    loads.start("q2_out", wide.at[:, 3 * model : 4 * model], q2_out)
    need("ckv")
    for part in range(2):
        columns = slice(part * model, (part + 1) * model)
        memory[:, columns] = dot(text[...], flat(held["ckv"][:, :, :, :, columns])).astype(BF16)
    loads.start("memory_out", memory, memory_out)
    mixed2 = big.at[0:slots, 3 * model : 4 * model]
    pair = attend(
        (wide, 3 * model), (memory, 0), (memory, model), text_bias, (mixed2, 0), head, size
    )

    def pair_2(p, carry):
        hook(p, ((2, 10), (5, 11)))
        return pair(p, carry)

    lax.fori_loop(0, HEADS // 2, pair_2, 0)
    loads.start("mixed2_out", mixed2, mixed2_out)
    need("cout")

    def join_2(rows):
        branch = dot(mixed2[rows, :], flat(held["cout"][...]))
        branch_2[rows, :] = branch
        after = after_self[rows, :] + row(5) * branch
        after_cross[rows, :] = after
        normed, _ = normalize(after)
        h3[rows, :] = (normed * (1.0 + row(7)) + row(6)).astype(BF16)
        db3[rows, :] = (row(8) * og[rows, :].astype(F32)).astype(BF16)

    tiles(slots, size, join_2)
    if comm:
        for name in BACK[1:]:
            loads.start("kept_" + name, held[name], kept_out[name])
    need("fc2")
    loads.wait("branch_out")
    rows_out[...] = jnp.zeros_like(rows_out)
    first, second = held["fc1"], held["fc2"]
    upstream_sum = branch_1
    width = inner_width // 2 // PARTS
    per = second.shape[0] * second.shape[1] // 2

    def chunk(t):
        return t // second.shape[1], t % second.shape[1]

    for part in range(PARTS):
        need("fc1", part)
        spans = [slice(k * inner_width // 2 + part * width, k * inner_width // 2 + (part + 1) * width) for k in range(2)]
        chunks = [chunk(part), chunk(per + part)]

        def feed(rows):
            matrix_1 = jnp.concatenate([flat(first[:, :, :, :, s]) for s in spans], 1)
            matrix_2 = jnp.concatenate([flat(second[a, b]) for a, b in chunks], 0)
            activated, slope = gelu_pair(dot(h3[rows, :], matrix_1))
            activated = activated.astype(BF16)
            dinner = (dot_nt(db3[rows, :], matrix_2) * slope).astype(BF16)
            act[rows, :] = activated
            din[rows, :] = dinner
            forward = dot(activated, matrix_2)
            backward = dot_nt(dinner, matrix_1)
            if part == 0:
                result[rows, :] = forward
                upstream_sum[rows, :] = backward
            else:
                result[rows, :] += forward
                upstream_sum[rows, :] += backward

        tiles(slots, size, feed)
        if comm:
            numbers = gather.numbers("fc1")[part : part + 1]
            if part == 0:
                numbers = gather.numbers("fc2") + numbers
            gather.sent(numbers)
        product = dot_tn(act[...], db3[...]).astype(BF16)
        for k, (a, b) in enumerate(chunks):
            second[a, b] = product[k * width : (k + 1) * width].reshape(second.shape[2:])
        product = dot_tn(h3[...], din[...]).astype(BF16)
        for k, span in enumerate(spans):
            first[:, :, :, :, span] = product[:, k * width : (k + 1) * width].reshape(
                first.shape[:4] + (width,)
            )

    loads.start("fc2_out", second, fc2_out)
    loads.start("fc1_out", first, fc1_out)

    def leave(rows):
        entering = after_cross[rows, :]
        branch = result[rows, :]
        grad = og[rows, :].astype(F32)
        result[rows, :] = entering + row(8) * branch
        normed, inverse = normalize(entering)
        back, dshift, dscale = norm_back(upstream_sum[rows, :], normed, inverse, row(7))
        dcross = grad + back
        after_cross[rows, :] = dcross
        rows_out[0:1, :] += jnp.sum(grad * branch, 0, keepdims=True)
        rows_out[1:2, :] += dshift[None]
        rows_out[2:3, :] += dscale[None]
        rows_out[3:4, :] += jnp.sum(dcross * branch_2[rows, :], 0, keepdims=True)

    tiles(slots, size, leave)
    loads.start("layer_out", result, layer_out)
    loads.start("dcross_out", after_cross, dcross_out)
    if comm:
        for number in order:
            gather.swap(number).wait_send()
        for name in BACK:
            gather.sent(gather.numbers(name))
            loads.wait("kept_" + name)
        everyone(dp_size, fsdp_size, lambda s, t, m: send_1(s, t, m, t // fsdp_size).wait_send())
        everyone(dp_size, fsdp_size, lambda s, t, m: send_2(s, t, m, t).wait_send())
    loads.wait("qkv_out", "h1_out", "mixed1_out", "h2_out", "q2_out", "mixed2_out")
    loads.wait("after_out", "memory_out", "layer_out", "dcross_out", "fc1_out", "fc2_out")


def forward(grid, latent, text_block, upstream, frame_bias, text_bias, ada, matrices):
    slots, model = latent.shape
    text_slots = text_block.shape[0]
    padded = frame_bias.shape[1]
    comm = grid.fits(matrices)
    lead = (4, 2, 2)
    devices = grid.dp * grid.fsdp
    if comm:
        wholes = [
            lead + (m.shape[0] * grid.dp // 16, m.shape[1] * grid.fsdp) for m in matrices
        ]
    else:
        wholes = [m.shape for m in matrices]
    inner_width = wholes[5][-1]
    shaped = jax.ShapeDtypeStruct
    narrow = shaped((slots, model), BF16)
    full = shaped((slots, model), F32)
    outs = [
        full,
        full,
        shaped((slots, 3 * model), BF16),
        narrow,
        narrow,
        narrow,
        narrow,
        narrow,
        shaped((text_slots, 2 * model), BF16),
        full,
        full,
    ]
    outs += [shaped(w if comm else (8, 128), BF16) for w in wholes[:5]]
    outs += [
        shaped(wholes[5], BF16),
        shaped(wholes[6], BF16),
        shaped((8, model), F32),
        shaped((1, 9 * model), F32),
        shaped((devices, 128), F32),
    ]
    vmem = pl.BlockSpec(memory_space=pltpu.VMEM)
    anywhere = pl.BlockSpec(memory_space=pl.ANY)
    scratch = [pltpu.VMEM(w, BF16) for w in wholes]
    scratch += [
        pltpu.VMEM((padded, 4 * model), BF16),
        pltpu.VMEM((slots, 4 * model), BF16),
    ]
    scratch += [pltpu.VMEM((slots, model), BF16)] * 4
    scratch += [pltpu.VMEM((text_slots, 2 * model), BF16)]
    scratch += [pltpu.VMEM((slots, model), F32)] * 5
    if comm:
        items = gather_items(dict(zip(WEIGHTS, [shaped(w, BF16) for w in wholes])))
        halves = [(m.shape[0] // 2, m.shape[1]) for m in matrices]
        span = ada[1].shape[1]
        scratch += [
            pltpu.VMEM((devices, 1, 128), F32),
            pltpu.VMEM((devices, 1, span), F32),
            pltpu.VMEM((devices, 1, span), F32),
            pltpu.SemaphoreType.DMA((2, 2, devices - 1)),
        ]
        scratch += [pltpu.VMEM(h, BF16) for h in halves] * 2
        scratch += [
            pltpu.SemaphoreType.DMA((3, len(matrices))),
            pltpu.SemaphoreType.DMA((len(items), lead[0] + 4)),
            pltpu.SemaphoreType.DMA((len(items), lead[0] + 4)),
        ]
    scratch += [pltpu.SemaphoreType.DMA((24,))]
    params = {"vmem_limit_bytes": 62 * 1024 * 1024}
    if comm:
        params.update(collective_id=0, has_side_effects=True)
    results = pl.pallas_call(
        functools.partial(forward_kernel, (grid.dp, grid.fsdp) if comm else None),
        out_shape=outs,
        in_specs=[vmem] * (5 + len(ada)) + [anywhere] * 7,
        out_specs=[anywhere] * 18 + [vmem] * 3,
        scratch_shapes=scratch,
        compiler_params=pltpu.CompilerParams(**params),
        name="forward",
    )(latent, text_block, upstream, frame_bias, text_bias, *ada, *matrices)
    kept_matrices = results[11:16] if comm else matrices[:5]
    return results[0], results[1:11], kept_matrices, results[16:]


BACK = ("qkv", "out", "cq", "ckv", "cout")


def backward_kernel(*refs):
    (lat, text, mod, frame_bias, text_bias), refs = refs[:5], refs[5:]
    names = ("dcross", "qkv_act", "h1", "mixed1", "h2", "q2", "mixed2", "memory", "after", "branch")
    given, refs = dict(zip(names, refs[:10])), refs[10:]
    matrices, refs = dict(zip(BACK, refs[:5])), refs[5:]
    (latent_out, text_out, rows_out), refs = refs[:3], refs[3:]
    grads_out, refs = dict(zip(BACK, refs[:5])), refs[5:]
    act, refs = dict(zip(names, refs[:10])), refs[10:]
    held, refs = dict(zip(BACK, refs[:5])), refs[5:]
    grad_qkv, above, sems = refs
    slots, model = lat.shape
    head = model // HEADS
    size = row_tile(slots)
    loads = Loads(sems)
    for name in ("dcross", "mixed2", "q2", "memory", "h2", "after", "branch", "mixed1", "h1"):
        loads.start(name, given[name], act[name])
    loads.start("qkv_act", given["qkv_act"], act["qkv_act"].at[0:slots, :])
    for name in ("cout", "cq", "ckv", "out", "qkv"):
        loads.start("w" + name, matrices[name], held[name])

    def row(k):
        return mod[:, k * model : (k + 1) * model]

    def place_grad(target, name, columns, left, right):
        product = dot_tn(left, right).astype(BF16)
        target[:, :, :, :, columns] = product.reshape(target.shape[:4] + (-1,))

    rows_out[...] = jnp.zeros_like(rows_out)
    dcross = act["dcross"]
    loads.wait("dcross", "wcout")

    def enter_2(rows):
        small = (row(5) * dcross[rows, :]).astype(BF16)
        above[0, rows, :] = small
        above[1, rows, :] = dot_nt(small, flat(held["cout"][...])).astype(BF16)

    tiles(slots, size, enter_2)
    loads.wait("mixed2")
    place_grad(held["cout"], "cout", slice(0, model), act["mixed2"][...], above[0])
    loads.start("gcout", held["cout"], grads_out["cout"])
    loads.wait("q2", "memory")
    pair = attend_back(
        (act["q2"], 0), (act["memory"], 0), (act["memory"], model), text_bias, above.at[1], head, size
    )
    lax.fori_loop(0, HEADS // 2, pair, 0)
    loads.wait("wcq", "wckv", "after", "branch", "h2")
    text_out[...] = dot_nt(act["memory"][...], flat(held["ckv"][...]))
    for part in range(2):
        columns = slice(part * model, (part + 1) * model)
        place_grad(held["ckv"], "ckv", columns, text[...], act["memory"][:, columns])
    loads.start("gckv", held["ckv"], grads_out["ckv"])
    loads.wait("wout")

    def leave_2(rows):
        upstream = dot_nt(act["q2"][rows, :], flat(held["cq"][...]))
        normed, inverse = normalize(act["after"][rows, :])
        back, dshift, dscale = norm_back(upstream, normed, inverse, row(4))
        dself = dcross[rows, :] + back
        dcross[rows, :] = dself
        rows_out[0:1, :] += dshift[None]
        rows_out[1:2, :] += dscale[None]
        rows_out[2:3, :] += jnp.sum(dself * act["branch"][rows, :], 0, keepdims=True)
        small = (row(2) * dself).astype(BF16)
        above[0, rows, :] = small
        above[1, rows, :] = dot_nt(small, flat(held["out"][...])).astype(BF16)

    tiles(slots, size, leave_2)
    place_grad(held["cq"], "cq", slice(0, model), act["h2"][...], act["q2"][...])
    loads.start("gcq", held["cq"], grads_out["cq"])
    loads.wait("mixed1")
    place_grad(held["out"], "out", slice(0, model), act["mixed1"][...], above[0])
    loads.start("gout", held["out"], grads_out["out"])
    loads.wait("qkv_act")
    packed = act["qkv_act"]
    packed[slots:, :] = jnp.zeros((packed.shape[0] - slots, 3 * model), BF16)
    pair = attend_back(
        (packed, 0), (packed, model), (packed, 2 * model), frame_bias, above.at[1], head, 288
    )
    lax.fori_loop(0, HEADS // 2, pair, 0)
    loads.wait("h1", "wqkv")
    for part in range(3):
        columns = slice(part * model, (part + 1) * model)
        place_grad(grad_qkv, "qkv", columns, act["h1"][...], packed[0:slots, columns])
    loads.start("gqkv", grad_qkv, grads_out["qkv"])

    def leave_1(rows):
        upstream = dot_nt(packed[rows, :], flat(held["qkv"][...]))
        normed, inverse = normalize(lat[rows, :].astype(F32))
        back, dshift, dscale = norm_back(upstream, normed, inverse, row(1))
        dcross[rows, :] = dcross[rows, :] + back
        rows_out[3:4, :] += dshift[None]
        rows_out[4:5, :] += dscale[None]

    tiles(slots, size, leave_1)
    loads.start("latent", dcross, latent_out)
    loads.wait("gcout", "gckv", "gcq", "gout", "gqkv", "latent")


def backward(latent, text_block, modulation, frame_bias, text_bias, kept, matrices):
    slots, model = latent.shape
    text_slots = text_block.shape[0]
    padded = frame_bias.shape[1]
    shaped = jax.ShapeDtypeStruct
    outs = [
        shaped((slots, model), F32),
        shaped((text_slots, model), F32),
        shaped((8, model), F32),
    ]
    outs += [shaped(m.shape, BF16) for m in matrices]
    vmem = pl.BlockSpec(memory_space=pltpu.VMEM)
    anywhere = pl.BlockSpec(memory_space=pl.ANY)
    scratch = [pltpu.VMEM(k.shape, k.dtype) for k in kept]
    scratch[1] = pltpu.VMEM((padded, 3 * model), BF16)
    scratch += [pltpu.VMEM(m.shape, BF16) for m in matrices]
    scratch += [
        pltpu.VMEM(matrices[0].shape, BF16),
        pltpu.VMEM((2, slots, model), BF16),
        pltpu.SemaphoreType.DMA((24,)),
    ]
    return pl.pallas_call(
        backward_kernel,
        out_shape=outs,
        in_specs=[vmem] * 5 + [anywhere] * 15,
        out_specs=[anywhere, vmem, vmem] + [anywhere] * 5,
        scratch_shapes=scratch,
        compiler_params=pltpu.CompilerParams(vmem_limit_bytes=62 * 1024 * 1024),
        name="backward",
    )(latent, text_block, modulation, frame_bias, text_bias, *kept, *matrices)


def body(
    latents,
    text_rows,
    out_grad,
    frame_len,
    text_len,
    timestep,
    w_ada,
    w_qkv,
    w_out,
    w_cq,
    w_ckv,
    w_cout,
    w_fc1,
    w_fc2,
    *,
    dp_size,
    fsdp_size,
):
    grid = Grid(dp_size, fsdp_size)
    matrices = (w_qkv, w_out, w_cq, w_ckv, w_cout, w_fc1, w_fc2)
    slot_count, model_width = latents.shape[1:]
    text_slots = text_rows.shape[1]
    padded = -(-slot_count // 128) * 128
    frame_bias = jnp.where(jnp.arange(padded) < frame_len[0], 0.0, -1e30).astype(F32)[None]
    text_bias = jnp.where(jnp.arange(text_slots) < text_len[0], 0.0, -1e30).astype(F32)[None]
    if grid.fits(matrices):
        ada = ada_inputs(grid, timestep, w_ada)
    else:
        matrices = gather_weights(grid, matrices)
        conditions, modulation = modulate(grid, timestep, w_ada)
        ada = (modulation.reshape(1, -1),)
    layer_out, kept, kept_matrices, rest = forward(
        grid, latents[0], text_rows[0], out_grad[0], frame_bias, text_bias, ada, matrices
    )
    grad_fc1, grad_fc2, rows_3, modulation, rows = rest
    if len(ada) > 1:
        conditions = rows[:, : w_ada.shape[0]].astype(BF16)
    results = backward(
        latents[0], text_rows[0], modulation, frame_bias, text_bias, kept, kept_matrices
    )
    latent_grad, text_grad, rows_1 = results[:3]
    order = (
        rows_1[3:4],
        rows_1[4:5],
        rows_1[2:3],
        rows_1[0:1],
        rows_1[1:2],
        rows_3[3:4],
        rows_3[1:2],
        rows_3[2:3],
        rows_3[0:1],
    )
    dmodulation = jnp.concatenate(order, 0).reshape(1, -1).astype(BF16)
    grad_ada = ada_gradient(grid, conditions, dmodulation)
    owned = reduce_gradients(grid, (*results[3:8], grad_fc1, grad_fc2))
    return (
        layer_out[None],
        latent_grad[None],
        text_grad[None],
        grad_ada,
        *owned,
    )


def solution(mesh):
    placed = (P(("dp", "fsdp"), None, None),) * 3 + (P(("dp", "fsdp")),) * 3 + (P("dp", "fsdp"),) * 8
    return jax.shard_map(
        functools.partial(body, dp_size=mesh.shape["dp"], fsdp_size=mesh.shape["fsdp"]),
        mesh=mesh,
        in_specs=placed,
        out_specs=(P(("dp", "fsdp"), None, None),) * 3 + (P("dp", "fsdp"),) * 8,
        check_vma=False,
    )
```

```python
import functools
import math

import jax
import jax.numpy as jnp
from jax import lax
from jax.experimental import pallas as pl
from jax.experimental.pallas import tpu as pltpu
from jax.sharding import PartitionSpec as P

HEADS = 12


norm_eps = 1e-06


def sinusoid(time_value, model_width):
    half_width = model_width // 2
    frequency = jnp.exp(-math.log(10000.0) * jnp.arange(half_width, dtype=jnp.float32) / half_width)
    angles = time_value.astype(jnp.float32) * frequency
    return jnp.concatenate([jnp.cos(angles), jnp.sin(angles)], axis=-1)


def normalize(values):
    center = values - jnp.mean(values, -1, keepdims=True)
    spread = jnp.mean(center * center, -1, keepdims=True)
    inverse = lax.rsqrt(spread + norm_eps)
    return (center * inverse, inverse)


def norm_back(upstream, normed, inverse, scale_row):
    dshift = jnp.sum(upstream, 0)
    dscale = jnp.sum(upstream * normed, 0)
    scaled = upstream * (1.0 + scale_row)
    centered = (
        scaled
        - jnp.mean(scaled, -1, keepdims=True)
        - normed * jnp.mean(scaled * normed, -1, keepdims=True)
    )
    return (inverse * centered, dshift, dscale)


def outer_sum(left, right):
    return lax.dot_general(
        left, right, (((0,), (0,)), ((), ())), preferred_element_type=jnp.float32
    )


MESH = pl.DeviceIdType.MESH


class Grid:
    def __init__(self, dp_size, fsdp_size):
        self.dp = dp_size
        self.fsdp = fsdp_size

    def fits(self, matrices):
        if self.fsdp != 4 or self.dp != 8:
            return False
        for matrix in matrices:
            rows, columns = matrix.shape
            if rows % 32 or (2 * columns) % 128:
                return False
        return True


def place():
    dp_index = lax.axis_index("dp")
    fsdp_index = lax.axis_index("fsdp")
    return dp_index // 2, dp_index % 2, fsdp_index // 2, fsdp_index % 2


def device(z, y, x, core):
    return {"dp": z * 2 + y, "fsdp": x * 2 + core}


def gather_weights(grid, matrices):
    return tuple(
        lax.all_gather(
            lax.all_gather(m, "fsdp", axis=1, tiled=True), "dp", axis=0, tiled=True
        ).reshape(4, 2, 2, m.shape[0] * grid.dp // 16, m.shape[1] * grid.fsdp)
        for m in matrices
    )


def reduce_gradients(grid, gradients):
    out = []
    for gradient in gradients:
        part = gradient.reshape(-1, gradient.shape[-1])
        part = lax.psum_scatter(part, "dp", scatter_dimension=0, tiled=True)
        part = lax.psum_scatter(part, "fsdp", scatter_dimension=1, tiled=True)
        out.append(part.astype(jnp.float32))
    return tuple(out)


def modulate(grid, timestep, w_ada):
    rows, columns = w_ada.shape
    model_width = rows * grid.dp
    times = lax.all_gather(timestep, ("dp", "fsdp"), axis=0, tiled=True)
    conditions = jax.nn.silu(
        jax.vmap(lambda value: sinusoid(value, model_width))(times)
    ).astype(jnp.bfloat16)
    mine = lax.dynamic_slice_in_dim(conditions, lax.axis_index("dp") * rows, rows, 1)
    partial = jnp.dot(mine, w_ada, preferred_element_type=jnp.float32)
    summed = lax.psum_scatter(partial, "dp", scatter_dimension=0, tiled=True)
    mixed = lax.all_to_all(summed, "fsdp", split_axis=0, concat_axis=0, tiled=True)
    return mine, mixed.reshape(9, model_width)


def ada_gradient(grid, conditions, dmodulation):
    spread = dmodulation.reshape(grid.fsdp, -1)
    swapped = lax.all_to_all(spread, "fsdp", split_axis=0, concat_axis=0, tiled=True)
    everyone = lax.all_gather(swapped, "dp", axis=0, tiled=True)
    return outer_sum(conditions, everyone)


def ada_inputs(grid, timestep, w_ada):
    rows, columns = w_ada.shape
    condition = jax.nn.silu(sinusoid(timestep[0], rows * grid.dp)).astype(jnp.bfloat16)
    mine = jnp.pad(
        condition.astype(jnp.float32).reshape(grid.dp, 1, rows), ((0, 0), (0, 0), (0, 128 - rows))
    )
    span = -(-columns // 128) * 128
    spare = span - columns
    block = jnp.where(
        lax.axis_index("fsdp") % 2 == 0,
        jnp.pad(w_ada, ((0, 128 - rows), (0, spare))),
        jnp.pad(w_ada, ((0, 128 - rows), (spare, 0))),
    )
    return mine, block


F32 = jnp.float32
BF16 = jnp.bfloat16
NT = (((1,), (1,)), ((), ()))
TN = (((0,), (0,)), ((), ()))


def flat(value):
    return value.reshape(-1, value.shape[-1])


def dot(left, right):
    return jnp.dot(left, right, preferred_element_type=F32)


def dot_nt(left, right):
    return lax.dot_general(left, right, NT, preferred_element_type=F32)


def dot_tn(left, right):
    return lax.dot_general(left, right, TN, preferred_element_type=F32)


def tiles(total, size, body):
    def step(t, carry):
        body(pl.ds(pl.multiple_of(t * size, size), size))
        return carry

    lax.fori_loop(0, total // size, step, 0)


def row_tile(rows):
    for size in (432, 288, 256, 128):
        if rows % size == 0:
            return size
    return rows


def gelu_pair(inner):
    slope = math.sqrt(2.0 / math.pi)
    square = inner * inner
    turned = jnp.tanh(inner * (slope + (slope * 0.044715) * square))
    half = 0.5 + 0.5 * turned
    rise = inner * (slope + (3.0 * slope * 0.044715) * square)
    return inner * half, half + (0.5 - 0.5 * turned * turned) * rise


def half_lanes(shape):
    return lax.broadcasted_iota(jnp.int32, shape, 1) < shape[1] // 2


def attend(queries, keys, values, bias, mixed, heads_wide, size):
    query_ref, query_at = queries
    key_ref, key_at = keys
    value_ref, value_at = values
    mixed_ref, mixed_at = mixed
    rows = mixed_ref.shape[0]
    width = 2 * heads_wide

    def pair(p, carry):
        def at(start):
            return pl.ds(pl.multiple_of(start + p * width, width), width)

        key_pair = key_ref[:, at(key_at)]
        value_pair = value_ref[:, at(value_at)]
        low = half_lanes((size, width))
        for start in range(0, rows, size):
            scaled = query_ref[start : start + size, at(query_at)] * BF16(heads_wide**-0.5)
            outs = []
            for head in range(2):
                own = jnp.where(low if head == 0 else ~low, scaled, BF16(0))
                scores = dot_nt(own, key_pair) + bias[...]
                raised = jnp.exp(scores - jnp.max(scores, -1, keepdims=True))
                summed = jnp.sum(raised, -1, keepdims=True)
                outs.append(dot(raised.astype(BF16), value_pair) * (1.0 / summed))
            mixed_ref[start : start + size, at(mixed_at)] = jnp.where(
                low, outs[0], outs[1]
            ).astype(BF16)
        return carry

    return pair


def attend_back(queries, keys, values, bias, upstream, heads_wide, size):
    query_ref, query_at = queries
    key_ref, key_at = keys
    value_ref, value_at = values
    rows = upstream.shape[0]
    slots = bias.shape[1]
    width = 2 * heads_wide
    factor = BF16(heads_wide**-0.5)

    def pair(p, carry):
        def at(start):
            return pl.ds(pl.multiple_of(start + p * width, width), width)

        key_pair = key_ref[:, at(key_at)]
        value_pair = value_ref[:, at(value_at)]
        low = half_lanes((size, width))
        low_keys = half_lanes((slots, width))
        key_grad = jnp.zeros((slots, width), F32)
        value_grad = jnp.zeros((slots, width), F32)
        for start in range(0, rows, size):
            scaled = query_ref[start : start + size, at(query_at)] * factor
            above = upstream[start : start + size, at(0)]
            query_grad = jnp.zeros((size, width), F32)
            for head in range(2):
                mask = low if head == 0 else ~low
                own = jnp.where(mask, scaled, BF16(0))
                own_above = jnp.where(mask, above, BF16(0))
                own_keys = jnp.where(low_keys if head == 0 else ~low_keys, key_pair, BF16(0))
                scores = dot_nt(own, key_pair) + bias[...]
                raised = jnp.exp(scores - jnp.max(scores, -1, keepdims=True))
                shares = raised * (1.0 / jnp.sum(raised, -1, keepdims=True))
                share_grad = dot_nt(own_above, value_pair)
                total = jnp.sum(shares * share_grad, -1, keepdims=True)
                score_grad = (shares * (share_grad - total)).astype(BF16)
                value_grad += dot_tn(shares.astype(BF16), own_above)
                key_grad += dot_tn(score_grad, own)
                query_grad += dot(score_grad, own_keys)
            query_ref[start : start + size, at(query_at)] = (
                query_grad * heads_wide**-0.5
            ).astype(BF16)
        key_ref[:, at(key_at)] = key_grad.astype(BF16)
        value_ref[:, at(value_at)] = value_grad.astype(BF16)
        return carry

    return pair


class Loads:
    def __init__(self, sems):
        self.sems = sems
        self.copies = {}

    def start(self, name, src, dst):
        copy = pltpu.make_async_copy(src, dst, self.sems.at[len(self.copies)])
        copy.start()
        self.copies[name] = copy

    def wait(self, *names):
        for name in names:
            self.copies[name].wait()


WEIGHTS = ("qkv", "out", "cq", "ckv", "cout", "fc1", "fc2")
PARTS = 4


def half_columns(ref, which, first=0, width=None):
    half = ref.shape[-1] // 2
    if width is None:
        width = half
    return pl.ds(pl.multiple_of(which * half + first, 128), width)


class Item:
    def __init__(self, name, rows=None, first=0, width=None):
        self.name = name
        self.rows = rows
        self.first = first
        self.width = width


def gather_items(held):
    items = []
    rows = held["qkv"].shape[3]
    items += [Item("qkv", (r, 16)) for r in range(0, rows, 16)]
    items += [Item("out"), Item("cq"), Item("ckv"), Item("cout")]
    rows = held["fc2"].shape[3]
    items += [Item("fc2", (r, rows // 4)) for r in range(0, rows, rows // 4)]
    width = held["fc1"].shape[-1] // 2 // PARTS
    items += [Item("fc1", None, part * width, width) for part in range(PARTS)]
    return items


class Gather:
    def __init__(self, where, given, held, own, swapped, items, sems):
        self.z, self.y, self.x, self.core = where
        self.given, self.held, self.own, self.swapped, self.items = given, held, own, swapped, items
        self.swap_sem, self.send_sem, self.recv_sem = sems
        self.nz = held["out"].shape[0]
        z, y, x, core = where
        self.sibling = device(z, y, x, 1 - core)
        self.first = device(
            z, y * (1 - core) + (1 - y) * core, (1 - x) * (1 - core) + x * core, core
        )
        self.second = device(
            z, (1 - y) * (1 - core) + y * core, x * (1 - core) + (1 - x) * core, core
        )
        self.others = [device((z + step) % self.nz, y, x, core) for step in range(1, self.nz)]
        self.done = 0

    def swap(self, number):
        name = WEIGHTS[number]
        rows = self.own[name].shape[0]
        start = pl.multiple_of((1 - self.core) * rows, 16)
        return pltpu.make_async_remote_copy(
            src_ref=self.given[name].at[pl.ds(start, rows), :],
            dst_ref=self.swapped[name],
            send_sem=self.swap_sem.at[0, number],
            recv_sem=self.swap_sem.at[1, number],
            device_id=self.sibling,
            device_id_type=MESH,
        )

    def keep(self, number):
        name = WEIGHTS[number]
        rows = self.own[name].shape[0]
        start = pl.multiple_of(self.core * rows, 16)
        return pltpu.make_async_copy(
            self.given[name].at[pl.ds(start, rows), :], self.own[name], self.swap_sem.at[2, number]
        )

    def assemble(self, number):
        name = WEIGHTS[number]
        self.keep(number).wait()
        self.swap(number).wait_recv()
        mine, theirs = self.own[name][...], self.swapped[name][...]
        whole = self.held[name]
        whole[self.z, self.y, self.core, :, half_columns(whole, self.x)] = jnp.where(
            self.core == 0,
            jnp.concatenate([mine, theirs], 1),
            jnp.concatenate([theirs, mine], 1),
        )

    def remote(self, number, slot, part, partner):
        return pltpu.make_async_remote_copy(
            src_ref=part,
            dst_ref=part,
            send_sem=self.send_sem.at[number, slot],
            recv_sem=self.recv_sem.at[number, slot],
            device_id=partner,
            device_id_type=MESH,
        )

    def view(self, number):
        item = self.items[number]
        whole = self.held[item.name]
        rows = slice(None) if item.rows is None else pl.ds(*item.rows)
        return whole, rows, lambda which: half_columns(whole, which, item.first, item.width)

    def along_z(self, number):
        whole, rows, columns = self.view(number)
        part = whole.at[self.z, self.y, self.core, rows, columns(self.x)]
        return [self.remote(number, s, part, partner) for s, partner in enumerate(self.others)]

    def to_first(self, number):
        whole, rows, columns = self.view(number)
        part = whole.at[:, self.y, self.core, rows, columns(self.x)]
        return [self.remote(number, self.nz - 1, part, self.first)]

    def to_second(self, number):
        whole, rows, columns = self.view(number)
        copies = []
        for k in range(2):
            row = self.y * (1 - self.core) + k * self.core
            column = k * (1 - self.core) + self.x * self.core
            part = whole.at[:, row, self.core, rows, columns(column)]
            copies.append(self.remote(number, self.nz + k, part, self.second))
        return copies

    def to_core(self, number):
        whole, rows, columns = self.view(number)
        if self.items[number].width is None:
            parts = [whole.at[:, :, self.core, rows, :]]
        else:
            parts = [whole.at[:, :, self.core, rows, columns(k)] for k in range(2)]
        return [
            self.remote(number, self.nz + 2 + k, part, self.sibling) for k, part in enumerate(parts)
        ]

    def advance(self, steps):
        stages = [self.along_z, self.to_first, self.to_second, self.to_core]
        while self.done < steps:
            for depth in range(1, 4):
                number = self.done - depth + 1
                if 0 <= number < len(self.items):
                    for copy in stages[depth - 1](number):
                        copy.wait_recv()
                    for copy in stages[depth](number):
                        copy.start()
            self.done += 1

    def numbers(self, name):
        return [i for i, item in enumerate(self.items) if item.name == name]

    def need(self, numbers):
        self.advance(max(numbers) + 3)
        for number in numbers:
            for copy in self.to_core(number):
                copy.wait_recv()

    def sent(self, numbers):
        for number in numbers:
            for stage in (self.along_z, self.to_first, self.to_second, self.to_core):
                for copy in stage(number):
                    copy.wait_send()


def everyone(dp_size, fsdp_size, body):
    count = dp_size * fsdp_size
    me = lax.axis_index("dp") * fsdp_size + lax.axis_index("fsdp")

    def one(step, carry):
        body(step, (me + step) % count, me)
        return carry

    lax.fori_loop(1, count, one, 0)


def modulate_start(dp_size, fsdp_size, mine, everything, sems):
    def copy(step, target, me, row):
        return pltpu.make_async_remote_copy(
            src_ref=mine.at[row],
            dst_ref=everything.at[me],
            send_sem=sems.at[0, step - 1],
            recv_sem=sems.at[1, step - 1],
            device_id={"dp": target // fsdp_size, "fsdp": target % fsdp_size},
            device_id_type=MESH,
        )

    return copy


def forward_kernel(comm, *refs):
    (lat, text, og, frame_bias, text_bias), refs = refs[:5], refs[5:]
    if comm:
        (mine, w_ada), refs = refs[:2], refs[2:]
    else:
        (mod_in,), refs = refs[:1], refs[1:]
    given, refs = dict(zip(WEIGHTS, refs[:7])), refs[7:]
    (layer_out, dcross_out, qkv_out, h1_out, mixed1_out, h2_out, q2_out, mixed2_out), refs = (
        refs[:8],
        refs[8:],
    )
    (memory_out, after_out, branch_out), refs = refs[:3], refs[3:]
    kept_out, refs = dict(zip(BACK, refs[:5])), refs[5:]
    (fc1_out, fc2_out, rows_out, mod, conditions), refs = refs[:5], refs[5:]
    held, refs = dict(zip(WEIGHTS, refs[:7])), refs[7:]
    big, wide, h3, db3, act, din, memory, after_self, branch_1, branch_2, after_cross, result = (
        refs[:12]
    )
    refs = refs[12:]
    slots, model = lat.shape
    inner_width = held["fc1"].shape[-1]
    head = model // HEADS
    size = row_tile(slots)
    if comm:
        dp_size, fsdp_size = comm
        (everybody, partial, modulations, ada_sems), refs = refs[:4], refs[4:]
        own, refs = dict(zip(WEIGHTS, refs[:7])), refs[7:]
        swapped, refs = dict(zip(WEIGHTS, refs[:7])), refs[7:]
        gather_sems, sems = refs[:3], refs[3]
        items = gather_items(held)
        gather = Gather(place(), given, held, own, swapped, items, gather_sems)
        order = [WEIGHTS.index(n) for n in dict.fromkeys(item.name for item in items)]
        for number in order:
            gather.keep(number).start()
        barrier = pltpu.get_barrier_semaphore()

        def greet_one(step, target, me):
            pl.semaphore_signal(
                barrier,
                inc=1,
                device_id={"dp": target // fsdp_size, "fsdp": target % fsdp_size},
                device_id_type=MESH,
            )

        everyone(dp_size, fsdp_size, greet_one)
        pl.semaphore_wait(barrier, dp_size * fsdp_size - 1)
        for number in order:
            gather.swap(number).start()
        dp_index = lax.axis_index("dp")
        me = dp_index * fsdp_size + lax.axis_index("fsdp")
        send_1 = modulate_start(dp_size, fsdp_size, mine, everybody, ada_sems.at[0])
        send_2 = modulate_start(dp_size, fsdp_size, partial, modulations, ada_sems.at[1])
        everyone(dp_size, fsdp_size, lambda s, t, m: send_1(s, t, m, t // fsdp_size).start())
        everybody[me] = mine[dp_index]

        def launch(name):
            gather.assemble(WEIGHTS.index(name))
            for number in gather.numbers(name):
                for copy in gather.along_z(number):
                    copy.start()

        launch("qkv")
        everyone(dp_size, fsdp_size, lambda s, t, m: send_1(s, t, m, t // fsdp_size).wait_recv())
        for k in range(dp_size * fsdp_size):
            conditions[k : k + 1, :] = everybody[k]
        product = dot(conditions[...].astype(BF16), w_ada[...])
        for k in range(dp_size * fsdp_size):
            partial[k] = product[k : k + 1, :]
        everyone(dp_size, fsdp_size, lambda s, t, m: send_2(s, t, m, t).start())
        modulations[me] = partial[me]
        for number in order[1:]:
            launch(WEIGHTS[number])
        gather.advance(2)
        everyone(dp_size, fsdp_size, lambda s, t, m: send_2(s, t, m, t).wait_recv())
        mod[...] = jnp.zeros_like(mod)
        span = partial.shape[-1]
        for j in range(fsdp_size):
            total = modulations[j]
            for i in range(1, dp_size):
                total += modulations[i * fsdp_size + j]
            start = j * mod.shape[1] // fsdp_size // 128 * 128
            mod[:, start : start + span] += total
    else:
        sems = refs[0]
        mod[...] = mod_in[...]
        conditions[...] = jnp.zeros_like(conditions)
    loads = Loads(sems)
    if not comm:
        for name in WEIGHTS:
            loads.start(name, given[name], held[name])

    def need(name, part=None):
        if not comm:
            if not part:
                loads.wait(name)
            return
        numbers = gather.numbers(name)
        gather.need(numbers if part is None else [numbers[part]])

    def hook(p, plan):
        if comm:
            for at, steps in plan:

                @pl.when(p == at)
                def _():
                    gather.advance(steps)

    def row(k):
        return mod[:, k * model : (k + 1) * model]

    big[slots:, :] = jnp.zeros((big.shape[0] - slots, big.shape[1]), BF16)

    def norm_1(rows):
        normed, _ = normalize(lat[rows, :].astype(F32))
        wide[rows, 0:model] = (normed * (1.0 + row(1)) + row(0)).astype(BF16)

    tiles(slots, size, norm_1)
    need("qkv")
    for part in range(3):
        columns = slice(part * model, (part + 1) * model)

        def project(rows):
            big[rows, columns] = dot(
                wide[rows, 0:model], flat(held["qkv"][:, :, :, :, columns])
            ).astype(BF16)

        tiles(slots, size, project)
    loads.start("qkv_out", big.at[0:slots, 0 : 3 * model], qkv_out)
    loads.start("h1_out", wide.at[:, 0:model], h1_out)
    if comm:
        loads.start("kept_qkv", held["qkv"], kept_out["qkv"])
    pair = attend(
        (big, 0), (big, model), (big, 2 * model), frame_bias, (wide, model), head, size
    )

    def pair_1(p, carry):
        hook(p, ((1, 6), (2, 7), (4, 8), (5, 9)))
        return pair(p, carry)

    lax.fori_loop(0, HEADS // 2, pair_1, 0)
    loads.start("mixed1_out", wide.at[:, model : 2 * model], mixed1_out)
    need("out")
    need("cq")

    def join_1(rows):
        branch = dot(wide[rows, model : 2 * model], flat(held["out"][...]))
        branch_1[rows, :] = branch
        after = lat[rows, :].astype(F32) + row(2) * branch
        after_self[rows, :] = after
        normed, _ = normalize(after)
        hidden = (normed * (1.0 + row(4)) + row(3)).astype(BF16)
        wide[rows, 2 * model : 3 * model] = hidden
        wide[rows, 3 * model : 4 * model] = dot(hidden, flat(held["cq"][...])).astype(BF16)

    tiles(slots, size, join_1)
    loads.start("branch_out", branch_1, branch_out)
    loads.start("after_out", after_self, after_out)
    loads.start("h2_out", wide.at[:, 2 * model : 3 * model], h2_out)
    loads.start("q2_out", wide.at[:, 3 * model : 4 * model], q2_out)
    need("ckv")
    for part in range(2):
        columns = slice(part * model, (part + 1) * model)
        memory[:, columns] = dot(text[...], flat(held["ckv"][:, :, :, :, columns])).astype(BF16)
    loads.start("memory_out", memory, memory_out)
    mixed2 = big.at[0:slots, 3 * model : 4 * model]
    pair = attend(
        (wide, 3 * model), (memory, 0), (memory, model), text_bias, (mixed2, 0), head, size
    )

    def pair_2(p, carry):
        hook(p, ((2, 10), (5, 11)))
        return pair(p, carry)

    lax.fori_loop(0, HEADS // 2, pair_2, 0)
    loads.start("mixed2_out", mixed2, mixed2_out)
    need("cout")

    def join_2(rows):
        branch = dot(mixed2[rows, :], flat(held["cout"][...]))
        branch_2[rows, :] = branch
        after = after_self[rows, :] + row(5) * branch
        after_cross[rows, :] = after
        normed, _ = normalize(after)
        h3[rows, :] = (normed * (1.0 + row(7)) + row(6)).astype(BF16)
        db3[rows, :] = (row(8) * og[rows, :].astype(F32)).astype(BF16)

    tiles(slots, size, join_2)
    if comm:
        for name in BACK[1:]:
            loads.start("kept_" + name, held[name], kept_out[name])
    need("fc2")
    loads.wait("branch_out")
    rows_out[...] = jnp.zeros_like(rows_out)
    first, second = held["fc1"], held["fc2"]
    upstream_sum = branch_1
    width = inner_width // 2 // PARTS
    per = second.shape[0] * second.shape[1] // 2

    def chunk(t):
        return t // second.shape[1], t % second.shape[1]

    for part in range(PARTS):
        need("fc1", part)
        spans = [slice(k * inner_width // 2 + part * width, k * inner_width // 2 + (part + 1) * width) for k in range(2)]
        chunks = [chunk(part), chunk(per + part)]

        def feed(rows):
            matrix_1 = jnp.concatenate([flat(first[:, :, :, :, s]) for s in spans], 1)
            matrix_2 = jnp.concatenate([flat(second[a, b]) for a, b in chunks], 0)
            activated, slope = gelu_pair(dot(h3[rows, :], matrix_1))
            activated = activated.astype(BF16)
            dinner = (dot_nt(db3[rows, :], matrix_2) * slope).astype(BF16)
            act[rows, :] = activated
            din[rows, :] = dinner
            forward = dot(activated, matrix_2)
            backward = dot_nt(dinner, matrix_1)
            if part == 0:
                result[rows, :] = forward
                upstream_sum[rows, :] = backward
            else:
                result[rows, :] += forward
                upstream_sum[rows, :] += backward

        tiles(slots, size, feed)
        if comm:
            numbers = gather.numbers("fc1")[part : part + 1]
            if part == 0:
                numbers = gather.numbers("fc2") + numbers
            gather.sent(numbers)
        product = dot_tn(act[...], db3[...]).astype(BF16)
        for k, (a, b) in enumerate(chunks):
            second[a, b] = product[k * width : (k + 1) * width].reshape(second.shape[2:])
        product = dot_tn(h3[...], din[...]).astype(BF16)
        for k, span in enumerate(spans):
            first[:, :, :, :, span] = product[:, k * width : (k + 1) * width].reshape(
                first.shape[:4] + (width,)
            )

    loads.start("fc2_out", second, fc2_out)
    loads.start("fc1_out", first, fc1_out)

    def leave(rows):
        entering = after_cross[rows, :]
        branch = result[rows, :]
        grad = og[rows, :].astype(F32)
        result[rows, :] = entering + row(8) * branch
        normed, inverse = normalize(entering)
        back, dshift, dscale = norm_back(upstream_sum[rows, :], normed, inverse, row(7))
        dcross = grad + back
        after_cross[rows, :] = dcross
        rows_out[0:1, :] += jnp.sum(grad * branch, 0, keepdims=True)
        rows_out[1:2, :] += dshift[None]
        rows_out[2:3, :] += dscale[None]
        rows_out[3:4, :] += jnp.sum(dcross * branch_2[rows, :], 0, keepdims=True)

    tiles(slots, size, leave)
    loads.start("layer_out", result, layer_out)
    loads.start("dcross_out", after_cross, dcross_out)
    if comm:
        for number in order:
            gather.swap(number).wait_send()
        for name in BACK:
            gather.sent(gather.numbers(name))
            loads.wait("kept_" + name)
        everyone(dp_size, fsdp_size, lambda s, t, m: send_1(s, t, m, t // fsdp_size).wait_send())
        everyone(dp_size, fsdp_size, lambda s, t, m: send_2(s, t, m, t).wait_send())
    loads.wait("qkv_out", "h1_out", "mixed1_out", "h2_out", "q2_out", "mixed2_out")
    loads.wait("after_out", "memory_out", "layer_out", "dcross_out", "fc1_out", "fc2_out")


def forward(grid, latent, text_block, upstream, frame_bias, text_bias, ada, matrices):
    slots, model = latent.shape
    text_slots = text_block.shape[0]
    padded = frame_bias.shape[1]
    comm = grid.fits(matrices)
    lead = (4, 2, 2)
    devices = grid.dp * grid.fsdp
    if comm:
        wholes = [
            lead + (m.shape[0] * grid.dp // 16, m.shape[1] * grid.fsdp) for m in matrices
        ]
    else:
        wholes = [m.shape for m in matrices]
    inner_width = wholes[5][-1]
    shaped = jax.ShapeDtypeStruct
    narrow = shaped((slots, model), BF16)
    full = shaped((slots, model), F32)
    outs = [
        full,
        full,
        shaped((slots, 3 * model), BF16),
        narrow,
        narrow,
        narrow,
        narrow,
        narrow,
        shaped((text_slots, 2 * model), BF16),
        full,
        full,
    ]
    outs += [shaped(w if comm else (8, 128), BF16) for w in wholes[:5]]
    outs += [
        shaped(wholes[5], BF16),
        shaped(wholes[6], BF16),
        shaped((8, model), F32),
        shaped((1, 9 * model), F32),
        shaped((devices, 128), F32),
    ]
    vmem = pl.BlockSpec(memory_space=pltpu.VMEM)
    anywhere = pl.BlockSpec(memory_space=pl.ANY)
    scratch = [pltpu.VMEM(w, BF16) for w in wholes]
    scratch += [
        pltpu.VMEM((padded, 4 * model), BF16),
        pltpu.VMEM((slots, 4 * model), BF16),
    ]
    scratch += [pltpu.VMEM((slots, model), BF16)] * 4
    scratch += [pltpu.VMEM((text_slots, 2 * model), BF16)]
    scratch += [pltpu.VMEM((slots, model), F32)] * 5
    if comm:
        items = gather_items(dict(zip(WEIGHTS, [shaped(w, BF16) for w in wholes])))
        halves = [(m.shape[0] // 2, m.shape[1]) for m in matrices]
        span = ada[1].shape[1]
        scratch += [
            pltpu.VMEM((devices, 1, 128), F32),
            pltpu.VMEM((devices, 1, span), F32),
            pltpu.VMEM((devices, 1, span), F32),
            pltpu.SemaphoreType.DMA((2, 2, devices - 1)),
        ]
        scratch += [pltpu.VMEM(h, BF16) for h in halves] * 2
        scratch += [
            pltpu.SemaphoreType.DMA((3, len(matrices))),
            pltpu.SemaphoreType.DMA((len(items), lead[0] + 4)),
            pltpu.SemaphoreType.DMA((len(items), lead[0] + 4)),
        ]
    scratch += [pltpu.SemaphoreType.DMA((24,))]
    params = {"vmem_limit_bytes": 62 * 1024 * 1024}
    if comm:
        params.update(collective_id=0, has_side_effects=True)
    results = pl.pallas_call(
        functools.partial(forward_kernel, (grid.dp, grid.fsdp) if comm else None),
        out_shape=outs,
        in_specs=[vmem] * (5 + len(ada)) + [anywhere] * 7,
        out_specs=[anywhere] * 18 + [vmem] * 3,
        scratch_shapes=scratch,
        compiler_params=pltpu.CompilerParams(**params),
        name="forward",
    )(latent, text_block, upstream, frame_bias, text_bias, *ada, *matrices)
    kept_matrices = results[11:16] if comm else matrices[:5]
    return results[0], results[1:11], kept_matrices, results[16:]


BACK = ("qkv", "out", "cq", "ckv", "cout")


def reduce_items(shapes):
    items = []
    rows = shapes["fc2"][3]
    items += [Item("fc2", (r, rows // 4)) for r in range(0, rows, rows // 4)]
    width = shapes["fc1"][-1] // 2 // PARTS
    items += [Item("fc1", None, part * width, width) for part in range(PARTS)]
    items += [Item("cout"), Item("ckv"), Item("cq"), Item("out")]
    width = shapes["qkv"][-1] // 2 // 3
    items += [Item("qkv", None, part * width, width) for part in range(3)]
    return items


class Reduce:
    def __init__(self, where, sources, kept, landing, first, second, along, sums, owned, items, sems):
        self.z, self.y, self.x, self.core = where
        self.sources, self.kept, self.landing = sources, kept, landing
        self.from_first, self.from_second, self.from_z = first, second, along
        self.sums, self.owned, self.items = sums, owned, items
        self.send_sem, self.recv_sem, self.last_sem, self.free_sem = sems
        self.nz = sources["out"].shape[0]
        z, y, x, core = where
        self.sibling = device(z, y, x, 1 - core)
        self.first = device(
            z, (1 - y) * (1 - core) + y * core, x * (1 - core) + (1 - x) * core, core
        )
        self.second = device(
            z, y * (1 - core) + (1 - y) * core, (1 - x) * (1 - core) + x * core, core
        )
        self.done = 0

    def remote(self, number, slot, src, dst, partner):
        return pltpu.make_async_remote_copy(
            src_ref=src,
            dst_ref=dst,
            send_sem=self.send_sem.at[number, slot],
            recv_sem=self.recv_sem.at[number, slot],
            device_id=partner,
            device_id_type=MESH,
        )

    def rows(self, number, offset=0):
        item = self.items[number]
        height = self.sources[item.name].shape[3]
        start, size = (0, height) if item.rows is None else item.rows
        return pl.ds(start + offset, size)

    def columns(self, number, which):
        item = self.items[number]
        return half_columns(self.sources[item.name], which, item.first, item.width)

    def inside(self, number):
        item = self.items[number]
        width = self.sources[item.name].shape[-1] // 2 if item.width is None else item.width
        return pl.ds(item.first, width)

    def stay(self, number):
        name = self.items[number].name
        if name in self.kept:
            return self.kept[name], ()
        return self.sources[name], (self.core,)

    def kept_at(self, number, a, b, columns):
        ref, extra = self.stay(number)
        return ref.at[(a, b, *extra, self.rows(number), columns)]

    def to_core(self, number):
        item = self.items[number]
        landing, offset = self.landing[item.name]
        copies = []
        for k in range(2):
            columns = self.columns(number, k)
            src = self.sources[item.name].at[:, :, 1 - self.core, self.rows(number), columns]
            dst = landing.at[:, :, self.rows(number, offset), columns]
            copies.append(self.remote(number, self.nz + 2 + k, src, dst, self.sibling))
        return copies

    def to_first(self, number):
        copies = []
        for k in range(2):
            row = (1 - self.y) * (1 - self.core) + k * self.core
            column = k * (1 - self.core) + (1 - self.x) * self.core
            src = self.kept_at(number, slice(None), row, self.columns(number, column))
            dst = self.from_first[self.items[number].name].at[
                :, k, self.rows(number), self.inside(number)
            ]
            copies.append(self.remote(number, self.nz + k, src, dst, self.first))
        return copies

    def to_second(self, number):
        row = self.y * (1 - self.core) + (1 - self.y) * self.core
        column = (1 - self.x) * (1 - self.core) + self.x * self.core
        src = self.kept_at(number, slice(None), row, self.columns(number, column))
        dst = self.from_second[self.items[number].name].at[
            :, self.rows(number), self.inside(number)
        ]
        return [self.remote(number, self.nz - 1, src, dst, self.second)]

    def to_z(self, number):
        copies = []
        for step in range(1, self.nz):
            other = (self.z + step) % self.nz
            src = self.kept_at(number, other, self.y, self.columns(number, self.x))
            dst = self.from_z[self.items[number].name].at[
                step - 1, self.rows(number), self.inside(number)
            ]
            partner = device(other, self.y, self.x, self.core)
            copies.append(self.remote(number, step - 1, src, dst, partner))
        return copies

    def add_core(self, number):
        landing, offset = self.landing[self.items[number].name]
        for k in range(2):
            columns = self.columns(number, k)
            rows = self.rows(number, offset)

            def one(step, carry):
                a, b = step // 2, step % 2
                spot = self.kept_at(number, a, b, columns)
                spot[...] = spot[...] + landing[a, b, rows, columns]
                return carry

            lax.fori_loop(0, self.nz * 2, one, 0)

    def add_first(self, number):
        arrived = self.from_first[self.items[number].name]
        rows, inside = self.rows(number), self.inside(number)
        for k in range(2):
            row = self.y * (1 - self.core) + k * self.core
            columns = self.columns(number, k * (1 - self.core) + self.x * self.core)

            def one(a, carry):
                spot = self.kept_at(number, a, row, columns)
                spot[...] = spot[...] + arrived[a, k, rows, inside]
                return carry

            lax.fori_loop(0, self.nz, one, 0)

    def add_second(self, number):
        arrived = self.from_second[self.items[number].name]
        rows, inside = self.rows(number), self.inside(number)
        columns = self.columns(number, self.x)

        def one(a, carry):
            spot = self.kept_at(number, a, self.y, columns)
            spot[...] = spot[...] + arrived[a, rows, inside]
            return carry

        lax.fori_loop(0, self.nz, one, 0)

    def add_z(self, number):
        name = self.items[number].name
        arrived = self.from_z[name]
        rows, inside = self.rows(number), self.inside(number)
        total = self.kept_at(number, self.z, self.y, self.columns(number, self.x))[...].astype(F32)
        for step in range(self.nz - 1):
            total += arrived[step, rows, inside].astype(F32)
        self.sums[name][rows, inside] = total
        if number == max(i for i, item in enumerate(self.items) if item.name == name):
            self.share(name)

    def last(self, name):
        number = WEIGHTS.index(name)
        staged, owned = self.sums[name + "_sent"], self.owned[name]
        rows = staged.shape[0]
        return pltpu.make_async_remote_copy(
            src_ref=staged,
            dst_ref=owned.at[pl.ds(pl.multiple_of(self.core * rows, 16), rows), :],
            send_sem=self.last_sem.at[0, number],
            recv_sem=self.last_sem.at[1, number],
            device_id=self.sibling,
            device_id_type=MESH,
        )

    def share(self, name):
        total = self.sums[name][...]
        rows, width = total.shape
        left, right = total[:, : width // 2], total[:, width // 2 :]
        start = pl.multiple_of(self.core * rows, 16)
        self.owned[name][pl.ds(start, rows), :] = jnp.where(self.core == 0, left, right)
        self.sums[name + "_sent"][...] = jnp.where(self.core == 0, right, left)
        self.last(name).start()

    def launch(self, number):
        for copy in self.to_core(number):
            copy.start()

    def advance(self, steps, ready=None):
        stages = [self.to_core, self.to_first, self.to_second, self.to_z]
        adds = [self.add_core, self.add_first, self.add_second, self.add_z]
        while self.done < steps:
            for depth in range(4):
                number = self.done - depth
                if 0 <= number < len(self.items):
                    for copy in stages[depth](number):
                        copy.wait_recv()
                    adds[depth](number)
                    if depth < 3:
                        for copy in stages[depth + 1](number):
                            copy.start()
            self.done += 1

    def numbers(self, name):
        return [i for i, item in enumerate(self.items) if item.name == name]

    def free(self, which):
        pl.semaphore_signal(
            self.free_sem.at[which], inc=1, device_id=self.sibling, device_id_type=MESH
        )

    def finish(self):
        self.advance(len(self.items) + 3)
        for name in dict.fromkeys(item.name for item in self.items):
            self.last(name).wait()
        for number in range(len(self.items)):
            for stage in (self.to_core, self.to_first, self.to_second, self.to_z):
                for copy in stage(number):
                    copy.wait_send()


def backward_kernel(comm, *refs):
    (lat, text, mod, frame_bias, text_bias, rows_3, conditions), refs = refs[:7], refs[7:]
    names = ("dcross", "qkv_act", "h1", "mixed1", "h2", "q2", "mixed2", "memory", "after", "branch")
    given, refs = dict(zip(names, refs[:10])), refs[10:]
    matrices, refs = dict(zip(BACK, refs[:5])), refs[5:]
    if comm:
        (grad_fc1, grad_fc2), refs = refs[:2], refs[2:]
    (latent_out, text_out), refs = refs[:2], refs[2:]
    if comm:
        ada_out, refs = refs[0], refs[1:]
        owned, refs = dict(zip(WEIGHTS, refs[:7])), refs[7:]
    else:
        rows_out, refs = refs[0], refs[1:]
        grads_out, refs = dict(zip(BACK, refs[:5])), refs[5:]
    (dcross, packed, hidden, mixed, q2, memory, after, branch), refs = refs[:8], refs[8:]
    held, refs = dict(zip(BACK, refs[:5])), refs[5:]
    grad_qkv, above, sems = refs[:3]
    refs = refs[3:]
    slots, model = lat.shape
    head = model // HEADS
    size = row_tile(slots)
    loads = Loads(sems)
    act = {
        "dcross": dcross,
        "mixed2": mixed,
        "q2": q2,
        "memory": memory,
        "h2": hidden,
        "after": after,
        "branch": branch,
    }
    grads = dict(held, qkv=grad_qkv)
    if comm:
        dp_size, fsdp_size = comm
        (rows_out, dmod, pieces, everybody, ada_sems), refs = refs[:5], refs[5:]
        kept, refs = {"fc2": refs[0], "fc1": refs[1]}, refs[2:]
        land_fc2, land_fc1, land_ckv = refs[:3]
        refs = refs[3:]
        first, refs = dict(zip(WEIGHTS, refs[:7])), refs[7:]
        second, refs = dict(zip(WEIGHTS, refs[:7])), refs[7:]
        along, refs = dict(zip(WEIGHTS, refs[:7])), refs[7:]
        sums, refs = dict(zip(WEIGHTS, refs[:7])), refs[7:]
        sums.update(zip([name + "_sent" for name in WEIGHTS], refs[:7]))
        refs = refs[7:]
        reduce_sems = refs[:4]
        sources = dict(grads, fc1=grad_fc1, fc2=grad_fc2)
        items = reduce_items({name: ref.shape for name, ref in sources.items()})
        height = grad_qkv.shape[3]
        landing = {
            "fc2": (land_fc2, 0),
            "fc1": (land_fc1, 0),
            "cout": (land_fc2, 0),
            "cq": (land_fc2, height),
            "out": (land_fc2, 2 * height),
            "ckv": (land_ckv, 0),
            "qkv": (land_fc1, 0),
        }
        reduce = Reduce(
            place(), sources, kept, landing, first, second, along, sums, owned, items, reduce_sems
        )
        core = reduce.core
        for name, source in (("fc2", grad_fc2), ("fc1", grad_fc1)):
            loads.start("keep_" + name, source.at[:, :, core], kept[name])
    for name, target in act.items():
        loads.start(name, given[name], target)
    loads.start("qkv_act", given["qkv_act"], packed.at[0:slots, :])
    for name in ("cout", "cq", "ckv", "out", "qkv"):
        loads.start("w" + name, matrices[name], held[name])
    if comm:
        barrier = pltpu.get_barrier_semaphore()

        def greet_one(step, target, me):
            pl.semaphore_signal(
                barrier,
                inc=1,
                device_id={"dp": target // fsdp_size, "fsdp": target % fsdp_size},
                device_id_type=MESH,
            )

        everyone(dp_size, fsdp_size, greet_one)
        pl.semaphore_wait(barrier, dp_size * fsdp_size - 1)
        for name in ("fc2", "fc1"):
            for number in reduce.numbers(name):
                reduce.launch(number)
        loads.wait("keep_fc2", "keep_fc1")

    def advance(steps):
        if comm:
            reduce.advance(steps)

    def hook(p, plan):
        if comm:
            for at, steps in plan:

                @pl.when(p == at)
                def _():
                    reduce.advance(steps)

    def row(k):
        return mod[:, k * model : (k + 1) * model]

    def place_grad(name, columns, left, right):
        target = grads[name]
        product = dot_tn(left, right).astype(BF16)
        target[:, :, :, :, columns] = product.reshape(target.shape[:4] + (-1,))

    def ready(name):
        if not comm:
            loads.start("g" + name, grads[name], grads_out[name])
            return
        for number in reduce.numbers(name):
            reduce.launch(number)

    rows_out[...] = jnp.zeros_like(rows_out)
    loads.wait("dcross", "wcout")

    def enter_2(rows):
        small = (row(5) * dcross[rows, :]).astype(BF16)
        above[0, rows, :] = small
        above[1, rows, :] = dot_nt(small, flat(held["cout"][...])).astype(BF16)

    tiles(slots, size, enter_2)
    loads.wait("mixed2")
    place_grad("cout", slice(0, model), mixed[...], above[0])
    loads.start("mixed1", given["mixed1"], mixed)
    loads.wait("q2", "memory")
    advance(1)
    pair = attend_back(
        (q2, 0), (memory, 0), (memory, model), text_bias, above.at[1], head, size
    )

    def pair_2(p, carry):
        hook(p, ((2, 2), (5, 3)))
        return pair(p, carry)

    lax.fori_loop(0, HEADS // 2, pair_2, 0)
    loads.wait("wcq", "wckv", "after", "branch", "h2")
    text_out[...] = dot_nt(memory[...], flat(held["ckv"][...]))
    for part in range(2):
        columns = slice(part * model, (part + 1) * model)
        place_grad("ckv", columns, text[...], memory[:, columns])
    ready("ckv")
    loads.wait("wout")
    advance(4)
    if comm:
        reduce.free(0)

    def leave_2(rows):
        upstream = dot_nt(q2[rows, :], flat(held["cq"][...]))
        normed, inverse = normalize(after[rows, :])
        back, dshift, dscale = norm_back(upstream, normed, inverse, row(4))
        dself = dcross[rows, :] + back
        dcross[rows, :] = dself
        rows_out[0:1, :] += dshift[None]
        rows_out[1:2, :] += dscale[None]
        rows_out[2:3, :] += jnp.sum(dself * branch[rows, :], 0, keepdims=True)
        small = (row(2) * dself).astype(BF16)
        above[0, rows, :] = small
        above[1, rows, :] = dot_nt(small, flat(held["out"][...])).astype(BF16)

    tiles(slots, size, leave_2)
    advance(5)
    if comm:
        pl.semaphore_wait(reduce.free_sem.at[0], 1)
    ready("cout")
    place_grad("cq", slice(0, model), hidden[...], q2[...])
    ready("cq")
    loads.start("h1", given["h1"], hidden)
    loads.wait("mixed1")
    place_grad("out", slice(0, model), mixed[...], above[0])
    ready("out")
    loads.wait("qkv_act")
    packed[slots:, :] = jnp.zeros((packed.shape[0] - slots, 3 * model), BF16)
    pair = attend_back(
        (packed, 0), (packed, model), (packed, 2 * model), frame_bias, above.at[1], head, 288
    )

    def pair_1(p, carry):
        hook(p, ((0, 6), (1, 7), (2, 8), (3, 9), (4, 10), (5, 12)))
        return pair(p, carry)

    lax.fori_loop(0, HEADS // 2, pair_1, 0)
    if comm:
        reduce.free(1)
        pl.semaphore_wait(reduce.free_sem.at[1], 1)
    loads.wait("h1", "wqkv")
    half = 3 * model // 2
    for part in range(3):
        width = half // 3
        spans = [slice(k * half + part * width, k * half + (part + 1) * width) for k in range(2)]
        product = dot_tn(
            hidden[...], jnp.concatenate([packed[0:slots, span] for span in spans], 1)
        ).astype(BF16)
        for k, span in enumerate(spans):
            grad_qkv[:, :, :, :, span] = product[:, k * width : (k + 1) * width].reshape(
                grad_qkv.shape[:4] + (width,)
            )
        if comm:
            reduce.launch(reduce.numbers("qkv")[part])
    if not comm:
        ready("qkv")
    advance(13)

    def leave_1(rows):
        upstream = dot_nt(packed[rows, :], flat(held["qkv"][...]))
        normed, inverse = normalize(lat[rows, :].astype(F32))
        back, dshift, dscale = norm_back(upstream, normed, inverse, row(1))
        dcross[rows, :] = dcross[rows, :] + back
        rows_out[3:4, :] += dshift[None]
        rows_out[4:5, :] += dscale[None]

    tiles(slots, size, leave_1)
    loads.start("latent", dcross, latent_out)
    if not comm:
        loads.wait("gcout", "gckv", "gcq", "gout", "gqkv", "latent")
        return
    ordered = (
        rows_out[3:4, :],
        rows_out[4:5, :],
        rows_out[2:3, :],
        rows_out[0:1, :],
        rows_out[1:2, :],
        rows_3[3:4, :],
        rows_3[1:2, :],
        rows_3[2:3, :],
        rows_3[0:1, :],
    )
    for k, value in enumerate(ordered):
        dmod[:, k * model : (k + 1) * model] = value.astype(BF16).astype(F32)
    span = pieces.shape[-1]
    for j in range(fsdp_size):
        start = j * dmod.shape[1] // fsdp_size // 128 * 128
        pieces[j] = dmod[:, start : start + span]
    me = lax.axis_index("dp") * fsdp_size + lax.axis_index("fsdp")
    send = modulate_start(dp_size, fsdp_size, pieces, everybody, ada_sems)
    everyone(dp_size, fsdp_size, lambda s, t, m: send(s, t, m, t % fsdp_size).start())
    everybody[me] = pieces[lax.axis_index("fsdp")]
    reduce.advance(14)
    everyone(dp_size, fsdp_size, lambda s, t, m: send(s, t, m, t % fsdp_size).wait())
    gathered = jnp.concatenate([everybody[k] for k in range(dp_size * fsdp_size)], 0)
    product = dot_tn(conditions[...].astype(BF16), gathered.astype(BF16))
    ada_out[...] = product[: ada_out.shape[0]]
    reduce.finish()
    loads.wait("latent")


def backward(grid, comm, latent, text_block, modulation, frame_bias, text_bias, rest, kept, matrices, ff):
    slots, model = latent.shape
    text_slots = text_block.shape[0]
    padded = frame_bias.shape[1]
    rows_3, conditions = rest
    devices = grid.dp * grid.fsdp
    shaped = jax.ShapeDtypeStruct
    vmem = pl.BlockSpec(memory_space=pltpu.VMEM)
    anywhere = pl.BlockSpec(memory_space=pl.ANY)
    outs = [shaped((slots, model), F32), shaped((text_slots, model), F32)]
    narrow = pltpu.VMEM((slots, model), BF16)
    full = pltpu.VMEM((slots, model), F32)
    scratch = [
        full,
        pltpu.VMEM((padded, 3 * model), BF16),
        narrow,
        narrow,
        narrow,
        pltpu.VMEM((text_slots, 2 * model), BF16),
        full,
        full,
    ]
    scratch += [pltpu.VMEM(m.shape, BF16) for m in matrices]
    scratch += [
        pltpu.VMEM(matrices[0].shape, BF16),
        pltpu.VMEM((2, slots, model), BF16),
        pltpu.SemaphoreType.DMA((24,)),
    ]
    params = {"vmem_limit_bytes": 63 * 1024 * 1024}
    if comm:
        params.update(collective_id=1, has_side_effects=True)
        shapes = dict(zip(WEIGHTS, [m.shape for m in (*matrices, *ff)]))
        nz = shapes["out"][0]
        span = -(-9 * model // grid.fsdp // 128) * 128
        outs += [shaped((model // grid.dp, span), F32)]
        outs += [shaped((2 * s[3], s[4] // 4), F32) for s in shapes.values()]
        out_specs = [anywhere] + [vmem] * 9
        scratch += [
            pltpu.VMEM((8, model), F32),
            pltpu.VMEM((1, 9 * model), F32),
            pltpu.VMEM((grid.fsdp, 1, span), F32),
            pltpu.VMEM((devices, 1, span), F32),
            pltpu.SemaphoreType.DMA((2, devices - 1)),
        ]

        def share(name):
            s = shapes[name]
            return pltpu.VMEM((nz, 2, s[3], s[4]), BF16)

        scratch += [share("fc2"), share("fc1"), share("fc2"), share("fc1"), share("ckv")]
        scratch += [pltpu.VMEM((nz, 2, s[3], s[4] // 2), BF16) for s in shapes.values()]
        scratch += [pltpu.VMEM((nz, s[3], s[4] // 2), BF16) for s in shapes.values()]
        scratch += [pltpu.VMEM((nz - 1, s[3], s[4] // 2), BF16) for s in shapes.values()]
        scratch += [pltpu.VMEM((s[3], s[4] // 2), F32) for s in shapes.values()]
        scratch += [pltpu.VMEM((s[3], s[4] // 4), F32) for s in shapes.values()]
        count = len(reduce_items(shapes))
        scratch += [
            pltpu.SemaphoreType.DMA((count, nz + 4)),
            pltpu.SemaphoreType.DMA((count, nz + 4)),
            pltpu.SemaphoreType.DMA((2, 7)),
            pltpu.SemaphoreType.REGULAR((2,)),
        ]
    else:
        ff = ()
        outs += [shaped((8, model), F32)]
        outs += [shaped(m.shape, BF16) for m in matrices]
        out_specs = [anywhere, vmem, vmem] + [anywhere] * 5
    return pl.pallas_call(
        functools.partial(backward_kernel, (grid.dp, grid.fsdp) if comm else None),
        out_shape=outs,
        in_specs=[vmem] * 7 + [anywhere] * (15 + len(ff)),
        out_specs=out_specs,
        scratch_shapes=scratch,
        compiler_params=pltpu.CompilerParams(**params),
        name="backward",
    )(
        latent,
        text_block,
        modulation,
        frame_bias,
        text_bias,
        rows_3,
        conditions,
        *kept,
        *matrices,
        *ff,
    )


def body(
    latents,
    text_rows,
    out_grad,
    frame_len,
    text_len,
    timestep,
    w_ada,
    w_qkv,
    w_out,
    w_cq,
    w_ckv,
    w_cout,
    w_fc1,
    w_fc2,
    *,
    dp_size,
    fsdp_size,
):
    grid = Grid(dp_size, fsdp_size)
    matrices = (w_qkv, w_out, w_cq, w_ckv, w_cout, w_fc1, w_fc2)
    slot_count, model_width = latents.shape[1:]
    text_slots = text_rows.shape[1]
    padded = -(-slot_count // 128) * 128
    frame_bias = jnp.where(jnp.arange(padded) < frame_len[0], 0.0, -1e30).astype(F32)[None]
    text_bias = jnp.where(jnp.arange(text_slots) < text_len[0], 0.0, -1e30).astype(F32)[None]
    if grid.fits(matrices):
        ada = ada_inputs(grid, timestep, w_ada)
    else:
        matrices = gather_weights(grid, matrices)
        conditions, modulation = modulate(grid, timestep, w_ada)
        ada = (modulation.reshape(1, -1),)
    layer_out, kept, kept_matrices, rest = forward(
        grid, latents[0], text_rows[0], out_grad[0], frame_bias, text_bias, ada, matrices
    )
    grad_fc1, grad_fc2, rows_3, modulation, rows = rest
    comm = len(ada) > 1
    results = backward(
        grid,
        comm,
        latents[0],
        text_rows[0],
        modulation,
        frame_bias,
        text_bias,
        (rows_3, rows),
        kept,
        kept_matrices,
        (grad_fc1, grad_fc2),
    )
    latent_grad, text_grad, rows_1 = results[:3]
    if comm:
        spare = rows_1.shape[1] - w_ada.shape[1]
        grad_ada = jnp.where(
            lax.axis_index("fsdp") % 2 == 0, rows_1[:, : w_ada.shape[1]], rows_1[:, spare:]
        )
        owned = results[3:]
    else:
        order = (
            rows_1[3:4],
            rows_1[4:5],
            rows_1[2:3],
            rows_1[0:1],
            rows_1[1:2],
            rows_3[3:4],
            rows_3[1:2],
            rows_3[2:3],
            rows_3[0:1],
        )
        dmodulation = jnp.concatenate(order, 0).reshape(1, -1).astype(BF16)
        grad_ada = ada_gradient(grid, conditions, dmodulation)
        owned = reduce_gradients(grid, (*results[3:8], grad_fc1, grad_fc2))
    return (
        layer_out[None],
        latent_grad[None],
        text_grad[None],
        grad_ada,
        *owned,
    )


def solution(mesh):
    placed = (P(("dp", "fsdp"), None, None),) * 3 + (P(("dp", "fsdp")),) * 3 + (P("dp", "fsdp"),) * 8
    return jax.shard_map(
        functools.partial(body, dp_size=mesh.shape["dp"], fsdp_size=mesh.shape["fsdp"]),
        mesh=mesh,
        in_specs=placed,
        out_specs=(P(("dp", "fsdp"), None, None),) * 3 + (P("dp", "fsdp"),) * 8,
        check_vma=False,
    )
```

```python
import functools
import math

import jax
import jax.numpy as jnp
from jax import lax
from jax.experimental import pallas as pl
from jax.experimental.pallas import tpu as pltpu
from jax.sharding import PartitionSpec as P

HEADS = 12


norm_eps = 1e-06


def sinusoid(time_value, model_width):
    half_width = model_width // 2
    frequency = jnp.exp(-math.log(10000.0) * jnp.arange(half_width, dtype=jnp.float32) / half_width)
    angles = time_value.astype(jnp.float32) * frequency
    return jnp.concatenate([jnp.cos(angles), jnp.sin(angles)], axis=-1)


def normalize(values):
    center = values - jnp.mean(values, -1, keepdims=True)
    spread = jnp.mean(center * center, -1, keepdims=True)
    inverse = lax.rsqrt(spread + norm_eps)
    return (center * inverse, inverse)


def norm_back(upstream, normed, inverse, scale_row):
    dshift = jnp.sum(upstream, 0)
    dscale = jnp.sum(upstream * normed, 0)
    scaled = upstream * (1.0 + scale_row)
    centered = (
        scaled
        - jnp.mean(scaled, -1, keepdims=True)
        - normed * jnp.mean(scaled * normed, -1, keepdims=True)
    )
    return (inverse * centered, dshift, dscale)


def outer_sum(left, right):
    return lax.dot_general(
        left, right, (((0,), (0,)), ((), ())), preferred_element_type=jnp.float32
    )


MESH = pl.DeviceIdType.MESH


class Grid:
    def __init__(self, dp_size, fsdp_size):
        self.dp = dp_size
        self.fsdp = fsdp_size

    def fits(self, matrices):
        if self.fsdp != 4 or self.dp != 8:
            return False
        for matrix in matrices:
            rows, columns = matrix.shape
            if rows % 32 or (2 * columns) % 128:
                return False
        return True


def place():
    dp_index = lax.axis_index("dp")
    fsdp_index = lax.axis_index("fsdp")
    return dp_index // 2, dp_index % 2, fsdp_index // 2, fsdp_index % 2


def device(z, y, x, core):
    return {"dp": z * 2 + y, "fsdp": x * 2 + core}


def gather_weights(grid, matrices):
    return tuple(
        lax.all_gather(
            lax.all_gather(m, "fsdp", axis=1, tiled=True), "dp", axis=0, tiled=True
        ).reshape(4, 2, 2, m.shape[0] * grid.dp // 16, m.shape[1] * grid.fsdp)
        for m in matrices
    )


def reduce_gradients(grid, gradients):
    out = []
    for gradient in gradients:
        part = gradient.reshape(-1, gradient.shape[-1])
        part = lax.psum_scatter(part, "dp", scatter_dimension=0, tiled=True)
        part = lax.psum_scatter(part, "fsdp", scatter_dimension=1, tiled=True)
        out.append(part.astype(jnp.float32))
    return tuple(out)


def modulate(grid, timestep, w_ada):
    rows, columns = w_ada.shape
    model_width = rows * grid.dp
    times = lax.all_gather(timestep, ("dp", "fsdp"), axis=0, tiled=True)
    conditions = jax.nn.silu(
        jax.vmap(lambda value: sinusoid(value, model_width))(times)
    ).astype(jnp.bfloat16)
    mine = lax.dynamic_slice_in_dim(conditions, lax.axis_index("dp") * rows, rows, 1)
    partial = jnp.dot(mine, w_ada, preferred_element_type=jnp.float32)
    summed = lax.psum_scatter(partial, "dp", scatter_dimension=0, tiled=True)
    mixed = lax.all_to_all(summed, "fsdp", split_axis=0, concat_axis=0, tiled=True)
    return mine, mixed.reshape(9, model_width)


def ada_gradient(grid, conditions, dmodulation):
    spread = dmodulation.reshape(grid.fsdp, -1)
    swapped = lax.all_to_all(spread, "fsdp", split_axis=0, concat_axis=0, tiled=True)
    everyone = lax.all_gather(swapped, "dp", axis=0, tiled=True)
    return outer_sum(conditions, everyone)


def ada_inputs(grid, timestep, w_ada):
    rows, columns = w_ada.shape
    condition = jax.nn.silu(sinusoid(timestep[0], rows * grid.dp)).astype(jnp.bfloat16)
    mine = jnp.pad(
        condition.astype(jnp.float32).reshape(grid.dp, 1, rows), ((0, 0), (0, 0), (0, 128 - rows))
    )
    return mine, w_ada


F32 = jnp.float32
BF16 = jnp.bfloat16
NT = (((1,), (1,)), ((), ()))
TN = (((0,), (0,)), ((), ()))


def flat(value):
    return value.reshape(-1, value.shape[-1])


def dot(left, right):
    return jnp.dot(left, right, preferred_element_type=F32)


def dot_nt(left, right):
    return lax.dot_general(left, right, NT, preferred_element_type=F32)


def dot_tn(left, right):
    return lax.dot_general(left, right, TN, preferred_element_type=F32)


def tiles(total, size, body):
    def step(t, carry):
        body(pl.ds(pl.multiple_of(t * size, size), size))
        return carry

    lax.fori_loop(0, total // size, step, 0)


def row_tile(rows):
    for size in (432, 288, 256, 128):
        if rows % size == 0:
            return size
    return rows


def gelu_pair(inner):
    slope = math.sqrt(2.0 / math.pi)
    square = inner * inner
    turned = jnp.tanh(inner * (slope + (slope * 0.044715) * square))
    half = 0.5 + 0.5 * turned
    rise = inner * (slope + (3.0 * slope * 0.044715) * square)
    return inner * half, half + (0.5 - 0.5 * turned * turned) * rise


def half_lanes(shape):
    return lax.broadcasted_iota(jnp.int32, shape, 1) < shape[1] // 2


def lanes_of(shape):
    return lax.broadcasted_iota(jnp.int32, shape, 1)


def mark_keys(marks, length):
    shape = marks.shape
    excluded = jnp.where(lax.broadcasted_iota(jnp.int32, shape, 0) < length, 0.0, -1e30)
    marks[...] = jnp.where(lanes_of(shape) == shape[1] - 1, excluded, 0.0).astype(BF16)


def thirds(value, last):
    high = value.astype(BF16).astype(F32)
    middle = (value - high).astype(BF16).astype(F32)
    low = value - high - middle
    lane = lanes_of(value.shape)
    spread = high + pltpu.roll(middle, 32, 1) + pltpu.roll(low, 64, 1)
    return jnp.where(lane == value.shape[1] - 1, last, spread).astype(BF16)


def head_lanes(model, stat_at):
    shape = (model, 128)
    head = lax.broadcasted_iota(jnp.int32, shape, 0) // (model // HEADS)
    return jnp.where(lanes_of(shape) == head + stat_at, 1.0, 0.0).astype(BF16)


def head_sums(left, right, matrix):
    product = left.astype(F32) * right.astype(F32)
    high = product.astype(BF16)
    return dot(high, matrix) + dot((product - high.astype(F32)).astype(BF16), matrix)


def attend(queries, keys, values, marks, mixed, stats, heads_wide, size):
    query_ref, query_at = queries
    key_ref, key_at = keys
    value_ref, value_at = values
    mixed_ref, mixed_at = mixed
    stat_ref, stat_at = stats
    rows = mixed_ref.shape[0]
    width = 2 * heads_wide

    def pair(p, carry):
        def at(start):
            return pl.ds(pl.multiple_of(start + p * width, width), width)

        value_pair = value_ref[:, at(value_at)]
        marked = jnp.concatenate([key_ref[:, at(key_at)], marks[...]], 1)
        low = half_lanes((size, width))
        lane = lanes_of((size, width))
        last = (lane == width - 1).astype(F32).astype(BF16)
        for start in range(0, rows, size):
            span = slice(start, start + size)
            scaled = query_ref[span, at(query_at)] * BF16(heads_wide**-0.5)
            outs = []
            stat = stat_ref[span, :]
            for head in range(2):
                own = jnp.where(low if head == 0 else ~low, scaled, BF16(0))
                scores = dot_nt(jnp.concatenate([own, last], 1), marked)
                largest = jnp.max(scores, -1, keepdims=True)
                raised = jnp.exp(scores - largest)
                summed = jnp.sum(raised, -1, keepdims=True)
                outs.append(dot(raised.astype(BF16), value_pair) * (1.0 / summed))
                stat = jnp.where(lane == stat_at + 2 * p + head, largest + jnp.log(summed), stat)
            stat_ref[span, :] = stat
            mixed_ref[span, at(mixed_at)] = jnp.where(low, outs[0], outs[1]).astype(BF16)
        return carry

    return pair


def attend_back(
    queries, keys, values, marks, upstream, means, stats, total, heads_wide, size, before=None
):
    query_ref, query_at = queries
    key_ref, key_at = keys
    value_ref, value_at = values
    stat_ref, stat_at = stats
    rows = upstream.shape[0]
    slots = key_ref.shape[0]
    width = 2 * heads_wide

    def pair(p, carry):
        def at(start):
            return pl.ds(pl.multiple_of(start + p * width, width), width)

        low = half_lanes((rows, width))
        scaled = query_ref[0:rows, at(query_at)] * BF16(heads_wide**-0.5)
        above = upstream[:, at(0)]
        heads = []
        for head in range(2):
            mask = low if head == 0 else ~low
            own = jnp.where(mask, scaled, BF16(0))
            own_above = jnp.where(mask, above, BF16(0))
            heads.append(
                (
                    jnp.concatenate([own, stat_ref[...]], 1),
                    jnp.concatenate([own_above, means[...]], 1),
                    own,
                    own_above,
                )
            )
        low_keys = half_lanes((size, width))
        lane = lanes_of((size, width))

        def one_tile(span):
            key_pair = key_ref[span, at(key_at)]
            value_pair = value_ref[span, at(value_at)]
            query_grad = None
            key_grad = None
            value_grad = None
            for head in range(2):
                mask = low_keys if head == 0 else ~low_keys
                taken = lane - (stat_at + 2 * p + head)
                mark = jnp.where(
                    (taken == 0) | (taken == 32) | (taken == 64),
                    BF16(-1),
                    marks[span, :],
                )
                marked_query, marked_above, own, own_above = heads[head]
                shares = jnp.exp(dot_nt(jnp.concatenate([key_pair, mark], 1), marked_query))
                share_grad = dot_nt(jnp.concatenate([value_pair, mark], 1), marked_above)
                score_grad = (shares * share_grad).astype(BF16)
                values_part = dot(shares.astype(BF16), own_above)
                keys_part = dot(score_grad, own)
                queries_part = dot_tn(score_grad, jnp.where(mask, key_pair, BF16(0)))
                value_grad = values_part if head == 0 else value_grad + values_part
                key_grad = keys_part if head == 0 else key_grad + keys_part
                query_grad = queries_part if query_grad is None else query_grad + queries_part
            key_ref[span, at(key_at)] = key_grad.astype(BF16)
            value_ref[span, at(value_at)] = value_grad.astype(BF16)
            total[...] += query_grad

        total[...] = jnp.zeros_like(total)

        def step(t, carry):
            if before is not None:
                before(t)
            one_tile(pl.ds(pl.multiple_of(t * size, size), size))
            return carry

        lax.fori_loop(0, slots // size, step, 0)
        query_ref[0:rows, at(query_at)] = (total[...] * heads_wide**-0.5).astype(BF16)
        return carry

    return pair


class Loads:
    def __init__(self, sems):
        self.sems = sems
        self.copies = {}

    def start(self, name, src, dst):
        copy = pltpu.make_async_copy(src, dst, self.sems.at[len(self.copies)])
        copy.start()
        self.copies[name] = copy

    def wait(self, *names):
        for name in names:
            self.copies[name].wait()


WEIGHTS = ("qkv", "out", "cq", "ckv", "cout", "fc1", "fc2")
QKV, OUT, CQ, CKV, COUT, FC1, FC2 = WEIGHTS
PARTS = 4


def half_columns(ref, which, first=(0, 0), width=None):
    half = ref.shape[-1] // 2
    if width is None:
        width = half
    start = which * (half + first[1] - first[0]) + first[0]
    return pl.ds(pl.multiple_of(start, 128), width)


class Item:
    def __init__(self, name, rows=None, first=0, width=None, slot=None, summed=(0, 0)):
        self.name = name
        self.summed = summed
        self.rows = rows
        self.first = first if isinstance(first, tuple) else (first, first)
        self.width = width
        self.slot = self.first[0] if slot is None else slot


def gather_items(held):
    items = []
    rows = held[QKV].shape[3]
    items += [Item(QKV, (r, 16)) for r in range(0, rows, 16)]
    items += [Item(OUT), Item(CQ)]
    width = held[CKV].shape[-1] // 4
    items += [Item(CKV, None, k * width, width) for k in range(2)]
    items += [Item(COUT)]
    rows = held[FC2].shape[3] // PARTS
    width = held[FC1].shape[-1] // 2 // PARTS
    for part in range(PARTS):
        items += [Item(FC2, (part * rows, rows)), Item(FC1, None, part * width, width)]
    return items


class Gather:
    def __init__(self, where, given, held, own, swapped, items, sems):
        self.z, self.y, self.x, self.core = where
        self.given, self.held, self.own, self.swapped, self.items = given, held, own, swapped, items
        self.swap_sem, self.send_sem, self.recv_sem = sems
        self.nz = held[OUT].shape[0]
        z, y, x, core = where
        self.sibling = device(z, y, x, 1 - core)
        self.first = device(
            z, y * (1 - core) + (1 - y) * core, (1 - x) * (1 - core) + x * core, core
        )
        self.second = device(
            z, (1 - y) * (1 - core) + y * core, x * (1 - core) + (1 - x) * core, core
        )
        self.others = [device((z + step) % self.nz, y, x, core) for step in range(1, self.nz)]
        self.done = 0
        self.counts = [0, 0, 0, 0]
        self.record = None

    def half(self, number, which):
        staged = self.own[WEIGHTS[number]]
        rows = staged.shape[0] // 2
        return staged.at[pl.ds(pl.multiple_of(which * rows, 16), rows), :]

    def swap(self, number):
        return pltpu.make_async_remote_copy(
            src_ref=self.half(number, 1 - self.core),
            dst_ref=self.swapped[WEIGHTS[number]],
            send_sem=self.swap_sem.at[0, number],
            recv_sem=self.swap_sem.at[1, number],
            device_id=self.sibling,
            device_id_type=MESH,
        )

    def assemble(self, number):
        name = WEIGHTS[number]
        self.swap(number).wait_recv()
        mine, theirs = self.half(number, self.core)[...], self.swapped[name][...]
        whole = self.held[name]
        left = jnp.where(self.core == 0, mine, theirs)
        right = jnp.where(self.core == 0, theirs, mine)
        if name == FC1:
            four = left.shape[1] // 4
            step = four // PARTS
            pieces = [
                side[:, k * four + part * step : k * four + (part + 1) * step]
                for part in range(PARTS)
                for side in (left, right)
                for k in range(4)
            ]
        else:
            pieces = [left, right]
        whole[self.z, self.y, self.core, :, half_columns(whole, self.x)] = jnp.concatenate(
            pieces, 1
        )

    def remote(self, number, slot, part, partner):
        return pltpu.make_async_remote_copy(
            src_ref=part,
            dst_ref=part,
            send_sem=self.send_sem.at[number, slot],
            recv_sem=self.recv_sem.at[number, slot],
            device_id=partner,
            device_id_type=MESH,
        )

    def view(self, number):
        item = self.items[number]
        whole = self.held[item.name]
        rows = slice(None) if item.rows is None else pl.ds(*item.rows)
        return whole, rows, lambda which: half_columns(whole, which, item.first, item.width)

    def along_z(self, number):
        whole, rows, columns = self.view(number)
        part = whole.at[self.z, self.y, self.core, rows, columns(self.x)]
        return [self.remote(number, s, part, partner) for s, partner in enumerate(self.others)]

    def to_first(self, number):
        whole, rows, columns = self.view(number)
        part = whole.at[:, self.y, self.core, rows, columns(self.x)]
        return [self.remote(number, self.nz - 1, part, self.first)]

    def to_second(self, number):
        whole, rows, columns = self.view(number)
        copies = []
        for k in range(2):
            row = self.y * (1 - self.core) + k * self.core
            column = k * (1 - self.core) + self.x * self.core
            part = whole.at[:, row, self.core, rows, columns(column)]
            copies.append(self.remote(number, self.nz + k, part, self.second))
        return copies

    def to_core(self, number):
        whole, rows, columns = self.view(number)
        if self.items[number].width is None:
            parts = [whole.at[:, :, self.core, rows, :]]
        else:
            parts = [whole.at[:, :, self.core, rows, columns(k)] for k in range(2)]
        return [
            self.remote(number, self.nz + 2 + k, part, self.sibling) for k, part in enumerate(parts)
        ]

    def up_to(self, depth, number):
        while self.counts[depth] <= min(number, len(self.items) - 1):
            self.emit((depth, self.counts[depth]))
            self.counts[depth] += 1

    def emit(self, step):
        if self.record is not None:
            self.record.append(step)
            return
        depth, number = step
        stages = [self.along_z, self.to_first, self.to_second, self.to_core]
        if depth:
            for copy in stages[depth - 1](number):
                copy.wait_recv()
        if depth < 4:
            for copy in stages[depth](number):
                copy.start()

    def planned(self, body):
        self.record = []
        body()
        steps, self.record = self.record, None
        return steps

    def advance(self, steps, lag=2, ahead=3):
        while self.done < steps:
            self.up_to(0, self.done + ahead)
            for depth in range(1, 4):
                self.up_to(depth, self.done - (depth - 1) * lag)
            self.done += 1

    def numbers(self, name):
        return [i for i, item in enumerate(self.items) if item.name == name]

    def need(self, numbers):
        for depth in range(4):
            self.up_to(depth, max(numbers))
        for number in numbers:
            self.emit((4, number))

    def sent(self, numbers):
        for number in numbers:
            for stage in (self.along_z, self.to_first, self.to_second, self.to_core):
                for copy in stage(number):
                    copy.wait_send()


def everyone(dp_size, fsdp_size, body):
    count = dp_size * fsdp_size
    me = lax.axis_index("dp") * fsdp_size + lax.axis_index("fsdp")

    def one(step, carry):
        body(step, (me + step) % count, me)
        return carry

    lax.fori_loop(1, count, one, 0)


def modulate_start(dp_size, fsdp_size, mine, everything, sems):
    def copy(step, target, me, row):
        return pltpu.make_async_remote_copy(
            src_ref=mine.at[row],
            dst_ref=everything.at[me],
            send_sem=sems.at[0, step - 1],
            recv_sem=sems.at[1, step - 1],
            device_id={"dp": target // fsdp_size, "fsdp": target % fsdp_size},
            device_id_type=MESH,
        )

    return copy


def forward_kernel(comm, *refs):
    (frame_len, text_len, lat_in, text_in, og_in), refs = refs[:5], refs[5:]
    if comm:
        (mine, w_ada), refs = refs[:2], refs[2:]
    else:
        (mod_in,), refs = refs[:1], refs[1:]
    given, refs = dict(zip(WEIGHTS, refs[:7])), refs[7:]
    (layer_out, dcross_out, qkv_out, h1_out, mixed1_out, h2_out, q2_out, mixed2_out), refs = (
        refs[:8],
        refs[8:],
    )
    (memory_out, after_out), refs = refs[:2], refs[2:]
    kept_out, refs = dict(zip(BACK, refs[:5])), refs[5:]
    (stats_out, fc1_out, fc2_out, sums_fc1, sums_fc2), refs = refs[:5], refs[5:]
    (rows_out, mod, conditions), refs = refs[:3], refs[3:]
    held, refs = dict(zip(WEIGHTS, refs[:7])), refs[7:]
    big, wide, h3, db3, memory, after_self, upstream_sum, branch_2, after_cross, result = refs[:10]
    refs = refs[10:]
    lat, text, og, stats, split_stats, frame_marks, text_marks, sems = refs[:8]
    refs = refs[8:]
    loads = Loads(sems)
    loads.start("lat", lat_in, lat)
    loads.start("text", text_in, text)
    loads.start("og", og_in, og)
    slots, model = lat.shape
    inner_width = held[FC1].shape[-1]
    head = model // HEADS
    size = row_tile(slots)
    if comm:
        dp_size, fsdp_size = comm
        (everybody, partial, modulations, ada_sems), refs = refs[:4], refs[4:]
        (ada_block, ada_wide, turned), refs = refs[:3], refs[3:]
        own, refs = dict(zip(WEIGHTS, refs[:7])), refs[7:]
        swapped, refs = dict(zip(WEIGHTS, refs[:7])), refs[7:]
        gather_sems, refs = refs[:3], refs[3:]
        landing, from_first, from_second, from_z, sums = (
            {FC1: refs[2 * k], FC2: refs[2 * k + 1]} for k in range(5)
        )
        reduce_sems = refs[10:]
        per = held[FC2].shape[3] // PARTS, held[FC1].shape[-1] // 2 // PARTS
        reduce = Reduce(
            place(),
            {FC1: held[FC1], FC2: held[FC2]},
            {},
            landing,
            from_first,
            from_second,
            from_z,
            sums,
            None,
            part_items(*per, EARLY, 0),
            (*reduce_sems, None),
        )
        items = gather_items(held)
        gather = Gather(place(), given, held, own, swapped, items, gather_sems)
        order = [WEIGHTS.index(n) for n in dict.fromkeys(item.name for item in items)]
        barrier = pltpu.get_barrier_semaphore()

        def greet_one(step, target, me):
            pl.semaphore_signal(
                barrier,
                inc=1,
                device_id={"dp": target // fsdp_size, "fsdp": target % fsdp_size},
                device_id_type=MESH,
            )

        everyone(dp_size, fsdp_size, greet_one)
        loads.start("w_ada", w_ada, ada_block)
        for number in order:
            name = WEIGHTS[number]
            loads.start("w" + name, given[name], turned if name == FC2 else own[name])
        mark_keys(frame_marks, frame_len[0])
        mark_keys(text_marks, text_len[0])
        big[slots:, :] = jnp.zeros((big.shape[0] - slots, big.shape[1]), BF16)
        stats[...] = jnp.zeros_like(stats)
        loads.wait("w_ada")
        blank = jnp.zeros((ada_block.shape[0], ada_wide.shape[1] - ada_block.shape[1]), BF16)
        ada_wide[0 : ada_block.shape[0], :] = jnp.where(
            gather.core == 0,
            jnp.concatenate([ada_block[...], blank], 1),
            jnp.concatenate([blank, ada_block[...]], 1),
        )
        ada_wide[ada_block.shape[0] :, :] = jnp.zeros(
            (ada_wide.shape[0] - ada_block.shape[0], ada_wide.shape[1]), BF16
        )
        loads.wait(*["w" + name for name in WEIGHTS])
        own[FC2][...] = turned[...].T
        pl.semaphore_wait(barrier, dp_size * fsdp_size - 1)
        for number in order:
            gather.swap(number).start()
        dp_index = lax.axis_index("dp")
        me = dp_index * fsdp_size + lax.axis_index("fsdp")
        send_1 = modulate_start(dp_size, fsdp_size, mine, everybody, ada_sems.at[0])
        send_2 = modulate_start(dp_size, fsdp_size, partial, modulations, ada_sems.at[1])
        everyone(dp_size, fsdp_size, lambda s, t, m: send_1(s, t, m, t // fsdp_size).start())
        everybody[me] = mine[dp_index]
        gather.assemble(WEIGHTS.index(QKV))
        gather.up_to(0, 2)
        everyone(dp_size, fsdp_size, lambda s, t, m: send_1(s, t, m, t // fsdp_size).wait_recv())
        for k in range(dp_size * fsdp_size):
            conditions[k : k + 1, :] = everybody[k]
        product = dot(conditions[...].astype(BF16), ada_wide[...])
        for k in range(dp_size * fsdp_size):
            partial[k] = product[k : k + 1, :]
        everyone(dp_size, fsdp_size, lambda s, t, m: send_2(s, t, m, t).start())
        modulations[me] = partial[me]
        for number in order[1:]:
            gather.assemble(number)
        gather.advance(3, 1, 1)
        everyone(dp_size, fsdp_size, lambda s, t, m: send_2(s, t, m, t).wait_recv())
        mod[...] = jnp.zeros_like(mod)
        span = partial.shape[-1]
        for j in range(fsdp_size):
            total = modulations[j]
            for i in range(1, dp_size):
                total += modulations[i * fsdp_size + j]
            start = j * mod.shape[1] // fsdp_size // 128 * 128
            mod[:, start : start + span] += total
    else:
        mod[...] = mod_in[...]
        conditions[...] = jnp.zeros_like(conditions)
        for name in WEIGHTS:
            loads.start(name, given[name], held[name])

    def need(name, part=None):
        if not comm:
            if not part:
                loads.wait(name)
            return
        numbers = gather.numbers(name)
        gather.need(numbers if part is None else [numbers[part]])

    def hook(p, plan):
        if comm:
            for at, steps in plan:

                @pl.when(p == at)
                def _():
                    gather.advance(steps)

    def step_to(steps):
        if comm:
            gather.advance(steps)

    def row(k):
        return mod[:, k * model : (k + 1) * model]

    if not comm:
        mark_keys(frame_marks, frame_len[0])
        mark_keys(text_marks, text_len[0])
        big[slots:, :] = jnp.zeros((big.shape[0] - slots, big.shape[1]), BF16)
        stats[...] = jnp.zeros_like(stats)
    loads.wait("lat", "text", "og")

    def norm_1(rows):
        normed, _ = normalize(lat[rows, :].astype(F32))
        wide[rows, 0:model] = (normed * (1.0 + row(1)) + row(0)).astype(BF16)

    tiles(slots, size, norm_1)
    if comm:
        gather.advance(5, 1)
    need(QKV)

    def project_part(columns):
        def project(rows):
            big[rows, columns] = dot(
                wide[rows, 0:model], flat(held[QKV][:, :, :, :, columns])
            ).astype(BF16)

        tiles(slots, size, project)

    tiles(3 * model, model, project_part)
    loads.start("qkv_out", big.at[0:slots, 0 : 3 * model], qkv_out)
    loads.start("h1_out", wide.at[:, 0:model], h1_out)
    if comm:
        loads.start("kept_qkv", held[QKV], kept_out[QKV])
    pair = attend(
        (big, 0),
        (big, model),
        (big, 2 * model),
        frame_marks,
        (wide, model),
        (stats, 0),
        head,
        size,
    )

    def pair_1(p, carry):
        hook(p, ((0, 6), (1, 7), (3, 8), (4, 9), (5, 10)))
        return pair(p, carry)

    lax.fori_loop(0, HEADS // 2, pair_1, 0)
    loads.start("mixed1_out", wide.at[:, model : 2 * model], mixed1_out)
    need(OUT)
    need(CQ)

    def join_1(rows):
        branch = dot(wide[rows, model : 2 * model], flat(held[OUT][...]))
        after = lat[rows, :].astype(F32) + row(2) * branch
        after_self[rows, :] = after
        normed, _ = normalize(after)
        hidden = (normed * (1.0 + row(4)) + row(3)).astype(BF16)
        wide[rows, 2 * model : 3 * model] = hidden
        wide[rows, 3 * model : 4 * model] = dot(hidden, flat(held[CQ][...])).astype(BF16)

    tiles(slots, size, join_1)
    loads.start("after_out", after_self, after_out)
    loads.start("h2_out", wide.at[:, 2 * model : 3 * model], h2_out)
    loads.start("q2_out", wide.at[:, 3 * model : 4 * model], q2_out)
    step_to(11)
    need(CKV)

    def project_text(columns):
        memory[:, columns] = dot(text[...], flat(held[CKV][:, :, :, :, columns])).astype(BF16)

    tiles(2 * model, model, project_text)
    loads.start("memory_out", memory, memory_out)
    mixed2 = big.at[0:slots, 3 * model : 4 * model]
    pair = attend(
        (wide, 3 * model),
        (memory, 0),
        (memory, model),
        text_marks,
        (mixed2, 0),
        (stats, HEADS),
        head,
        size,
    )

    def pair_2(p, carry):
        hook(p, ((0, 12), (3, 13)))
        return pair(p, carry)

    lax.fori_loop(0, HEADS // 2, pair_2, 0)
    loads.start("mixed2_out", mixed2, mixed2_out)
    split_stats[...] = thirds(stats[...], 1.0)
    loads.start("stats_out", split_stats, stats_out)
    need(COUT)

    def join_2(rows):
        branch = dot(mixed2[rows, :], flat(held[COUT][...]))
        branch_2[rows, :] = branch
        after = after_self[rows, :] + row(5) * branch
        after_cross[rows, :] = after
        normed, _ = normalize(after)
        h3[rows, :] = (normed * (1.0 + row(7)) + row(6)).astype(BF16)
        db3[rows, :] = (row(8) * og[rows, :].astype(F32)).astype(BF16)

    step_to(14)
    tiles(slots, size, join_2)
    if comm:
        for name in BACK[1:]:
            loads.start("kept_" + name, held[name], kept_out[name])
    loads.wait("h1_out", "mixed1_out")
    act, din = wide.at[:, 0:model], wide.at[:, model : 2 * model]
    rows_out[...] = jnp.zeros_like(rows_out)
    first, second = held[FC1], held[FC2]
    width = inner_width // 2 // PARTS
    count = second.shape[3] // PARTS
    lead = second.shape[:3]

    def clear(rows):
        result[rows, :] = jnp.zeros((16, model), F32)
        upstream_sum[rows, :] = jnp.zeros((16, model), F32)

    tiles(slots, 16, clear)

    def at_part(part, bodies):
        for k, body in enumerate(bodies):
            pl.when(part == k)(body)

    arrivals, middles, ends = [], [], []
    for k in range(PARTS):

        def arrive(k=k):
            need(FC2, k)
            need(FC1, k)
            step_to(15 + 2 * k)

        def middle(k=k):
            step_to(16 + 2 * k)
            if k + 1 < PARTS:
                for depth in range(4):
                    gather.up_to(depth, gather.numbers(FC1)[k + 1])

        if comm:
            plans = gather.planned(arrive), gather.planned(middle)

            def emit_arrival(steps=plans[0]):
                for step in steps:
                    gather.emit(step)

            def emit_middle(steps=plans[1], k=k):
                for step in steps:
                    gather.emit(step)
                gather.sent([gather.numbers(name)[k] for name in (FC2, FC1)])
                for step in ((), (), ((0, 0), (0, 1)), ((1, 0), (1, 1)))[k]:
                    reduce.step(*step)

            def emit_end(k=k):
                if k < EARLY:
                    reduce.launch(2 * k)
                    reduce.launch(2 * k + 1)
                for step in ((), (), (), ((2, 0), (2, 1)))[k]:
                    reduce.step(*step)

            arrivals.append(emit_arrival)
            middles.append(emit_middle)
            ends.append(emit_end)
        else:
            arrive()

    def feed_part(part, carry):
        at_part(part, arrivals)
        spans = [
            pl.ds(pl.multiple_of(k * inner_width // 2 + part * width, 128), width) for k in range(2)
        ]
        chunk = pl.ds(pl.multiple_of(part * count, 16), count)

        def feed(rows):
            matrix_1 = jnp.concatenate([flat(first[:, :, :, :, s]) for s in spans], 1)
            matrix_2 = flat(second[:, :, :, chunk, :])
            activated, slope = gelu_pair(dot(h3[rows, :], matrix_1))
            activated = activated.astype(BF16)
            dinner = (dot_nt(db3[rows, :], matrix_2) * slope).astype(BF16)
            act[rows, :] = activated
            din[rows, :] = dinner
            result[rows, :] += dot(activated, matrix_2)
            upstream_sum[rows, :] += dot_nt(dinner, matrix_1)

        tiles(slots, size, feed)
        at_part(part, middles)
        product = dot_tn(act[...], db3[...]).astype(BF16)
        second[:, :, :, chunk, :] = product.reshape(lead + (count, model))
        product = dot_tn(h3[...], din[...]).astype(BF16)
        for k, span in enumerate(spans):
            first[:, :, :, :, span] = product[:, k * width : (k + 1) * width].reshape(
                first.shape[:4] + (width,)
            )
        at_part(part, ends)
        return carry

    lax.fori_loop(0, PARTS, feed_part, 0)
    if comm:
        loads.start("fc2_out", second.at[:, :, :, EARLY * count :, :], fc2_out)
        for k in range(2):
            loads.start(
                "fc1_out" + "b" * k,
                first.at[:, :, :, :, (k * PARTS + EARLY) * width : (k + 1) * PARTS * width],
                fc1_out.at[
                    :, :, :, :, k * (PARTS - EARLY) * width : (k + 1) * (PARTS - EARLY) * width
                ],
            )
    else:
        loads.start("fc2_out", second, fc2_out)
        loads.start("fc1_out", first, fc1_out)

    def leave(rows):
        entering = after_cross[rows, :]
        branch = result[rows, :]
        grad = og[rows, :].astype(F32)
        result[rows, :] = entering + row(8) * branch
        normed, inverse = normalize(entering)
        back, dshift, dscale = norm_back(upstream_sum[rows, :], normed, inverse, row(7))
        dcross = grad + back
        after_cross[rows, :] = dcross
        rows_out[0:1, :] += jnp.sum(grad * branch, 0, keepdims=True)
        rows_out[1:2, :] += dshift[None]
        rows_out[2:3, :] += dscale[None]
        rows_out[3:4, :] += jnp.sum(dcross * branch_2[rows, :], 0, keepdims=True)

    tiles(slots, size, leave)
    loads.start("layer_out", result, layer_out)
    loads.start("dcross_out", after_cross, dcross_out)
    if comm:
        for number in order:
            gather.swap(number).wait_send()
        for name in BACK:
            gather.sent(gather.numbers(name))
            loads.wait("kept_" + name)
        for number in range(2 * EARLY):
            reduce.step(3, number)
        loads.start("sums1", sums[FC1], sums_fc1)
        loads.start("sums2", sums[FC2], sums_fc2)
        everyone(dp_size, fsdp_size, lambda s, t, m: send_1(s, t, m, t // fsdp_size).wait_send())
        everyone(dp_size, fsdp_size, lambda s, t, m: send_2(s, t, m, t).wait_send())
        reduce.sent()
        loads.wait("sums1", "sums2", "fc1_outb")
    loads.wait("qkv_out", "h2_out", "q2_out", "mixed2_out")
    loads.wait("stats_out", "after_out", "memory_out", "layer_out", "dcross_out", "fc1_out", "fc2_out")


def forward(grid, lengths, latent, text_block, upstream, ada, matrices):
    slots, model = latent.shape
    text_slots = text_block.shape[0]
    padded = -(-slots // 128) * 128
    comm = len(ada) > 1
    lead = (4, 2, 2)
    devices = grid.dp * grid.fsdp
    if comm:
        blocks = [m.shape for m in matrices[:6]] + [matrices[6].shape[::-1]]
        wholes = [lead + (b[0] * grid.dp // 16, b[1] * grid.fsdp) for b in blocks]
    else:
        wholes = [m.shape for m in matrices]
    inner_width = wholes[5][-1]
    late_1, late_2 = wholes[5], wholes[6]
    if comm:
        later = PARTS - EARLY
        late_1 = (*late_1[:4], late_1[4] // PARTS * later)
        late_2 = (*late_2[:3], late_2[3] // PARTS * later, late_2[4])
    shaped = jax.ShapeDtypeStruct
    narrow = shaped((slots, model), BF16)
    full = shaped((slots, model), F32)
    outs = [
        full,
        full,
        shaped((slots, 3 * model), BF16),
        narrow,
        narrow,
        narrow,
        narrow,
        narrow,
        shaped((text_slots, 2 * model), BF16),
        full,
    ]
    outs += [shaped(w if comm else (8, 128), BF16) for w in wholes[:5]]
    outs += [
        shaped((slots, 128), BF16),
        shaped(late_1, BF16),
        shaped(late_2, BF16),
        *[shaped((s[3], s[4] // 2) if comm else (8, 128), F32) for s in wholes[5:]],
        shaped((8, model), F32),
        shaped((1, 9 * model), F32),
        shaped((devices, 128), F32),
    ]
    vmem = pl.BlockSpec(memory_space=pltpu.VMEM)
    anywhere = pl.BlockSpec(memory_space=pl.ANY)
    smem = pl.BlockSpec(memory_space=pltpu.SMEM)
    scratch = [pltpu.VMEM(w, BF16) for w in wholes]
    scratch += [
        pltpu.VMEM((padded, 4 * model), BF16),
        pltpu.VMEM((slots, 4 * model), BF16),
    ]
    scratch += [pltpu.VMEM((slots, model), BF16)] * 2
    scratch += [pltpu.VMEM((text_slots, 2 * model), BF16)]
    scratch += [pltpu.VMEM((slots, model), F32)] * 5
    scratch += [
        pltpu.VMEM((slots, model), BF16),
        pltpu.VMEM((text_slots, model), BF16),
        pltpu.VMEM((slots, model), BF16),
        pltpu.VMEM((slots, 128), F32),
        pltpu.VMEM((slots, 128), BF16),
        pltpu.VMEM((padded, 128), BF16),
        pltpu.VMEM((text_slots, 128), BF16),
        pltpu.SemaphoreType.DMA((40,)),
    ]
    if comm:
        items = gather_items(dict(zip(WEIGHTS, [shaped(w, BF16) for w in wholes])))
        rows, columns = ada[1].shape
        span = -(-columns // 128) * 128
        scratch += [
            pltpu.VMEM((devices, 1, 128), F32),
            pltpu.VMEM((devices, 1, span), F32),
            pltpu.VMEM((devices, 1, span), F32),
            pltpu.SemaphoreType.DMA((2, 2, devices - 1)),
            pltpu.VMEM((rows, columns), BF16),
            pltpu.VMEM((128, span), BF16),
            pltpu.VMEM(matrices[6].shape, BF16),
        ]
        scratch += [pltpu.VMEM(b, BF16) for b in blocks]
        scratch += [pltpu.VMEM((b[0] // 2, b[1]), BF16) for b in blocks]
        scratch += [
            pltpu.SemaphoreType.DMA((2, len(matrices))),
            pltpu.SemaphoreType.DMA((len(items), lead[0] + 4)),
            pltpu.SemaphoreType.DMA((len(items), lead[0] + 4)),
        ]
        early = [
            (*wholes[5][:4], wholes[5][4] // PARTS * EARLY),
            (*wholes[6][:3], wholes[6][3] // PARTS * EARLY, wholes[6][4]),
        ]
        scratch += reduce_scratch(early, lead[0])
        scratch += [pltpu.VMEM((s[3], s[4] // 2), F32) for s in wholes[5:]]
        scratch += [pltpu.SemaphoreType.DMA((2 * EARLY, lead[0] + 4))] * 2
    params = {"vmem_limit_bytes": 63 * 1024 * 1024}
    if comm:
        params.update(collective_id=0, has_side_effects=True)
    results = pl.pallas_call(
        functools.partial(forward_kernel, (grid.dp, grid.fsdp) if comm else None),
        out_shape=outs,
        in_specs=[smem] * 2 + [anywhere] * 3 + [vmem] + [anywhere] * (6 + len(ada)),
        out_specs=[anywhere] * 20 + [vmem] * 3,
        scratch_shapes=scratch,
        compiler_params=pltpu.CompilerParams(**params),
        name="forward",
    )(*lengths, latent, text_block, upstream, *ada, *matrices)
    kept_matrices = results[10:15] if comm else matrices[:5]
    return results[0], (*results[1:10], results[15]), kept_matrices, results[16:]


BACK = (QKV, OUT, CQ, CKV, COUT)


EARLY = 1


def part_items(rows, width, parts, before):
    items = []
    for part in range(parts):
        items += [
            Item(FC2, (part * rows, rows), summed=(before * rows, 0)),
            Item(FC1, None, part * width, width, summed=(0, before * width)),
        ]
    return items


def reduce_items(shapes):
    parts = PARTS - EARLY
    items = part_items(shapes[FC2][3] // parts, shapes[FC1][-1] // 2 // parts, parts, EARLY)
    items += [Item(COUT)]
    width = shapes[CKV][-1] // 4
    items += [Item(CKV, None, k * width, width) for k in range(2)]
    items += [Item(CQ), Item(OUT)]
    model = shapes[QKV][-1] // 3
    third, half = model // 3, model // 2
    items += [
        Item(QKV, None, (0, half), third, 0),
        Item(QKV, None, (2 * third, half + 2 * third), third, third),
        Item(QKV, None, (model, 2 * third - half), third, 2 * third),
        Item(QKV, None, (third, half + third), third, model),
        Item(QKV, None, (model + third, 0), third // 2, model + third),
    ]
    return items


class Reduce:
    def __init__(self, where, sources, kept, landing, first, second, along, sums, owned, items, sems):
        self.z, self.y, self.x, self.core = where
        self.sources, self.kept, self.landing = sources, kept, landing
        self.from_first, self.from_second, self.from_z = first, second, along
        self.sums, self.owned, self.items = sums, owned, items
        self.send_sem, self.recv_sem, self.last_sem = sems
        self.nz = sources[FC2].shape[0]
        self.counts = [0, 0, 0, 0]
        z, y, x, core = where
        self.sibling = device(z, y, x, 1 - core)
        self.first = device(
            z, (1 - y) * (1 - core) + y * core, x * (1 - core) + (1 - x) * core, core
        )
        self.second = device(
            z, y * (1 - core) + (1 - y) * core, (1 - x) * (1 - core) + x * core, core
        )
        self.done = 0

    def remote(self, number, slot, src, dst, partner):
        return pltpu.make_async_remote_copy(
            src_ref=src,
            dst_ref=dst,
            send_sem=self.send_sem.at[number, slot],
            recv_sem=self.recv_sem.at[number, slot],
            device_id=partner,
            device_id_type=MESH,
        )

    def rows(self, number, offset=0):
        item = self.items[number]
        height = self.sources[item.name].shape[3]
        start, size = (0, height) if item.rows is None else item.rows
        return pl.ds(start + offset, size)

    def columns(self, number, which):
        item = self.items[number]
        return half_columns(self.sources[item.name], which, item.first, item.width)

    def inside(self, number):
        item = self.items[number]
        width = self.sources[item.name].shape[-1] // 2 if item.width is None else item.width
        return pl.ds(item.slot, width)

    def landed(self, number, which):
        item = self.items[number]
        half = self.landing[item.name].shape[-1] // 2
        return pl.ds(which * half + item.slot, half if item.width is None else item.width)

    def stay(self, number):
        name = self.items[number].name
        if name in self.kept:
            return self.kept[name], ()
        return self.sources[name], (self.core,)

    def kept_at(self, number, a, b, columns):
        ref, extra = self.stay(number)
        return ref.at[(a, b, *extra, self.rows(number), columns)]

    def to_core(self, number):
        item = self.items[number]
        landing = self.landing[item.name]
        copies = []
        for k in range(2):
            columns = self.columns(number, k)
            src = self.sources[item.name].at[:, :, 1 - self.core, self.rows(number), columns]
            dst = landing.at[:, :, self.rows(number), self.landed(number, k)]
            copies.append(self.remote(number, self.nz + 2 + k, src, dst, self.sibling))
        return copies

    def to_first(self, number):
        copies = []
        for k in range(2):
            row = (1 - self.y) * (1 - self.core) + k * self.core
            column = k * (1 - self.core) + (1 - self.x) * self.core
            src = self.kept_at(number, slice(None), row, self.columns(number, column))
            dst = self.from_first[self.items[number].name].at[
                :, k, self.rows(number), self.inside(number)
            ]
            copies.append(self.remote(number, self.nz + k, src, dst, self.first))
        return copies

    def to_second(self, number):
        row = self.y * (1 - self.core) + (1 - self.y) * self.core
        column = (1 - self.x) * (1 - self.core) + self.x * self.core
        src = self.kept_at(number, slice(None), row, self.columns(number, column))
        dst = self.from_second[self.items[number].name].at[
            :, self.rows(number), self.inside(number)
        ]
        return [self.remote(number, self.nz - 1, src, dst, self.second)]

    def to_z(self, number):
        copies = []
        for step in range(1, self.nz):
            other = (self.z + step) % self.nz
            src = self.kept_at(number, other, self.y, self.columns(number, self.x))
            dst = self.from_z[self.items[number].name].at[
                step - 1, self.rows(number), self.inside(number)
            ]
            partner = device(other, self.y, self.x, self.core)
            copies.append(self.remote(number, step - 1, src, dst, partner))
        return copies

    def add_core(self, number):
        landing = self.landing[self.items[number].name]
        for k in range(2):
            columns = self.columns(number, k)
            rows, landed = self.rows(number), self.landed(number, k)

            def one(step, carry):
                a, b = step // 2, step % 2
                spot = self.kept_at(number, a, b, columns)
                spot[...] = spot[...] + landing[a, b, rows, landed]
                return carry

            lax.fori_loop(0, self.nz * 2, one, 0)

    def add_first(self, number):
        arrived = self.from_first[self.items[number].name]
        rows, inside = self.rows(number), self.inside(number)
        for k in range(2):
            row = self.y * (1 - self.core) + k * self.core
            columns = self.columns(number, k * (1 - self.core) + self.x * self.core)

            def one(a, carry):
                spot = self.kept_at(number, a, row, columns)
                spot[...] = spot[...] + arrived[a, k, rows, inside]
                return carry

            lax.fori_loop(0, self.nz, one, 0)

    def add_second(self, number):
        arrived = self.from_second[self.items[number].name]
        rows, inside = self.rows(number), self.inside(number)
        columns = self.columns(number, self.x)

        def one(a, carry):
            spot = self.kept_at(number, a, self.y, columns)
            spot[...] = spot[...] + arrived[a, rows, inside]
            return carry

        lax.fori_loop(0, self.nz, one, 0)

    def add_z(self, number):
        name = self.items[number].name
        arrived = self.from_z[name]
        rows, inside = self.rows(number), self.inside(number)
        total = self.kept_at(number, self.z, self.y, self.columns(number, self.x))[...].astype(F32)
        for step in range(self.nz - 1):
            total += arrived[step, rows, inside].astype(F32)
        item = self.items[number]
        down, along = item.summed
        start = item.first[0] + self.x * (item.first[1] - item.first[0]) + along
        self.sums[name][
            self.rows(number, down), pl.ds(pl.multiple_of(start, 128), total.shape[1])
        ] = total
        if self.owned and number == max(i for i, item in enumerate(self.items) if item.name == name):
            self.share(name)

    def last(self, name):
        number = WEIGHTS.index(name)
        staged, owned = self.sums[name + "_sent"], self.owned[name]
        rows = staged.shape[0]
        return pltpu.make_async_remote_copy(
            src_ref=staged,
            dst_ref=owned.at[pl.ds(pl.multiple_of(self.core * rows, 16), rows), :],
            send_sem=self.last_sem.at[0, number],
            recv_sem=self.last_sem.at[1, number],
            device_id=self.sibling,
            device_id_type=MESH,
        )

    def share(self, name):
        total = self.sums[name][...]
        rows, width = total.shape
        left, right = total[:, : width // 2], total[:, width // 2 :]
        if name == FC1:
            step = width // 8 // PARTS
            left, right = (
                jnp.concatenate(
                    [
                        total[:, start : start + step]
                        for k in range(4)
                        for part in range(PARTS)
                        for start in [((part * 2 + side) * 4 + k) * step]
                    ],
                    1,
                )
                for side in range(2)
            )
        start = pl.multiple_of(self.core * rows, 16)
        self.owned[name][pl.ds(start, rows), :] = jnp.where(self.core == 0, left, right)
        self.sums[name + "_sent"][...] = jnp.where(self.core == 0, right, left)
        self.last(name).start()

    def launch(self, number):
        for copy in self.to_core(number):
            copy.start()

    def step(self, depth, number):
        stages = [self.to_core, self.to_first, self.to_second, self.to_z]
        adds = [self.add_core, self.add_first, self.add_second, self.add_z]
        for copy in stages[depth](number):
            copy.wait_recv()
        adds[depth](number)
        if depth < 3:
            for copy in stages[depth + 1](number):
                copy.start()

    def up_to(self, depth, number):
        while self.counts[depth] <= min(number, len(self.items) - 1):
            self.step(depth, self.counts[depth])
            self.counts[depth] += 1

    def targets(self, numbers):
        for depth, number in enumerate(numbers):
            self.up_to(depth, number)

    def advance(self, steps):
        while self.done < steps:
            lag = 2
            for depth in range(4):
                self.up_to(depth, self.done - depth * lag)
            self.done += 1

    def numbers(self, name):
        return [i for i, item in enumerate(self.items) if item.name == name]

    def sent(self):
        for number in range(len(self.items)):
            for stage in (self.to_core, self.to_first, self.to_second, self.to_z):
                for copy in stage(number):
                    copy.wait_send()

    def finish(self):
        count = len(self.items)
        self.up_to(0, count)
        for number in range(count + 2):
            for depth in range(1, 4):
                self.up_to(depth, number - depth + 1)
        for name in dict.fromkeys(item.name for item in self.items):
            self.last(name).wait()
        self.sent()


def reduce_scratch(shapes, nz):
    scratch = [pltpu.VMEM((nz, 2, s[3], s[4]), BF16) for s in shapes]
    scratch += [pltpu.VMEM((nz, 2, s[3], s[4] // 2), BF16) for s in shapes]
    scratch += [pltpu.VMEM((nz, s[3], s[4] // 2), BF16) for s in shapes]
    scratch += [pltpu.VMEM((nz - 1, s[3], s[4] // 2), BF16) for s in shapes]
    return scratch


def backward_kernel(comm, *refs):
    (frame_len, text_len, mod, rows_3, lat_in, text_in), refs = refs[:6], refs[6:]
    names = (
        "dcross",
        "qkv_act",
        "h1",
        "mixed1",
        "h2",
        "q2",
        "mixed2",
        "memory",
        "after",
        "stats",
    )
    given, refs = dict(zip(names, refs[:10])), refs[10:]
    matrices, refs = dict(zip(BACK, refs[:5])), refs[5:]
    if comm:
        (grad_fc1, grad_fc2, sums_fc1, sums_fc2), refs = refs[:4], refs[4:]
    (latent_out, text_out), refs = refs[:2], refs[2:]
    if comm:
        everybody, refs = refs[0], refs[1:]
        owned, refs = dict(zip(WEIGHTS, refs[:7])), refs[7:]
    else:
        rows_out, refs = refs[0], refs[1:]
        grads_out, refs = dict(zip(BACK, refs[:5])), refs[5:]
    (dcross, packed, hidden, mixed, q2, memory, after), refs = refs[:7], refs[7:]
    text, stats, means, frame_marks, text_marks, query_sum, lanes = refs[:7]
    refs = refs[7:]
    held, refs = dict(zip(BACK, refs[:5])), refs[5:]
    grad_qkv, above, sems = refs[:3]
    refs = refs[3:]
    slots, model = dcross.shape
    lat = above.at[0]
    head = model // HEADS
    size = row_tile(slots)
    loads = Loads(sems)
    act = {
        "dcross": dcross,
        "mixed2": mixed,
        "q2": q2,
        "memory": memory,
        "h2": hidden,
        "stats": stats,
        "after": after,
    }
    grads = dict(held, qkv=grad_qkv)
    if comm:
        dp_size, fsdp_size = comm
        (rows_out, dmod, pieces, ada_sems, fc2_rows), refs = refs[:5], refs[5:]
        turned, owned[FC2] = owned[FC2], fc2_rows
        kept, refs = {FC2: refs[0], FC1: refs[1]}, refs[2:]
        landing, refs = dict(zip(WEIGHTS, refs[:7])), refs[7:]
        first, refs = dict(zip(WEIGHTS, refs[:7])), refs[7:]
        second, refs = dict(zip(WEIGHTS, refs[:7])), refs[7:]
        along, refs = dict(zip(WEIGHTS, refs[:7])), refs[7:]
        sums, refs = dict(zip(WEIGHTS, refs[:7])), refs[7:]
        sums.update(zip([name + "_sent" for name in WEIGHTS], refs[:7]))
        refs = refs[7:]
        reduce_sems = refs[:3]
        sources = dict(grads, fc1=grad_fc1, fc2=grad_fc2)
        items = reduce_items({name: ref.shape for name, ref in sources.items()})
        reduce = Reduce(
            place(), sources, kept, landing, first, second, along, sums, owned, items, reduce_sems
        )
        core = reduce.core
    loads.start("wcout", matrices[COUT], held[COUT])
    for name in ("dcross", "mixed2", "q2", "memory", "stats"):
        loads.start(name, given[name], act[name])
    if comm:
        barrier = pltpu.get_barrier_semaphore()

        def greet_one(step, target, me):
            pl.semaphore_signal(
                barrier,
                inc=1,
                device_id={"dp": target // fsdp_size, "fsdp": target % fsdp_size},
                device_id_type=MESH,
            )

        everyone(dp_size, fsdp_size, greet_one)
        pl.semaphore_wait(barrier, dp_size * fsdp_size - 1)
        for name in (FC2, FC1):
            for number in reduce.numbers(name):
                reduce.launch(number)
        for name, source in ((FC2, grad_fc2), (FC1, grad_fc1)):
            loads.start("keep_" + name, source.at[:, :, core], kept[name])
        for name, source in ((FC2, sums_fc2), (FC1, sums_fc1)):
            loads.start("s" + name, source, sums[name])
    for name in (CQ, CKV, OUT, QKV):
        loads.start("w" + name, matrices[name], held[name])
    for name in ("h2", "after"):
        loads.start(name, given[name], act[name])
    loads.start("text", text_in, text)
    loads.start("qkv_act", given["qkv_act"], packed.at[0:slots, :])

    def advance(steps):
        if comm:
            reduce.advance(steps)

    def hook(p, plan):
        if comm:
            for at, steps in plan:

                @pl.when(p == at)
                def _():
                    if isinstance(steps, tuple):
                        reduce.targets(steps)
                    else:
                        reduce.advance(steps)

    def row(k):
        return mod[:, k * model : (k + 1) * model]

    def place_grad(name, columns, left, right):
        target = grads[name]
        product = dot_tn(left, right).astype(BF16)
        target[:, :, :, :, columns] = product.reshape(target.shape[:4] + (-1,))

    def ready(name):
        if not comm:
            loads.start("g" + name, grads[name], grads_out[name])
            return
        for number in reduce.numbers(name):
            reduce.launch(number)

    rows_out[...] = jnp.zeros_like(rows_out)
    mark_keys(frame_marks, frame_len[0])
    mark_keys(text_marks, text_len[0])
    loads.wait("dcross", "wcout")

    def enter_2(rows):
        small = (row(5) * dcross[rows, :]).astype(BF16)
        above[0, rows, :] = small
        upstream = dot_nt(small, flat(held[COUT][...])).astype(BF16)
        above[1, rows, :] = upstream
        means[rows, :] = thirds(head_sums(upstream, mixed[rows, :], lanes[...]), 0.0)

    loads.wait("mixed2")
    lanes[...] = head_lanes(model, HEADS)
    tiles(slots, size, enter_2)
    place_grad(COUT, slice(0, model), mixed[...], above[0])
    ready(COUT)
    loads.wait("q2", "memory", "stats")
    if comm:
        loads.wait("keep_fc2", "keep_fc1", "sfc2", "sfc1")
    advance(1)
    pair = attend_back(
        (q2, 0),
        (memory, 0),
        (memory, model),
        text_marks,
        above.at[1],
        means,
        (stats, HEADS),
        query_sum,
        head,
        memory.shape[0],
    )

    def pair_2(p, carry):
        hook(p, ((0, 2), (2, 3), (4, 4)))
        return pair(p, carry)

    lax.fori_loop(0, HEADS // 2, pair_2, 0)
    loads.start("mixed1", given["mixed1"], mixed)
    loads.wait("wcq", "wckv", "after", "h2", "text")
    text_out[...] = dot_nt(memory[...], flat(held[CKV][...]))
    tiles(
        2 * model,
        model,
        lambda columns: place_grad(CKV, columns, text[...], memory[:, columns]),
    )
    ready(CKV)
    loads.wait("wout")
    advance(5)

    def leave_2(rows):
        upstream = dot_nt(q2[rows, :], flat(held[CQ][...]))
        normed, inverse = normalize(after[rows, :])
        back, dshift, dscale = norm_back(upstream, normed, inverse, row(4))
        dself = dcross[rows, :] + back
        dcross[rows, :] = dself
        rows_out[0:1, :] += dshift[None]
        rows_out[1:2, :] += dscale[None]
        branch = dot(mixed[rows, :], flat(held[OUT][...]))
        rows_out[2:3, :] += jnp.sum(dself * branch, 0, keepdims=True)
        small = (row(2) * dself).astype(BF16)
        above[0, rows, :] = small
        upstream = dot_nt(small, flat(held[OUT][...])).astype(BF16)
        above[1, rows, :] = upstream
        means[rows, :] = thirds(head_sums(upstream, mixed[rows, :], lanes[...]), 0.0)

    loads.wait("mixed1")
    lanes[...] = head_lanes(model, 0)
    tiles(slots, size, leave_2)
    advance(6)
    place_grad(CQ, slice(0, model), hidden[...], q2[...])
    ready(CQ)
    loads.start("h1", given["h1"], hidden)
    place_grad(OUT, slice(0, model), mixed[...], above[0])
    ready(OUT)
    loads.start("lat", lat_in, lat)
    advance(7)
    loads.wait("qkv_act")
    packed[slots:, :] = jnp.zeros((packed.shape[0] - slots, 3 * model), BF16)
    place_in_loop = []
    pairs = HEADS // 2

    def tile_hook(t):
        plan = []
        for j in range(pairs):
            plan += [
                (2 * j, (6 + j, 5 + j, 3 + j, 1 + j)),
                (2 * j + 1, (7 + j, 6 + j, 4 + j, 1 + j)),
            ]
        hook(2 * place_in_loop[-1] + t, plan)

    pair = attend_back(
        (packed, 0),
        (packed, model),
        (packed, 2 * model),
        frame_marks,
        above.at[1],
        means,
        (stats, 0),
        query_sum,
        head,
        packed.shape[0] // 2,
        tile_hook,
    )

    third, half = model // 3, 3 * model // 2

    def grad_columns(*starts, width):
        spans = [slice(start, start + width) for start in starts]
        product = dot_tn(
            hidden[...], jnp.concatenate([packed[0:slots, span] for span in spans], 1)
        ).astype(BF16)
        for k, span in enumerate(spans):
            grad_qkv[:, :, :, :, span] = product[:, k * width : (k + 1) * width].reshape(
                grad_qkv.shape[:4] + (width,)
            )

    def launch(part):
        if comm:
            reduce.launch(reduce.numbers(QKV)[part])

    def pair_1(i, carry):
        place_in_loop.append(i)
        group = i // (pairs // 3)
        pair(group * (7 - 3 * group) * pairs // 6 + i % (pairs // 3), carry)

        @pl.when(i == pairs // 3 - 1)
        def _():
            loads.wait("h1")
            grad_columns(0, 2 * model, width=third)
            launch(0)

        @pl.when(i == 2 * pairs // 3 - 1)
        def _():
            grad_columns(2 * third, 2 * model + 2 * third, width=third)
            launch(1)
            grad_columns(model, model + 2 * third, width=third)
            launch(2)

        return carry

    lax.fori_loop(0, pairs, pair_1, 0)
    grad_columns(third, 2 * model + third, width=third)
    launch(3)
    grad_columns(model + third, half, width=third // 2)
    launch(4)
    loads.wait("wqkv", "lat")
    if not comm:
        ready(QKV)

    def leave_1(rows):
        upstream = dot_nt(packed[rows, :], flat(held[QKV][...]))
        normed, inverse = normalize(lat[rows, :].astype(F32))
        back, dshift, dscale = norm_back(upstream, normed, inverse, row(1))
        dcross[rows, :] = dcross[rows, :] + back
        rows_out[3:4, :] += dshift[None]
        rows_out[4:5, :] += dscale[None]


    def leave_step(t, carry):
        hook(t, ((0, (13, 12, 10, 8)), (1, (14, 13, 11, 9))))
        leave_1(pl.ds(pl.multiple_of(t * size, size), size))
        return carry

    lax.fori_loop(0, slots // size, leave_step, 0)
    hook(0, ((0, (15, 14, 12, 10)),))
    loads.start("latent", dcross, latent_out)
    if not comm:
        loads.wait("gcout", "gckv", "gcq", "gout", "gqkv", "latent")
        return
    ordered = (
        rows_out[3:4, :],
        rows_out[4:5, :],
        rows_out[2:3, :],
        rows_out[0:1, :],
        rows_out[1:2, :],
        rows_3[3:4, :],
        rows_3[1:2, :],
        rows_3[2:3, :],
        rows_3[0:1, :],
    )
    for k, value in enumerate(ordered):
        dmod[:, k * model : (k + 1) * model] = value.astype(BF16).astype(F32)
    span = pieces.shape[-1]
    for j in range(fsdp_size):
        start = j * dmod.shape[1] // fsdp_size // 128 * 128
        pieces[j] = dmod[:, start : start + span]
    me = lax.axis_index("dp") * fsdp_size + lax.axis_index("fsdp")
    send = modulate_start(dp_size, fsdp_size, pieces, everybody, ada_sems)
    everyone(dp_size, fsdp_size, lambda s, t, m: send(s, t, m, t % fsdp_size).start())
    everybody[me] = pieces[lax.axis_index("fsdp")]
    reduce.finish()
    everyone(dp_size, fsdp_size, lambda s, t, m: send(s, t, m, t % fsdp_size).wait())
    turned[...] = fc2_rows[...].T
    loads.wait("latent")


def backward(grid, comm, lengths, latent, text_block, modulation, rest, kept, matrices, ff):
    slots, model = latent.shape
    text_slots = text_block.shape[0]
    padded = -(-slots // 128) * 128
    rows_3 = rest
    devices = grid.dp * grid.fsdp
    shaped = jax.ShapeDtypeStruct
    vmem = pl.BlockSpec(memory_space=pltpu.VMEM)
    anywhere = pl.BlockSpec(memory_space=pl.ANY)
    smem = pl.BlockSpec(memory_space=pltpu.SMEM)
    outs = [shaped((slots, model), F32), shaped((text_slots, model), F32)]
    narrow = pltpu.VMEM((slots, model), BF16)
    full = pltpu.VMEM((slots, model), F32)
    scratch = [
        full,
        pltpu.VMEM((padded, 3 * model), BF16),
        narrow,
        narrow,
        narrow,
        pltpu.VMEM((text_slots, 2 * model), BF16),
        full,
        pltpu.VMEM((text_slots, model), BF16),
        pltpu.VMEM((slots, 128), BF16),
        pltpu.VMEM((slots, 128), BF16),
        pltpu.VMEM((padded, 128), BF16),
        pltpu.VMEM((text_slots, 128), BF16),
        pltpu.VMEM((slots, 128), F32),
        pltpu.VMEM((model, 128), BF16),
    ]
    scratch += [pltpu.VMEM(m.shape, BF16) for m in matrices]
    scratch += [
        pltpu.VMEM(matrices[0].shape, BF16),
        pltpu.VMEM((2, slots, model), BF16),
        pltpu.SemaphoreType.DMA((24,)),
    ]
    params = {"vmem_limit_bytes": 63 * 1024 * 1024}
    if comm:
        params.update(collective_id=1, has_side_effects=True)
        shapes = dict(zip(WEIGHTS, [m.shape for m in (*matrices, *ff[:2])]))
        wholes = dict(shapes)
        wholes[FC1] = (*shapes[FC1][:4], 2 * ff[2].shape[1])
        wholes[FC2] = (*shapes[FC2][:3], *ff[3].shape[:1], 2 * ff[3].shape[1])
        nz = shapes[OUT][0]
        span = -(-9 * model // grid.fsdp // 128) * 128
        outs += [shaped((devices, 1, span), F32)]
        outs += [shaped((2 * s[3], s[4] // 4), F32) for s in (*wholes.values(),)[:6]]
        outs += [shaped((wholes[FC2][4] // 4, 2 * wholes[FC2][3]), F32)]
        out_specs = [anywhere] + [vmem] * 9
        scratch += [
            pltpu.VMEM((8, model), F32),
            pltpu.VMEM((1, 9 * model), F32),
            pltpu.VMEM((grid.fsdp, 1, span), F32),
            pltpu.SemaphoreType.DMA((2, devices - 1)),
            pltpu.VMEM((2 * wholes[FC2][3], wholes[FC2][4] // 4), F32),
        ]

        scratch += [pltpu.VMEM((nz, 2, *shapes[name][3:]), BF16) for name in (FC2, FC1)]
        scratch += reduce_scratch(shapes.values(), nz)
        scratch += [pltpu.VMEM((s[3], s[4] // 2), F32) for s in wholes.values()]
        scratch += [pltpu.VMEM((s[3], s[4] // 4), F32) for s in wholes.values()]
        count = len(reduce_items(shapes))
        scratch += [
            pltpu.SemaphoreType.DMA((count, nz + 4)),
            pltpu.SemaphoreType.DMA((count, nz + 4)),
            pltpu.SemaphoreType.DMA((2, 7)),
        ]
    else:
        ff = ()
        outs += [shaped((8, model), F32)]
        outs += [shaped(m.shape, BF16) for m in matrices]
        out_specs = [anywhere, vmem, vmem] + [anywhere] * 5
    return pl.pallas_call(
        functools.partial(backward_kernel, (grid.dp, grid.fsdp) if comm else None),
        out_shape=outs,
        in_specs=[smem] * 2 + [vmem] * 2 + [anywhere] * (17 + len(ff)),
        out_specs=out_specs,
        scratch_shapes=scratch,
        compiler_params=pltpu.CompilerParams(**params),
        name="backward",
    )(
        *lengths,
        modulation,
        rows_3,
        latent,
        text_block,
        *kept,
        *matrices,
        *ff,
    )


def deliver_kernel(count, conditions, gathered, *refs):
    given, ada_out, taken = refs[:count], refs[count], refs[count + 1 : 2 * count + 1]
    staged, sems = refs[2 * count + 1 : -1], refs[-1]
    inward = [
        pltpu.make_async_copy(src, mid, sems.at[0, k])
        for k, (src, mid) in enumerate(zip(given, staged))
    ]
    outward = [
        pltpu.make_async_copy(mid, dst, sems.at[1, k])
        for k, (mid, dst) in enumerate(zip(staged, taken))
    ]
    for copy in inward:
        copy.start()
    for before, after in zip(inward, outward):
        before.wait()
        after.start()
    rows, columns = ada_out.shape
    stacked = jnp.concatenate([gathered[k] for k in range(gathered.shape[0])], 0)
    product = dot_tn(conditions[...].astype(BF16), stacked.astype(BF16))[:rows]
    spare = product.shape[1] - columns
    ada_out[...] = jnp.where(
        lax.axis_index("fsdp") % 2 == 0, product[:, :columns], product[:, spare:]
    )
    for copy in outward:
        copy.wait()


def deliver(conditions, gathered, shape, results):
    vmem = pl.BlockSpec(memory_space=pltpu.VMEM)
    anywhere = pl.BlockSpec(memory_space=pl.ANY)
    count = len(results)
    return pl.pallas_call(
        functools.partial(deliver_kernel, count),
        out_shape=[jax.ShapeDtypeStruct(shape, F32)]
        + [jax.ShapeDtypeStruct(r.shape, r.dtype) for r in results],
        in_specs=[vmem] * 2 + [anywhere] * count,
        out_specs=[vmem] + [anywhere] * count,
        scratch_shapes=[pltpu.VMEM(r.shape, r.dtype) for r in results]
        + [pltpu.SemaphoreType.DMA((2, count))],
        compiler_params=pltpu.CompilerParams(vmem_limit_bytes=63 * 1024 * 1024),
        name="deliver",
    )(conditions, gathered, *results)


def by_part(matrix):
    split = matrix.reshape(*matrix.shape[:-1], 2, 2, 4, PARTS, matrix.shape[-1] // 16 // PARTS)
    return jnp.moveaxis(split, -2, -4).reshape(matrix.shape)


def from_part(matrix):
    split = matrix.reshape(*matrix.shape[:-1], 2, PARTS, 2, 4, matrix.shape[-1] // 16 // PARTS)
    return jnp.moveaxis(split, -4, -2).reshape(matrix.shape)


def body(
    latents,
    text_rows,
    out_grad,
    frame_len,
    text_len,
    timestep,
    w_ada,
    w_qkv,
    w_out,
    w_cq,
    w_ckv,
    w_cout,
    w_fc1,
    w_fc2,
    *,
    dp_size,
    fsdp_size,
):
    grid = Grid(dp_size, fsdp_size)
    matrices = (w_qkv, w_out, w_cq, w_ckv, w_cout, w_fc1, w_fc2)
    lengths = (frame_len, text_len)
    if grid.fits(matrices):
        ada = ada_inputs(grid, timestep, w_ada)
        matrices = (*matrices[:6], w_fc2.T)
    else:
        *others, full_fc1, full_fc2 = gather_weights(grid, matrices)
        matrices = (*others, by_part(full_fc1), full_fc2)
        conditions, modulation = modulate(grid, timestep, w_ada)
        ada = (modulation.reshape(1, -1),)
    layer_out, kept, kept_matrices, rest = forward(
        grid, lengths, latents[0], text_rows[0], out_grad[0], ada, matrices
    )
    grad_fc1, grad_fc2, sums_1, sums_2, rows_3, modulation, rows = rest
    comm = len(ada) > 1
    results = backward(
        grid,
        comm,
        lengths,
        latents[0],
        text_rows[0],
        modulation,
        rows_3,
        kept,
        kept_matrices,
        (grad_fc1, grad_fc2, sums_1, sums_2),
    )
    latent_grad, text_grad, rows_1 = results[:3]
    if comm:
        results = (layer_out, latent_grad, text_grad, *results[3:])
        grad_ada, layer_out, latent_grad, text_grad, *owned, fc2 = deliver(
            rows, rows_1, w_ada.shape, results
        )
        owned = (*owned, fc2.T)
    else:
        order = (
            rows_1[3:4],
            rows_1[4:5],
            rows_1[2:3],
            rows_1[0:1],
            rows_1[1:2],
            rows_3[3:4],
            rows_3[1:2],
            rows_3[2:3],
            rows_3[0:1],
        )
        dmodulation = jnp.concatenate(order, 0).reshape(1, -1).astype(BF16)
        grad_ada = ada_gradient(grid, conditions, dmodulation)
        owned = reduce_gradients(grid, (*results[3:8], from_part(grad_fc1), grad_fc2))
    return (
        layer_out[None],
        latent_grad[None],
        text_grad[None],
        grad_ada,
        *owned,
    )


def solution(mesh):
    placed = (P(("dp", "fsdp"), None, None),) * 3 + (P(("dp", "fsdp")),) * 3 + (P("dp", "fsdp"),) * 8
    return jax.shard_map(
        functools.partial(body, dp_size=mesh.shape["dp"], fsdp_size=mesh.shape["fsdp"]),
        mesh=mesh,
        in_specs=placed,
        out_specs=(P(("dp", "fsdp"), None, None),) * 3 + (P("dp", "fsdp"),) * 8,
        check_vma=False,
    )
```

```python
import functools
import math

import jax
import jax.numpy as jnp
from jax import lax
from jax.experimental import pallas as pl
from jax.experimental.pallas import tpu as pltpu
from jax.sharding import PartitionSpec as P

HEADS = 12


norm_eps = 1e-06


def sinusoid(time_value, model_width):
    half_width = model_width // 2
    frequency = jnp.exp(-math.log(10000.0) * jnp.arange(half_width, dtype=jnp.float32) / half_width)
    angles = time_value.astype(jnp.float32) * frequency
    return jnp.concatenate([jnp.cos(angles), jnp.sin(angles)], axis=-1)


def normalize(values):
    center = values - jnp.mean(values, -1, keepdims=True)
    spread = jnp.mean(center * center, -1, keepdims=True)
    inverse = lax.rsqrt(spread + norm_eps)
    return (center * inverse, inverse)


def norm_back(upstream, normed, inverse, scale_row):
    dshift = jnp.sum(upstream, 0)
    dscale = jnp.sum(upstream * normed, 0)
    scaled = upstream * (1.0 + scale_row)
    centered = (
        scaled
        - jnp.mean(scaled, -1, keepdims=True)
        - normed * jnp.mean(scaled * normed, -1, keepdims=True)
    )
    return (inverse * centered, dshift, dscale)


def outer_sum(left, right):
    return lax.dot_general(
        left, right, (((0,), (0,)), ((), ())), preferred_element_type=jnp.float32
    )


MESH = pl.DeviceIdType.MESH


class Grid:
    def __init__(self, dp_size, fsdp_size):
        self.dp = dp_size
        self.fsdp = fsdp_size

    def fits(self, matrices):
        if self.fsdp != 4 or self.dp != 8:
            return False
        for matrix in matrices:
            rows, columns = matrix.shape
            if rows % 32 or (2 * columns) % 128:
                return False
        return True


def place():
    dp_index = lax.axis_index("dp")
    fsdp_index = lax.axis_index("fsdp")
    return dp_index // 2, dp_index % 2, fsdp_index // 2, fsdp_index % 2


def device(z, y, x, core):
    return {"dp": z * 2 + y, "fsdp": x * 2 + core}


def gather_weights(grid, matrices):
    return tuple(
        lax.all_gather(
            lax.all_gather(m, "fsdp", axis=1, tiled=True), "dp", axis=0, tiled=True
        ).reshape(4, 2, 2, m.shape[0] * grid.dp // 16, m.shape[1] * grid.fsdp)
        for m in matrices
    )


def reduce_gradients(grid, gradients):
    out = []
    for gradient in gradients:
        part = gradient.reshape(-1, gradient.shape[-1])
        part = lax.psum_scatter(part, "dp", scatter_dimension=0, tiled=True)
        part = lax.psum_scatter(part, "fsdp", scatter_dimension=1, tiled=True)
        out.append(part.astype(jnp.float32))
    return tuple(out)


def modulate(grid, timestep, w_ada):
    rows, columns = w_ada.shape
    model_width = rows * grid.dp
    times = lax.all_gather(timestep, ("dp", "fsdp"), axis=0, tiled=True)
    conditions = jax.nn.silu(
        jax.vmap(lambda value: sinusoid(value, model_width))(times)
    ).astype(jnp.bfloat16)
    mine = lax.dynamic_slice_in_dim(conditions, lax.axis_index("dp") * rows, rows, 1)
    partial = jnp.dot(mine, w_ada, preferred_element_type=jnp.float32)
    summed = lax.psum_scatter(partial, "dp", scatter_dimension=0, tiled=True)
    mixed = lax.all_to_all(summed, "fsdp", split_axis=0, concat_axis=0, tiled=True)
    return mine, mixed.reshape(9, model_width)


def ada_gradient(grid, conditions, dmodulation):
    spread = dmodulation.reshape(grid.fsdp, -1)
    swapped = lax.all_to_all(spread, "fsdp", split_axis=0, concat_axis=0, tiled=True)
    everyone = lax.all_gather(swapped, "dp", axis=0, tiled=True)
    return outer_sum(conditions, everyone)


def ada_inputs(grid, timestep, w_ada):
    rows, columns = w_ada.shape
    condition = jax.nn.silu(sinusoid(timestep[0], rows * grid.dp)).astype(jnp.bfloat16)
    mine = jnp.pad(
        condition.astype(jnp.float32).reshape(grid.dp, 1, rows), ((0, 0), (0, 0), (0, 128 - rows))
    )
    return mine, w_ada


F32 = jnp.float32
BF16 = jnp.bfloat16
NT = (((1,), (1,)), ((), ()))
TN = (((0,), (0,)), ((), ()))


def flat(value):
    return value.reshape(-1, value.shape[-1])


def dot(left, right):
    return jnp.dot(left, right, preferred_element_type=F32)


def dot_nt(left, right):
    return lax.dot_general(left, right, NT, preferred_element_type=F32)


def dot_tn(left, right):
    return lax.dot_general(left, right, TN, preferred_element_type=F32)


def tiles(total, size, body):
    def step(t, carry):
        body(pl.ds(pl.multiple_of(t * size, size), size))
        return carry

    lax.fori_loop(0, total // size, step, 0)


def row_tile(rows):
    for size in (432, 288, 256, 128):
        if rows % size == 0:
            return size
    return rows


def gelu_pair(inner):
    slope = math.sqrt(2.0 / math.pi)
    square = inner * inner
    turned = jnp.tanh(inner * (slope + (slope * 0.044715) * square))
    half = 0.5 + 0.5 * turned
    rise = inner * (slope + (3.0 * slope * 0.044715) * square)
    return inner * half, half + (0.5 - 0.5 * turned * turned) * rise


def half_lanes(shape):
    return lax.broadcasted_iota(jnp.int32, shape, 1) < shape[1] // 2


def lanes_of(shape):
    return lax.broadcasted_iota(jnp.int32, shape, 1)


def mark_keys(marks, length):
    shape = marks.shape
    excluded = jnp.where(lax.broadcasted_iota(jnp.int32, shape, 0) < length, 0.0, -1e30)
    marks[...] = jnp.where(lanes_of(shape) == shape[1] - 1, excluded, 0.0).astype(BF16)


def thirds(value, last):
    high = value.astype(BF16).astype(F32)
    middle = (value - high).astype(BF16).astype(F32)
    low = value - high - middle
    lane = lanes_of(value.shape)
    spread = high + pltpu.roll(middle, 32, 1) + pltpu.roll(low, 64, 1)
    return jnp.where(lane == value.shape[1] - 1, last, spread).astype(BF16)


def head_lanes(model, stat_at):
    shape = (model, 128)
    head = lax.broadcasted_iota(jnp.int32, shape, 0) // (model // HEADS)
    return jnp.where(lanes_of(shape) == head + stat_at, 1.0, 0.0).astype(BF16)


def head_sums(left, right, matrix):
    product = left.astype(F32) * right.astype(F32)
    high = product.astype(BF16)
    return dot(high, matrix) + dot((product - high.astype(F32)).astype(BF16), matrix)


def attend(queries, keys, values, marks, mixed, stats, heads_wide, size):
    query_ref, query_at = queries
    key_ref, key_at = keys
    value_ref, value_at = values
    mixed_ref, mixed_at = mixed
    stat_ref, stat_at = stats
    rows = mixed_ref.shape[0]
    width = 2 * heads_wide

    def pair(p, carry):
        def at(start):
            return pl.ds(pl.multiple_of(start + p * width, width), width)

        value_pair = value_ref[:, at(value_at)]
        marked = jnp.concatenate([key_ref[:, at(key_at)], marks[...]], 1)
        low = half_lanes((size, width))
        lane = lanes_of((size, width))
        last = (lane == width - 1).astype(F32).astype(BF16)
        for start in range(0, rows, size):
            span = slice(start, start + size)
            scaled = query_ref[span, at(query_at)] * BF16(heads_wide**-0.5)
            outs = []
            stat = stat_ref[span, :]
            for head in range(2):
                own = jnp.where(low if head == 0 else ~low, scaled, BF16(0))
                scores = dot_nt(jnp.concatenate([own, last], 1), marked)
                largest = jnp.max(scores, -1, keepdims=True)
                raised = jnp.exp(scores - largest)
                summed = jnp.sum(raised, -1, keepdims=True)
                outs.append(dot(raised.astype(BF16), value_pair) * (1.0 / summed))
                stat = jnp.where(lane == stat_at + 2 * p + head, largest + jnp.log(summed), stat)
            stat_ref[span, :] = stat
            mixed_ref[span, at(mixed_at)] = jnp.where(low, outs[0], outs[1]).astype(BF16)
        return carry

    return pair


def attend_back(
    queries, keys, values, marks, upstream, means, stats, total, heads_wide, size, before=None
):
    query_ref, query_at = queries
    key_ref, key_at = keys
    value_ref, value_at = values
    stat_ref, stat_at = stats
    rows = upstream.shape[0]
    slots = key_ref.shape[0]
    width = 2 * heads_wide

    def pair(p, carry):
        def at(start):
            return pl.ds(pl.multiple_of(start + p * width, width), width)

        low = half_lanes((rows, width))
        scaled = query_ref[0:rows, at(query_at)] * BF16(heads_wide**-0.5)
        above = upstream[:, at(0)]
        heads = []
        for head in range(2):
            mask = low if head == 0 else ~low
            own = jnp.where(mask, scaled, BF16(0))
            own_above = jnp.where(mask, above, BF16(0))
            heads.append(
                (
                    jnp.concatenate([own, stat_ref[...]], 1),
                    jnp.concatenate([own_above, means[...]], 1),
                    own,
                    own_above,
                )
            )
        low_keys = half_lanes((size, width))
        lane = lanes_of((size, width))

        def one_tile(span):
            key_pair = key_ref[span, at(key_at)]
            value_pair = value_ref[span, at(value_at)]
            query_grad = None
            key_grad = None
            value_grad = None
            for head in range(2):
                mask = low_keys if head == 0 else ~low_keys
                taken = lane - (stat_at + 2 * p + head)
                mark = jnp.where(
                    (taken == 0) | (taken == 32) | (taken == 64),
                    BF16(-1),
                    marks[span, :],
                )
                marked_query, marked_above, own, own_above = heads[head]
                shares = jnp.exp(dot_nt(jnp.concatenate([key_pair, mark], 1), marked_query))
                share_grad = dot_nt(jnp.concatenate([value_pair, mark], 1), marked_above)
                score_grad = (shares * share_grad).astype(BF16)
                values_part = dot(shares.astype(BF16), own_above)
                keys_part = dot(score_grad, own)
                queries_part = dot_tn(score_grad, jnp.where(mask, key_pair, BF16(0)))
                value_grad = values_part if head == 0 else value_grad + values_part
                key_grad = keys_part if head == 0 else key_grad + keys_part
                query_grad = queries_part if query_grad is None else query_grad + queries_part
            key_ref[span, at(key_at)] = key_grad.astype(BF16)
            value_ref[span, at(value_at)] = value_grad.astype(BF16)
            total[...] += query_grad

        total[...] = jnp.zeros_like(total)

        def step(t, carry):
            if before is not None:
                before(t)
            one_tile(pl.ds(pl.multiple_of(t * size, size), size))
            return carry

        lax.fori_loop(0, slots // size, step, 0)
        query_ref[0:rows, at(query_at)] = (total[...] * heads_wide**-0.5).astype(BF16)
        return carry

    return pair


class Loads:
    def __init__(self, sems):
        self.sems = sems
        self.copies = {}

    def start(self, name, src, dst):
        copy = pltpu.make_async_copy(src, dst, self.sems.at[len(self.copies)])
        copy.start()
        self.copies[name] = copy

    def wait(self, *names):
        for name in names:
            self.copies[name].wait()


WEIGHTS = ("qkv", "out", "cq", "ckv", "cout", "fc1", "fc2")
QKV, OUT, CQ, CKV, COUT, FC1, FC2 = WEIGHTS
PARTS = 4


def half_columns(ref, which, first=(0, 0), width=None):
    half = ref.shape[-1] // 2
    if width is None:
        width = half
    start = which * (half + first[1] - first[0]) + first[0]
    return pl.ds(pl.multiple_of(start, 128), width)


class Item:
    def __init__(self, name, rows=None, first=0, width=None, slot=None, summed=(0, 0)):
        self.name = name
        self.summed = summed
        self.rows = rows
        self.first = first if isinstance(first, tuple) else (first, first)
        self.width = width
        self.slot = self.first[0] if slot is None else slot


def gather_items(held):
    items = []
    rows = held[QKV].shape[3]
    items += [Item(QKV, (r, 16)) for r in range(0, rows, 16)]
    items += [Item(OUT), Item(CQ)]
    width = held[CKV].shape[-1] // 4
    items += [Item(CKV, None, k * width, width) for k in range(2)]
    items += [Item(COUT)]
    rows = held[FC2].shape[3] // PARTS
    width = held[FC1].shape[-1] // 2 // PARTS
    for part in range(PARTS):
        items += [Item(FC2, (part * rows, rows)), Item(FC1, None, part * width, width)]
    return items


class Gather:
    def __init__(self, where, given, held, own, swapped, items, sems):
        self.z, self.y, self.x, self.core = where
        self.given, self.held, self.own, self.swapped, self.items = given, held, own, swapped, items
        self.swap_sem, self.send_sem, self.recv_sem = sems
        self.nz = held[OUT].shape[0]
        z, y, x, core = where
        self.sibling = device(z, y, x, 1 - core)
        self.first = device(
            z, y * (1 - core) + (1 - y) * core, (1 - x) * (1 - core) + x * core, core
        )
        self.second = device(
            z, (1 - y) * (1 - core) + y * core, x * (1 - core) + (1 - x) * core, core
        )
        self.others = [device((z + step) % self.nz, y, x, core) for step in range(1, self.nz)]
        self.done = 0
        self.counts = [0, 0, 0, 0]
        self.record = None

    def half(self, number, which):
        staged = self.own[WEIGHTS[number]]
        rows = staged.shape[0] // 2
        return staged.at[pl.ds(pl.multiple_of(which * rows, 16), rows), :]

    def swap(self, number):
        return pltpu.make_async_remote_copy(
            src_ref=self.half(number, 1 - self.core),
            dst_ref=self.swapped[WEIGHTS[number]],
            send_sem=self.swap_sem.at[0, number],
            recv_sem=self.swap_sem.at[1, number],
            device_id=self.sibling,
            device_id_type=MESH,
        )

    def assemble(self, number):
        name = WEIGHTS[number]
        self.swap(number).wait_recv()
        mine, theirs = self.half(number, self.core)[...], self.swapped[name][...]
        whole = self.held[name]
        left = jnp.where(self.core == 0, mine, theirs)
        right = jnp.where(self.core == 0, theirs, mine)
        if name == FC1:
            four = left.shape[1] // 4
            step = four // PARTS
            pieces = [
                side[:, k * four + part * step : k * four + (part + 1) * step]
                for part in range(PARTS)
                for side in (left, right)
                for k in range(4)
            ]
        else:
            pieces = [left, right]
        whole[self.z, self.y, self.core, :, half_columns(whole, self.x)] = jnp.concatenate(
            pieces, 1
        )

    def remote(self, number, slot, part, partner):
        return pltpu.make_async_remote_copy(
            src_ref=part,
            dst_ref=part,
            send_sem=self.send_sem.at[number, slot],
            recv_sem=self.recv_sem.at[number, slot],
            device_id=partner,
            device_id_type=MESH,
        )

    def view(self, number):
        item = self.items[number]
        whole = self.held[item.name]
        rows = slice(None) if item.rows is None else pl.ds(*item.rows)
        return whole, rows, lambda which: half_columns(whole, which, item.first, item.width)

    def along_z(self, number):
        whole, rows, columns = self.view(number)
        part = whole.at[self.z, self.y, self.core, rows, columns(self.x)]
        return [self.remote(number, s, part, partner) for s, partner in enumerate(self.others)]

    def to_first(self, number):
        whole, rows, columns = self.view(number)
        part = whole.at[:, self.y, self.core, rows, columns(self.x)]
        return [self.remote(number, self.nz - 1, part, self.first)]

    def to_second(self, number):
        whole, rows, columns = self.view(number)
        copies = []
        for k in range(2):
            row = self.y * (1 - self.core) + k * self.core
            column = k * (1 - self.core) + self.x * self.core
            part = whole.at[:, row, self.core, rows, columns(column)]
            copies.append(self.remote(number, self.nz + k, part, self.second))
        return copies

    def to_core(self, number):
        whole, rows, columns = self.view(number)
        if self.items[number].width is None:
            parts = [whole.at[:, :, self.core, rows, :]]
        else:
            parts = [whole.at[:, :, self.core, rows, columns(k)] for k in range(2)]
        return [
            self.remote(number, self.nz + 2 + k, part, self.sibling) for k, part in enumerate(parts)
        ]

    def up_to(self, depth, number):
        while self.counts[depth] <= min(number, len(self.items) - 1):
            self.emit((depth, self.counts[depth]))
            self.counts[depth] += 1

    def emit(self, step):
        if self.record is not None:
            self.record.append(step)
            return
        depth, number = step
        stages = [self.along_z, self.to_first, self.to_second, self.to_core]
        if depth:
            for copy in stages[depth - 1](number):
                copy.wait_recv()
        if depth < 4:
            for copy in stages[depth](number):
                copy.start()

    def planned(self, body):
        self.record = []
        body()
        steps, self.record = self.record, None
        return steps

    def advance(self, steps, lag=2, ahead=3):
        while self.done < steps:
            self.up_to(0, self.done + ahead)
            for depth in range(1, 4):
                self.up_to(depth, self.done - (depth - 1) * lag)
            self.done += 1

    def numbers(self, name):
        return [i for i, item in enumerate(self.items) if item.name == name]

    def need(self, numbers):
        for depth in range(4):
            self.up_to(depth, max(numbers))
        for number in numbers:
            self.emit((4, number))

    def sent(self, numbers):
        for number in numbers:
            for stage in (self.along_z, self.to_first, self.to_second, self.to_core):
                for copy in stage(number):
                    copy.wait_send()


def everyone(dp_size, fsdp_size, body):
    count = dp_size * fsdp_size
    me = lax.axis_index("dp") * fsdp_size + lax.axis_index("fsdp")

    def one(step, carry):
        body(step, (me + step) % count, me)
        return carry

    lax.fori_loop(1, count, one, 0)


def modulate_start(dp_size, fsdp_size, mine, everything, sems):
    def copy(step, target, me, row):
        return pltpu.make_async_remote_copy(
            src_ref=mine.at[row],
            dst_ref=everything.at[me],
            send_sem=sems.at[0, step - 1],
            recv_sem=sems.at[1, step - 1],
            device_id={"dp": target // fsdp_size, "fsdp": target % fsdp_size},
            device_id_type=MESH,
        )

    return copy


def forward_kernel(comm, *refs):
    (frame_len, text_len, lat_in, text_in, og_in), refs = refs[:5], refs[5:]
    if comm:
        (mine, w_ada), refs = refs[:2], refs[2:]
    else:
        (mod_in,), refs = refs[:1], refs[1:]
    given, refs = dict(zip(WEIGHTS, refs[:7])), refs[7:]
    (layer_out, dcross_out, qkv_out, h1_out, mixed1_out, h2_out, q2_out, mixed2_out), refs = (
        refs[:8],
        refs[8:],
    )
    (memory_out, after_out), refs = refs[:2], refs[2:]
    kept_out, refs = dict(zip(BACK, refs[:5])), refs[5:]
    (stats_out, fc1_out, fc2_out, sums_fc1, sums_fc2), refs = refs[:5], refs[5:]
    (rows_sent, mod_sent, conditions_sent), refs = refs[:3], refs[3:]
    held, refs = dict(zip(WEIGHTS, refs[:7])), refs[7:]
    big, wide, h3, db3, memory, after_self, upstream_sum, branch_2, after_cross, result = refs[:10]
    refs = refs[10:]
    lat, text, og, stats, split_stats, frame_marks, text_marks, sems = refs[:8]
    rows_out, mod, conditions = refs[8:11]
    refs = refs[11:]
    loads = Loads(sems)
    loads.start("lat", lat_in, lat)
    loads.start("text", text_in, text)
    loads.start("og", og_in, og)
    slots, model = lat.shape
    inner_width = held[FC1].shape[-1]
    head = model // HEADS
    size = row_tile(slots)
    if comm:
        dp_size, fsdp_size = comm
        (everybody, partial, modulations, ada_sems), refs = refs[:4], refs[4:]
        (ada_block, ada_wide, turned), refs = refs[:3], refs[3:]
        own, refs = dict(zip(WEIGHTS, refs[:7])), refs[7:]
        swapped, refs = dict(zip(WEIGHTS, refs[:7])), refs[7:]
        gather_sems, refs = refs[:3], refs[3:]
        landing, from_first, from_second, from_z, sums = (
            {FC1: refs[2 * k], FC2: refs[2 * k + 1]} for k in range(5)
        )
        reduce_sems = refs[10:]
        per = held[FC2].shape[3] // PARTS, held[FC1].shape[-1] // 2 // PARTS
        reduce = Reduce(
            place(),
            {FC1: held[FC1], FC2: held[FC2]},
            {},
            landing,
            from_first,
            from_second,
            from_z,
            sums,
            None,
            part_items(*per, EARLY, 0),
            (*reduce_sems, None),
        )
        items = gather_items(held)
        gather = Gather(place(), given, held, own, swapped, items, gather_sems)
        order = [WEIGHTS.index(n) for n in dict.fromkeys(item.name for item in items)]
        barrier = pltpu.get_barrier_semaphore()

        def greet_one(step, target, me):
            pl.semaphore_signal(
                barrier,
                inc=1,
                device_id={"dp": target // fsdp_size, "fsdp": target % fsdp_size},
                device_id_type=MESH,
            )

        everyone(dp_size, fsdp_size, greet_one)
        loads.start("w_ada", w_ada, ada_block)
        for number in order:
            name = WEIGHTS[number]
            loads.start("w" + name, given[name], turned if name == FC2 else own[name])
        mark_keys(frame_marks, frame_len[0])
        mark_keys(text_marks, text_len[0])
        big[slots:, :] = jnp.zeros((big.shape[0] - slots, big.shape[1]), BF16)
        stats[...] = jnp.zeros_like(stats)
        loads.wait("w_ada")
        blank = jnp.zeros((ada_block.shape[0], ada_wide.shape[1] - ada_block.shape[1]), BF16)
        ada_wide[0 : ada_block.shape[0], :] = jnp.where(
            gather.core == 0,
            jnp.concatenate([ada_block[...], blank], 1),
            jnp.concatenate([blank, ada_block[...]], 1),
        )
        ada_wide[ada_block.shape[0] :, :] = jnp.zeros(
            (ada_wide.shape[0] - ada_block.shape[0], ada_wide.shape[1]), BF16
        )
        loads.wait(*["w" + name for name in WEIGHTS])
        own[FC2][...] = turned[...].T
        pl.semaphore_wait(barrier, dp_size * fsdp_size - 1)
        for number in order:
            gather.swap(number).start()
        dp_index = lax.axis_index("dp")
        me = dp_index * fsdp_size + lax.axis_index("fsdp")
        send_1 = modulate_start(dp_size, fsdp_size, mine, everybody, ada_sems.at[0])
        send_2 = modulate_start(dp_size, fsdp_size, partial, modulations, ada_sems.at[1])
        everyone(dp_size, fsdp_size, lambda s, t, m: send_1(s, t, m, t // fsdp_size).start())
        everybody[me] = mine[dp_index]
        gather.assemble(WEIGHTS.index(QKV))
        gather.up_to(0, 2)
        everyone(dp_size, fsdp_size, lambda s, t, m: send_1(s, t, m, t // fsdp_size).wait_recv())
        for k in range(dp_size * fsdp_size):
            conditions[k : k + 1, :] = everybody[k]
        product = dot(conditions[...].astype(BF16), ada_wide[...])
        for k in range(dp_size * fsdp_size):
            partial[k] = product[k : k + 1, :]
        everyone(dp_size, fsdp_size, lambda s, t, m: send_2(s, t, m, t).start())
        modulations[me] = partial[me]
        for number in order[1:]:
            gather.assemble(number)
        gather.advance(3, 1, 1)
        everyone(dp_size, fsdp_size, lambda s, t, m: send_2(s, t, m, t).wait_recv())
        mod[...] = jnp.zeros_like(mod)
        span = partial.shape[-1]
        for j in range(fsdp_size):
            total = modulations[j]
            for i in range(1, dp_size):
                total += modulations[i * fsdp_size + j]
            start = j * mod.shape[1] // fsdp_size // 128 * 128
            mod[:, start : start + span] += total
    else:
        mod[...] = mod_in[...]
        conditions[...] = jnp.zeros_like(conditions)
        for name in WEIGHTS:
            loads.start(name, given[name], held[name])

    def need(name, part=None):
        if not comm:
            if not part:
                loads.wait(name)
            return
        numbers = gather.numbers(name)
        gather.need(numbers if part is None else [numbers[part]])

    def hook(p, plan):
        if comm:
            for at, steps in plan:

                @pl.when(p == at)
                def _():
                    gather.advance(steps)

    def step_to(steps):
        if comm:
            gather.advance(steps)

    def row(k):
        return mod[:, k * model : (k + 1) * model]

    loads.start("mod", mod, mod_sent)
    loads.start("cond", conditions, conditions_sent)
    if not comm:
        mark_keys(frame_marks, frame_len[0])
        mark_keys(text_marks, text_len[0])
        big[slots:, :] = jnp.zeros((big.shape[0] - slots, big.shape[1]), BF16)
        stats[...] = jnp.zeros_like(stats)
    loads.wait("lat", "text", "og")

    def norm_1(rows):
        normed, _ = normalize(lat[rows, :].astype(F32))
        wide[rows, 0:model] = (normed * (1.0 + row(1)) + row(0)).astype(BF16)

    tiles(slots, size, norm_1)
    if comm:
        gather.advance(5, 1)
    need(QKV)

    def project_part(columns):
        def project(rows):
            big[rows, columns] = dot(
                wide[rows, 0:model], flat(held[QKV][:, :, :, :, columns])
            ).astype(BF16)

        tiles(slots, size, project)

    tiles(3 * model, model, project_part)
    loads.start("qkv_out", big.at[0:slots, 0 : 3 * model], qkv_out)
    loads.start("h1_out", wide.at[:, 0:model], h1_out)
    if comm:
        loads.start("kept_qkv", held[QKV], kept_out[QKV])
    pair = attend(
        (big, 0),
        (big, model),
        (big, 2 * model),
        frame_marks,
        (wide, model),
        (stats, 0),
        head,
        size,
    )

    def pair_1(p, carry):
        hook(p, ((0, 6), (1, 7), (3, 8), (4, 9), (5, 10)))
        return pair(p, carry)

    lax.fori_loop(0, HEADS // 2, pair_1, 0)
    loads.start("mixed1_out", wide.at[:, model : 2 * model], mixed1_out)
    need(OUT)
    need(CQ)

    def join_1(rows):
        branch = dot(wide[rows, model : 2 * model], flat(held[OUT][...]))
        after = lat[rows, :].astype(F32) + row(2) * branch
        after_self[rows, :] = after
        normed, _ = normalize(after)
        hidden = (normed * (1.0 + row(4)) + row(3)).astype(BF16)
        wide[rows, 2 * model : 3 * model] = hidden
        wide[rows, 3 * model : 4 * model] = dot(hidden, flat(held[CQ][...])).astype(BF16)

    tiles(slots, size, join_1)
    loads.start("after_out", after_self, after_out)
    loads.start("h2_out", wide.at[:, 2 * model : 3 * model], h2_out)
    loads.start("q2_out", wide.at[:, 3 * model : 4 * model], q2_out)
    step_to(11)
    need(CKV)

    def project_text(columns):
        memory[:, columns] = dot(text[...], flat(held[CKV][:, :, :, :, columns])).astype(BF16)

    tiles(2 * model, model, project_text)
    loads.start("memory_out", memory, memory_out)
    mixed2 = big.at[0:slots, 3 * model : 4 * model]
    pair = attend(
        (wide, 3 * model),
        (memory, 0),
        (memory, model),
        text_marks,
        (mixed2, 0),
        (stats, HEADS),
        head,
        size,
    )

    def pair_2(p, carry):
        hook(p, ((0, 12), (3, 13)))
        return pair(p, carry)

    lax.fori_loop(0, HEADS // 2, pair_2, 0)
    loads.start("mixed2_out", mixed2, mixed2_out)
    split_stats[...] = thirds(stats[...], 1.0)
    loads.start("stats_out", split_stats, stats_out)
    need(COUT)

    def join_2(rows):
        branch = dot(mixed2[rows, :], flat(held[COUT][...]))
        branch_2[rows, :] = branch
        after = after_self[rows, :] + row(5) * branch
        after_cross[rows, :] = after
        normed, _ = normalize(after)
        h3[rows, :] = (normed * (1.0 + row(7)) + row(6)).astype(BF16)
        db3[rows, :] = (row(8) * og[rows, :].astype(F32)).astype(BF16)

    step_to(14)
    tiles(slots, size, join_2)
    if comm:
        for name in BACK[1:]:
            loads.start("kept_" + name, held[name], kept_out[name])
    loads.wait("h1_out", "mixed1_out")
    act, din = wide.at[:, 0:model], wide.at[:, model : 2 * model]
    rows_out[...] = jnp.zeros_like(rows_out)
    first, second = held[FC1], held[FC2]
    width = inner_width // 2 // PARTS
    count = second.shape[3] // PARTS
    lead = second.shape[:3]

    def clear(rows):
        result[rows, :] = jnp.zeros((16, model), F32)
        upstream_sum[rows, :] = jnp.zeros((16, model), F32)

    tiles(slots, 16, clear)

    def at_part(part, bodies):
        for k, body in enumerate(bodies):
            pl.when(part == k)(body)

    arrivals, middles, ends = [], [], []
    for k in range(PARTS):

        def arrive(k=k):
            need(FC2, k)
            need(FC1, k)
            step_to(15 + 2 * k)

        def middle(k=k):
            step_to(16 + 2 * k)
            if k + 1 < PARTS:
                for depth in range(4):
                    gather.up_to(depth, gather.numbers(FC1)[k + 1])

        if comm:
            plans = gather.planned(arrive), gather.planned(middle)

            def emit_arrival(steps=plans[0]):
                for step in steps:
                    gather.emit(step)

            def emit_middle(steps=plans[1], k=k):
                for step in steps:
                    gather.emit(step)
                gather.sent([gather.numbers(name)[k] for name in (FC2, FC1)])
                for step in ((), ((0, 0), (0, 1)), (), ((2, 0), (2, 1)))[k]:
                    reduce.step(*step)

            def emit_end(k=k):
                if k < EARLY:
                    reduce.launch(2 * k)
                    reduce.launch(2 * k + 1)
                for step in ((), (), ((1, 0), (1, 1)), ())[k]:
                    reduce.step(*step)

            arrivals.append(emit_arrival)
            middles.append(emit_middle)
            ends.append(emit_end)
        else:
            arrive()

    def feed_part(part, carry):
        at_part(part, arrivals)
        spans = [
            pl.ds(pl.multiple_of(k * inner_width // 2 + part * width, 128), width) for k in range(2)
        ]
        chunk = pl.ds(pl.multiple_of(part * count, 16), count)

        def feed(rows):
            matrix_1 = jnp.concatenate([flat(first[:, :, :, :, s]) for s in spans], 1)
            matrix_2 = flat(second[:, :, :, chunk, :])
            activated, slope = gelu_pair(dot(h3[rows, :], matrix_1))
            activated = activated.astype(BF16)
            dinner = (dot_nt(db3[rows, :], matrix_2) * slope).astype(BF16)
            act[rows, :] = activated
            din[rows, :] = dinner
            result[rows, :] += dot(activated, matrix_2)
            upstream_sum[rows, :] += dot_nt(dinner, matrix_1)

        tiles(slots, size, feed)
        at_part(part, middles)
        product = dot_tn(act[...], db3[...]).astype(BF16)
        second[:, :, :, chunk, :] = product.reshape(lead + (count, model))
        product = dot_tn(h3[...], din[...]).astype(BF16)
        for k, span in enumerate(spans):
            first[:, :, :, :, span] = product[:, k * width : (k + 1) * width].reshape(
                first.shape[:4] + (width,)
            )
        at_part(part, ends)
        return carry

    lax.fori_loop(0, PARTS, feed_part, 0)
    if comm:
        loads.start("fc2_out", second.at[:, :, :, EARLY * count :, :], fc2_out)
        for k in range(2):
            loads.start(
                "fc1_out" + "b" * k,
                first.at[:, :, :, :, (k * PARTS + EARLY) * width : (k + 1) * PARTS * width],
                fc1_out.at[
                    :, :, :, :, k * (PARTS - EARLY) * width : (k + 1) * (PARTS - EARLY) * width
                ],
            )
    else:
        loads.start("fc2_out", second, fc2_out)
        loads.start("fc1_out", first, fc1_out)

    def leave(rows):
        entering = after_cross[rows, :]
        branch = result[rows, :]
        grad = og[rows, :].astype(F32)
        result[rows, :] = entering + row(8) * branch
        normed, inverse = normalize(entering)
        back, dshift, dscale = norm_back(upstream_sum[rows, :], normed, inverse, row(7))
        dcross = grad + back
        after_cross[rows, :] = dcross
        rows_out[0:1, :] += jnp.sum(grad * branch, 0, keepdims=True)
        rows_out[1:2, :] += dshift[None]
        rows_out[2:3, :] += dscale[None]
        rows_out[3:4, :] += jnp.sum(dcross * branch_2[rows, :], 0, keepdims=True)

    tiles(slots, size, leave)
    loads.start("layer_out", result, layer_out)
    loads.start("rows", rows_out, rows_sent)
    loads.start("dcross_out", after_cross, dcross_out)
    if comm:
        for number in order:
            gather.swap(number).wait_send()
        for name in BACK:
            gather.sent(gather.numbers(name))
            loads.wait("kept_" + name)
        for number in range(2 * EARLY):
            reduce.step(3, number)
        loads.start("sums1", sums[FC1], sums_fc1)
        loads.start("sums2", sums[FC2], sums_fc2)
        everyone(dp_size, fsdp_size, lambda s, t, m: send_1(s, t, m, t // fsdp_size).wait_send())
        everyone(dp_size, fsdp_size, lambda s, t, m: send_2(s, t, m, t).wait_send())
        reduce.sent()
        loads.wait("sums1", "sums2", "fc1_outb")
    loads.wait("qkv_out", "h2_out", "q2_out", "mixed2_out")
    loads.wait("mod", "cond", "rows", "stats_out", "after_out", "memory_out", "layer_out", "dcross_out", "fc1_out", "fc2_out")


def forward(grid, lengths, latent, text_block, upstream, ada, matrices):
    slots, model = latent.shape
    text_slots = text_block.shape[0]
    padded = -(-slots // 128) * 128
    comm = len(ada) > 1
    lead = (4, 2, 2)
    devices = grid.dp * grid.fsdp
    if comm:
        blocks = [m.shape for m in matrices[:6]] + [matrices[6].shape[::-1]]
        wholes = [lead + (b[0] * grid.dp // 16, b[1] * grid.fsdp) for b in blocks]
    else:
        wholes = [m.shape for m in matrices]
    inner_width = wholes[5][-1]
    late_1, late_2 = wholes[5], wholes[6]
    if comm:
        later = PARTS - EARLY
        late_1 = (*late_1[:4], late_1[4] // PARTS * later)
        late_2 = (*late_2[:3], late_2[3] // PARTS * later, late_2[4])
    shaped = jax.ShapeDtypeStruct
    narrow = shaped((slots, model), BF16)
    full = shaped((slots, model), F32)
    outs = [
        full,
        full,
        shaped((slots, 3 * model), BF16),
        narrow,
        narrow,
        narrow,
        narrow,
        narrow,
        shaped((text_slots, 2 * model), BF16),
        full,
    ]
    outs += [shaped(w if comm else (8, 128), BF16) for w in wholes[:5]]
    outs += [
        shaped((slots, 128), BF16),
        shaped(late_1, BF16),
        shaped(late_2, BF16),
        *[shaped((s[3], s[4] // 2) if comm else (8, 128), F32) for s in wholes[5:]],
        shaped((8, model), F32),
        shaped((1, 9 * model), F32),
        shaped((devices, 128), F32),
    ]
    vmem = pl.BlockSpec(memory_space=pltpu.VMEM)
    anywhere = pl.BlockSpec(memory_space=pl.ANY)
    smem = pl.BlockSpec(memory_space=pltpu.SMEM)
    scratch = [pltpu.VMEM(w, BF16) for w in wholes]
    scratch += [
        pltpu.VMEM((padded, 4 * model), BF16),
        pltpu.VMEM((slots, 4 * model), BF16),
    ]
    scratch += [pltpu.VMEM((slots, model), BF16)] * 2
    scratch += [pltpu.VMEM((text_slots, 2 * model), BF16)]
    scratch += [pltpu.VMEM((slots, model), F32)] * 5
    scratch += [
        pltpu.VMEM((slots, model), BF16),
        pltpu.VMEM((text_slots, model), BF16),
        pltpu.VMEM((slots, model), BF16),
        pltpu.VMEM((slots, 128), F32),
        pltpu.VMEM((slots, 128), BF16),
        pltpu.VMEM((padded, 128), BF16),
        pltpu.VMEM((text_slots, 128), BF16),
        pltpu.SemaphoreType.DMA((48,)),
        pltpu.VMEM((8, model), F32),
        pltpu.VMEM((1, 9 * model), F32),
        pltpu.VMEM((devices, 128), F32),
    ]
    if comm:
        items = gather_items(dict(zip(WEIGHTS, [shaped(w, BF16) for w in wholes])))
        rows, columns = ada[1].shape
        span = -(-columns // 128) * 128
        scratch += [
            pltpu.VMEM((devices, 1, 128), F32),
            pltpu.VMEM((devices, 1, span), F32),
            pltpu.VMEM((devices, 1, span), F32),
            pltpu.SemaphoreType.DMA((2, 2, devices - 1)),
            pltpu.VMEM((rows, columns), BF16),
            pltpu.VMEM((128, span), BF16),
            pltpu.VMEM(matrices[6].shape, BF16),
        ]
        scratch += [pltpu.VMEM(b, BF16) for b in blocks]
        scratch += [pltpu.VMEM((b[0] // 2, b[1]), BF16) for b in blocks]
        scratch += [
            pltpu.SemaphoreType.DMA((2, len(matrices))),
            pltpu.SemaphoreType.DMA((len(items), lead[0] + 4)),
            pltpu.SemaphoreType.DMA((len(items), lead[0] + 4)),
        ]
        early = [
            (*wholes[5][:4], wholes[5][4] // PARTS * EARLY),
            (*wholes[6][:3], wholes[6][3] // PARTS * EARLY, wholes[6][4]),
        ]
        scratch += reduce_scratch(early, lead[0])
        scratch += [pltpu.VMEM((s[3], s[4] // 2), F32) for s in wholes[5:]]
        scratch += [pltpu.SemaphoreType.DMA((2 * EARLY, lead[0] + 4))] * 2
    params = {"vmem_limit_bytes": 63 * 1024 * 1024}
    if comm:
        params.update(collective_id=0, has_side_effects=True)
    results = pl.pallas_call(
        functools.partial(forward_kernel, (grid.dp, grid.fsdp) if comm else None),
        out_shape=outs,
        in_specs=[smem] * 2 + [anywhere] * 3 + [vmem] + [anywhere] * (6 + len(ada)),
        out_specs=[anywhere] * 23,
        scratch_shapes=scratch,
        compiler_params=pltpu.CompilerParams(**params),
        name="forward",
    )(*lengths, latent, text_block, upstream, *ada, *matrices)
    kept_matrices = results[10:15] if comm else matrices[:5]
    return results[0], (*results[1:10], results[15]), kept_matrices, results[16:]


BACK = (QKV, OUT, CQ, CKV, COUT)


EARLY = 1


def part_items(rows, width, parts, before):
    items = []
    for part in range(parts):
        items += [
            Item(FC2, (part * rows, rows), summed=(before * rows, 0)),
            Item(FC1, None, part * width, width, summed=(0, before * width)),
        ]
    return items


def reduce_items(shapes):
    parts = PARTS - EARLY
    items = part_items(shapes[FC2][3] // parts, shapes[FC1][-1] // 2 // parts, parts, EARLY)
    items += [Item(COUT)]
    width = shapes[CKV][-1] // 4
    items += [Item(CKV, None, k * width, width) for k in range(2)]
    items += [Item(CQ), Item(OUT)]
    model = shapes[QKV][-1] // 3
    third, half = model // 3, model // 2
    items += [
        Item(QKV, None, (0, half), third, 0),
        Item(QKV, None, (2 * third, half + 2 * third), third, third),
        Item(QKV, None, (model, 2 * third - half), third, 2 * third),
        Item(QKV, None, (third, half + third), third, model),
        Item(QKV, None, (model + third, 0), third // 2, model + third),
    ]
    return items


class Reduce:
    def __init__(self, where, sources, kept, landing, first, second, along, sums, owned, items, sems):
        self.z, self.y, self.x, self.core = where
        self.sources, self.kept, self.landing = sources, kept, landing
        self.from_first, self.from_second, self.from_z = first, second, along
        self.sums, self.owned, self.items = sums, owned, items
        self.send_sem, self.recv_sem, self.last_sem = sems
        self.nz = sources[FC2].shape[0]
        self.counts = [0, 0, 0, 0]
        z, y, x, core = where
        self.sibling = device(z, y, x, 1 - core)
        self.first = device(
            z, (1 - y) * (1 - core) + y * core, x * (1 - core) + (1 - x) * core, core
        )
        self.second = device(
            z, y * (1 - core) + (1 - y) * core, (1 - x) * (1 - core) + x * core, core
        )
        self.done = 0

    def remote(self, number, slot, src, dst, partner):
        return pltpu.make_async_remote_copy(
            src_ref=src,
            dst_ref=dst,
            send_sem=self.send_sem.at[number, slot],
            recv_sem=self.recv_sem.at[number, slot],
            device_id=partner,
            device_id_type=MESH,
        )

    def rows(self, number, offset=0):
        item = self.items[number]
        height = self.sources[item.name].shape[3]
        start, size = (0, height) if item.rows is None else item.rows
        return pl.ds(start + offset, size)

    def columns(self, number, which):
        item = self.items[number]
        return half_columns(self.sources[item.name], which, item.first, item.width)

    def inside(self, number):
        item = self.items[number]
        width = self.sources[item.name].shape[-1] // 2 if item.width is None else item.width
        return pl.ds(item.slot, width)

    def landed(self, number, which):
        item = self.items[number]
        half = self.landing[item.name].shape[-1] // 2
        return pl.ds(which * half + item.slot, half if item.width is None else item.width)

    def stay(self, number):
        name = self.items[number].name
        if name in self.kept:
            return self.kept[name], ()
        return self.sources[name], (self.core,)

    def kept_at(self, number, a, b, columns):
        ref, extra = self.stay(number)
        return ref.at[(a, b, *extra, self.rows(number), columns)]

    def to_core(self, number):
        item = self.items[number]
        landing = self.landing[item.name]
        copies = []
        for k in range(2):
            columns = self.columns(number, k)
            src = self.sources[item.name].at[:, :, 1 - self.core, self.rows(number), columns]
            dst = landing.at[:, :, self.rows(number), self.landed(number, k)]
            copies.append(self.remote(number, self.nz + 2 + k, src, dst, self.sibling))
        return copies

    def to_first(self, number):
        copies = []
        for k in range(2):
            row = (1 - self.y) * (1 - self.core) + k * self.core
            column = k * (1 - self.core) + (1 - self.x) * self.core
            src = self.kept_at(number, slice(None), row, self.columns(number, column))
            dst = self.from_first[self.items[number].name].at[
                :, k, self.rows(number), self.inside(number)
            ]
            copies.append(self.remote(number, self.nz + k, src, dst, self.first))
        return copies

    def to_second(self, number):
        row = self.y * (1 - self.core) + (1 - self.y) * self.core
        column = (1 - self.x) * (1 - self.core) + self.x * self.core
        src = self.kept_at(number, slice(None), row, self.columns(number, column))
        dst = self.from_second[self.items[number].name].at[
            :, self.rows(number), self.inside(number)
        ]
        return [self.remote(number, self.nz - 1, src, dst, self.second)]

    def to_z(self, number):
        copies = []
        for step in range(1, self.nz):
            other = (self.z + step) % self.nz
            src = self.kept_at(number, other, self.y, self.columns(number, self.x))
            dst = self.from_z[self.items[number].name].at[
                step - 1, self.rows(number), self.inside(number)
            ]
            partner = device(other, self.y, self.x, self.core)
            copies.append(self.remote(number, step - 1, src, dst, partner))
        return copies

    def add_core(self, number):
        landing = self.landing[self.items[number].name]
        for k in range(2):
            columns = self.columns(number, k)
            rows, landed = self.rows(number), self.landed(number, k)

            def one(step, carry):
                a, b = step // 2, step % 2
                spot = self.kept_at(number, a, b, columns)
                spot[...] = spot[...] + landing[a, b, rows, landed]
                return carry

            lax.fori_loop(0, self.nz * 2, one, 0)

    def add_first(self, number):
        arrived = self.from_first[self.items[number].name]
        rows, inside = self.rows(number), self.inside(number)
        for k in range(2):
            row = self.y * (1 - self.core) + k * self.core
            columns = self.columns(number, k * (1 - self.core) + self.x * self.core)

            def one(a, carry):
                spot = self.kept_at(number, a, row, columns)
                spot[...] = spot[...] + arrived[a, k, rows, inside]
                return carry

            lax.fori_loop(0, self.nz, one, 0)

    def add_second(self, number):
        arrived = self.from_second[self.items[number].name]
        rows, inside = self.rows(number), self.inside(number)
        columns = self.columns(number, self.x)

        def one(a, carry):
            spot = self.kept_at(number, a, self.y, columns)
            spot[...] = spot[...] + arrived[a, rows, inside]
            return carry

        lax.fori_loop(0, self.nz, one, 0)

    def add_z(self, number):
        name = self.items[number].name
        arrived = self.from_z[name]
        rows, inside = self.rows(number), self.inside(number)
        total = self.kept_at(number, self.z, self.y, self.columns(number, self.x))[...].astype(F32)
        for step in range(self.nz - 1):
            total += arrived[step, rows, inside].astype(F32)
        item = self.items[number]
        down, along = item.summed
        start = item.first[0] + self.x * (item.first[1] - item.first[0]) + along
        self.sums[name][
            self.rows(number, down), pl.ds(pl.multiple_of(start, 128), total.shape[1])
        ] = total
        if self.owned and number == max(i for i, item in enumerate(self.items) if item.name == name):
            self.share(name)

    def last(self, name):
        number = WEIGHTS.index(name)
        staged, owned = self.sums[name + "_sent"], self.owned[name]
        rows = staged.shape[0]
        return pltpu.make_async_remote_copy(
            src_ref=staged,
            dst_ref=owned.at[pl.ds(pl.multiple_of(self.core * rows, 16), rows), :],
            send_sem=self.last_sem.at[0, number],
            recv_sem=self.last_sem.at[1, number],
            device_id=self.sibling,
            device_id_type=MESH,
        )

    def share(self, name):
        total = self.sums[name][...]
        rows, width = total.shape
        left, right = total[:, : width // 2], total[:, width // 2 :]
        if name == FC1:
            step = width // 8 // PARTS
            left, right = (
                jnp.concatenate(
                    [
                        total[:, start : start + step]
                        for k in range(4)
                        for part in range(PARTS)
                        for start in [((part * 2 + side) * 4 + k) * step]
                    ],
                    1,
                )
                for side in range(2)
            )
        start = pl.multiple_of(self.core * rows, 16)
        self.owned[name][pl.ds(start, rows), :] = jnp.where(self.core == 0, left, right)
        self.sums[name + "_sent"][...] = jnp.where(self.core == 0, right, left)
        self.last(name).start()

    def launch(self, number):
        for copy in self.to_core(number):
            copy.start()

    def step(self, depth, number):
        stages = [self.to_core, self.to_first, self.to_second, self.to_z]
        adds = [self.add_core, self.add_first, self.add_second, self.add_z]
        for copy in stages[depth](number):
            copy.wait_recv()
        adds[depth](number)
        if depth < 3:
            for copy in stages[depth + 1](number):
                copy.start()

    def up_to(self, depth, number):
        while self.counts[depth] <= min(number, len(self.items) - 1):
            self.step(depth, self.counts[depth])
            self.counts[depth] += 1

    def targets(self, numbers):
        for depth, number in enumerate(numbers):
            self.up_to(depth, number)

    def advance(self, steps):
        while self.done < steps:
            lag = 2
            for depth in range(4):
                self.up_to(depth, self.done - depth * lag)
            self.done += 1

    def numbers(self, name):
        return [i for i, item in enumerate(self.items) if item.name == name]

    def sent(self):
        for number in range(len(self.items)):
            for stage in (self.to_core, self.to_first, self.to_second, self.to_z):
                for copy in stage(number):
                    copy.wait_send()

    def finish(self):
        count = len(self.items)
        self.up_to(0, count)
        for number in range(count + 2):
            for depth in range(1, 4):
                self.up_to(depth, number - depth + 1)
        for name in dict.fromkeys(item.name for item in self.items):
            self.last(name).wait()
        self.sent()


def reduce_scratch(shapes, nz):
    scratch = [pltpu.VMEM((nz, 2, s[3], s[4]), BF16) for s in shapes]
    scratch += [pltpu.VMEM((nz, 2, s[3], s[4] // 2), BF16) for s in shapes]
    scratch += [pltpu.VMEM((nz, s[3], s[4] // 2), BF16) for s in shapes]
    scratch += [pltpu.VMEM((nz - 1, s[3], s[4] // 2), BF16) for s in shapes]
    return scratch


def backward_kernel(comm, *refs):
    (frame_len, text_len, mod_in, rows_3_in, lat_in, text_in), refs = refs[:6], refs[6:]
    names = (
        "dcross",
        "qkv_act",
        "h1",
        "mixed1",
        "h2",
        "q2",
        "mixed2",
        "memory",
        "after",
        "stats",
    )
    given, refs = dict(zip(names, refs[:10])), refs[10:]
    matrices, refs = dict(zip(BACK, refs[:5])), refs[5:]
    if comm:
        (grad_fc1, grad_fc2, sums_fc1, sums_fc2), refs = refs[:4], refs[4:]
    (latent_out, text_sent), refs = refs[:2], refs[2:]
    if comm:
        everybody_sent, refs = refs[0], refs[1:]
        owned_sent, refs = dict(zip(WEIGHTS, refs[:7])), refs[7:]
    else:
        rows_out, refs = refs[0], refs[1:]
        grads_out, refs = dict(zip(BACK, refs[:5])), refs[5:]
    (dcross, packed, hidden, mixed, q2, memory, after), refs = refs[:7], refs[7:]
    text, stats, means, frame_marks, text_marks, query_sum, lanes = refs[:7]
    mod, rows_3, text_out = refs[7:10]
    refs = refs[10:]
    held, refs = dict(zip(BACK, refs[:5])), refs[5:]
    grad_qkv, above, sems = refs[:3]
    refs = refs[3:]
    slots, model = dcross.shape
    lat = above.at[0]
    head = model // HEADS
    size = row_tile(slots)
    loads = Loads(sems)
    act = {
        "dcross": dcross,
        "mixed2": mixed,
        "q2": q2,
        "memory": memory,
        "h2": hidden,
        "stats": stats,
        "after": after,
    }
    grads = dict(held, qkv=grad_qkv)
    if comm:
        dp_size, fsdp_size = comm
        (rows_out, dmod, pieces, ada_sems, fc2_rows), refs = refs[:5], refs[5:]
        owned, refs = dict(zip(WEIGHTS, refs[:6])), refs[6:]
        turned, everybody, refs = refs[0], refs[1], refs[2:]
        owned[FC2] = fc2_rows
        kept, refs = {FC2: refs[0], FC1: refs[1]}, refs[2:]
        landing, refs = dict(zip(WEIGHTS, refs[:7])), refs[7:]
        first, refs = dict(zip(WEIGHTS, refs[:7])), refs[7:]
        second, refs = dict(zip(WEIGHTS, refs[:7])), refs[7:]
        along, refs = dict(zip(WEIGHTS, refs[:7])), refs[7:]
        sums, refs = dict(zip(WEIGHTS, refs[:7])), refs[7:]
        sums.update(zip([name + "_sent" for name in WEIGHTS], refs[:7]))
        refs = refs[7:]
        reduce_sems = refs[:3]
        sources = dict(grads, fc1=grad_fc1, fc2=grad_fc2)
        items = reduce_items({name: ref.shape for name, ref in sources.items()})
        reduce = Reduce(
            place(), sources, kept, landing, first, second, along, sums, owned, items, reduce_sems
        )
        core = reduce.core
    loads.start("mod", mod_in, mod)
    loads.start("rows", rows_3_in, rows_3)
    loads.start("wcout", matrices[COUT], held[COUT])
    for name in ("dcross", "mixed2", "q2", "memory", "stats"):
        loads.start(name, given[name], act[name])
    if comm:
        barrier = pltpu.get_barrier_semaphore()

        def greet_one(step, target, me):
            pl.semaphore_signal(
                barrier,
                inc=1,
                device_id={"dp": target // fsdp_size, "fsdp": target % fsdp_size},
                device_id_type=MESH,
            )

        everyone(dp_size, fsdp_size, greet_one)
        pl.semaphore_wait(barrier, dp_size * fsdp_size - 1)
        for name in (FC2, FC1):
            for number in reduce.numbers(name):
                reduce.launch(number)
        for name, source in ((FC2, grad_fc2), (FC1, grad_fc1)):
            loads.start("keep_" + name, source.at[:, :, core], kept[name])
        for name, source in ((FC2, sums_fc2), (FC1, sums_fc1)):
            loads.start("s" + name, source, sums[name])
    for name in (CQ, CKV, OUT, QKV):
        loads.start("w" + name, matrices[name], held[name])
    for name in ("h2", "after"):
        loads.start(name, given[name], act[name])
    loads.start("text", text_in, text)
    loads.start("qkv_act", given["qkv_act"], packed.at[0:slots, :])

    def advance(steps):
        if comm:
            reduce.advance(steps)

    def hook(p, plan):
        if comm:
            for at, steps in plan:

                @pl.when(p == at)
                def _():
                    if isinstance(steps, tuple):
                        reduce.targets(steps)
                    else:
                        reduce.advance(steps)

    def row(k):
        return mod[:, k * model : (k + 1) * model]

    def place_grad(name, columns, left, right):
        target = grads[name]
        product = dot_tn(left, right).astype(BF16)
        target[:, :, :, :, columns] = product.reshape(target.shape[:4] + (-1,))

    def ready(name):
        if not comm:
            loads.start("g" + name, grads[name], grads_out[name])
            return
        for number in reduce.numbers(name):
            reduce.launch(number)

    rows_out[...] = jnp.zeros_like(rows_out)
    mark_keys(frame_marks, frame_len[0])
    mark_keys(text_marks, text_len[0])
    loads.wait("dcross", "wcout", "mod", "rows")

    def enter_2(rows):
        small = (row(5) * dcross[rows, :]).astype(BF16)
        above[0, rows, :] = small
        upstream = dot_nt(small, flat(held[COUT][...])).astype(BF16)
        above[1, rows, :] = upstream
        means[rows, :] = thirds(head_sums(upstream, mixed[rows, :], lanes[...]), 0.0)

    loads.wait("mixed2")
    lanes[...] = head_lanes(model, HEADS)
    tiles(slots, size, enter_2)
    place_grad(COUT, slice(0, model), mixed[...], above[0])
    ready(COUT)
    loads.wait("q2", "memory", "stats")
    if comm:
        loads.wait("keep_fc2", "keep_fc1", "sfc2", "sfc1")
    advance(1)
    pair = attend_back(
        (q2, 0),
        (memory, 0),
        (memory, model),
        text_marks,
        above.at[1],
        means,
        (stats, HEADS),
        query_sum,
        head,
        memory.shape[0],
    )

    def pair_2(p, carry):
        hook(p, ((1, 2), (3, 3), (5, 4)))
        return pair(p, carry)

    lax.fori_loop(0, HEADS // 2, pair_2, 0)
    loads.start("mixed1", given["mixed1"], mixed)
    loads.wait("wcq", "wckv", "after", "h2", "text")
    text_out[...] = dot_nt(memory[...], flat(held[CKV][...]))
    loads.start("text_out", text_out, text_sent)
    tiles(
        2 * model,
        model,
        lambda columns: place_grad(CKV, columns, text[...], memory[:, columns]),
    )
    ready(CKV)
    loads.wait("wout")
    advance(5)

    def leave_2(rows):
        upstream = dot_nt(q2[rows, :], flat(held[CQ][...]))
        normed, inverse = normalize(after[rows, :])
        back, dshift, dscale = norm_back(upstream, normed, inverse, row(4))
        dself = dcross[rows, :] + back
        dcross[rows, :] = dself
        rows_out[0:1, :] += dshift[None]
        rows_out[1:2, :] += dscale[None]
        branch = dot(mixed[rows, :], flat(held[OUT][...]))
        rows_out[2:3, :] += jnp.sum(dself * branch, 0, keepdims=True)
        small = (row(2) * dself).astype(BF16)
        above[0, rows, :] = small
        upstream = dot_nt(small, flat(held[OUT][...])).astype(BF16)
        above[1, rows, :] = upstream
        means[rows, :] = thirds(head_sums(upstream, mixed[rows, :], lanes[...]), 0.0)

    loads.wait("mixed1")
    lanes[...] = head_lanes(model, 0)
    tiles(slots, size, leave_2)
    advance(6)
    place_grad(CQ, slice(0, model), hidden[...], q2[...])
    ready(CQ)
    loads.start("h1", given["h1"], hidden)
    place_grad(OUT, slice(0, model), mixed[...], above[0])
    ready(OUT)
    loads.start("lat", lat_in, lat)
    advance(7)
    loads.wait("qkv_act")
    packed[slots:, :] = jnp.zeros((packed.shape[0] - slots, 3 * model), BF16)
    place_in_loop = []
    pairs = HEADS // 2

    def tile_hook(t):
        plan = []
        for j in range(pairs):
            late = j // 4
            plan += [
                (2 * j, (6 + j, 4 + j + late, 2 + j + late, j)),
                (2 * j + 1, (7 + j, 5 + j + late, 3 + j + late, 1 + j)),
            ]
        hook(2 * place_in_loop[-1] + t, plan)

    pair = attend_back(
        (packed, 0),
        (packed, model),
        (packed, 2 * model),
        frame_marks,
        above.at[1],
        means,
        (stats, 0),
        query_sum,
        head,
        packed.shape[0] // 2,
        tile_hook,
    )

    third, half = model // 3, 3 * model // 2

    def grad_columns(*starts, width):
        spans = [slice(start, start + width) for start in starts]
        product = dot_tn(
            hidden[...], jnp.concatenate([packed[0:slots, span] for span in spans], 1)
        ).astype(BF16)
        for k, span in enumerate(spans):
            grad_qkv[:, :, :, :, span] = product[:, k * width : (k + 1) * width].reshape(
                grad_qkv.shape[:4] + (width,)
            )

    def launch(part):
        if comm:
            reduce.launch(reduce.numbers(QKV)[part])

    def pair_1(i, carry):
        place_in_loop.append(i)
        group = i // (pairs // 3)
        pair(group * (7 - 3 * group) * pairs // 6 + i % (pairs // 3), carry)

        @pl.when(i == pairs // 3 - 1)
        def _():
            loads.wait("h1")
            grad_columns(0, 2 * model, width=third)
            launch(0)

        @pl.when(i == 2 * pairs // 3 - 1)
        def _():
            grad_columns(2 * third, 2 * model + 2 * third, width=third)
            launch(1)
            grad_columns(model, model + 2 * third, width=third)
            launch(2)

        return carry

    lax.fori_loop(0, pairs, pair_1, 0)
    grad_columns(third, 2 * model + third, width=third)
    launch(3)
    grad_columns(model + third, half, width=third // 2)
    launch(4)
    loads.wait("wqkv", "lat")
    if not comm:
        ready(QKV)

    def leave_1(rows):
        upstream = dot_nt(packed[rows, :], flat(held[QKV][...]))
        normed, inverse = normalize(lat[rows, :].astype(F32))
        back, dshift, dscale = norm_back(upstream, normed, inverse, row(1))
        dcross[rows, :] = dcross[rows, :] + back
        rows_out[3:4, :] += dshift[None]
        rows_out[4:5, :] += dscale[None]


    def leave_step(t, carry):
        hook(t, ((0, (13, 12, 10, 8)), (1, (15, 12, 11, 9)), (2, (15, 13, 12, 10))))
        leave_1(pl.ds(pl.multiple_of(t * last, 16), last))
        return carry

    last = slots // 3
    lax.fori_loop(0, 3, leave_step, 0)
    hook(0, ((0, (15, 14, 13, 11)),))
    loads.start("latent", dcross, latent_out)
    if not comm:
        loads.wait("gcout", "gckv", "gcq", "gout", "gqkv", "latent", "text_out")
        return
    ordered = (
        rows_out[3:4, :],
        rows_out[4:5, :],
        rows_out[2:3, :],
        rows_out[0:1, :],
        rows_out[1:2, :],
        rows_3[3:4, :],
        rows_3[1:2, :],
        rows_3[2:3, :],
        rows_3[0:1, :],
    )
    for k, value in enumerate(ordered):
        dmod[:, k * model : (k + 1) * model] = value.astype(BF16).astype(F32)
    span = pieces.shape[-1]
    for j in range(fsdp_size):
        start = j * dmod.shape[1] // fsdp_size // 128 * 128
        pieces[j] = dmod[:, start : start + span]
    me = lax.axis_index("dp") * fsdp_size + lax.axis_index("fsdp")
    send = modulate_start(dp_size, fsdp_size, pieces, everybody, ada_sems)
    everyone(dp_size, fsdp_size, lambda s, t, m: send(s, t, m, t % fsdp_size).start())
    everybody[me] = pieces[lax.axis_index("fsdp")]
    reduce.finish()
    everyone(dp_size, fsdp_size, lambda s, t, m: send(s, t, m, t % fsdp_size).wait())
    loads.start("all", everybody, everybody_sent)
    for name in WEIGHTS[:6]:
        loads.start("o" + name, owned[name], owned_sent[name])
    turned[...] = fc2_rows[...].T
    loads.start("ofc2", turned, owned_sent[FC2])
    loads.wait("all", "text_out", *["o" + name for name in WEIGHTS])
    loads.wait("latent")


def backward(grid, comm, lengths, latent, text_block, modulation, rest, kept, matrices, ff):
    slots, model = latent.shape
    text_slots = text_block.shape[0]
    padded = -(-slots // 128) * 128
    rows_3 = rest
    devices = grid.dp * grid.fsdp
    shaped = jax.ShapeDtypeStruct
    vmem = pl.BlockSpec(memory_space=pltpu.VMEM)
    anywhere = pl.BlockSpec(memory_space=pl.ANY)
    smem = pl.BlockSpec(memory_space=pltpu.SMEM)
    outs = [shaped((slots, model), F32), shaped((text_slots, model), F32)]
    narrow = pltpu.VMEM((slots, model), BF16)
    full = pltpu.VMEM((slots, model), F32)
    scratch = [
        full,
        pltpu.VMEM((padded, 3 * model), BF16),
        narrow,
        narrow,
        narrow,
        pltpu.VMEM((text_slots, 2 * model), BF16),
        full,
        pltpu.VMEM((text_slots, model), BF16),
        pltpu.VMEM((slots, 128), BF16),
        pltpu.VMEM((slots, 128), BF16),
        pltpu.VMEM((padded, 128), BF16),
        pltpu.VMEM((text_slots, 128), BF16),
        pltpu.VMEM((slots, 128), F32),
        pltpu.VMEM((model, 128), BF16),
        pltpu.VMEM((1, 9 * model), F32),
        pltpu.VMEM((8, model), F32),
        pltpu.VMEM((text_slots, model), F32),
    ]
    scratch += [pltpu.VMEM(m.shape, BF16) for m in matrices]
    scratch += [
        pltpu.VMEM(matrices[0].shape, BF16),
        pltpu.VMEM((2, slots, model), BF16),
        pltpu.SemaphoreType.DMA((48,)),
    ]
    params = {"vmem_limit_bytes": 63 * 1024 * 1024}
    if comm:
        params.update(collective_id=1, has_side_effects=True)
        shapes = dict(zip(WEIGHTS, [m.shape for m in (*matrices, *ff[:2])]))
        wholes = dict(shapes)
        wholes[FC1] = (*shapes[FC1][:4], 2 * ff[2].shape[1])
        wholes[FC2] = (*shapes[FC2][:3], *ff[3].shape[:1], 2 * ff[3].shape[1])
        nz = shapes[OUT][0]
        span = -(-9 * model // grid.fsdp // 128) * 128
        outs += [shaped((devices, 1, span), F32)]
        outs += [shaped((2 * s[3], s[4] // 4), F32) for s in (*wholes.values(),)[:6]]
        outs += [shaped((wholes[FC2][4] // 4, 2 * wholes[FC2][3]), F32)]
        out_specs = [anywhere] * 10
        scratch += [
            pltpu.VMEM((8, model), F32),
            pltpu.VMEM((1, 9 * model), F32),
            pltpu.VMEM((grid.fsdp, 1, span), F32),
            pltpu.SemaphoreType.DMA((2, devices - 1)),
            pltpu.VMEM((2 * wholes[FC2][3], wholes[FC2][4] // 4), F32),
        ]
        scratch += [pltpu.VMEM(o.shape, F32) for o in outs[3:]]
        scratch += [pltpu.VMEM(outs[2].shape, F32)]

        scratch += [pltpu.VMEM((nz, 2, *shapes[name][3:]), BF16) for name in (FC2, FC1)]
        scratch += reduce_scratch(shapes.values(), nz)
        scratch += [pltpu.VMEM((s[3], s[4] // 2), F32) for s in wholes.values()]
        scratch += [pltpu.VMEM((s[3], s[4] // 4), F32) for s in wholes.values()]
        count = len(reduce_items(shapes))
        scratch += [
            pltpu.SemaphoreType.DMA((count, nz + 4)),
            pltpu.SemaphoreType.DMA((count, nz + 4)),
            pltpu.SemaphoreType.DMA((2, 7)),
        ]
    else:
        ff = ()
        outs += [shaped((8, model), F32)]
        outs += [shaped(m.shape, BF16) for m in matrices]
        out_specs = [anywhere, anywhere, vmem] + [anywhere] * 5
    return pl.pallas_call(
        functools.partial(backward_kernel, (grid.dp, grid.fsdp) if comm else None),
        out_shape=outs,
        in_specs=[smem] * 2 + [anywhere] * (19 + len(ff)),
        out_specs=out_specs,
        scratch_shapes=scratch,
        compiler_params=pltpu.CompilerParams(**params),
        name="backward",
    )(
        *lengths,
        modulation,
        rows_3,
        latent,
        text_block,
        *kept,
        *matrices,
        *ff,
    )


def deliver_kernel(count, conditions, gathered, *refs):
    given, ada_out, taken = refs[:count], refs[count], refs[count + 1 : 2 * count + 1]
    staged, sems = refs[2 * count + 1 : -1], refs[-1]
    inward = [
        pltpu.make_async_copy(src, mid, sems.at[0, k])
        for k, (src, mid) in enumerate(zip(given, staged))
    ]
    outward = [
        pltpu.make_async_copy(mid, dst, sems.at[1, k])
        for k, (mid, dst) in enumerate(zip(staged, taken))
    ]
    for copy in inward:
        copy.start()
    for before, after in zip(inward, outward):
        before.wait()
        after.start()
    rows, columns = ada_out.shape
    stacked = jnp.concatenate([gathered[k] for k in range(gathered.shape[0])], 0)
    product = dot_tn(conditions[...].astype(BF16), stacked.astype(BF16))[:rows]
    spare = product.shape[1] - columns
    ada_out[...] = jnp.where(
        lax.axis_index("fsdp") % 2 == 0, product[:, :columns], product[:, spare:]
    )
    for copy in outward:
        copy.wait()


def deliver(conditions, gathered, shape, results):
    vmem = pl.BlockSpec(memory_space=pltpu.VMEM)
    anywhere = pl.BlockSpec(memory_space=pl.ANY)
    count = len(results)
    return pl.pallas_call(
        functools.partial(deliver_kernel, count),
        out_shape=[jax.ShapeDtypeStruct(shape, F32)]
        + [jax.ShapeDtypeStruct(r.shape, r.dtype) for r in results],
        in_specs=[vmem] * 2 + [anywhere] * count,
        out_specs=[vmem] + [anywhere] * count,
        scratch_shapes=[pltpu.VMEM(r.shape, r.dtype) for r in results]
        + [pltpu.SemaphoreType.DMA((2, count))],
        compiler_params=pltpu.CompilerParams(vmem_limit_bytes=63 * 1024 * 1024),
        name="deliver",
    )(conditions, gathered, *results)


def by_part(matrix):
    split = matrix.reshape(*matrix.shape[:-1], 2, 2, 4, PARTS, matrix.shape[-1] // 16 // PARTS)
    return jnp.moveaxis(split, -2, -4).reshape(matrix.shape)


def from_part(matrix):
    split = matrix.reshape(*matrix.shape[:-1], 2, PARTS, 2, 4, matrix.shape[-1] // 16 // PARTS)
    return jnp.moveaxis(split, -4, -2).reshape(matrix.shape)


def body(
    latents,
    text_rows,
    out_grad,
    frame_len,
    text_len,
    timestep,
    w_ada,
    w_qkv,
    w_out,
    w_cq,
    w_ckv,
    w_cout,
    w_fc1,
    w_fc2,
    *,
    dp_size,
    fsdp_size,
):
    grid = Grid(dp_size, fsdp_size)
    matrices = (w_qkv, w_out, w_cq, w_ckv, w_cout, w_fc1, w_fc2)
    lengths = (frame_len, text_len)
    if grid.fits(matrices):
        ada = ada_inputs(grid, timestep, w_ada)
        matrices = (*matrices[:6], w_fc2.T)
    else:
        *others, full_fc1, full_fc2 = gather_weights(grid, matrices)
        matrices = (*others, by_part(full_fc1), full_fc2)
        conditions, modulation = modulate(grid, timestep, w_ada)
        ada = (modulation.reshape(1, -1),)
    layer_out, kept, kept_matrices, rest = forward(
        grid, lengths, latents[0], text_rows[0], out_grad[0], ada, matrices
    )
    grad_fc1, grad_fc2, sums_1, sums_2, rows_3, modulation, rows = rest
    comm = len(ada) > 1
    results = backward(
        grid,
        comm,
        lengths,
        latents[0],
        text_rows[0],
        modulation,
        rows_3,
        kept,
        kept_matrices,
        (grad_fc1, grad_fc2, sums_1, sums_2),
    )
    latent_grad, text_grad, rows_1 = results[:3]
    if comm:
        results = (layer_out, latent_grad, text_grad, *results[3:])
        grad_ada, layer_out, latent_grad, text_grad, *owned, fc2 = deliver(
            rows, rows_1, w_ada.shape, results
        )
        owned = (*owned, fc2.T)
    else:
        order = (
            rows_1[3:4],
            rows_1[4:5],
            rows_1[2:3],
            rows_1[0:1],
            rows_1[1:2],
            rows_3[3:4],
            rows_3[1:2],
            rows_3[2:3],
            rows_3[0:1],
        )
        dmodulation = jnp.concatenate(order, 0).reshape(1, -1).astype(BF16)
        grad_ada = ada_gradient(grid, conditions, dmodulation)
        owned = reduce_gradients(grid, (*results[3:8], from_part(grad_fc1), grad_fc2))
    return (
        layer_out[None],
        latent_grad[None],
        text_grad[None],
        grad_ada,
        *owned,
    )


def solution(mesh):
    placed = (P(("dp", "fsdp"), None, None),) * 3 + (P(("dp", "fsdp")),) * 3 + (P("dp", "fsdp"),) * 8
    return jax.shard_map(
        functools.partial(body, dp_size=mesh.shape["dp"], fsdp_size=mesh.shape["fsdp"]),
        mesh=mesh,
        in_specs=placed,
        out_specs=(P(("dp", "fsdp"), None, None),) * 3 + (P("dp", "fsdp"),) * 8,
        check_vma=False,
    )
```

```python
import functools
import math

import jax
import jax.numpy as jnp
from jax import lax
from jax.experimental import pallas as pl
from jax.experimental.pallas import tpu as pltpu
from jax.sharding import PartitionSpec as P

HEADS = 12


norm_eps = 1e-06


def sinusoid(time_value, model_width):
    half_width = model_width // 2
    frequency = jnp.exp(-math.log(10000.0) * jnp.arange(half_width, dtype=jnp.float32) / half_width)
    angles = time_value.astype(jnp.float32) * frequency
    return jnp.concatenate([jnp.cos(angles), jnp.sin(angles)], axis=-1)


def normalize(values):
    center = values - jnp.mean(values, -1, keepdims=True)
    spread = jnp.mean(center * center, -1, keepdims=True)
    inverse = lax.rsqrt(spread + norm_eps)
    return (center * inverse, inverse)


def norm_back(upstream, normed, inverse, scale_row):
    dshift = jnp.sum(upstream, 0)
    dscale = jnp.sum(upstream * normed, 0)
    scaled = upstream * (1.0 + scale_row)
    centered = (
        scaled
        - jnp.mean(scaled, -1, keepdims=True)
        - normed * jnp.mean(scaled * normed, -1, keepdims=True)
    )
    return (inverse * centered, dshift, dscale)


def outer_sum(left, right):
    return lax.dot_general(
        left, right, (((0,), (0,)), ((), ())), preferred_element_type=jnp.float32
    )


MESH = pl.DeviceIdType.MESH


class Grid:
    def __init__(self, dp_size, fsdp_size):
        self.dp = dp_size
        self.fsdp = fsdp_size

    def fits(self, matrices):
        if self.fsdp != 4 or self.dp != 8:
            return False
        for matrix in matrices:
            rows, columns = matrix.shape
            if rows % 32 or (2 * columns) % 128:
                return False
        return True


def place():
    dp_index = lax.axis_index("dp")
    fsdp_index = lax.axis_index("fsdp")
    return dp_index // 2, dp_index % 2, fsdp_index // 2, fsdp_index % 2


def device(z, y, x, core):
    return {"dp": z * 2 + y, "fsdp": x * 2 + core}


def gather_weights(grid, matrices):
    return tuple(
        lax.all_gather(
            lax.all_gather(m, "fsdp", axis=1, tiled=True), "dp", axis=0, tiled=True
        ).reshape(4, 2, 2, m.shape[0] * grid.dp // 16, m.shape[1] * grid.fsdp)
        for m in matrices
    )


def reduce_gradients(grid, gradients):
    out = []
    for gradient in gradients:
        part = gradient.reshape(-1, gradient.shape[-1])
        part = lax.psum_scatter(part, "dp", scatter_dimension=0, tiled=True)
        part = lax.psum_scatter(part, "fsdp", scatter_dimension=1, tiled=True)
        out.append(part.astype(jnp.float32))
    return tuple(out)


def modulate(grid, timestep, w_ada):
    rows, columns = w_ada.shape
    model_width = rows * grid.dp
    times = lax.all_gather(timestep, ("dp", "fsdp"), axis=0, tiled=True)
    conditions = jax.nn.silu(
        jax.vmap(lambda value: sinusoid(value, model_width))(times)
    ).astype(jnp.bfloat16)
    mine = lax.dynamic_slice_in_dim(conditions, lax.axis_index("dp") * rows, rows, 1)
    partial = jnp.dot(mine, w_ada, preferred_element_type=jnp.float32)
    summed = lax.psum_scatter(partial, "dp", scatter_dimension=0, tiled=True)
    mixed = lax.all_to_all(summed, "fsdp", split_axis=0, concat_axis=0, tiled=True)
    return mine, mixed.reshape(9, model_width)


def ada_gradient(grid, conditions, dmodulation):
    spread = dmodulation.reshape(grid.fsdp, -1)
    swapped = lax.all_to_all(spread, "fsdp", split_axis=0, concat_axis=0, tiled=True)
    everyone = lax.all_gather(swapped, "dp", axis=0, tiled=True)
    return outer_sum(conditions, everyone)


def ada_inputs(grid, timestep, w_ada):
    rows, columns = w_ada.shape
    condition = jax.nn.silu(sinusoid(timestep[0], rows * grid.dp)).astype(jnp.bfloat16)
    mine = jnp.pad(
        condition.astype(jnp.float32).reshape(grid.dp, 1, rows), ((0, 0), (0, 0), (0, 128 - rows))
    )
    return mine, w_ada


F32 = jnp.float32
BF16 = jnp.bfloat16
NT = (((1,), (1,)), ((), ()))
TN = (((0,), (0,)), ((), ()))


def flat(value):
    return value.reshape(-1, value.shape[-1])


def dot(left, right):
    return jnp.dot(left, right, preferred_element_type=F32)


def dot_nt(left, right):
    return lax.dot_general(left, right, NT, preferred_element_type=F32)


def dot_tn(left, right):
    return lax.dot_general(left, right, TN, preferred_element_type=F32)


def tiles(total, size, body):
    def step(t, carry):
        body(pl.ds(pl.multiple_of(t * size, size), size))
        return carry

    lax.fori_loop(0, total // size, step, 0)


def row_tile(rows):
    for size in (432, 288, 256, 128):
        if rows % size == 0:
            return size
    return rows


def gelu_pair(inner):
    slope = math.sqrt(2.0 / math.pi)
    square = inner * inner
    turned = jnp.tanh(inner * (slope + (slope * 0.044715) * square))
    half = 0.5 + 0.5 * turned
    rise = inner * (slope + (3.0 * slope * 0.044715) * square)
    return inner * half, half + (0.5 - 0.5 * turned * turned) * rise


def half_lanes(shape):
    return lax.broadcasted_iota(jnp.int32, shape, 1) < shape[1] // 2


def lanes_of(shape):
    return lax.broadcasted_iota(jnp.int32, shape, 1)


def mark_keys(marks, length):
    shape = marks.shape
    excluded = jnp.where(lax.broadcasted_iota(jnp.int32, shape, 0) < length, 0.0, -1e30)
    marks[...] = jnp.where(lanes_of(shape) == shape[1] - 1, excluded, 0.0).astype(BF16)


def thirds(value, last):
    high = value.astype(BF16).astype(F32)
    middle = (value - high).astype(BF16).astype(F32)
    low = value - high - middle
    lane = lanes_of(value.shape)
    spread = high + pltpu.roll(middle, 32, 1) + pltpu.roll(low, 64, 1)
    return jnp.where(lane == value.shape[1] - 1, last, spread).astype(BF16)


def head_lanes(model, stat_at):
    shape = (model, 128)
    head = lax.broadcasted_iota(jnp.int32, shape, 0) // (model // HEADS)
    return jnp.where(lanes_of(shape) == head + stat_at, 1.0, 0.0).astype(BF16)


def head_sums(left, right, matrix):
    product = left.astype(F32) * right.astype(F32)
    high = product.astype(BF16)
    return dot(high, matrix) + dot((product - high.astype(F32)).astype(BF16), matrix)


def attend(queries, keys, values, marks, mixed, stats, heads_wide, size):
    query_ref, query_at = queries
    key_ref, key_at = keys
    value_ref, value_at = values
    mixed_ref, mixed_at = mixed
    stat_ref, stat_at = stats
    rows = mixed_ref.shape[0]
    width = 2 * heads_wide

    def pair(p, carry):
        def at(start):
            return pl.ds(pl.multiple_of(start + p * width, width), width)

        value_pair = value_ref[:, at(value_at)]
        marked = jnp.concatenate([key_ref[:, at(key_at)], marks[...]], 1)
        low = half_lanes((size, width))
        lane = lanes_of((size, width))
        last = (lane == width - 1).astype(F32).astype(BF16)
        for start in range(0, rows, size):
            span = slice(start, start + size)
            scaled = query_ref[span, at(query_at)] * BF16(heads_wide**-0.5)
            outs = []
            stat = stat_ref[span, :]
            for head in range(2):
                own = jnp.where(low if head == 0 else ~low, scaled, BF16(0))
                scores = dot_nt(jnp.concatenate([own, last], 1), marked)
                largest = jnp.max(scores, -1, keepdims=True)
                raised = jnp.exp(scores - largest)
                summed = jnp.sum(raised, -1, keepdims=True)
                outs.append(dot(raised.astype(BF16), value_pair) * (1.0 / summed))
                stat = jnp.where(lane == stat_at + 2 * p + head, largest + jnp.log(summed), stat)
            stat_ref[span, :] = stat
            mixed_ref[span, at(mixed_at)] = jnp.where(low, outs[0], outs[1]).astype(BF16)
        return carry

    return pair


def attend_back(
    queries, keys, values, marks, upstream, means, stats, total, heads_wide, size, before=None
):
    query_ref, query_at = queries
    key_ref, key_at = keys
    value_ref, value_at = values
    stat_ref, stat_at = stats
    rows = upstream.shape[0]
    slots = key_ref.shape[0]
    width = 2 * heads_wide

    def pair(p, carry):
        def at(start):
            return pl.ds(pl.multiple_of(start + p * width, width), width)

        low = half_lanes((rows, width))
        scaled = query_ref[0:rows, at(query_at)] * BF16(heads_wide**-0.5)
        above = upstream[:, at(0)]
        heads = []
        for head in range(2):
            mask = low if head == 0 else ~low
            own = jnp.where(mask, scaled, BF16(0))
            own_above = jnp.where(mask, above, BF16(0))
            heads.append(
                (
                    jnp.concatenate([own, stat_ref[...]], 1),
                    jnp.concatenate([own_above, means[...]], 1),
                    own,
                    own_above,
                )
            )
        low_keys = half_lanes((size, width))
        lane = lanes_of((size, width))

        def one_tile(span):
            key_pair = key_ref[span, at(key_at)]
            value_pair = value_ref[span, at(value_at)]
            query_grad = None
            key_grad = None
            value_grad = None
            for head in range(2):
                mask = low_keys if head == 0 else ~low_keys
                taken = lane - (stat_at + 2 * p + head)
                mark = jnp.where(
                    (taken == 0) | (taken == 32) | (taken == 64),
                    BF16(-1),
                    marks[span, :],
                )
                marked_query, marked_above, own, own_above = heads[head]
                shares = jnp.exp(dot_nt(jnp.concatenate([key_pair, mark], 1), marked_query))
                share_grad = dot_nt(jnp.concatenate([value_pair, mark], 1), marked_above)
                score_grad = (shares * share_grad).astype(BF16)
                values_part = dot(shares.astype(BF16), own_above)
                keys_part = dot(score_grad, own)
                queries_part = dot_tn(score_grad, jnp.where(mask, key_pair, BF16(0)))
                value_grad = values_part if head == 0 else value_grad + values_part
                key_grad = keys_part if head == 0 else key_grad + keys_part
                query_grad = queries_part if query_grad is None else query_grad + queries_part
            key_ref[span, at(key_at)] = key_grad.astype(BF16)
            value_ref[span, at(value_at)] = value_grad.astype(BF16)
            total[...] += query_grad

        total[...] = jnp.zeros_like(total)

        def step(t, carry):
            if before is not None:
                before(t)
            one_tile(pl.ds(pl.multiple_of(t * size, size), size))
            return carry

        lax.fori_loop(0, slots // size, step, 0)
        query_ref[0:rows, at(query_at)] = (total[...] * heads_wide**-0.5).astype(BF16)
        return carry

    return pair


class Loads:
    def __init__(self, sems):
        self.sems = sems
        self.copies = {}

    def start(self, name, src, dst):
        copy = pltpu.make_async_copy(src, dst, self.sems.at[len(self.copies)])
        copy.start()
        self.copies[name] = copy

    def wait(self, *names):
        for name in names:
            self.copies[name].wait()


WEIGHTS = ("qkv", "out", "cq", "ckv", "cout", "fc1", "fc2")
QKV, OUT, CQ, CKV, COUT, FC1, FC2 = WEIGHTS
PARTS = 4


def half_columns(ref, which, first=(0, 0), width=None):
    half = ref.shape[-1] // 2
    if width is None:
        width = half
    start = which * (half + first[1] - first[0]) + first[0]
    return pl.ds(pl.multiple_of(start, 128), width)


class Item:
    def __init__(self, name, rows=None, first=0, width=None, slot=None, summed=(0, 0)):
        self.name = name
        self.summed = summed
        self.rows = rows
        self.first = first if isinstance(first, tuple) else (first, first)
        self.width = width
        self.slot = self.first[0] if slot is None else slot


def gather_items(held):
    items = []
    rows = held[QKV].shape[3]
    items += [Item(QKV, (r, 16)) for r in range(0, rows, 16)]
    items += [Item(OUT), Item(CQ)]
    width = held[CKV].shape[-1] // 4
    items += [Item(CKV, None, k * width, width) for k in range(2)]
    items += [Item(COUT)]
    rows = held[FC2].shape[3] // PARTS
    width = held[FC1].shape[-1] // 2 // PARTS
    for part in range(PARTS):
        items += [Item(FC2, (part * rows, rows)), Item(FC1, None, part * width, width)]
    return items


class Gather:
    def __init__(self, where, given, held, own, swapped, items, sems):
        self.z, self.y, self.x, self.core = where
        self.given, self.held, self.own, self.swapped, self.items = given, held, own, swapped, items
        self.swap_sem, self.send_sem, self.recv_sem = sems
        self.nz = held[OUT].shape[0]
        z, y, x, core = where
        self.sibling = device(z, y, x, 1 - core)
        self.first = device(
            z, y * (1 - core) + (1 - y) * core, (1 - x) * (1 - core) + x * core, core
        )
        self.second = device(
            z, (1 - y) * (1 - core) + y * core, x * (1 - core) + (1 - x) * core, core
        )
        self.others = [device((z + step) % self.nz, y, x, core) for step in range(1, self.nz)]
        self.done = 0
        self.counts = [0, 0, 0, 0]
        self.record = None

    def half(self, number, which):
        staged = self.own[WEIGHTS[number]]
        rows = staged.shape[0] // 2
        return staged.at[pl.ds(pl.multiple_of(which * rows, 16), rows), :]

    def swap(self, number):
        return pltpu.make_async_remote_copy(
            src_ref=self.half(number, 1 - self.core),
            dst_ref=self.swapped[WEIGHTS[number]],
            send_sem=self.swap_sem.at[0, number],
            recv_sem=self.swap_sem.at[1, number],
            device_id=self.sibling,
            device_id_type=MESH,
        )

    def assemble(self, number):
        name = WEIGHTS[number]
        self.swap(number).wait_recv()
        mine, theirs = self.half(number, self.core)[...], self.swapped[name][...]
        whole = self.held[name]
        left = jnp.where(self.core == 0, mine, theirs)
        right = jnp.where(self.core == 0, theirs, mine)
        if name == FC1:
            four = left.shape[1] // 4
            step = four // PARTS
            pieces = [
                side[:, k * four + part * step : k * four + (part + 1) * step]
                for part in range(PARTS)
                for side in (left, right)
                for k in range(4)
            ]
        else:
            pieces = [left, right]
        whole[self.z, self.y, self.core, :, half_columns(whole, self.x)] = jnp.concatenate(
            pieces, 1
        )

    def remote(self, number, slot, part, partner):
        return pltpu.make_async_remote_copy(
            src_ref=part,
            dst_ref=part,
            send_sem=self.send_sem.at[number, slot],
            recv_sem=self.recv_sem.at[number, slot],
            device_id=partner,
            device_id_type=MESH,
        )

    def view(self, number):
        item = self.items[number]
        whole = self.held[item.name]
        rows = slice(None) if item.rows is None else pl.ds(*item.rows)
        return whole, rows, lambda which: half_columns(whole, which, item.first, item.width)

    def along_z(self, number):
        whole, rows, columns = self.view(number)
        part = whole.at[self.z, self.y, self.core, rows, columns(self.x)]
        return [self.remote(number, s, part, partner) for s, partner in enumerate(self.others)]

    def to_first(self, number):
        whole, rows, columns = self.view(number)
        part = whole.at[:, self.y, self.core, rows, columns(self.x)]
        return [self.remote(number, self.nz - 1, part, self.first)]

    def to_second(self, number):
        whole, rows, columns = self.view(number)
        copies = []
        for k in range(2):
            row = self.y * (1 - self.core) + k * self.core
            column = k * (1 - self.core) + self.x * self.core
            part = whole.at[:, row, self.core, rows, columns(column)]
            copies.append(self.remote(number, self.nz + k, part, self.second))
        return copies

    def to_core(self, number):
        whole, rows, columns = self.view(number)
        if self.items[number].width is None:
            parts = [whole.at[:, :, self.core, rows, :]]
        else:
            parts = [whole.at[:, :, self.core, rows, columns(k)] for k in range(2)]
        return [
            self.remote(number, self.nz + 2 + k, part, self.sibling) for k, part in enumerate(parts)
        ]

    def up_to(self, depth, number):
        while self.counts[depth] <= min(number, len(self.items) - 1):
            self.emit((depth, self.counts[depth]))
            self.counts[depth] += 1

    def emit(self, step):
        if self.record is not None:
            self.record.append(step)
            return
        depth, number = step
        stages = [self.along_z, self.to_first, self.to_second, self.to_core]
        if depth:
            for copy in stages[depth - 1](number):
                copy.wait_recv()
        if depth < 4:
            for copy in stages[depth](number):
                copy.start()

    def planned(self, body):
        self.record = []
        body()
        steps, self.record = self.record, None
        return steps

    def advance(self, steps, lag=2, ahead=3):
        while self.done < steps:
            self.up_to(0, self.done + ahead)
            for depth in range(1, 4):
                self.up_to(depth, self.done - (depth - 1) * lag)
            self.done += 1

    def numbers(self, name):
        return [i for i, item in enumerate(self.items) if item.name == name]

    def need(self, numbers):
        for depth in range(4):
            self.up_to(depth, max(numbers))
        for number in numbers:
            self.emit((4, number))

    def sent(self, numbers):
        for number in numbers:
            for stage in (self.along_z, self.to_first, self.to_second, self.to_core):
                for copy in stage(number):
                    copy.wait_send()


def everyone(dp_size, fsdp_size, body):
    count = dp_size * fsdp_size
    me = lax.axis_index("dp") * fsdp_size + lax.axis_index("fsdp")

    def one(step, carry):
        body(step, (me + step) % count, me)
        return carry

    lax.fori_loop(1, count, one, 0)


def modulate_start(dp_size, fsdp_size, mine, everything, sems):
    def copy(step, target, me, row):
        return pltpu.make_async_remote_copy(
            src_ref=mine.at[row],
            dst_ref=everything.at[me],
            send_sem=sems.at[0, step - 1],
            recv_sem=sems.at[1, step - 1],
            device_id={"dp": target // fsdp_size, "fsdp": target % fsdp_size},
            device_id_type=MESH,
        )

    return copy


def forward_kernel(comm, *refs):
    (frame_len, text_len, lat_in, text_in, og_in), refs = refs[:5], refs[5:]
    if comm:
        (mine, w_ada), refs = refs[:2], refs[2:]
    else:
        (mod_in,), refs = refs[:1], refs[1:]
    given, refs = dict(zip(WEIGHTS, refs[:7])), refs[7:]
    (layer_out, dcross_out, qkv_out, h1_out, mixed1_out, h2_out, q2_out, mixed2_out), refs = (
        refs[:8],
        refs[8:],
    )
    (memory_out, after_out), refs = refs[:2], refs[2:]
    kept_out, refs = dict(zip(BACK, refs[:5])), refs[5:]
    (stats_out, fc1_out, fc2_out, sums_fc1, sums_fc2), refs = refs[:5], refs[5:]
    (rows_sent, mod_sent, conditions_sent), refs = refs[:3], refs[3:]
    held, refs = dict(zip(WEIGHTS, refs[:7])), refs[7:]
    big, wide, h3, db3, memory, after_self, upstream_sum, branch_2, after_cross, result = refs[:10]
    refs = refs[10:]
    lat, text, og, stats, split_stats, frame_marks, text_marks, sems = refs[:8]
    rows_out, mod, conditions = refs[8:11]
    refs = refs[11:]
    loads = Loads(sems)
    loads.start("lat", lat_in, lat)
    loads.start("text", text_in, text)
    loads.start("og", og_in, og)
    slots, model = lat.shape
    inner_width = held[FC1].shape[-1]
    head = model // HEADS
    size = row_tile(slots)
    if comm:
        dp_size, fsdp_size = comm
        (everybody, partial, modulations, ada_sems), refs = refs[:4], refs[4:]
        (ada_block, ada_wide, turned), refs = refs[:3], refs[3:]
        own, refs = dict(zip(WEIGHTS, refs[:7])), refs[7:]
        swapped, refs = dict(zip(WEIGHTS, refs[:7])), refs[7:]
        gather_sems, refs = refs[:3], refs[3:]
        landing, from_first, from_second, from_z, sums = (
            {FC1: refs[2 * k], FC2: refs[2 * k + 1]} for k in range(5)
        )
        reduce_sems = refs[10:]
        per = held[FC2].shape[3] // PARTS, held[FC1].shape[-1] // 2 // PARTS
        reduce = Reduce(
            place(),
            {FC1: held[FC1], FC2: held[FC2]},
            {},
            landing,
            from_first,
            from_second,
            from_z,
            sums,
            None,
            part_items(*per, EARLY, 0),
            (*reduce_sems, None),
        )
        items = gather_items(held)
        gather = Gather(place(), given, held, own, swapped, items, gather_sems)
        order = [WEIGHTS.index(n) for n in dict.fromkeys(item.name for item in items)]
        barrier = pltpu.get_barrier_semaphore()

        def greet_one(step, target, me):
            pl.semaphore_signal(
                barrier,
                inc=1,
                device_id={"dp": target // fsdp_size, "fsdp": target % fsdp_size},
                device_id_type=MESH,
            )

        everyone(dp_size, fsdp_size, greet_one)
        loads.start("w_ada", w_ada, ada_block)
        for number in order:
            name = WEIGHTS[number]
            loads.start("w" + name, given[name], turned if name == FC2 else own[name])
        mark_keys(frame_marks, frame_len[0])
        mark_keys(text_marks, text_len[0])
        big[slots:, :] = jnp.zeros((big.shape[0] - slots, big.shape[1]), BF16)
        stats[...] = jnp.zeros_like(stats)
        loads.wait("w_ada")
        blank = jnp.zeros((ada_block.shape[0], ada_wide.shape[1] - ada_block.shape[1]), BF16)
        ada_wide[0 : ada_block.shape[0], :] = jnp.where(
            gather.core == 0,
            jnp.concatenate([ada_block[...], blank], 1),
            jnp.concatenate([blank, ada_block[...]], 1),
        )
        ada_wide[ada_block.shape[0] :, :] = jnp.zeros(
            (ada_wide.shape[0] - ada_block.shape[0], ada_wide.shape[1]), BF16
        )
        loads.wait(*["w" + name for name in WEIGHTS])
        own[FC2][...] = turned[...].T
        pl.semaphore_wait(barrier, dp_size * fsdp_size - 1)
        for number in order:
            gather.swap(number).start()
        dp_index = lax.axis_index("dp")
        me = dp_index * fsdp_size + lax.axis_index("fsdp")
        send_1 = modulate_start(dp_size, fsdp_size, mine, everybody, ada_sems.at[0])
        send_2 = modulate_start(dp_size, fsdp_size, partial, modulations, ada_sems.at[1])
        everyone(dp_size, fsdp_size, lambda s, t, m: send_1(s, t, m, t // fsdp_size).start())
        everybody[me] = mine[dp_index]
        gather.assemble(WEIGHTS.index(QKV))
        gather.up_to(0, 2)
        everyone(dp_size, fsdp_size, lambda s, t, m: send_1(s, t, m, t // fsdp_size).wait_recv())
        for k in range(dp_size * fsdp_size):
            conditions[k : k + 1, :] = everybody[k]
        product = dot(conditions[...].astype(BF16), ada_wide[...])
        for k in range(dp_size * fsdp_size):
            partial[k] = product[k : k + 1, :]
        everyone(dp_size, fsdp_size, lambda s, t, m: send_2(s, t, m, t).start())
        modulations[me] = partial[me]
        for number in order[1:]:
            gather.assemble(number)
        gather.advance(3, 1, 1)
        everyone(dp_size, fsdp_size, lambda s, t, m: send_2(s, t, m, t).wait_recv())
        mod[...] = jnp.zeros_like(mod)
        span = partial.shape[-1]
        for j in range(fsdp_size):
            total = modulations[j]
            for i in range(1, dp_size):
                total += modulations[i * fsdp_size + j]
            start = j * mod.shape[1] // fsdp_size // 128 * 128
            mod[:, start : start + span] += total
    else:
        mod[...] = mod_in[...]
        conditions[...] = jnp.zeros_like(conditions)
        for name in WEIGHTS:
            loads.start(name, given[name], held[name])

    def need(name, part=None):
        if not comm:
            if not part:
                loads.wait(name)
            return
        numbers = gather.numbers(name)
        gather.need(numbers if part is None else [numbers[part]])

    def hook(p, plan):
        if comm:
            for at, steps in plan:

                @pl.when(p == at)
                def _():
                    gather.advance(steps)

    def step_to(steps):
        if comm:
            gather.advance(steps)

    def row(k):
        return mod[:, k * model : (k + 1) * model]

    loads.start("mod", mod, mod_sent)
    loads.start("cond", conditions, conditions_sent)
    if not comm:
        mark_keys(frame_marks, frame_len[0])
        mark_keys(text_marks, text_len[0])
        big[slots:, :] = jnp.zeros((big.shape[0] - slots, big.shape[1]), BF16)
        stats[...] = jnp.zeros_like(stats)
    loads.wait("lat", "text", "og")

    def norm_1(rows):
        normed, _ = normalize(lat[rows, :].astype(F32))
        wide[rows, 0:model] = (normed * (1.0 + row(1)) + row(0)).astype(BF16)

    tiles(slots, size, norm_1)
    if comm:
        gather.advance(5, 1)
    need(QKV)

    def project_part(columns):
        def project(rows):
            big[rows, columns] = dot(
                wide[rows, 0:model], flat(held[QKV][:, :, :, :, columns])
            ).astype(BF16)

        tiles(slots, size, project)

    tiles(3 * model, model, project_part)
    loads.start("qkv_out", big.at[0:slots, 0 : 3 * model], qkv_out)
    loads.start("h1_out", wide.at[:, 0:model], h1_out)
    if comm:
        loads.start("kept_qkv", held[QKV], kept_out[QKV])
    pair = attend(
        (big, 0),
        (big, model),
        (big, 2 * model),
        frame_marks,
        (wide, model),
        (stats, 0),
        head,
        size,
    )

    def pair_1(p, carry):
        hook(p, ((0, 6), (1, 7), (3, 8), (4, 9), (5, 10)))
        return pair(p, carry)

    lax.fori_loop(0, HEADS // 2, pair_1, 0)
    loads.start("mixed1_out", wide.at[:, model : 2 * model], mixed1_out)
    need(OUT)
    need(CQ)

    def join_1(rows):
        branch = dot(wide[rows, model : 2 * model], flat(held[OUT][...]))
        after = lat[rows, :].astype(F32) + row(2) * branch
        after_self[rows, :] = after
        normed, _ = normalize(after)
        hidden = (normed * (1.0 + row(4)) + row(3)).astype(BF16)
        wide[rows, 2 * model : 3 * model] = hidden
        wide[rows, 3 * model : 4 * model] = dot(hidden, flat(held[CQ][...])).astype(BF16)

    tiles(slots, size, join_1)
    loads.start("after_out", after_self, after_out)
    loads.start("h2_out", wide.at[:, 2 * model : 3 * model], h2_out)
    loads.start("q2_out", wide.at[:, 3 * model : 4 * model], q2_out)
    step_to(11)
    need(CKV)

    def project_text(columns):
        memory[:, columns] = dot(text[...], flat(held[CKV][:, :, :, :, columns])).astype(BF16)

    tiles(2 * model, model, project_text)
    loads.start("memory_out", memory, memory_out)
    mixed2 = big.at[0:slots, 3 * model : 4 * model]
    pair = attend(
        (wide, 3 * model),
        (memory, 0),
        (memory, model),
        text_marks,
        (mixed2, 0),
        (stats, HEADS),
        head,
        size,
    )

    def pair_2(p, carry):
        hook(p, ((0, 12), (3, 13)))
        return pair(p, carry)

    lax.fori_loop(0, HEADS // 2, pair_2, 0)
    loads.start("mixed2_out", mixed2, mixed2_out)
    split_stats[...] = thirds(stats[...], 1.0)
    loads.start("stats_out", split_stats, stats_out)
    need(COUT)

    def join_2(rows):
        branch = dot(mixed2[rows, :], flat(held[COUT][...]))
        branch_2[rows, :] = branch
        after = after_self[rows, :] + row(5) * branch
        after_cross[rows, :] = after
        normed, _ = normalize(after)
        h3[rows, :] = (normed * (1.0 + row(7)) + row(6)).astype(BF16)
        db3[rows, :] = (row(8) * og[rows, :].astype(F32)).astype(BF16)

    step_to(14)
    tiles(slots, size, join_2)
    if comm:
        for name in BACK[1:]:
            loads.start("kept_" + name, held[name], kept_out[name])
    loads.wait("h1_out", "mixed1_out")
    act, din = wide.at[:, 0:model], wide.at[:, model : 2 * model]
    rows_out[...] = jnp.zeros_like(rows_out)
    first, second = held[FC1], held[FC2]
    width = inner_width // 2 // PARTS
    count = second.shape[3] // PARTS
    lead = second.shape[:3]

    def clear(rows):
        result[rows, :] = jnp.zeros((16, model), F32)
        upstream_sum[rows, :] = jnp.zeros((16, model), F32)

    tiles(slots, 16, clear)

    def at_part(part, bodies):
        for k, body in enumerate(bodies):
            pl.when(part == k)(body)

    arrivals, middles, ends = [], [], []
    for k in range(PARTS):

        def arrive(k=k):
            need(FC2, k)
            need(FC1, k)
            step_to(15 + 2 * k)

        def middle(k=k):
            step_to(16 + 2 * k)
            if k + 1 < PARTS:
                for depth in range(4):
                    gather.up_to(depth, gather.numbers(FC1)[k + 1])

        if comm:
            plans = gather.planned(arrive), gather.planned(middle)

            def emit_arrival(steps=plans[0]):
                for step in steps:
                    gather.emit(step)

            def emit_middle(steps=plans[1], k=k):
                for step in steps:
                    gather.emit(step)
                gather.sent([gather.numbers(name)[k] for name in (FC2, FC1)])
                for step in ((), ((0, 0), (0, 1)), (), ((2, 0), (2, 1)))[k]:
                    reduce.step(*step)

            def emit_end(k=k):
                if k < EARLY:
                    reduce.launch(2 * k)
                    reduce.launch(2 * k + 1)
                for step in ((), (), ((1, 0), (1, 1)), ())[k]:
                    reduce.step(*step)

            arrivals.append(emit_arrival)
            middles.append(emit_middle)
            ends.append(emit_end)
        else:
            arrive()

    def feed_part(part, carry):
        at_part(part, arrivals)
        spans = [
            pl.ds(pl.multiple_of(k * inner_width // 2 + part * width, 128), width) for k in range(2)
        ]
        chunk = pl.ds(pl.multiple_of(part * count, 16), count)

        def feed(rows):
            matrix_1 = jnp.concatenate([flat(first[:, :, :, :, s]) for s in spans], 1)
            matrix_2 = flat(second[:, :, :, chunk, :])
            activated, slope = gelu_pair(dot(h3[rows, :], matrix_1))
            activated = activated.astype(BF16)
            dinner = (dot_nt(db3[rows, :], matrix_2) * slope).astype(BF16)
            act[rows, :] = activated
            din[rows, :] = dinner
            result[rows, :] += dot(activated, matrix_2)
            upstream_sum[rows, :] += dot_nt(dinner, matrix_1)

        tiles(slots, size, feed)
        at_part(part, middles)
        product = dot_tn(act[...], db3[...]).astype(BF16)
        second[:, :, :, chunk, :] = product.reshape(lead + (count, model))
        product = dot_tn(h3[...], din[...]).astype(BF16)
        for k, span in enumerate(spans):
            first[:, :, :, :, span] = product[:, k * width : (k + 1) * width].reshape(
                first.shape[:4] + (width,)
            )
        at_part(part, ends)
        return carry

    lax.fori_loop(0, PARTS, feed_part, 0)
    if comm:
        loads.start("fc2_out", second.at[:, :, :, EARLY * count :, :], fc2_out)
        for k in range(2):
            loads.start(
                "fc1_out" + "b" * k,
                first.at[:, :, :, :, (k * PARTS + EARLY) * width : (k + 1) * PARTS * width],
                fc1_out.at[
                    :, :, :, :, k * (PARTS - EARLY) * width : (k + 1) * (PARTS - EARLY) * width
                ],
            )
    else:
        loads.start("fc2_out", second, fc2_out)
        loads.start("fc1_out", first, fc1_out)

    def leave(rows):
        entering = after_cross[rows, :]
        branch = result[rows, :]
        grad = og[rows, :].astype(F32)
        result[rows, :] = entering + row(8) * branch
        normed, inverse = normalize(entering)
        back, dshift, dscale = norm_back(upstream_sum[rows, :], normed, inverse, row(7))
        dcross = grad + back
        after_cross[rows, :] = dcross
        rows_out[0:1, :] += jnp.sum(grad * branch, 0, keepdims=True)
        rows_out[1:2, :] += dshift[None]
        rows_out[2:3, :] += dscale[None]
        rows_out[3:4, :] += jnp.sum(dcross * branch_2[rows, :], 0, keepdims=True)

    tiles(slots, size, leave)
    loads.start("layer_out", result, layer_out)
    loads.start("rows", rows_out, rows_sent)
    loads.start("dcross_out", after_cross, dcross_out)
    if comm:
        for number in order:
            gather.swap(number).wait_send()
        for name in BACK:
            gather.sent(gather.numbers(name))
            loads.wait("kept_" + name)
        for number in range(2 * EARLY):
            reduce.step(3, number)
        loads.start("sums1", sums[FC1], sums_fc1)
        loads.start("sums2", sums[FC2], sums_fc2)
        everyone(dp_size, fsdp_size, lambda s, t, m: send_1(s, t, m, t // fsdp_size).wait_send())
        everyone(dp_size, fsdp_size, lambda s, t, m: send_2(s, t, m, t).wait_send())
        reduce.sent()
        loads.wait("sums1", "sums2", "fc1_outb")
    loads.wait("qkv_out", "h2_out", "q2_out", "mixed2_out")
    loads.wait("mod", "cond", "rows", "stats_out", "after_out", "memory_out", "layer_out", "dcross_out", "fc1_out", "fc2_out")


def forward(grid, lengths, latent, text_block, upstream, ada, matrices):
    slots, model = latent.shape
    text_slots = text_block.shape[0]
    padded = -(-slots // 128) * 128
    comm = len(ada) > 1
    lead = (4, 2, 2)
    devices = grid.dp * grid.fsdp
    if comm:
        blocks = [m.shape for m in matrices[:6]] + [matrices[6].shape[::-1]]
        wholes = [lead + (b[0] * grid.dp // 16, b[1] * grid.fsdp) for b in blocks]
    else:
        wholes = [m.shape for m in matrices]
    inner_width = wholes[5][-1]
    late_1, late_2 = wholes[5], wholes[6]
    if comm:
        later = PARTS - EARLY
        late_1 = (*late_1[:4], late_1[4] // PARTS * later)
        late_2 = (*late_2[:3], late_2[3] // PARTS * later, late_2[4])
    shaped = jax.ShapeDtypeStruct
    narrow = shaped((slots, model), BF16)
    full = shaped((slots, model), F32)
    outs = [
        full,
        full,
        shaped((slots, 3 * model), BF16),
        narrow,
        narrow,
        narrow,
        narrow,
        narrow,
        shaped((text_slots, 2 * model), BF16),
        full,
    ]
    outs += [shaped(w if comm else (8, 128), BF16) for w in wholes[:5]]
    outs += [
        shaped((slots, 128), BF16),
        shaped(late_1, BF16),
        shaped(late_2, BF16),
        *[shaped((s[3], s[4] // 2) if comm else (8, 128), F32) for s in wholes[5:]],
        shaped((8, model), F32),
        shaped((1, 9 * model), F32),
        shaped((devices, 128), F32),
    ]
    vmem = pl.BlockSpec(memory_space=pltpu.VMEM)
    anywhere = pl.BlockSpec(memory_space=pl.ANY)
    smem = pl.BlockSpec(memory_space=pltpu.SMEM)
    scratch = [pltpu.VMEM(w, BF16) for w in wholes]
    scratch += [
        pltpu.VMEM((padded, 4 * model), BF16),
        pltpu.VMEM((slots, 4 * model), BF16),
    ]
    scratch += [pltpu.VMEM((slots, model), BF16)] * 2
    scratch += [pltpu.VMEM((text_slots, 2 * model), BF16)]
    scratch += [pltpu.VMEM((slots, model), F32)] * 5
    scratch += [
        pltpu.VMEM((slots, model), BF16),
        pltpu.VMEM((text_slots, model), BF16),
        pltpu.VMEM((slots, model), BF16),
        pltpu.VMEM((slots, 128), F32),
        pltpu.VMEM((slots, 128), BF16),
        pltpu.VMEM((padded, 128), BF16),
        pltpu.VMEM((text_slots, 128), BF16),
        pltpu.SemaphoreType.DMA((48,)),
        pltpu.VMEM((8, model), F32),
        pltpu.VMEM((1, 9 * model), F32),
        pltpu.VMEM((devices, 128), F32),
    ]
    if comm:
        items = gather_items(dict(zip(WEIGHTS, [shaped(w, BF16) for w in wholes])))
        rows, columns = ada[1].shape
        span = -(-columns // 128) * 128
        scratch += [
            pltpu.VMEM((devices, 1, 128), F32),
            pltpu.VMEM((devices, 1, span), F32),
            pltpu.VMEM((devices, 1, span), F32),
            pltpu.SemaphoreType.DMA((2, 2, devices - 1)),
            pltpu.VMEM((rows, columns), BF16),
            pltpu.VMEM((128, span), BF16),
            pltpu.VMEM(matrices[6].shape, BF16),
        ]
        scratch += [pltpu.VMEM(b, BF16) for b in blocks]
        scratch += [pltpu.VMEM((b[0] // 2, b[1]), BF16) for b in blocks]
        scratch += [
            pltpu.SemaphoreType.DMA((2, len(matrices))),
            pltpu.SemaphoreType.DMA((len(items), lead[0] + 4)),
            pltpu.SemaphoreType.DMA((len(items), lead[0] + 4)),
        ]
        early = [
            (*wholes[5][:4], wholes[5][4] // PARTS * EARLY),
            (*wholes[6][:3], wholes[6][3] // PARTS * EARLY, wholes[6][4]),
        ]
        scratch += reduce_scratch(early, lead[0])
        scratch += [pltpu.VMEM((s[3], s[4] // 2), F32) for s in wholes[5:]]
        scratch += [pltpu.SemaphoreType.DMA((2 * EARLY, lead[0] + 4))] * 2
    params = {"vmem_limit_bytes": 63 * 1024 * 1024}
    if comm:
        params.update(collective_id=0, has_side_effects=True)
    results = pl.pallas_call(
        functools.partial(forward_kernel, (grid.dp, grid.fsdp) if comm else None),
        out_shape=outs,
        in_specs=[smem] * 2 + [anywhere] * 3 + [vmem] + [anywhere] * (6 + len(ada)),
        out_specs=[anywhere] * 23,
        scratch_shapes=scratch,
        compiler_params=pltpu.CompilerParams(**params),
        name="forward",
    )(*lengths, latent, text_block, upstream, *ada, *matrices)
    kept_matrices = results[10:15] if comm else matrices[:5]
    return results[0], (*results[1:10], results[15]), kept_matrices, results[16:]


BACK = (QKV, OUT, CQ, CKV, COUT)


EARLY = 1


def part_items(rows, width, parts, before):
    items = []
    for part in range(parts):
        items += [
            Item(FC2, (part * rows, rows), summed=(before * rows, 0)),
            Item(FC1, None, part * width, width, summed=(0, before * width)),
        ]
    return items


def reduce_items(shapes):
    parts = PARTS - EARLY
    items = part_items(shapes[FC2][3] // parts, shapes[FC1][-1] // 2 // parts, parts, EARLY)
    items += [Item(COUT)]
    width = shapes[CKV][-1] // 4
    items += [Item(CKV, None, k * width, width) for k in range(2)]
    items += [Item(CQ), Item(OUT)]
    model = shapes[QKV][-1] // 3
    third, half = model // 3, model // 2
    items += [
        Item(QKV, None, (0, half), third, 0),
        Item(QKV, None, (2 * third, half + 2 * third), third, third),
        Item(QKV, None, (model, 2 * third - half), third, 2 * third),
        Item(QKV, None, (third, half + third), third, model),
        Item(QKV, None, (model + third, 0), third // 2, model + third),
    ]
    return items


class Reduce:
    def __init__(self, where, sources, kept, landing, first, second, along, sums, owned, items, sems):
        self.z, self.y, self.x, self.core = where
        self.sources, self.kept, self.landing = sources, kept, landing
        self.from_first, self.from_second, self.from_z = first, second, along
        self.sums, self.owned, self.items = sums, owned, items
        self.send_sem, self.recv_sem, self.last_sem = sems
        self.nz = sources[FC2].shape[0]
        self.counts = [0, 0, 0, 0]
        z, y, x, core = where
        self.sibling = device(z, y, x, 1 - core)
        self.first = device(
            z, (1 - y) * (1 - core) + y * core, x * (1 - core) + (1 - x) * core, core
        )
        self.second = device(
            z, y * (1 - core) + (1 - y) * core, (1 - x) * (1 - core) + x * core, core
        )
        self.done = 0

    def remote(self, number, slot, src, dst, partner):
        return pltpu.make_async_remote_copy(
            src_ref=src,
            dst_ref=dst,
            send_sem=self.send_sem.at[number, slot],
            recv_sem=self.recv_sem.at[number, slot],
            device_id=partner,
            device_id_type=MESH,
        )

    def rows(self, number, offset=0):
        item = self.items[number]
        height = self.sources[item.name].shape[3]
        start, size = (0, height) if item.rows is None else item.rows
        return pl.ds(start + offset, size)

    def columns(self, number, which):
        item = self.items[number]
        return half_columns(self.sources[item.name], which, item.first, item.width)

    def inside(self, number):
        item = self.items[number]
        width = self.sources[item.name].shape[-1] // 2 if item.width is None else item.width
        return pl.ds(item.slot, width)

    def landed(self, number, which):
        item = self.items[number]
        half = self.landing[item.name].shape[-1] // 2
        return pl.ds(which * half + item.slot, half if item.width is None else item.width)

    def stay(self, number):
        name = self.items[number].name
        if name in self.kept:
            return self.kept[name], ()
        return self.sources[name], (self.core,)

    def kept_at(self, number, a, b, columns):
        ref, extra = self.stay(number)
        return ref.at[(a, b, *extra, self.rows(number), columns)]

    def to_core(self, number):
        item = self.items[number]
        landing = self.landing[item.name]
        copies = []
        for k in range(2):
            columns = self.columns(number, k)
            src = self.sources[item.name].at[:, :, 1 - self.core, self.rows(number), columns]
            dst = landing.at[:, :, self.rows(number), self.landed(number, k)]
            copies.append(self.remote(number, self.nz + 2 + k, src, dst, self.sibling))
        return copies

    def to_first(self, number):
        copies = []
        for k in range(2):
            row = (1 - self.y) * (1 - self.core) + k * self.core
            column = k * (1 - self.core) + (1 - self.x) * self.core
            src = self.kept_at(number, slice(None), row, self.columns(number, column))
            dst = self.from_first[self.items[number].name].at[
                :, k, self.rows(number), self.inside(number)
            ]
            copies.append(self.remote(number, self.nz + k, src, dst, self.first))
        return copies

    def to_second(self, number):
        row = self.y * (1 - self.core) + (1 - self.y) * self.core
        column = (1 - self.x) * (1 - self.core) + self.x * self.core
        src = self.kept_at(number, slice(None), row, self.columns(number, column))
        dst = self.from_second[self.items[number].name].at[
            :, self.rows(number), self.inside(number)
        ]
        return [self.remote(number, self.nz - 1, src, dst, self.second)]

    def to_z(self, number):
        copies = []
        for step in range(1, self.nz):
            other = (self.z + step) % self.nz
            src = self.kept_at(number, other, self.y, self.columns(number, self.x))
            dst = self.from_z[self.items[number].name].at[
                step - 1, self.rows(number), self.inside(number)
            ]
            partner = device(other, self.y, self.x, self.core)
            copies.append(self.remote(number, step - 1, src, dst, partner))
        return copies

    def add_core(self, number):
        landing = self.landing[self.items[number].name]
        for k in range(2):
            columns = self.columns(number, k)
            rows, landed = self.rows(number), self.landed(number, k)

            def one(step, carry):
                a, b = step // 2, step % 2
                spot = self.kept_at(number, a, b, columns)
                spot[...] = spot[...] + landing[a, b, rows, landed]
                return carry

            lax.fori_loop(0, self.nz * 2, one, 0)

    def add_first(self, number):
        arrived = self.from_first[self.items[number].name]
        rows, inside = self.rows(number), self.inside(number)
        for k in range(2):
            row = self.y * (1 - self.core) + k * self.core
            columns = self.columns(number, k * (1 - self.core) + self.x * self.core)

            def one(a, carry):
                spot = self.kept_at(number, a, row, columns)
                spot[...] = spot[...] + arrived[a, k, rows, inside]
                return carry

            lax.fori_loop(0, self.nz, one, 0)

    def add_second(self, number):
        arrived = self.from_second[self.items[number].name]
        rows, inside = self.rows(number), self.inside(number)
        columns = self.columns(number, self.x)

        def one(a, carry):
            spot = self.kept_at(number, a, self.y, columns)
            spot[...] = spot[...] + arrived[a, rows, inside]
            return carry

        lax.fori_loop(0, self.nz, one, 0)

    def add_z(self, number):
        name = self.items[number].name
        arrived = self.from_z[name]
        rows, inside = self.rows(number), self.inside(number)
        total = self.kept_at(number, self.z, self.y, self.columns(number, self.x))[...].astype(F32)
        for step in range(self.nz - 1):
            total += arrived[step, rows, inside].astype(F32)
        item = self.items[number]
        down, along = item.summed
        start = item.first[0] + self.x * (item.first[1] - item.first[0]) + along
        self.sums[name][
            self.rows(number, down), pl.ds(pl.multiple_of(start, 128), total.shape[1])
        ] = total
        if self.owned and number == max(i for i, item in enumerate(self.items) if item.name == name):
            self.share(name)

    def last(self, name):
        number = WEIGHTS.index(name)
        staged, owned = self.sums[name + "_sent"], self.owned[name]
        rows = staged.shape[0]
        return pltpu.make_async_remote_copy(
            src_ref=staged,
            dst_ref=owned.at[pl.ds(pl.multiple_of(self.core * rows, 16), rows), :],
            send_sem=self.last_sem.at[0, number],
            recv_sem=self.last_sem.at[1, number],
            device_id=self.sibling,
            device_id_type=MESH,
        )

    def share(self, name):
        total = self.sums[name][...]
        rows, width = total.shape
        left, right = total[:, : width // 2], total[:, width // 2 :]
        if name == FC1:
            step = width // 8 // PARTS
            left, right = (
                jnp.concatenate(
                    [
                        total[:, start : start + step]
                        for k in range(4)
                        for part in range(PARTS)
                        for start in [((part * 2 + side) * 4 + k) * step]
                    ],
                    1,
                )
                for side in range(2)
            )
        start = pl.multiple_of(self.core * rows, 16)
        self.owned[name][pl.ds(start, rows), :] = jnp.where(self.core == 0, left, right)
        self.sums[name + "_sent"][...] = jnp.where(self.core == 0, right, left)
        self.last(name).start()

    def launch(self, number):
        for copy in self.to_core(number):
            copy.start()

    def step(self, depth, number):
        stages = [self.to_core, self.to_first, self.to_second, self.to_z]
        adds = [self.add_core, self.add_first, self.add_second, self.add_z]
        for copy in stages[depth](number):
            copy.wait_recv()
        adds[depth](number)
        if depth < 3:
            for copy in stages[depth + 1](number):
                copy.start()

    def up_to(self, depth, number):
        while self.counts[depth] <= min(number, len(self.items) - 1):
            self.step(depth, self.counts[depth])
            self.counts[depth] += 1

    def targets(self, numbers):
        for depth, number in enumerate(numbers):
            self.up_to(depth, number)

    def advance(self, steps):
        while self.done < steps:
            lag = 2
            for depth in range(4):
                self.up_to(depth, self.done - depth * lag)
            self.done += 1

    def numbers(self, name):
        return [i for i, item in enumerate(self.items) if item.name == name]

    def sent(self):
        for number in range(len(self.items)):
            for stage in (self.to_core, self.to_first, self.to_second, self.to_z):
                for copy in stage(number):
                    copy.wait_send()

    def finish(self):
        count = len(self.items)
        self.up_to(0, count)
        for number in range(count + 2):
            for depth in range(1, 4):
                self.up_to(depth, number - depth + 1)
        for name in dict.fromkeys(item.name for item in self.items):
            self.last(name).wait()
        self.sent()


def reduce_scratch(shapes, nz):
    scratch = [pltpu.VMEM((nz, 2, s[3], s[4]), BF16) for s in shapes]
    scratch += [pltpu.VMEM((nz, 2, s[3], s[4] // 2), BF16) for s in shapes]
    scratch += [pltpu.VMEM((nz, s[3], s[4] // 2), BF16) for s in shapes]
    scratch += [pltpu.VMEM((nz - 1, s[3], s[4] // 2), BF16) for s in shapes]
    return scratch


def backward_kernel(comm, *refs):
    (frame_len, text_len, mod_in, rows_3_in, lat_in, text_in), refs = refs[:6], refs[6:]
    names = (
        "dcross",
        "qkv_act",
        "h1",
        "mixed1",
        "h2",
        "q2",
        "mixed2",
        "memory",
        "after",
        "stats",
    )
    given, refs = dict(zip(names, refs[:10])), refs[10:]
    matrices, refs = dict(zip(BACK, refs[:5])), refs[5:]
    if comm:
        (grad_fc1, grad_fc2, sums_fc1, sums_fc2), refs = refs[:4], refs[4:]
    (latent_out, text_sent), refs = refs[:2], refs[2:]
    if comm:
        everybody_sent, refs = refs[0], refs[1:]
        owned_sent, refs = dict(zip(WEIGHTS, refs[:7])), refs[7:]
    else:
        rows_out, refs = refs[0], refs[1:]
        grads_out, refs = dict(zip(BACK, refs[:5])), refs[5:]
    (dcross, packed, hidden, mixed, q2, memory, after), refs = refs[:7], refs[7:]
    text, stats, means, frame_marks, text_marks, query_sum, lanes = refs[:7]
    mod, rows_3, text_out = refs[7:10]
    refs = refs[10:]
    held, refs = dict(zip(BACK, refs[:5])), refs[5:]
    grad_qkv, above, sems = refs[:3]
    refs = refs[3:]
    slots, model = dcross.shape
    lat = above.at[0]
    head = model // HEADS
    size = row_tile(slots)
    loads = Loads(sems)
    act = {
        "dcross": dcross,
        "mixed2": mixed,
        "q2": q2,
        "memory": memory,
        "h2": hidden,
        "stats": stats,
        "after": after,
    }
    grads = dict(held, qkv=grad_qkv)
    if comm:
        dp_size, fsdp_size = comm
        (rows_out, dmod, pieces, ada_sems, fc2_rows), refs = refs[:5], refs[5:]
        owned, refs = dict(zip(WEIGHTS, refs[:6])), refs[6:]
        turned, everybody, refs = refs[0], refs[1], refs[2:]
        owned[FC2] = fc2_rows
        kept, refs = {FC2: refs[0], FC1: refs[1]}, refs[2:]
        landing, refs = dict(zip(WEIGHTS, refs[:7])), refs[7:]
        first, refs = dict(zip(WEIGHTS, refs[:7])), refs[7:]
        second, refs = dict(zip(WEIGHTS, refs[:7])), refs[7:]
        along, refs = dict(zip(WEIGHTS, refs[:7])), refs[7:]
        sums, refs = dict(zip(WEIGHTS, refs[:7])), refs[7:]
        sums.update(zip([name + "_sent" for name in WEIGHTS], refs[:7]))
        refs = refs[7:]
        reduce_sems = refs[:3]
        sources = dict(grads, fc1=grad_fc1, fc2=grad_fc2)
        items = reduce_items({name: ref.shape for name, ref in sources.items()})
        reduce = Reduce(
            place(), sources, kept, landing, first, second, along, sums, owned, items, reduce_sems
        )
        core = reduce.core
    loads.start("mod", mod_in, mod)
    loads.start("rows", rows_3_in, rows_3)
    loads.start("wcout", matrices[COUT], held[COUT])
    for name in ("dcross", "mixed2", "q2", "memory", "stats"):
        loads.start(name, given[name], act[name])
    if comm:
        barrier = pltpu.get_barrier_semaphore()

        def greet_one(step, target, me):
            pl.semaphore_signal(
                barrier,
                inc=1,
                device_id={"dp": target // fsdp_size, "fsdp": target % fsdp_size},
                device_id_type=MESH,
            )

        everyone(dp_size, fsdp_size, greet_one)
        pl.semaphore_wait(barrier, dp_size * fsdp_size - 1)
        for name in (FC2, FC1):
            for number in reduce.numbers(name):
                reduce.launch(number)
        for name, source in ((FC2, grad_fc2), (FC1, grad_fc1)):
            loads.start("keep_" + name, source.at[:, :, core], kept[name])
        for name, source in ((FC2, sums_fc2), (FC1, sums_fc1)):
            loads.start("s" + name, source, sums[name])
    for name in (CQ, CKV, OUT, QKV):
        loads.start("w" + name, matrices[name], held[name])
    for name in ("h2", "after"):
        loads.start(name, given[name], act[name])
    loads.start("text", text_in, text)
    loads.start("qkv_act", given["qkv_act"], packed.at[0:slots, :])

    def advance(steps):
        if comm:
            reduce.advance(steps)

    def hook(p, plan):
        if comm:
            for at, steps in plan:

                @pl.when(p == at)
                def _():
                    if isinstance(steps, tuple):
                        reduce.targets(steps)
                    else:
                        reduce.advance(steps)

    def row(k):
        return mod[:, k * model : (k + 1) * model]

    def place_grad(name, columns, left, right):
        target = grads[name]
        product = dot_tn(left, right).astype(BF16)
        target[:, :, :, :, columns] = product.reshape(target.shape[:4] + (-1,))

    def ready(name):
        if not comm:
            loads.start("g" + name, grads[name], grads_out[name])
            return
        for number in reduce.numbers(name):
            reduce.launch(number)

    rows_out[...] = jnp.zeros_like(rows_out)
    mark_keys(frame_marks, frame_len[0])
    mark_keys(text_marks, text_len[0])
    loads.wait("dcross", "wcout", "mod", "rows")

    def enter_2(rows):
        small = (row(5) * dcross[rows, :]).astype(BF16)
        above[0, rows, :] = small
        upstream = dot_nt(small, flat(held[COUT][...])).astype(BF16)
        above[1, rows, :] = upstream
        means[rows, :] = thirds(head_sums(upstream, mixed[rows, :], lanes[...]), 0.0)

    loads.wait("mixed2")
    lanes[...] = head_lanes(model, HEADS)
    tiles(slots, size, enter_2)
    place_grad(COUT, slice(0, model), mixed[...], above[0])
    ready(COUT)
    loads.wait("q2", "memory", "stats")
    if comm:
        loads.wait("keep_fc2", "keep_fc1", "sfc2", "sfc1")
    advance(1)
    pair = attend_back(
        (q2, 0),
        (memory, 0),
        (memory, model),
        text_marks,
        above.at[1],
        means,
        (stats, HEADS),
        query_sum,
        head,
        memory.shape[0],
    )

    def pair_2(p, carry):
        hook(p, ((1, 2), (3, 3), (5, 4)))
        return pair(p, carry)

    lax.fori_loop(0, HEADS // 2, pair_2, 0)
    loads.start("mixed1", given["mixed1"], mixed)
    loads.wait("wcq", "wckv", "after", "h2", "text")
    text_out[...] = dot_nt(memory[...], flat(held[CKV][...]))
    loads.start("text_out", text_out, text_sent)
    tiles(
        2 * model,
        model,
        lambda columns: place_grad(CKV, columns, text[...], memory[:, columns]),
    )
    ready(CKV)
    loads.wait("wout")
    advance(5)

    def leave_2(rows):
        upstream = dot_nt(q2[rows, :], flat(held[CQ][...]))
        normed, inverse = normalize(after[rows, :])
        back, dshift, dscale = norm_back(upstream, normed, inverse, row(4))
        dself = dcross[rows, :] + back
        dcross[rows, :] = dself
        rows_out[0:1, :] += dshift[None]
        rows_out[1:2, :] += dscale[None]
        branch = dot(mixed[rows, :], flat(held[OUT][...]))
        rows_out[2:3, :] += jnp.sum(dself * branch, 0, keepdims=True)
        small = (row(2) * dself).astype(BF16)
        above[0, rows, :] = small
        upstream = dot_nt(small, flat(held[OUT][...])).astype(BF16)
        above[1, rows, :] = upstream
        means[rows, :] = thirds(head_sums(upstream, mixed[rows, :], lanes[...]), 0.0)

    loads.wait("mixed1")
    lanes[...] = head_lanes(model, 0)
    tiles(slots, size, leave_2)
    advance(6)
    place_grad(CQ, slice(0, model), hidden[...], q2[...])
    ready(CQ)
    loads.start("h1", given["h1"], hidden)
    place_grad(OUT, slice(0, model), mixed[...], above[0])
    ready(OUT)
    loads.start("lat", lat_in, lat)
    advance(7)
    loads.wait("qkv_act")
    packed[slots:, :] = jnp.zeros((packed.shape[0] - slots, 3 * model), BF16)
    place_in_loop = []
    pairs = HEADS // 2

    def tile_hook(t):
        plan = []
        for j in range(pairs):
            late = j // 4
            plan += [
                (2 * j, (6 + j, 4 + j + late, 2 + j + late, j)),
                (2 * j + 1, (7 + j, 5 + j + late, 3 + j + late, 1 + j)),
            ]
        hook(2 * place_in_loop[-1] + t, plan)

    pair = attend_back(
        (packed, 0),
        (packed, model),
        (packed, 2 * model),
        frame_marks,
        above.at[1],
        means,
        (stats, 0),
        query_sum,
        head,
        packed.shape[0] // 2,
        tile_hook,
    )

    third, half = model // 3, 3 * model // 2

    def grad_columns(*starts, width):
        spans = [slice(start, start + width) for start in starts]
        product = dot_tn(
            hidden[...], jnp.concatenate([packed[0:slots, span] for span in spans], 1)
        ).astype(BF16)
        for k, span in enumerate(spans):
            grad_qkv[:, :, :, :, span] = product[:, k * width : (k + 1) * width].reshape(
                grad_qkv.shape[:4] + (width,)
            )

    def launch(part):
        if comm:
            reduce.launch(reduce.numbers(QKV)[part])

    def pair_1(i, carry):
        place_in_loop.append(i)
        group = i // (pairs // 3)
        pair(group * (7 - 3 * group) * pairs // 6 + i % (pairs // 3), carry)

        @pl.when(i == pairs // 3 - 1)
        def _():
            loads.wait("h1")
            grad_columns(0, 2 * model, width=third)
            launch(0)

        @pl.when(i == 2 * pairs // 3 - 1)
        def _():
            grad_columns(2 * third, 2 * model + 2 * third, width=third)
            launch(1)
            grad_columns(model, model + 2 * third, width=third)
            launch(2)

        return carry

    lax.fori_loop(0, pairs, pair_1, 0)
    grad_columns(third, 2 * model + third, width=third)
    launch(3)
    grad_columns(model + third, half, width=third // 2)
    launch(4)
    loads.wait("wqkv", "lat")
    if not comm:
        ready(QKV)

    def leave_1(rows):
        upstream = dot_nt(packed[rows, :], flat(held[QKV][...]))
        normed, inverse = normalize(lat[rows, :].astype(F32))
        back, dshift, dscale = norm_back(upstream, normed, inverse, row(1))
        dcross[rows, :] = dcross[rows, :] + back
        rows_out[3:4, :] += dshift[None]
        rows_out[4:5, :] += dscale[None]


    def leave_step(t, carry):
        hook(t, ((0, (13, 12, 10, 8)), (1, (15, 12, 11, 9)), (2, (15, 13, 12, 10))))
        leave_1(pl.ds(pl.multiple_of(t * last, 16), last))
        return carry

    last = slots // 3
    lax.fori_loop(0, 3, leave_step, 0)
    hook(0, ((0, (15, 14, 13, 11)),))
    loads.start("latent", dcross, latent_out)
    if not comm:
        loads.wait("gcout", "gckv", "gcq", "gout", "gqkv", "latent", "text_out")
        return
    ordered = (
        rows_out[3:4, :],
        rows_out[4:5, :],
        rows_out[2:3, :],
        rows_out[0:1, :],
        rows_out[1:2, :],
        rows_3[3:4, :],
        rows_3[1:2, :],
        rows_3[2:3, :],
        rows_3[0:1, :],
    )
    for k, value in enumerate(ordered):
        dmod[:, k * model : (k + 1) * model] = value.astype(BF16).astype(F32)
    span = pieces.shape[-1]
    for j in range(fsdp_size):
        start = j * dmod.shape[1] // fsdp_size // 128 * 128
        pieces[j] = dmod[:, start : start + span]
    me = lax.axis_index("dp") * fsdp_size + lax.axis_index("fsdp")
    send = modulate_start(dp_size, fsdp_size, pieces, everybody, ada_sems)
    everyone(dp_size, fsdp_size, lambda s, t, m: send(s, t, m, t % fsdp_size).start())
    everybody[me] = pieces[lax.axis_index("fsdp")]
    reduce.finish()
    everyone(dp_size, fsdp_size, lambda s, t, m: send(s, t, m, t % fsdp_size).wait())
    loads.start("all", everybody, everybody_sent)
    for name in WEIGHTS[:6]:
        loads.start("o" + name, owned[name], owned_sent[name])
    turned[...] = fc2_rows[...].T
    loads.start("ofc2", turned, owned_sent[FC2])
    loads.wait("all", "text_out", *["o" + name for name in WEIGHTS])
    loads.wait("latent")


def backward(grid, comm, lengths, latent, text_block, modulation, rest, kept, matrices, ff):
    slots, model = latent.shape
    text_slots = text_block.shape[0]
    padded = -(-slots // 128) * 128
    rows_3 = rest
    devices = grid.dp * grid.fsdp
    shaped = jax.ShapeDtypeStruct
    vmem = pl.BlockSpec(memory_space=pltpu.VMEM)
    anywhere = pl.BlockSpec(memory_space=pl.ANY)
    smem = pl.BlockSpec(memory_space=pltpu.SMEM)
    outs = [shaped((slots, model), F32), shaped((text_slots, model), F32)]
    narrow = pltpu.VMEM((slots, model), BF16)
    full = pltpu.VMEM((slots, model), F32)
    scratch = [
        full,
        pltpu.VMEM((padded, 3 * model), BF16),
        narrow,
        narrow,
        narrow,
        pltpu.VMEM((text_slots, 2 * model), BF16),
        full,
        pltpu.VMEM((text_slots, model), BF16),
        pltpu.VMEM((slots, 128), BF16),
        pltpu.VMEM((slots, 128), BF16),
        pltpu.VMEM((padded, 128), BF16),
        pltpu.VMEM((text_slots, 128), BF16),
        pltpu.VMEM((slots, 128), F32),
        pltpu.VMEM((model, 128), BF16),
        pltpu.VMEM((1, 9 * model), F32),
        pltpu.VMEM((8, model), F32),
        pltpu.VMEM((text_slots, model), F32),
    ]
    scratch += [pltpu.VMEM(m.shape, BF16) for m in matrices]
    scratch += [
        pltpu.VMEM(matrices[0].shape, BF16),
        pltpu.VMEM((2, slots, model), BF16),
        pltpu.SemaphoreType.DMA((48,)),
    ]
    params = {"vmem_limit_bytes": 63 * 1024 * 1024}
    if comm:
        params.update(collective_id=1, has_side_effects=True)
        shapes = dict(zip(WEIGHTS, [m.shape for m in (*matrices, *ff[:2])]))
        wholes = dict(shapes)
        wholes[FC1] = (*shapes[FC1][:4], 2 * ff[2].shape[1])
        wholes[FC2] = (*shapes[FC2][:3], *ff[3].shape[:1], 2 * ff[3].shape[1])
        nz = shapes[OUT][0]
        span = -(-9 * model // grid.fsdp // 128) * 128
        outs += [shaped((devices, 1, span), F32)]
        outs += [shaped((2 * s[3], s[4] // 4), F32) for s in (*wholes.values(),)[:6]]
        outs += [shaped((wholes[FC2][4] // 4, 2 * wholes[FC2][3]), F32)]
        out_specs = [anywhere] * 10
        scratch += [
            pltpu.VMEM((8, model), F32),
            pltpu.VMEM((1, 9 * model), F32),
            pltpu.VMEM((grid.fsdp, 1, span), F32),
            pltpu.SemaphoreType.DMA((2, devices - 1)),
            pltpu.VMEM((2 * wholes[FC2][3], wholes[FC2][4] // 4), F32),
        ]
        scratch += [pltpu.VMEM(o.shape, F32) for o in outs[3:]]
        scratch += [pltpu.VMEM(outs[2].shape, F32)]

        scratch += [pltpu.VMEM((nz, 2, *shapes[name][3:]), BF16) for name in (FC2, FC1)]
        scratch += reduce_scratch(shapes.values(), nz)
        scratch += [pltpu.VMEM((s[3], s[4] // 2), F32) for s in wholes.values()]
        scratch += [pltpu.VMEM((s[3], s[4] // 4), F32) for s in wholes.values()]
        count = len(reduce_items(shapes))
        scratch += [
            pltpu.SemaphoreType.DMA((count, nz + 4)),
            pltpu.SemaphoreType.DMA((count, nz + 4)),
            pltpu.SemaphoreType.DMA((2, 7)),
        ]
    else:
        ff = ()
        outs += [shaped((8, model), F32)]
        outs += [shaped(m.shape, BF16) for m in matrices]
        out_specs = [anywhere, anywhere, vmem] + [anywhere] * 5
    return pl.pallas_call(
        functools.partial(backward_kernel, (grid.dp, grid.fsdp) if comm else None),
        out_shape=outs,
        in_specs=[smem] * 2 + [anywhere] * (19 + len(ff)),
        out_specs=out_specs,
        scratch_shapes=scratch,
        compiler_params=pltpu.CompilerParams(**params),
        name="backward",
    )(
        *lengths,
        modulation,
        rows_3,
        latent,
        text_block,
        *kept,
        *matrices,
        *ff,
    )


def row_pieces(rows):
    count = 4 if rows >= 256 and rows % 32 == 0 else 1
    return [slice(k * rows // count, (k + 1) * rows // count) for k in range(count)]


def deliver_kernel(count, conditions, gathered, *refs):
    given, ada_out, taken = refs[:count], refs[count], refs[count + 1 : 2 * count + 1]
    staged, sems = refs[2 * count + 1 : -1], refs[-1]
    inward, outward = [], []
    for src, mid, dst in zip(given, staged, taken):
        for rows in row_pieces(src.shape[0]):
            number = len(inward)
            inward.append(pltpu.make_async_copy(src.at[rows, :], mid.at[rows, :], sems.at[0, number]))
            outward.append(pltpu.make_async_copy(mid.at[rows, :], dst.at[rows, :], sems.at[1, number]))
    for copy in inward:
        copy.start()
    for before, after in zip(inward, outward):
        before.wait()
        after.start()
    rows, columns = ada_out.shape
    stacked = jnp.concatenate([gathered[k] for k in range(gathered.shape[0])], 0)
    product = dot_tn(conditions[...].astype(BF16), stacked.astype(BF16))[:rows]
    spare = product.shape[1] - columns
    ada_out[...] = jnp.where(
        lax.axis_index("fsdp") % 2 == 0, product[:, :columns], product[:, spare:]
    )
    for copy in outward:
        copy.wait()


def deliver(conditions, gathered, shape, results):
    vmem = pl.BlockSpec(memory_space=pltpu.VMEM)
    anywhere = pl.BlockSpec(memory_space=pl.ANY)
    count = len(results)
    return pl.pallas_call(
        functools.partial(deliver_kernel, count),
        out_shape=[jax.ShapeDtypeStruct(shape, F32)]
        + [jax.ShapeDtypeStruct(r.shape, r.dtype) for r in results],
        in_specs=[vmem] * 2 + [anywhere] * count,
        out_specs=[vmem] + [anywhere] * count,
        scratch_shapes=[pltpu.VMEM(r.shape, r.dtype) for r in results]
        + [pltpu.SemaphoreType.DMA((2, 4 * count))],
        compiler_params=pltpu.CompilerParams(vmem_limit_bytes=63 * 1024 * 1024),
        name="deliver",
    )(conditions, gathered, *results)


def by_part(matrix):
    split = matrix.reshape(*matrix.shape[:-1], 2, 2, 4, PARTS, matrix.shape[-1] // 16 // PARTS)
    return jnp.moveaxis(split, -2, -4).reshape(matrix.shape)


def from_part(matrix):
    split = matrix.reshape(*matrix.shape[:-1], 2, PARTS, 2, 4, matrix.shape[-1] // 16 // PARTS)
    return jnp.moveaxis(split, -4, -2).reshape(matrix.shape)


def body(
    latents,
    text_rows,
    out_grad,
    frame_len,
    text_len,
    timestep,
    w_ada,
    w_qkv,
    w_out,
    w_cq,
    w_ckv,
    w_cout,
    w_fc1,
    w_fc2,
    *,
    dp_size,
    fsdp_size,
):
    grid = Grid(dp_size, fsdp_size)
    matrices = (w_qkv, w_out, w_cq, w_ckv, w_cout, w_fc1, w_fc2)
    lengths = (frame_len, text_len)
    if grid.fits(matrices):
        ada = ada_inputs(grid, timestep, w_ada)
        matrices = (*matrices[:6], w_fc2.T)
    else:
        *others, full_fc1, full_fc2 = gather_weights(grid, matrices)
        matrices = (*others, by_part(full_fc1), full_fc2)
        conditions, modulation = modulate(grid, timestep, w_ada)
        ada = (modulation.reshape(1, -1),)
    layer_out, kept, kept_matrices, rest = forward(
        grid, lengths, latents[0], text_rows[0], out_grad[0], ada, matrices
    )
    grad_fc1, grad_fc2, sums_1, sums_2, rows_3, modulation, rows = rest
    comm = len(ada) > 1
    results = backward(
        grid,
        comm,
        lengths,
        latents[0],
        text_rows[0],
        modulation,
        rows_3,
        kept,
        kept_matrices,
        (grad_fc1, grad_fc2, sums_1, sums_2),
    )
    latent_grad, text_grad, rows_1 = results[:3]
    if comm:
        results = (layer_out, latent_grad, text_grad, *results[3:])
        grad_ada, layer_out, latent_grad, text_grad, *owned, fc2 = deliver(
            rows, rows_1, w_ada.shape, results
        )
        owned = (*owned, fc2.T)
    else:
        order = (
            rows_1[3:4],
            rows_1[4:5],
            rows_1[2:3],
            rows_1[0:1],
            rows_1[1:2],
            rows_3[3:4],
            rows_3[1:2],
            rows_3[2:3],
            rows_3[0:1],
        )
        dmodulation = jnp.concatenate(order, 0).reshape(1, -1).astype(BF16)
        grad_ada = ada_gradient(grid, conditions, dmodulation)
        owned = reduce_gradients(grid, (*results[3:8], from_part(grad_fc1), grad_fc2))
    return (
        layer_out[None],
        latent_grad[None],
        text_grad[None],
        grad_ada,
        *owned,
    )


def solution(mesh):
    placed = (P(("dp", "fsdp"), None, None),) * 3 + (P(("dp", "fsdp")),) * 3 + (P("dp", "fsdp"),) * 8
    return jax.shard_map(
        functools.partial(body, dp_size=mesh.shape["dp"], fsdp_size=mesh.shape["fsdp"]),
        mesh=mesh,
        in_specs=placed,
        out_specs=(P(("dp", "fsdp"), None, None),) * 3 + (P("dp", "fsdp"),) * 8,
        check_vma=False,
    )
```

```python
import functools
import math

import jax
import jax.numpy as jnp
from jax import lax
from jax.experimental import pallas as pl
from jax.experimental.pallas import tpu as pltpu
from jax.sharding import PartitionSpec as P

HEADS = 12


norm_eps = 1e-06


def sinusoid(time_value, model_width):
    half_width = model_width // 2
    frequency = jnp.exp(-math.log(10000.0) * jnp.arange(half_width, dtype=jnp.float32) / half_width)
    angles = time_value.astype(jnp.float32) * frequency
    return jnp.concatenate([jnp.cos(angles), jnp.sin(angles)], axis=-1)


def normalize(values):
    center = values - jnp.mean(values, -1, keepdims=True)
    spread = jnp.mean(center * center, -1, keepdims=True)
    inverse = lax.rsqrt(spread + norm_eps)
    return (center * inverse, inverse)


def norm_back(upstream, normed, inverse, scale_row):
    dshift = jnp.sum(upstream, 0)
    dscale = jnp.sum(upstream * normed, 0)
    scaled = upstream * (1.0 + scale_row)
    centered = (
        scaled
        - jnp.mean(scaled, -1, keepdims=True)
        - normed * jnp.mean(scaled * normed, -1, keepdims=True)
    )
    return (inverse * centered, dshift, dscale)


def outer_sum(left, right):
    return lax.dot_general(
        left, right, (((0,), (0,)), ((), ())), preferred_element_type=jnp.float32
    )


MESH = pl.DeviceIdType.MESH


class Grid:
    def __init__(self, dp_size, fsdp_size):
        self.dp = dp_size
        self.fsdp = fsdp_size

    def fits(self, matrices):
        if self.fsdp != 4 or self.dp != 8:
            return False
        for matrix in matrices:
            rows, columns = matrix.shape
            if rows % 32 or (2 * columns) % 128:
                return False
        return True


def place():
    dp_index = lax.axis_index("dp")
    fsdp_index = lax.axis_index("fsdp")
    return dp_index // 2, dp_index % 2, fsdp_index // 2, fsdp_index % 2


def device(z, y, x, core):
    return {"dp": z * 2 + y, "fsdp": x * 2 + core}


def gather_weights(grid, matrices):
    return tuple(
        lax.all_gather(
            lax.all_gather(m, "fsdp", axis=1, tiled=True), "dp", axis=0, tiled=True
        ).reshape(4, 2, 2, m.shape[0] * grid.dp // 16, m.shape[1] * grid.fsdp)
        for m in matrices
    )


def reduce_gradients(grid, gradients):
    out = []
    for gradient in gradients:
        part = gradient.reshape(-1, gradient.shape[-1])
        part = lax.psum_scatter(part, "dp", scatter_dimension=0, tiled=True)
        part = lax.psum_scatter(part, "fsdp", scatter_dimension=1, tiled=True)
        out.append(part.astype(jnp.float32))
    return tuple(out)


def modulate(grid, timestep, w_ada):
    rows, columns = w_ada.shape
    model_width = rows * grid.dp
    times = lax.all_gather(timestep, ("dp", "fsdp"), axis=0, tiled=True)
    conditions = jax.nn.silu(
        jax.vmap(lambda value: sinusoid(value, model_width))(times)
    ).astype(jnp.bfloat16)
    mine = lax.dynamic_slice_in_dim(conditions, lax.axis_index("dp") * rows, rows, 1)
    partial = jnp.dot(mine, w_ada, preferred_element_type=jnp.float32)
    summed = lax.psum_scatter(partial, "dp", scatter_dimension=0, tiled=True)
    mixed = lax.all_to_all(summed, "fsdp", split_axis=0, concat_axis=0, tiled=True)
    return mine, mixed.reshape(9, model_width)


def ada_gradient(grid, conditions, dmodulation):
    spread = dmodulation.reshape(grid.fsdp, -1)
    swapped = lax.all_to_all(spread, "fsdp", split_axis=0, concat_axis=0, tiled=True)
    everyone = lax.all_gather(swapped, "dp", axis=0, tiled=True)
    return outer_sum(conditions, everyone)


def ada_inputs(grid, timestep, w_ada):
    rows, columns = w_ada.shape
    condition = jax.nn.silu(sinusoid(timestep[0], rows * grid.dp)).astype(jnp.bfloat16)
    mine = jnp.pad(
        condition.astype(jnp.float32).reshape(grid.dp, 1, rows), ((0, 0), (0, 0), (0, 128 - rows))
    )
    return mine, w_ada


F32 = jnp.float32
BF16 = jnp.bfloat16
NT = (((1,), (1,)), ((), ()))
TN = (((0,), (0,)), ((), ()))


def flat(value):
    return value.reshape(-1, value.shape[-1])


def dot(left, right):
    return jnp.dot(left, right, preferred_element_type=F32)


def dot_nt(left, right):
    return lax.dot_general(left, right, NT, preferred_element_type=F32)


def dot_tn(left, right):
    return lax.dot_general(left, right, TN, preferred_element_type=F32)


def tiles(total, size, body):
    def step(t, carry):
        body(pl.ds(pl.multiple_of(t * size, size), size))
        return carry

    lax.fori_loop(0, total // size, step, 0)


def row_tile(rows):
    for size in (432, 288, 256, 128):
        if rows % size == 0:
            return size
    return rows


def gelu_pair(inner):
    slope = math.sqrt(2.0 / math.pi)
    square = inner * inner
    turned = jnp.tanh(inner * (slope + (slope * 0.044715) * square))
    half = 0.5 + 0.5 * turned
    rise = inner * (slope + (3.0 * slope * 0.044715) * square)
    return inner * half, half + (0.5 - 0.5 * turned * turned) * rise


def half_lanes(shape):
    return lax.broadcasted_iota(jnp.int32, shape, 1) < shape[1] // 2


def lanes_of(shape):
    return lax.broadcasted_iota(jnp.int32, shape, 1)


def mark_keys(marks, length):
    shape = marks.shape
    excluded = jnp.where(lax.broadcasted_iota(jnp.int32, shape, 0) < length, 0.0, -1e30)
    marks[...] = jnp.where(lanes_of(shape) == shape[1] - 1, excluded, 0.0).astype(BF16)


def thirds(value, last):
    high = value.astype(BF16).astype(F32)
    middle = (value - high).astype(BF16).astype(F32)
    low = value - high - middle
    lane = lanes_of(value.shape)
    spread = high + pltpu.roll(middle, 32, 1) + pltpu.roll(low, 64, 1)
    return jnp.where(lane == value.shape[1] - 1, last, spread).astype(BF16)


def head_lanes(model, stat_at):
    shape = (model, 128)
    head = lax.broadcasted_iota(jnp.int32, shape, 0) // (model // HEADS)
    return jnp.where(lanes_of(shape) == head + stat_at, 1.0, 0.0).astype(BF16)


def head_sums(left, right, matrix):
    product = left.astype(F32) * right.astype(F32)
    high = product.astype(BF16)
    return dot(high, matrix) + dot((product - high.astype(F32)).astype(BF16), matrix)


def attend(queries, keys, values, marks, mixed, stats, heads_wide, size):
    query_ref, query_at = queries
    key_ref, key_at = keys
    value_ref, value_at = values
    mixed_ref, mixed_at = mixed
    stat_ref, stat_at = stats
    rows = mixed_ref.shape[0]
    width = 2 * heads_wide

    def pair(p, carry):
        def at(start):
            return pl.ds(pl.multiple_of(start + p * width, width), width)

        value_pair = value_ref[:, at(value_at)]
        marked = jnp.concatenate([key_ref[:, at(key_at)], marks[...]], 1)
        low = half_lanes((size, width))
        lane = lanes_of((size, width))
        last = (lane == width - 1).astype(F32).astype(BF16)
        for start in range(0, rows, size):
            span = slice(start, start + size)
            scaled = query_ref[span, at(query_at)] * BF16(heads_wide**-0.5)
            outs = []
            stat = stat_ref[span, :]
            for head in range(2):
                own = jnp.where(low if head == 0 else ~low, scaled, BF16(0))
                scores = dot_nt(jnp.concatenate([own, last], 1), marked)
                largest = jnp.max(scores, -1, keepdims=True)
                raised = jnp.exp(scores - largest)
                summed = jnp.sum(raised, -1, keepdims=True)
                outs.append(dot(raised.astype(BF16), value_pair) * (1.0 / summed))
                stat = jnp.where(lane == stat_at + 2 * p + head, largest + jnp.log(summed), stat)
            stat_ref[span, :] = stat
            mixed_ref[span, at(mixed_at)] = jnp.where(low, outs[0], outs[1]).astype(BF16)
        return carry

    return pair


def attend_back(
    queries, keys, values, marks, upstream, means, stats, total, heads_wide, size, before=None
):
    query_ref, query_at = queries
    key_ref, key_at = keys
    value_ref, value_at = values
    stat_ref, stat_at = stats
    rows = upstream.shape[0]
    slots = key_ref.shape[0]
    width = 2 * heads_wide

    def pair(p, carry):
        def at(start):
            return pl.ds(pl.multiple_of(start + p * width, width), width)

        low = half_lanes((rows, width))
        scaled = query_ref[0:rows, at(query_at)] * BF16(heads_wide**-0.5)
        above = upstream[:, at(0)]
        heads = []
        for head in range(2):
            mask = low if head == 0 else ~low
            own = jnp.where(mask, scaled, BF16(0))
            own_above = jnp.where(mask, above, BF16(0))
            heads.append(
                (
                    jnp.concatenate([own, stat_ref[...]], 1),
                    jnp.concatenate([own_above, means[...]], 1),
                    own,
                    own_above,
                )
            )
        low_keys = half_lanes((size, width))
        lane = lanes_of((size, width))

        def one_tile(span):
            key_pair = key_ref[span, at(key_at)]
            value_pair = value_ref[span, at(value_at)]
            query_grad = None
            key_grad = None
            value_grad = None
            for head in range(2):
                mask = low_keys if head == 0 else ~low_keys
                taken = lane - (stat_at + 2 * p + head)
                mark = jnp.where(
                    (taken == 0) | (taken == 32) | (taken == 64),
                    BF16(-1),
                    marks[span, :],
                )
                marked_query, marked_above, own, own_above = heads[head]
                shares = jnp.exp(dot_nt(jnp.concatenate([key_pair, mark], 1), marked_query))
                share_grad = dot_nt(jnp.concatenate([value_pair, mark], 1), marked_above)
                score_grad = (shares * share_grad).astype(BF16)
                values_part = dot(shares.astype(BF16), own_above)
                keys_part = dot(score_grad, own)
                queries_part = dot_tn(score_grad, jnp.where(mask, key_pair, BF16(0)))
                value_grad = values_part if head == 0 else value_grad + values_part
                key_grad = keys_part if head == 0 else key_grad + keys_part
                query_grad = queries_part if query_grad is None else query_grad + queries_part
            key_ref[span, at(key_at)] = key_grad.astype(BF16)
            value_ref[span, at(value_at)] = value_grad.astype(BF16)
            total[...] += query_grad

        total[...] = jnp.zeros_like(total)

        def step(t, carry):
            if before is not None:
                before(t)
            one_tile(pl.ds(pl.multiple_of(t * size, size), size))
            return carry

        lax.fori_loop(0, slots // size, step, 0)
        query_ref[0:rows, at(query_at)] = (total[...] * heads_wide**-0.5).astype(BF16)
        return carry

    return pair


class Loads:
    def __init__(self, sems):
        self.sems = sems
        self.copies = {}

    def start(self, name, src, dst):
        copy = pltpu.make_async_copy(src, dst, self.sems.at[len(self.copies)])
        copy.start()
        self.copies[name] = copy

    def wait(self, *names):
        for name in names:
            self.copies[name].wait()


WEIGHTS = ("qkv", "out", "cq", "ckv", "cout", "fc1", "fc2")
QKV, OUT, CQ, CKV, COUT, FC1, FC2 = WEIGHTS
PARTS = 4


def half_columns(ref, which, first=(0, 0), width=None):
    half = ref.shape[-1] // 2
    if width is None:
        width = half
    start = which * (half + first[1] - first[0]) + first[0]
    return pl.ds(pl.multiple_of(start, 128), width)


class Item:
    def __init__(self, name, rows=None, first=0, width=None, slot=None, summed=(0, 0)):
        self.name = name
        self.summed = summed
        self.rows = rows
        self.first = first if isinstance(first, tuple) else (first, first)
        self.width = width
        self.slot = self.first[0] if slot is None else slot


def gather_items(held):
    items = []
    rows = held[QKV].shape[3]
    items += [Item(QKV, (r, 16)) for r in range(0, rows, 16)]
    items += [Item(OUT), Item(CQ)]
    width = held[CKV].shape[-1] // 4
    items += [Item(CKV, None, k * width, width) for k in range(2)]
    items += [Item(COUT)]
    rows = held[FC2].shape[3] // PARTS
    width = held[FC1].shape[-1] // 2 // PARTS
    for part in range(PARTS):
        items += [Item(FC2, (part * rows, rows)), Item(FC1, None, part * width, width)]
    return items


class Gather:
    def __init__(self, where, given, held, own, swapped, items, sems):
        self.z, self.y, self.x, self.core = where
        self.given, self.held, self.own, self.swapped, self.items = given, held, own, swapped, items
        self.swap_sem, self.send_sem, self.recv_sem = sems
        self.nz = held[OUT].shape[0]
        z, y, x, core = where
        self.sibling = device(z, y, x, 1 - core)
        self.first = device(
            z, y * (1 - core) + (1 - y) * core, (1 - x) * (1 - core) + x * core, core
        )
        self.second = device(
            z, (1 - y) * (1 - core) + y * core, x * (1 - core) + (1 - x) * core, core
        )
        self.others = [device((z + step) % self.nz, y, x, core) for step in range(1, self.nz)]
        self.done = 0
        self.counts = [0, 0, 0, 0]
        self.record = None

    def half(self, number, which):
        staged = self.own[WEIGHTS[number]]
        rows = staged.shape[0] // 2
        return staged.at[pl.ds(pl.multiple_of(which * rows, 16), rows), :]

    def swap(self, number):
        return pltpu.make_async_remote_copy(
            src_ref=self.half(number, 1 - self.core),
            dst_ref=self.swapped[WEIGHTS[number]],
            send_sem=self.swap_sem.at[0, number],
            recv_sem=self.swap_sem.at[1, number],
            device_id=self.sibling,
            device_id_type=MESH,
        )

    def assemble(self, number):
        name = WEIGHTS[number]
        self.swap(number).wait_recv()
        mine, theirs = self.half(number, self.core)[...], self.swapped[name][...]
        whole = self.held[name]
        left = jnp.where(self.core == 0, mine, theirs)
        right = jnp.where(self.core == 0, theirs, mine)
        if name == FC1:
            four = left.shape[1] // 4
            step = four // PARTS
            pieces = [
                side[:, k * four + part * step : k * four + (part + 1) * step]
                for part in range(PARTS)
                for side in (left, right)
                for k in range(4)
            ]
        else:
            pieces = [left, right]
        whole[self.z, self.y, self.core, :, half_columns(whole, self.x)] = jnp.concatenate(
            pieces, 1
        )

    def remote(self, number, slot, part, partner):
        return pltpu.make_async_remote_copy(
            src_ref=part,
            dst_ref=part,
            send_sem=self.send_sem.at[number, slot],
            recv_sem=self.recv_sem.at[number, slot],
            device_id=partner,
            device_id_type=MESH,
        )

    def view(self, number):
        item = self.items[number]
        whole = self.held[item.name]
        rows = slice(None) if item.rows is None else pl.ds(*item.rows)
        return whole, rows, lambda which: half_columns(whole, which, item.first, item.width)

    def along_z(self, number):
        whole, rows, columns = self.view(number)
        part = whole.at[self.z, self.y, self.core, rows, columns(self.x)]
        return [self.remote(number, s, part, partner) for s, partner in enumerate(self.others)]

    def to_first(self, number):
        whole, rows, columns = self.view(number)
        part = whole.at[:, self.y, self.core, rows, columns(self.x)]
        return [self.remote(number, self.nz - 1, part, self.first)]

    def to_second(self, number):
        whole, rows, columns = self.view(number)
        copies = []
        for k in range(2):
            row = self.y * (1 - self.core) + k * self.core
            column = k * (1 - self.core) + self.x * self.core
            part = whole.at[:, row, self.core, rows, columns(column)]
            copies.append(self.remote(number, self.nz + k, part, self.second))
        return copies

    def to_core(self, number):
        whole, rows, columns = self.view(number)
        if self.items[number].width is None:
            parts = [whole.at[:, :, self.core, rows, :]]
        else:
            parts = [whole.at[:, :, self.core, rows, columns(k)] for k in range(2)]
        return [
            self.remote(number, self.nz + 2 + k, part, self.sibling) for k, part in enumerate(parts)
        ]

    def up_to(self, depth, number):
        while self.counts[depth] <= min(number, len(self.items) - 1):
            self.emit((depth, self.counts[depth]))
            self.counts[depth] += 1

    def emit(self, step):
        if self.record is not None:
            self.record.append(step)
            return
        depth, number = step
        stages = [self.along_z, self.to_first, self.to_second, self.to_core]
        if depth:
            for copy in stages[depth - 1](number):
                copy.wait_recv()
        if depth < 4:
            for copy in stages[depth](number):
                copy.start()

    def planned(self, body):
        self.record = []
        body()
        steps, self.record = self.record, None
        return steps

    def advance(self, steps, lag=2, ahead=3):
        while self.done < steps:
            self.up_to(0, self.done + ahead)
            for depth in range(1, 4):
                self.up_to(depth, self.done - (depth - 1) * lag)
            self.done += 1

    def numbers(self, name):
        return [i for i, item in enumerate(self.items) if item.name == name]

    def need(self, numbers):
        for depth in range(4):
            self.up_to(depth, max(numbers))
        for number in numbers:
            self.emit((4, number))

    def sent(self, numbers):
        for number in numbers:
            for stage in (self.along_z, self.to_first, self.to_second, self.to_core):
                for copy in stage(number):
                    copy.wait_send()


def everyone(dp_size, fsdp_size, body):
    count = dp_size * fsdp_size
    me = lax.axis_index("dp") * fsdp_size + lax.axis_index("fsdp")

    def one(step, carry):
        body(step, (me + step) % count, me)
        return carry

    lax.fori_loop(1, count, one, 0)


def modulate_start(dp_size, fsdp_size, mine, everything, sems):
    def copy(step, target, me, row):
        return pltpu.make_async_remote_copy(
            src_ref=mine.at[row],
            dst_ref=everything.at[me],
            send_sem=sems.at[0, step - 1],
            recv_sem=sems.at[1, step - 1],
            device_id={"dp": target // fsdp_size, "fsdp": target % fsdp_size},
            device_id_type=MESH,
        )

    return copy


def forward_kernel(comm, *refs):
    (frame_len, text_len, lat_in, text_in, og_in), refs = refs[:5], refs[5:]
    if comm:
        (mine, w_ada), refs = refs[:2], refs[2:]
    else:
        (mod_in,), refs = refs[:1], refs[1:]
    given, refs = dict(zip(WEIGHTS, refs[:7])), refs[7:]
    (layer_out, dcross_out, qkv_out, h1_out, mixed1_out, h2_out, q2_out, mixed2_out), refs = (
        refs[:8],
        refs[8:],
    )
    (memory_out, after_out), refs = refs[:2], refs[2:]
    kept_out, refs = dict(zip(BACK, refs[:5])), refs[5:]
    (stats_out, fc1_out, fc2_out, sums_fc1, sums_fc2), refs = refs[:5], refs[5:]
    (rows_sent, mod_sent, conditions_sent), refs = refs[:3], refs[3:]
    held, refs = dict(zip(WEIGHTS, refs[:7])), refs[7:]
    big, wide, h3, db3, memory, after_self, upstream_sum, branch_2, after_cross, result = refs[:10]
    refs = refs[10:]
    lat, text, og, stats, split_stats, frame_marks, text_marks, sems = refs[:8]
    rows_out, mod, conditions = refs[8:11]
    refs = refs[11:]
    loads = Loads(sems)
    loads.start("lat", lat_in, lat)
    loads.start("text", text_in, text)
    loads.start("og", og_in, og)
    slots, model = lat.shape
    inner_width = held[FC1].shape[-1]
    head = model // HEADS
    size = row_tile(slots)
    if comm:
        dp_size, fsdp_size = comm
        (everybody, partial, modulations, ada_sems), refs = refs[:4], refs[4:]
        (ada_block, ada_wide, turned), refs = refs[:3], refs[3:]
        own, refs = dict(zip(WEIGHTS, refs[:7])), refs[7:]
        swapped, refs = dict(zip(WEIGHTS, refs[:7])), refs[7:]
        gather_sems, refs = refs[:3], refs[3:]
        landing, from_first, from_second, from_z, sums = (
            {FC1: refs[2 * k], FC2: refs[2 * k + 1]} for k in range(5)
        )
        reduce_sems = refs[10:]
        per = held[FC2].shape[3] // PARTS, held[FC1].shape[-1] // 2 // PARTS
        reduce = Reduce(
            place(),
            {FC1: held[FC1], FC2: held[FC2]},
            {},
            landing,
            from_first,
            from_second,
            from_z,
            sums,
            None,
            part_items(*per, EARLY, 0),
            (*reduce_sems, None),
        )
        items = gather_items(held)
        gather = Gather(place(), given, held, own, swapped, items, gather_sems)
        order = [WEIGHTS.index(n) for n in dict.fromkeys(item.name for item in items)]
        barrier = pltpu.get_barrier_semaphore()

        def greet_one(step, target, me):
            pl.semaphore_signal(
                barrier,
                inc=1,
                device_id={"dp": target // fsdp_size, "fsdp": target % fsdp_size},
                device_id_type=MESH,
            )

        everyone(dp_size, fsdp_size, greet_one)
        loads.start("w_ada", w_ada, ada_block)
        for number in order:
            name = WEIGHTS[number]
            loads.start("w" + name, given[name], turned if name == FC2 else own[name])
        mark_keys(frame_marks, frame_len[0])
        mark_keys(text_marks, text_len[0])
        big[slots:, :] = jnp.zeros((big.shape[0] - slots, big.shape[1]), BF16)
        stats[...] = jnp.zeros_like(stats)
        loads.wait("w_ada")
        blank = jnp.zeros((ada_block.shape[0], ada_wide.shape[1] - ada_block.shape[1]), BF16)
        ada_wide[0 : ada_block.shape[0], :] = jnp.where(
            gather.core == 0,
            jnp.concatenate([ada_block[...], blank], 1),
            jnp.concatenate([blank, ada_block[...]], 1),
        )
        ada_wide[ada_block.shape[0] :, :] = jnp.zeros(
            (ada_wide.shape[0] - ada_block.shape[0], ada_wide.shape[1]), BF16
        )
        loads.wait(*["w" + name for name in WEIGHTS])
        own[FC2][...] = turned[...].T
        pl.semaphore_wait(barrier, dp_size * fsdp_size - 1)
        for number in order:
            gather.swap(number).start()
        dp_index = lax.axis_index("dp")
        me = dp_index * fsdp_size + lax.axis_index("fsdp")
        send_1 = modulate_start(dp_size, fsdp_size, mine, everybody, ada_sems.at[0])
        send_2 = modulate_start(dp_size, fsdp_size, partial, modulations, ada_sems.at[1])
        everyone(dp_size, fsdp_size, lambda s, t, m: send_1(s, t, m, t // fsdp_size).start())
        everybody[me] = mine[dp_index]
        gather.assemble(WEIGHTS.index(QKV))
        gather.up_to(0, 2)
        everyone(dp_size, fsdp_size, lambda s, t, m: send_1(s, t, m, t // fsdp_size).wait_recv())
        for k in range(dp_size * fsdp_size):
            conditions[k : k + 1, :] = everybody[k]
        product = dot(conditions[...].astype(BF16), ada_wide[...])
        for k in range(dp_size * fsdp_size):
            partial[k] = product[k : k + 1, :]
        everyone(dp_size, fsdp_size, lambda s, t, m: send_2(s, t, m, t).start())
        modulations[me] = partial[me]
        for number in order[1:]:
            gather.assemble(number)
        gather.advance(3, 1, 1)
        everyone(dp_size, fsdp_size, lambda s, t, m: send_2(s, t, m, t).wait_recv())
        mod[...] = jnp.zeros_like(mod)
        span = partial.shape[-1]
        for j in range(fsdp_size):
            total = modulations[j]
            for i in range(1, dp_size):
                total += modulations[i * fsdp_size + j]
            start = j * mod.shape[1] // fsdp_size // 128 * 128
            mod[:, start : start + span] += total
    else:
        mod[...] = mod_in[...]
        conditions[...] = jnp.zeros_like(conditions)
        for name in WEIGHTS:
            loads.start(name, given[name], held[name])

    def need(name, part=None):
        if not comm:
            if not part:
                loads.wait(name)
            return
        numbers = gather.numbers(name)
        gather.need(numbers if part is None else [numbers[part]])

    def hook(p, plan):
        if comm:
            for at, steps in plan:

                @pl.when(p == at)
                def _():
                    gather.advance(steps)

    def step_to(steps):
        if comm:
            gather.advance(steps)

    def row(k):
        return mod[:, k * model : (k + 1) * model]

    loads.start("mod", mod, mod_sent)
    loads.start("cond", conditions, conditions_sent)
    if not comm:
        mark_keys(frame_marks, frame_len[0])
        mark_keys(text_marks, text_len[0])
        big[slots:, :] = jnp.zeros((big.shape[0] - slots, big.shape[1]), BF16)
        stats[...] = jnp.zeros_like(stats)
    loads.wait("lat", "text", "og")

    def norm_1(rows):
        normed, _ = normalize(lat[rows, :].astype(F32))
        wide[rows, 0:model] = (normed * (1.0 + row(1)) + row(0)).astype(BF16)

    tiles(slots, size, norm_1)
    if comm:
        gather.advance(5, 1)
    need(QKV)

    def project_part(columns):
        def project(rows):
            big[rows, columns] = dot(
                wide[rows, 0:model], flat(held[QKV][:, :, :, :, columns])
            ).astype(BF16)

        tiles(slots, size, project)

    tiles(3 * model, model, project_part)
    loads.start("qkv_out", big.at[0:slots, 0 : 3 * model], qkv_out)
    loads.start("h1_out", wide.at[:, 0:model], h1_out)
    if comm:
        loads.start("kept_qkv", held[QKV], kept_out[QKV])
    pair = attend(
        (big, 0),
        (big, model),
        (big, 2 * model),
        frame_marks,
        (wide, model),
        (stats, 0),
        head,
        size,
    )

    def pair_1(p, carry):
        hook(p, ((0, 6), (1, 7), (3, 8), (4, 9), (5, 10)))
        return pair(p, carry)

    lax.fori_loop(0, HEADS // 2, pair_1, 0)
    loads.start("mixed1_out", wide.at[:, model : 2 * model], mixed1_out)
    need(OUT)
    need(CQ)

    def join_1(rows):
        branch = dot(wide[rows, model : 2 * model], flat(held[OUT][...]))
        after = lat[rows, :].astype(F32) + row(2) * branch
        after_self[rows, :] = after
        normed, _ = normalize(after)
        hidden = (normed * (1.0 + row(4)) + row(3)).astype(BF16)
        wide[rows, 2 * model : 3 * model] = hidden
        wide[rows, 3 * model : 4 * model] = dot(hidden, flat(held[CQ][...])).astype(BF16)

    tiles(slots, size, join_1)
    loads.start("after_out", after_self, after_out)
    loads.start("h2_out", wide.at[:, 2 * model : 3 * model], h2_out)
    loads.start("q2_out", wide.at[:, 3 * model : 4 * model], q2_out)
    step_to(11)
    need(CKV)

    def project_text(columns):
        memory[:, columns] = dot(text[...], flat(held[CKV][:, :, :, :, columns])).astype(BF16)

    tiles(2 * model, model, project_text)
    loads.start("memory_out", memory, memory_out)
    mixed2 = big.at[0:slots, 3 * model : 4 * model]
    pair = attend(
        (wide, 3 * model),
        (memory, 0),
        (memory, model),
        text_marks,
        (mixed2, 0),
        (stats, HEADS),
        head,
        size,
    )

    def pair_2(p, carry):
        hook(p, ((0, 12), (3, 13)))
        return pair(p, carry)

    lax.fori_loop(0, HEADS // 2, pair_2, 0)
    loads.start("mixed2_out", mixed2, mixed2_out)
    split_stats[...] = thirds(stats[...], 1.0)
    loads.start("stats_out", split_stats, stats_out)
    need(COUT)

    def join_2(rows):
        branch = dot(mixed2[rows, :], flat(held[COUT][...]))
        branch_2[rows, :] = branch
        after = after_self[rows, :] + row(5) * branch
        after_cross[rows, :] = after
        normed, _ = normalize(after)
        h3[rows, :] = (normed * (1.0 + row(7)) + row(6)).astype(BF16)
        db3[rows, :] = (row(8) * og[rows, :].astype(F32)).astype(BF16)

    step_to(14)
    tiles(slots, size, join_2)
    if comm:
        for name in BACK[1:]:
            loads.start("kept_" + name, held[name], kept_out[name])
    loads.wait("h1_out", "mixed1_out")
    act, din = wide.at[:, 0:model], wide.at[:, model : 2 * model]
    rows_out[...] = jnp.zeros_like(rows_out)
    first, second = held[FC1], held[FC2]
    width = inner_width // 2 // PARTS
    count = second.shape[3] // PARTS
    lead = second.shape[:3]

    def clear(rows):
        result[rows, :] = jnp.zeros((16, model), F32)
        upstream_sum[rows, :] = jnp.zeros((16, model), F32)

    tiles(slots, 16, clear)

    def at_part(part, bodies):
        for k, body in enumerate(bodies):
            pl.when(part == k)(body)

    arrivals, middles, ends = [], [], []
    for k in range(PARTS):

        def arrive(k=k):
            need(FC2, k)
            need(FC1, k)
            step_to(15 + 2 * k)

        def middle(k=k):
            step_to(16 + 2 * k)
            if k + 1 < PARTS:
                for depth in range(4):
                    gather.up_to(depth, gather.numbers(FC1)[k + 1])

        if comm:
            plans = gather.planned(arrive), gather.planned(middle)

            def emit_arrival(steps=plans[0]):
                for step in steps:
                    gather.emit(step)

            def emit_middle(steps=plans[1], k=k):
                for step in steps:
                    gather.emit(step)
                gather.sent([gather.numbers(name)[k] for name in (FC2, FC1)])
                for step in ((), ((0, 0), (0, 1)), (), ((2, 0), (2, 1)))[k]:
                    reduce.step(*step)

            def emit_end(k=k):
                if k < EARLY:
                    reduce.launch(2 * k)
                    reduce.launch(2 * k + 1)
                for step in ((), (), ((1, 0), (1, 1)), ())[k]:
                    reduce.step(*step)

            arrivals.append(emit_arrival)
            middles.append(emit_middle)
            ends.append(emit_end)
        else:
            arrive()

    def feed_part(part, carry):
        at_part(part, arrivals)
        spans = [
            pl.ds(pl.multiple_of(k * inner_width // 2 + part * width, 128), width) for k in range(2)
        ]
        chunk = pl.ds(pl.multiple_of(part * count, 16), count)

        def feed(rows):
            matrix_1 = jnp.concatenate([flat(first[:, :, :, :, s]) for s in spans], 1)
            matrix_2 = flat(second[:, :, :, chunk, :])
            activated, slope = gelu_pair(dot(h3[rows, :], matrix_1))
            activated = activated.astype(BF16)
            dinner = (dot_nt(db3[rows, :], matrix_2) * slope).astype(BF16)
            act[rows, :] = activated
            din[rows, :] = dinner
            result[rows, :] += dot(activated, matrix_2)
            upstream_sum[rows, :] += dot_nt(dinner, matrix_1)

        tiles(slots, size, feed)
        at_part(part, middles)
        product = dot_tn(act[...], db3[...]).astype(BF16)
        second[:, :, :, chunk, :] = product.reshape(lead + (count, model))
        product = dot_tn(h3[...], din[...]).astype(BF16)
        for k, span in enumerate(spans):
            first[:, :, :, :, span] = product[:, k * width : (k + 1) * width].reshape(
                first.shape[:4] + (width,)
            )
        at_part(part, ends)
        return carry

    lax.fori_loop(0, PARTS, feed_part, 0)
    if comm:
        loads.start("fc2_out", second.at[:, :, :, EARLY * count :, :], fc2_out)
        for k in range(2):
            loads.start(
                "fc1_out" + "b" * k,
                first.at[:, :, :, :, (k * PARTS + EARLY) * width : (k + 1) * PARTS * width],
                fc1_out.at[
                    :, :, :, :, k * (PARTS - EARLY) * width : (k + 1) * (PARTS - EARLY) * width
                ],
            )
    else:
        loads.start("fc2_out", second, fc2_out)
        loads.start("fc1_out", first, fc1_out)

    def leave(rows):
        entering = after_cross[rows, :]
        branch = result[rows, :]
        grad = og[rows, :].astype(F32)
        result[rows, :] = entering + row(8) * branch
        normed, inverse = normalize(entering)
        back, dshift, dscale = norm_back(upstream_sum[rows, :], normed, inverse, row(7))
        dcross = grad + back
        after_cross[rows, :] = dcross
        rows_out[0:1, :] += jnp.sum(grad * branch, 0, keepdims=True)
        rows_out[1:2, :] += dshift[None]
        rows_out[2:3, :] += dscale[None]
        rows_out[3:4, :] += jnp.sum(dcross * branch_2[rows, :], 0, keepdims=True)

    tiles(slots, size, leave)
    loads.start("layer_out", result, layer_out)
    loads.start("rows", rows_out, rows_sent)
    loads.start("dcross_out", after_cross, dcross_out)
    if comm:
        for number in order:
            gather.swap(number).wait_send()
        for name in BACK:
            gather.sent(gather.numbers(name))
            loads.wait("kept_" + name)
        for number in range(2 * EARLY):
            reduce.step(3, number)
        loads.start("sums1", sums[FC1], sums_fc1)
        loads.start("sums2", sums[FC2], sums_fc2)
        everyone(dp_size, fsdp_size, lambda s, t, m: send_1(s, t, m, t // fsdp_size).wait_send())
        everyone(dp_size, fsdp_size, lambda s, t, m: send_2(s, t, m, t).wait_send())
        reduce.sent()
        loads.wait("sums1", "sums2", "fc1_outb")
    loads.wait("qkv_out", "h2_out", "q2_out", "mixed2_out")
    loads.wait("mod", "cond", "rows", "stats_out", "after_out", "memory_out", "layer_out", "dcross_out", "fc1_out", "fc2_out")


def forward(grid, lengths, latent, text_block, upstream, ada, matrices):
    slots, model = latent.shape
    text_slots = text_block.shape[0]
    padded = -(-slots // 128) * 128
    comm = len(ada) > 1
    lead = (4, 2, 2)
    devices = grid.dp * grid.fsdp
    if comm:
        blocks = [m.shape for m in matrices[:6]] + [matrices[6].shape[::-1]]
        wholes = [lead + (b[0] * grid.dp // 16, b[1] * grid.fsdp) for b in blocks]
    else:
        wholes = [m.shape for m in matrices]
    inner_width = wholes[5][-1]
    late_1, late_2 = wholes[5], wholes[6]
    if comm:
        later = PARTS - EARLY
        late_1 = (*late_1[:4], late_1[4] // PARTS * later)
        late_2 = (*late_2[:3], late_2[3] // PARTS * later, late_2[4])
    shaped = jax.ShapeDtypeStruct
    narrow = shaped((slots, model), BF16)
    full = shaped((slots, model), F32)
    outs = [
        full,
        full,
        shaped((slots, 3 * model), BF16),
        narrow,
        narrow,
        narrow,
        narrow,
        narrow,
        shaped((text_slots, 2 * model), BF16),
        full,
    ]
    outs += [shaped(w if comm else (8, 128), BF16) for w in wholes[:5]]
    outs += [
        shaped((slots, 128), BF16),
        shaped(late_1, BF16),
        shaped(late_2, BF16),
        *[shaped((s[3], s[4] // 2) if comm else (8, 128), F32) for s in wholes[5:]],
        shaped((8, model), F32),
        shaped((1, 9 * model), F32),
        shaped((devices, 128), F32),
    ]
    vmem = pl.BlockSpec(memory_space=pltpu.VMEM)
    anywhere = pl.BlockSpec(memory_space=pl.ANY)
    smem = pl.BlockSpec(memory_space=pltpu.SMEM)
    scratch = [pltpu.VMEM(w, BF16) for w in wholes]
    scratch += [
        pltpu.VMEM((padded, 4 * model), BF16),
        pltpu.VMEM((slots, 4 * model), BF16),
    ]
    scratch += [pltpu.VMEM((slots, model), BF16)] * 2
    scratch += [pltpu.VMEM((text_slots, 2 * model), BF16)]
    scratch += [pltpu.VMEM((slots, model), F32)] * 5
    scratch += [
        pltpu.VMEM((slots, model), BF16),
        pltpu.VMEM((text_slots, model), BF16),
        pltpu.VMEM((slots, model), BF16),
        pltpu.VMEM((slots, 128), F32),
        pltpu.VMEM((slots, 128), BF16),
        pltpu.VMEM((padded, 128), BF16),
        pltpu.VMEM((text_slots, 128), BF16),
        pltpu.SemaphoreType.DMA((48,)),
        pltpu.VMEM((8, model), F32),
        pltpu.VMEM((1, 9 * model), F32),
        pltpu.VMEM((devices, 128), F32),
    ]
    if comm:
        items = gather_items(dict(zip(WEIGHTS, [shaped(w, BF16) for w in wholes])))
        rows, columns = ada[1].shape
        span = -(-columns // 128) * 128
        scratch += [
            pltpu.VMEM((devices, 1, 128), F32),
            pltpu.VMEM((devices, 1, span), F32),
            pltpu.VMEM((devices, 1, span), F32),
            pltpu.SemaphoreType.DMA((2, 2, devices - 1)),
            pltpu.VMEM((rows, columns), BF16),
            pltpu.VMEM((128, span), BF16),
            pltpu.VMEM(matrices[6].shape, BF16),
        ]
        scratch += [pltpu.VMEM(b, BF16) for b in blocks]
        scratch += [pltpu.VMEM((b[0] // 2, b[1]), BF16) for b in blocks]
        scratch += [
            pltpu.SemaphoreType.DMA((2, len(matrices))),
            pltpu.SemaphoreType.DMA((len(items), lead[0] + 4)),
            pltpu.SemaphoreType.DMA((len(items), lead[0] + 4)),
        ]
        early = [
            (*wholes[5][:4], wholes[5][4] // PARTS * EARLY),
            (*wholes[6][:3], wholes[6][3] // PARTS * EARLY, wholes[6][4]),
        ]
        scratch += reduce_scratch(early, lead[0])
        scratch += [pltpu.VMEM((s[3], s[4] // 2), F32) for s in wholes[5:]]
        scratch += [pltpu.SemaphoreType.DMA((2 * EARLY, lead[0] + 4))] * 2
    params = {"vmem_limit_bytes": 63 * 1024 * 1024}
    if comm:
        params.update(collective_id=0, has_side_effects=True)
    results = pl.pallas_call(
        functools.partial(forward_kernel, (grid.dp, grid.fsdp) if comm else None),
        out_shape=outs,
        in_specs=[smem] * 2 + [anywhere] * 3 + [vmem] + [anywhere] * (6 + len(ada)),
        out_specs=[anywhere] * 23,
        scratch_shapes=scratch,
        compiler_params=pltpu.CompilerParams(**params),
        name="forward",
    )(*lengths, latent, text_block, upstream, *ada, *matrices)
    kept_matrices = results[10:15] if comm else matrices[:5]
    return results[0], (*results[1:10], results[15]), kept_matrices, results[16:]


BACK = (QKV, OUT, CQ, CKV, COUT)


EARLY = 1


def part_items(rows, width, parts, before):
    items = []
    for part in range(parts):
        items += [
            Item(FC2, (part * rows, rows), summed=(before * rows, 0)),
            Item(FC1, None, part * width, width, summed=(0, before * width)),
        ]
    return items


def reduce_items(shapes):
    parts = PARTS - EARLY
    items = part_items(shapes[FC2][3] // parts, shapes[FC1][-1] // 2 // parts, parts, EARLY)
    items += [Item(COUT)]
    width = shapes[CKV][-1] // 4
    items += [Item(CKV, None, k * width, width) for k in range(2)]
    items += [Item(CQ), Item(OUT)]
    model = shapes[QKV][-1] // 3
    third, half = model // 3, model // 2
    items += [
        Item(QKV, None, (0, half), third, 0),
        Item(QKV, None, (2 * third, half + 2 * third), third, third),
        Item(QKV, None, (model, 2 * third - half), third, 2 * third),
        Item(QKV, None, (third, half + third), third, model),
        Item(QKV, None, (model + third, 0), third // 2, model + third),
    ]
    return items


class Reduce:
    def __init__(self, where, sources, kept, landing, first, second, along, sums, owned, items, sems):
        self.z, self.y, self.x, self.core = where
        self.sources, self.kept, self.landing = sources, kept, landing
        self.from_first, self.from_second, self.from_z = first, second, along
        self.sums, self.owned, self.items = sums, owned, items
        self.send_sem, self.recv_sem, self.last_sem = sems
        self.nz = sources[FC2].shape[0]
        self.counts = [0, 0, 0, 0]
        z, y, x, core = where
        self.sibling = device(z, y, x, 1 - core)
        self.first = device(
            z, (1 - y) * (1 - core) + y * core, x * (1 - core) + (1 - x) * core, core
        )
        self.second = device(
            z, y * (1 - core) + (1 - y) * core, (1 - x) * (1 - core) + x * core, core
        )
        self.done = 0

    def remote(self, number, slot, src, dst, partner):
        return pltpu.make_async_remote_copy(
            src_ref=src,
            dst_ref=dst,
            send_sem=self.send_sem.at[number, slot],
            recv_sem=self.recv_sem.at[number, slot],
            device_id=partner,
            device_id_type=MESH,
        )

    def rows(self, number, offset=0):
        item = self.items[number]
        height = self.sources[item.name].shape[3]
        start, size = (0, height) if item.rows is None else item.rows
        return pl.ds(start + offset, size)

    def columns(self, number, which):
        item = self.items[number]
        return half_columns(self.sources[item.name], which, item.first, item.width)

    def inside(self, number):
        item = self.items[number]
        width = self.sources[item.name].shape[-1] // 2 if item.width is None else item.width
        return pl.ds(item.slot, width)

    def landed(self, number, which):
        item = self.items[number]
        half = self.landing[item.name].shape[-1] // 2
        return pl.ds(which * half + item.slot, half if item.width is None else item.width)

    def stay(self, number):
        name = self.items[number].name
        if name in self.kept:
            return self.kept[name], ()
        return self.sources[name], (self.core,)

    def kept_at(self, number, a, b, columns):
        ref, extra = self.stay(number)
        return ref.at[(a, b, *extra, self.rows(number), columns)]

    def to_core(self, number):
        item = self.items[number]
        landing = self.landing[item.name]
        copies = []
        for k in range(2):
            columns = self.columns(number, k)
            src = self.sources[item.name].at[:, :, 1 - self.core, self.rows(number), columns]
            dst = landing.at[:, :, self.rows(number), self.landed(number, k)]
            copies.append(self.remote(number, self.nz + 2 + k, src, dst, self.sibling))
        return copies

    def to_first(self, number):
        copies = []
        for k in range(2):
            row = (1 - self.y) * (1 - self.core) + k * self.core
            column = k * (1 - self.core) + (1 - self.x) * self.core
            src = self.kept_at(number, slice(None), row, self.columns(number, column))
            dst = self.from_first[self.items[number].name].at[
                :, k, self.rows(number), self.inside(number)
            ]
            copies.append(self.remote(number, self.nz + k, src, dst, self.first))
        return copies

    def to_second(self, number):
        row = self.y * (1 - self.core) + (1 - self.y) * self.core
        column = (1 - self.x) * (1 - self.core) + self.x * self.core
        src = self.kept_at(number, slice(None), row, self.columns(number, column))
        dst = self.from_second[self.items[number].name].at[
            :, self.rows(number), self.inside(number)
        ]
        return [self.remote(number, self.nz - 1, src, dst, self.second)]

    def to_z(self, number):
        copies = []
        for step in range(1, self.nz):
            other = (self.z + step) % self.nz
            src = self.kept_at(number, other, self.y, self.columns(number, self.x))
            dst = self.from_z[self.items[number].name].at[
                step - 1, self.rows(number), self.inside(number)
            ]
            partner = device(other, self.y, self.x, self.core)
            copies.append(self.remote(number, step - 1, src, dst, partner))
        return copies

    def add_core(self, number):
        landing = self.landing[self.items[number].name]
        for k in range(2):
            columns = self.columns(number, k)
            rows, landed = self.rows(number), self.landed(number, k)

            def one(step, carry):
                a, b = step // 2, step % 2
                spot = self.kept_at(number, a, b, columns)
                spot[...] = spot[...] + landing[a, b, rows, landed]
                return carry

            lax.fori_loop(0, self.nz * 2, one, 0)

    def add_first(self, number):
        arrived = self.from_first[self.items[number].name]
        rows, inside = self.rows(number), self.inside(number)
        for k in range(2):
            row = self.y * (1 - self.core) + k * self.core
            columns = self.columns(number, k * (1 - self.core) + self.x * self.core)

            def one(a, carry):
                spot = self.kept_at(number, a, row, columns)
                spot[...] = spot[...] + arrived[a, k, rows, inside]
                return carry

            lax.fori_loop(0, self.nz, one, 0)

    def add_second(self, number):
        arrived = self.from_second[self.items[number].name]
        rows, inside = self.rows(number), self.inside(number)
        columns = self.columns(number, self.x)

        def one(a, carry):
            spot = self.kept_at(number, a, self.y, columns)
            spot[...] = spot[...] + arrived[a, rows, inside]
            return carry

        lax.fori_loop(0, self.nz, one, 0)

    def add_z(self, number):
        name = self.items[number].name
        arrived = self.from_z[name]
        rows, inside = self.rows(number), self.inside(number)
        total = self.kept_at(number, self.z, self.y, self.columns(number, self.x))[...].astype(F32)
        for step in range(self.nz - 1):
            total += arrived[step, rows, inside].astype(F32)
        item = self.items[number]
        down, along = item.summed
        start = item.first[0] + self.x * (item.first[1] - item.first[0]) + along
        self.sums[name][
            self.rows(number, down), pl.ds(pl.multiple_of(start, 128), total.shape[1])
        ] = total
        if self.owned and number == max(i for i, item in enumerate(self.items) if item.name == name):
            self.share(name)

    def last(self, name):
        number = WEIGHTS.index(name)
        staged, owned = self.sums[name + "_sent"], self.owned[name]
        rows = staged.shape[0]
        return pltpu.make_async_remote_copy(
            src_ref=staged,
            dst_ref=owned.at[pl.ds(pl.multiple_of(self.core * rows, 16), rows), :],
            send_sem=self.last_sem.at[0, number],
            recv_sem=self.last_sem.at[1, number],
            device_id=self.sibling,
            device_id_type=MESH,
        )

    def share(self, name):
        total = self.sums[name][...]
        rows, width = total.shape
        left, right = total[:, : width // 2], total[:, width // 2 :]
        if name == FC1:
            step = width // 8 // PARTS
            left, right = (
                jnp.concatenate(
                    [
                        total[:, start : start + step]
                        for k in range(4)
                        for part in range(PARTS)
                        for start in [((part * 2 + side) * 4 + k) * step]
                    ],
                    1,
                )
                for side in range(2)
            )
        start = pl.multiple_of(self.core * rows, 16)
        self.owned[name][pl.ds(start, rows), :] = jnp.where(self.core == 0, left, right)
        self.sums[name + "_sent"][...] = jnp.where(self.core == 0, right, left)
        self.last(name).start()

    def launch(self, number):
        for copy in self.to_core(number):
            copy.start()

    def step(self, depth, number):
        stages = [self.to_core, self.to_first, self.to_second, self.to_z]
        adds = [self.add_core, self.add_first, self.add_second, self.add_z]
        for copy in stages[depth](number):
            copy.wait_recv()
        adds[depth](number)
        if depth < 3:
            for copy in stages[depth + 1](number):
                copy.start()

    def up_to(self, depth, number):
        while self.counts[depth] <= min(number, len(self.items) - 1):
            self.step(depth, self.counts[depth])
            self.counts[depth] += 1

    def targets(self, numbers):
        for depth, number in enumerate(numbers):
            self.up_to(depth, number)

    def advance(self, steps):
        while self.done < steps:
            lag = 2
            for depth in range(4):
                self.up_to(depth, self.done - depth * lag)
            self.done += 1

    def numbers(self, name):
        return [i for i, item in enumerate(self.items) if item.name == name]

    def sent(self):
        for number in range(len(self.items)):
            for stage in (self.to_core, self.to_first, self.to_second, self.to_z):
                for copy in stage(number):
                    copy.wait_send()

    def finish(self):
        count = len(self.items)
        self.up_to(0, count)
        for number in range(count + 2):
            for depth in range(1, 4):
                self.up_to(depth, number - depth + 1)
        for name in dict.fromkeys(item.name for item in self.items):
            self.last(name).wait()
        self.sent()


def reduce_scratch(shapes, nz):
    scratch = [pltpu.VMEM((nz, 2, s[3], s[4]), BF16) for s in shapes]
    scratch += [pltpu.VMEM((nz, 2, s[3], s[4] // 2), BF16) for s in shapes]
    scratch += [pltpu.VMEM((nz, s[3], s[4] // 2), BF16) for s in shapes]
    scratch += [pltpu.VMEM((nz - 1, s[3], s[4] // 2), BF16) for s in shapes]
    return scratch


def backward_kernel(comm, *refs):
    (frame_len, text_len, mod_in, rows_3_in, lat_in, text_in), refs = refs[:6], refs[6:]
    names = (
        "dcross",
        "qkv_act",
        "h1",
        "mixed1",
        "h2",
        "q2",
        "mixed2",
        "memory",
        "after",
        "stats",
    )
    given, refs = dict(zip(names, refs[:10])), refs[10:]
    matrices, refs = dict(zip(BACK, refs[:5])), refs[5:]
    if comm:
        (grad_fc1, grad_fc2, sums_fc1, sums_fc2), refs = refs[:4], refs[4:]
    (latent_out, text_sent), refs = refs[:2], refs[2:]
    if comm:
        everybody_sent, refs = refs[0], refs[1:]
        owned_sent, refs = dict(zip(WEIGHTS, refs[:7])), refs[7:]
    else:
        rows_out, refs = refs[0], refs[1:]
        grads_out, refs = dict(zip(BACK, refs[:5])), refs[5:]
    (dcross, packed, hidden, mixed, q2, memory, after), refs = refs[:7], refs[7:]
    text, stats, means, frame_marks, text_marks, query_sum, lanes = refs[:7]
    mod, rows_3, text_out = refs[7:10]
    refs = refs[10:]
    held, refs = dict(zip(BACK, refs[:5])), refs[5:]
    grad_qkv, above, sems = refs[:3]
    refs = refs[3:]
    slots, model = dcross.shape
    lat = above.at[0]
    head = model // HEADS
    size = row_tile(slots)
    loads = Loads(sems)
    act = {
        "dcross": dcross,
        "mixed2": mixed,
        "q2": q2,
        "memory": memory,
        "h2": hidden,
        "stats": stats,
        "after": after,
    }
    grads = dict(held, qkv=grad_qkv)
    if comm:
        dp_size, fsdp_size = comm
        (rows_out, dmod, pieces, ada_sems, fc2_rows), refs = refs[:5], refs[5:]
        owned, refs = dict(zip(WEIGHTS, refs[:6])), refs[6:]
        turned, everybody, refs = refs[0], refs[1], refs[2:]
        owned[FC2] = fc2_rows
        kept, refs = {FC2: refs[0], FC1: refs[1]}, refs[2:]
        landing, refs = dict(zip(WEIGHTS, refs[:7])), refs[7:]
        first, refs = dict(zip(WEIGHTS, refs[:7])), refs[7:]
        second, refs = dict(zip(WEIGHTS, refs[:7])), refs[7:]
        along, refs = dict(zip(WEIGHTS, refs[:7])), refs[7:]
        sums, refs = dict(zip(WEIGHTS, refs[:7])), refs[7:]
        sums.update(zip([name + "_sent" for name in WEIGHTS], refs[:7]))
        refs = refs[7:]
        reduce_sems = refs[:3]
        sources = dict(grads, fc1=grad_fc1, fc2=grad_fc2)
        items = reduce_items({name: ref.shape for name, ref in sources.items()})
        reduce = Reduce(
            place(), sources, kept, landing, first, second, along, sums, owned, items, reduce_sems
        )
        core = reduce.core
    loads.start("mod", mod_in, mod)
    loads.start("rows", rows_3_in, rows_3)
    loads.start("wcout", matrices[COUT], held[COUT])
    for name in ("dcross", "mixed2", "q2", "memory", "stats"):
        loads.start(name, given[name], act[name])
    if comm:
        barrier = pltpu.get_barrier_semaphore()

        def greet_one(step, target, me):
            pl.semaphore_signal(
                barrier,
                inc=1,
                device_id={"dp": target // fsdp_size, "fsdp": target % fsdp_size},
                device_id_type=MESH,
            )

        everyone(dp_size, fsdp_size, greet_one)
        pl.semaphore_wait(barrier, dp_size * fsdp_size - 1)
        for name in (FC2, FC1):
            for number in reduce.numbers(name):
                reduce.launch(number)
        for name, source in ((FC2, grad_fc2), (FC1, grad_fc1)):
            loads.start("keep_" + name, source.at[:, :, core], kept[name])
        for name, source in ((FC2, sums_fc2), (FC1, sums_fc1)):
            loads.start("s" + name, source, sums[name])
    for name in (CQ, CKV, OUT, QKV):
        loads.start("w" + name, matrices[name], held[name])
    for name in ("h2", "after"):
        loads.start(name, given[name], act[name])
    loads.start("text", text_in, text)
    loads.start("qkv_act", given["qkv_act"], packed.at[0:slots, :])

    def advance(steps):
        if comm:
            reduce.advance(steps)

    def hook(p, plan):
        if comm:
            for at, steps in plan:

                @pl.when(p == at)
                def _():
                    if isinstance(steps, tuple):
                        reduce.targets(steps)
                    else:
                        reduce.advance(steps)

    def row(k):
        return mod[:, k * model : (k + 1) * model]

    def place_grad(name, columns, left, right):
        target = grads[name]
        product = dot_tn(left, right).astype(BF16)
        target[:, :, :, :, columns] = product.reshape(target.shape[:4] + (-1,))

    def ready(name):
        if not comm:
            loads.start("g" + name, grads[name], grads_out[name])
            return
        for number in reduce.numbers(name):
            reduce.launch(number)

    rows_out[...] = jnp.zeros_like(rows_out)
    mark_keys(frame_marks, frame_len[0])
    mark_keys(text_marks, text_len[0])
    loads.wait("dcross", "wcout", "mod", "rows")

    def enter_2(rows):
        small = (row(5) * dcross[rows, :]).astype(BF16)
        above[0, rows, :] = small
        upstream = dot_nt(small, flat(held[COUT][...])).astype(BF16)
        above[1, rows, :] = upstream
        means[rows, :] = thirds(head_sums(upstream, mixed[rows, :], lanes[...]), 0.0)

    loads.wait("mixed2")
    lanes[...] = head_lanes(model, HEADS)
    tiles(slots, size, enter_2)
    place_grad(COUT, slice(0, model), mixed[...], above[0])
    ready(COUT)
    loads.wait("q2", "memory", "stats")
    if comm:
        loads.wait("keep_fc2", "keep_fc1", "sfc2", "sfc1")
    advance(1)
    pair = attend_back(
        (q2, 0),
        (memory, 0),
        (memory, model),
        text_marks,
        above.at[1],
        means,
        (stats, HEADS),
        query_sum,
        head,
        memory.shape[0],
    )

    def pair_2(p, carry):
        hook(p, ((1, 2), (3, 3), (5, 4)))
        return pair(p, carry)

    lax.fori_loop(0, HEADS // 2, pair_2, 0)
    loads.start("mixed1", given["mixed1"], mixed)
    loads.wait("wcq", "wckv", "after", "h2", "text")
    text_out[...] = dot_nt(memory[...], flat(held[CKV][...]))
    loads.start("text_out", text_out, text_sent)
    tiles(
        2 * model,
        model,
        lambda columns: place_grad(CKV, columns, text[...], memory[:, columns]),
    )
    ready(CKV)
    loads.wait("wout")
    advance(5)

    def leave_2(rows):
        upstream = dot_nt(q2[rows, :], flat(held[CQ][...]))
        normed, inverse = normalize(after[rows, :])
        back, dshift, dscale = norm_back(upstream, normed, inverse, row(4))
        dself = dcross[rows, :] + back
        dcross[rows, :] = dself
        rows_out[0:1, :] += dshift[None]
        rows_out[1:2, :] += dscale[None]
        branch = dot(mixed[rows, :], flat(held[OUT][...]))
        rows_out[2:3, :] += jnp.sum(dself * branch, 0, keepdims=True)
        small = (row(2) * dself).astype(BF16)
        above[0, rows, :] = small
        upstream = dot_nt(small, flat(held[OUT][...])).astype(BF16)
        above[1, rows, :] = upstream
        means[rows, :] = thirds(head_sums(upstream, mixed[rows, :], lanes[...]), 0.0)

    loads.wait("mixed1")
    lanes[...] = head_lanes(model, 0)
    tiles(slots, size, leave_2)
    advance(6)
    place_grad(CQ, slice(0, model), hidden[...], q2[...])
    ready(CQ)
    loads.start("h1", given["h1"], hidden)
    place_grad(OUT, slice(0, model), mixed[...], above[0])
    ready(OUT)
    loads.start("lat", lat_in, lat)
    advance(7)
    loads.wait("qkv_act")
    packed[slots:, :] = jnp.zeros((packed.shape[0] - slots, 3 * model), BF16)
    place_in_loop = []
    pairs = HEADS // 2

    def tile_hook(t):
        plan = []
        for j in range(pairs):
            late = j // 4
            plan += [
                (2 * j, (6 + j, 4 + j + late, 2 + j + late, j)),
                (2 * j + 1, (7 + j, 5 + j + late, 3 + j + late, 1 + j)),
            ]
        hook(2 * place_in_loop[-1] + t, plan)

    pair = attend_back(
        (packed, 0),
        (packed, model),
        (packed, 2 * model),
        frame_marks,
        above.at[1],
        means,
        (stats, 0),
        query_sum,
        head,
        packed.shape[0] // 2,
        tile_hook,
    )

    third, half = model // 3, 3 * model // 2

    def grad_columns(*starts, width):
        spans = [slice(start, start + width) for start in starts]
        product = dot_tn(
            hidden[...], jnp.concatenate([packed[0:slots, span] for span in spans], 1)
        ).astype(BF16)
        for k, span in enumerate(spans):
            grad_qkv[:, :, :, :, span] = product[:, k * width : (k + 1) * width].reshape(
                grad_qkv.shape[:4] + (width,)
            )

    def launch(part):
        if comm:
            reduce.launch(reduce.numbers(QKV)[part])

    def pair_1(i, carry):
        place_in_loop.append(i)
        group = i // (pairs // 3)
        pair(group * (7 - 3 * group) * pairs // 6 + i % (pairs // 3), carry)

        @pl.when(i == pairs // 3 - 1)
        def _():
            loads.wait("h1")
            grad_columns(0, 2 * model, width=third)
            launch(0)

        @pl.when(i == 2 * pairs // 3 - 1)
        def _():
            grad_columns(2 * third, 2 * model + 2 * third, width=third)
            launch(1)
            grad_columns(model, model + 2 * third, width=third)
            launch(2)

        return carry

    lax.fori_loop(0, pairs, pair_1, 0)
    grad_columns(third, 2 * model + third, width=third)
    launch(3)
    grad_columns(model + third, half, width=third // 2)
    launch(4)
    loads.wait("wqkv", "lat")
    if not comm:
        ready(QKV)

    def leave_1(rows):
        upstream = dot_nt(packed[rows, :], flat(held[QKV][...]))
        normed, inverse = normalize(lat[rows, :].astype(F32))
        back, dshift, dscale = norm_back(upstream, normed, inverse, row(1))
        dcross[rows, :] = dcross[rows, :] + back
        rows_out[3:4, :] += dshift[None]
        rows_out[4:5, :] += dscale[None]


    def leave_step(t, carry):
        hook(t, ((0, (13, 12, 10, 8)), (1, (15, 12, 11, 9)), (2, (15, 13, 12, 10))))
        leave_1(pl.ds(pl.multiple_of(t * last, 16), last))
        return carry

    last = slots // 3
    lax.fori_loop(0, 3, leave_step, 0)
    hook(0, ((0, (15, 14, 13, 11)),))
    loads.start("latent", dcross, latent_out)
    if not comm:
        loads.wait("gcout", "gckv", "gcq", "gout", "gqkv", "latent", "text_out")
        return
    ordered = (
        rows_out[3:4, :],
        rows_out[4:5, :],
        rows_out[2:3, :],
        rows_out[0:1, :],
        rows_out[1:2, :],
        rows_3[3:4, :],
        rows_3[1:2, :],
        rows_3[2:3, :],
        rows_3[0:1, :],
    )
    for k, value in enumerate(ordered):
        dmod[:, k * model : (k + 1) * model] = value.astype(BF16).astype(F32)
    span = pieces.shape[-1]
    for j in range(fsdp_size):
        start = j * dmod.shape[1] // fsdp_size // 128 * 128
        pieces[j] = dmod[:, start : start + span]
    me = lax.axis_index("dp") * fsdp_size + lax.axis_index("fsdp")
    send = modulate_start(dp_size, fsdp_size, pieces, everybody, ada_sems)
    everyone(dp_size, fsdp_size, lambda s, t, m: send(s, t, m, t % fsdp_size).start())
    everybody[me] = pieces[lax.axis_index("fsdp")]
    reduce.finish()
    everyone(dp_size, fsdp_size, lambda s, t, m: send(s, t, m, t % fsdp_size).wait())
    loads.start("all", everybody, everybody_sent)
    for name in WEIGHTS[:6]:
        loads.start("o" + name, owned[name], owned_sent[name])
    turned[...] = fc2_rows[...].T
    loads.start("ofc2", turned, owned_sent[FC2])
    loads.wait("all", "text_out", *["o" + name for name in WEIGHTS])
    loads.wait("latent")


def backward(grid, comm, lengths, latent, text_block, modulation, rest, kept, matrices, ff):
    slots, model = latent.shape
    text_slots = text_block.shape[0]
    padded = -(-slots // 128) * 128
    rows_3 = rest
    devices = grid.dp * grid.fsdp
    shaped = jax.ShapeDtypeStruct
    vmem = pl.BlockSpec(memory_space=pltpu.VMEM)
    anywhere = pl.BlockSpec(memory_space=pl.ANY)
    smem = pl.BlockSpec(memory_space=pltpu.SMEM)
    outs = [shaped((slots, model), F32), shaped((text_slots, model), F32)]
    narrow = pltpu.VMEM((slots, model), BF16)
    full = pltpu.VMEM((slots, model), F32)
    scratch = [
        full,
        pltpu.VMEM((padded, 3 * model), BF16),
        narrow,
        narrow,
        narrow,
        pltpu.VMEM((text_slots, 2 * model), BF16),
        full,
        pltpu.VMEM((text_slots, model), BF16),
        pltpu.VMEM((slots, 128), BF16),
        pltpu.VMEM((slots, 128), BF16),
        pltpu.VMEM((padded, 128), BF16),
        pltpu.VMEM((text_slots, 128), BF16),
        pltpu.VMEM((slots, 128), F32),
        pltpu.VMEM((model, 128), BF16),
        pltpu.VMEM((1, 9 * model), F32),
        pltpu.VMEM((8, model), F32),
        pltpu.VMEM((text_slots, model), F32),
    ]
    scratch += [pltpu.VMEM(m.shape, BF16) for m in matrices]
    scratch += [
        pltpu.VMEM(matrices[0].shape, BF16),
        pltpu.VMEM((2, slots, model), BF16),
        pltpu.SemaphoreType.DMA((48,)),
    ]
    params = {"vmem_limit_bytes": 63 * 1024 * 1024}
    if comm:
        params.update(collective_id=1, has_side_effects=True)
        shapes = dict(zip(WEIGHTS, [m.shape for m in (*matrices, *ff[:2])]))
        wholes = dict(shapes)
        wholes[FC1] = (*shapes[FC1][:4], 2 * ff[2].shape[1])
        wholes[FC2] = (*shapes[FC2][:3], *ff[3].shape[:1], 2 * ff[3].shape[1])
        nz = shapes[OUT][0]
        span = -(-9 * model // grid.fsdp // 128) * 128
        outs += [shaped((devices, 1, span), F32)]
        outs += [shaped((2 * s[3], s[4] // 4), F32) for s in (*wholes.values(),)[:6]]
        outs += [shaped((wholes[FC2][4] // 4, 2 * wholes[FC2][3]), F32)]
        out_specs = [anywhere] * 10
        scratch += [
            pltpu.VMEM((8, model), F32),
            pltpu.VMEM((1, 9 * model), F32),
            pltpu.VMEM((grid.fsdp, 1, span), F32),
            pltpu.SemaphoreType.DMA((2, devices - 1)),
            pltpu.VMEM((2 * wholes[FC2][3], wholes[FC2][4] // 4), F32),
        ]
        scratch += [pltpu.VMEM(o.shape, F32) for o in outs[3:]]
        scratch += [pltpu.VMEM(outs[2].shape, F32)]

        scratch += [pltpu.VMEM((nz, 2, *shapes[name][3:]), BF16) for name in (FC2, FC1)]
        scratch += reduce_scratch(shapes.values(), nz)
        scratch += [pltpu.VMEM((s[3], s[4] // 2), F32) for s in wholes.values()]
        scratch += [pltpu.VMEM((s[3], s[4] // 4), F32) for s in wholes.values()]
        count = len(reduce_items(shapes))
        scratch += [
            pltpu.SemaphoreType.DMA((count, nz + 4)),
            pltpu.SemaphoreType.DMA((count, nz + 4)),
            pltpu.SemaphoreType.DMA((2, 7)),
        ]
    else:
        ff = ()
        outs += [shaped((8, model), F32)]
        outs += [shaped(m.shape, BF16) for m in matrices]
        out_specs = [anywhere, anywhere, vmem] + [anywhere] * 5
    return pl.pallas_call(
        functools.partial(backward_kernel, (grid.dp, grid.fsdp) if comm else None),
        out_shape=outs,
        in_specs=[smem] * 2 + [anywhere] * (19 + len(ff)),
        out_specs=out_specs,
        scratch_shapes=scratch,
        compiler_params=pltpu.CompilerParams(**params),
        name="backward",
    )(
        *lengths,
        modulation,
        rows_3,
        latent,
        text_block,
        *kept,
        *matrices,
        *ff,
    )


def deliver_kernel(count, conditions, gathered, *refs):
    given, ada_sent, taken = refs[:count], refs[count], refs[count + 1 : 2 * count + 1]
    staged, ada_out, sems = refs[2 * count + 1 : -2], refs[-2], refs[-1]
    inward = [
        pltpu.make_async_copy(src, mid, sems.at[0, k])
        for k, (src, mid) in enumerate(zip(given, staged))
    ]
    outward = [
        pltpu.make_async_copy(mid, dst, sems.at[1, k])
        for k, (mid, dst) in enumerate(zip((*staged, ada_out), (*taken, ada_sent)))
    ]
    for copy in inward:
        copy.start()
    rows, columns = ada_out.shape
    stacked = jnp.concatenate([gathered[k] for k in range(gathered.shape[0])], 0)
    product = dot_tn(conditions[...].astype(BF16), stacked.astype(BF16))[:rows]
    spare = product.shape[1] - columns
    ada_out[...] = jnp.where(
        lax.axis_index("fsdp") % 2 == 0, product[:, :columns], product[:, spare:]
    )
    outward[count].start()
    for before, after in zip(inward, outward):
        before.wait()
        after.start()
    for copy in outward:
        copy.wait()


def deliver(conditions, gathered, shape, results):
    vmem = pl.BlockSpec(memory_space=pltpu.VMEM)
    anywhere = pl.BlockSpec(memory_space=pl.ANY)
    count = len(results)
    return pl.pallas_call(
        functools.partial(deliver_kernel, count),
        out_shape=[jax.ShapeDtypeStruct(shape, F32)]
        + [jax.ShapeDtypeStruct(r.shape, r.dtype) for r in results],
        in_specs=[vmem] * 2 + [anywhere] * count,
        out_specs=[anywhere] * (count + 1),
        scratch_shapes=[pltpu.VMEM(r.shape, r.dtype) for r in results]
        + [pltpu.VMEM(shape, F32), pltpu.SemaphoreType.DMA((2, count + 1))],
        compiler_params=pltpu.CompilerParams(vmem_limit_bytes=63 * 1024 * 1024),
        name="deliver",
    )(conditions, gathered, *results)


def by_part(matrix):
    split = matrix.reshape(*matrix.shape[:-1], 2, 2, 4, PARTS, matrix.shape[-1] // 16 // PARTS)
    return jnp.moveaxis(split, -2, -4).reshape(matrix.shape)


def from_part(matrix):
    split = matrix.reshape(*matrix.shape[:-1], 2, PARTS, 2, 4, matrix.shape[-1] // 16 // PARTS)
    return jnp.moveaxis(split, -4, -2).reshape(matrix.shape)


def body(
    latents,
    text_rows,
    out_grad,
    frame_len,
    text_len,
    timestep,
    w_ada,
    w_qkv,
    w_out,
    w_cq,
    w_ckv,
    w_cout,
    w_fc1,
    w_fc2,
    *,
    dp_size,
    fsdp_size,
):
    grid = Grid(dp_size, fsdp_size)
    matrices = (w_qkv, w_out, w_cq, w_ckv, w_cout, w_fc1, w_fc2)
    lengths = (frame_len, text_len)
    if grid.fits(matrices):
        ada = ada_inputs(grid, timestep, w_ada)
        matrices = (*matrices[:6], w_fc2.T)
    else:
        *others, full_fc1, full_fc2 = gather_weights(grid, matrices)
        matrices = (*others, by_part(full_fc1), full_fc2)
        conditions, modulation = modulate(grid, timestep, w_ada)
        ada = (modulation.reshape(1, -1),)
    layer_out, kept, kept_matrices, rest = forward(
        grid, lengths, latents[0], text_rows[0], out_grad[0], ada, matrices
    )
    grad_fc1, grad_fc2, sums_1, sums_2, rows_3, modulation, rows = rest
    comm = len(ada) > 1
    results = backward(
        grid,
        comm,
        lengths,
        latents[0],
        text_rows[0],
        modulation,
        rows_3,
        kept,
        kept_matrices,
        (grad_fc1, grad_fc2, sums_1, sums_2),
    )
    latent_grad, text_grad, rows_1 = results[:3]
    if comm:
        results = (layer_out, latent_grad, text_grad, *results[3:])
        grad_ada, layer_out, latent_grad, text_grad, *owned, fc2 = deliver(
            rows, rows_1, w_ada.shape, results
        )
        owned = (*owned, fc2.T)
    else:
        order = (
            rows_1[3:4],
            rows_1[4:5],
            rows_1[2:3],
            rows_1[0:1],
            rows_1[1:2],
            rows_3[3:4],
            rows_3[1:2],
            rows_3[2:3],
            rows_3[0:1],
        )
        dmodulation = jnp.concatenate(order, 0).reshape(1, -1).astype(BF16)
        grad_ada = ada_gradient(grid, conditions, dmodulation)
        owned = reduce_gradients(grid, (*results[3:8], from_part(grad_fc1), grad_fc2))
    return (
        layer_out[None],
        latent_grad[None],
        text_grad[None],
        grad_ada,
        *owned,
    )


def solution(mesh):
    placed = (P(("dp", "fsdp"), None, None),) * 3 + (P(("dp", "fsdp")),) * 3 + (P("dp", "fsdp"),) * 8
    return jax.shard_map(
        functools.partial(body, dp_size=mesh.shape["dp"], fsdp_size=mesh.shape["fsdp"]),
        mesh=mesh,
        in_specs=placed,
        out_specs=(P(("dp", "fsdp"), None, None),) * 3 + (P("dp", "fsdp"),) * 8,
        check_vma=False,
    )
```
